32 devices in a mesh: seq: 4 (over x, core), ctx: 8 (over z, y).
Axes of the slice: x: 2, y: 2, z: 4, core: 2. Of those that a mesh axis runs over, the one named last changes fastest.
Arguments:
- tokens: bfloat16 [4, 1024, 1536], P('seq', 'ctx'), may hold values from -6 to 6
- segments: int32 [4, 1024], P('seq'), may hold values from 0 to 2, as said below
- cotangent: bfloat16 [4, 1024, 1536], P('seq', 'ctx'), may hold values from -6 to 6
- query_weight: bfloat16 [2, 1536, 1536], P(None, ('seq', 'ctx')), may hold values from -0.15625 to 0.15625
- key_weight: bfloat16 [2, 1536, 768], P(None, ('seq', 'ctx')), may hold values from -0.15625 to 0.15625
- value_weight: bfloat16 [2, 1536, 768], P(None, ('seq', 'ctx')), may hold values from -0.15625 to 0.15625
- output_weight: bfloat16 [2, 1536, 1536], P(None, ('seq', 'ctx')), may hold values from -1.25 to 1.25
- attention_gain: bfloat16 [2, 1536], P(None, ('seq', 'ctx')), may hold values from 0.5 to 1.5
- gate_weight: bfloat16 [2, 1536, 4096], P(None, ('seq', 'ctx')), may hold values from -0.15625 to 0.15625
- up_weight: bfloat16 [2, 1536, 4096], P(None, ('seq', 'ctx')), may hold values from -0.15625 to 0.15625
- down_weight: bfloat16 [2, 4096, 1536], P(None, ('seq', 'ctx')), may hold values from -0.09375 to 0.09375
- feedforward_gain: bfloat16 [2, 1536], P(None, ('seq', 'ctx')), may hold values from 0.5 to 1.5
Outputs:
- block_output: bfloat16 [4, 1024, 1536], P('seq', 'ctx')
- tokens_gradient: float32 [4, 1024, 1536], P('seq', 'ctx')
- query_gradient: float32 [2, 1536, 1536], P(None, ('seq', 'ctx'))
- key_gradient: float32 [2, 1536, 768], P(None, ('seq', 'ctx'))
- value_gradient: float32 [2, 1536, 768], P(None, ('seq', 'ctx'))
- output_gradient: float32 [2, 1536, 1536], P(None, ('seq', 'ctx'))
- attention_gain_gradient: float32 [2, 1536], P(None, ('seq', 'ctx'))
- gate_gradient: float32 [2, 1536, 4096], P(None, ('seq', 'ctx'))
- up_gradient: float32 [2, 1536, 4096], P(None, ('seq', 'ctx'))
- down_gradient: float32 [2, 4096, 1536], P(None, ('seq', 'ctx'))
- feedforward_gain_gradient: float32 [2, 1536], P(None, ('seq', 'ctx'))
The draws below stay inside these ranges and needn't reach their ends.
Inputs may be any that keep to these rules, and one draw needn't show every extreme that they name: `segments`: segment numbers never fall along a sequence and count its documents from 0. In each aligned group of 1 sequence, one drawn from the seed has three documents, the first and the last of 1 to 127 tokens each. In the others every document but the last of the sequence has 52 to 512 tokens, and one of them has exactly 512.
All inputs are finite; a program needn't handle non-finite values.
Results may differ from the reference program's by a relative error of at most 0.03.
Values may be sent and summed in bfloat16 or wider, within the bound.
A program may use at most 512 MiB of HBM per device.

```python
import math
import jax
import jax.numpy as jnp
from jax import lax

D = 1536
H = 16
KVH = 8
HD = 96
FF = 4096
LAYERS = 2
SEQS = 1
SEG = 128
LEN = 1024
NSEQ = 4
DOCMIN = 52
DOCMAX = 512


def draw_segments(key, part):
    key = jax.random.fold_in(key, 7)
    keys_split = jax.random.split(key, 5)
    lengths = jax.random.randint(keys_split[0], (NSEQ, 20), DOCMIN, DOCMAX + 1, dtype=jnp.int32)
    longest = jax.random.randint(keys_split[1], (NSEQ, 1), 0, 2, dtype=jnp.int32)
    columns = jnp.arange(20, dtype=jnp.int32)
    lengths = jnp.where(columns[None, :] == longest, DOCMAX, lengths)
    doc_ends = jnp.cumsum(lengths, axis=1)
    places = jnp.arange(LEN, dtype=jnp.int32)
    numbers = jnp.sum((doc_ends[:, None, :] <= places[None, :, None]).astype(jnp.int32), axis=2)
    first_len = jax.random.randint(keys_split[3], (NSEQ, 1), 1, SEG, dtype=jnp.int32)
    last_len = jax.random.randint(keys_split[4], (NSEQ, 1), 1, SEG, dtype=jnp.int32)
    three_docs = (places[None, :] >= first_len).astype(jnp.int32) + (places[None, :] >= LEN - last_len).astype(jnp.int32)
    whole_row = jax.random.randint(keys_split[2], (NSEQ // SEQS, 1), 0, SEQS, dtype=jnp.int32)
    rows_within = (jnp.arange(NSEQ, dtype=jnp.int32) % SEQS).reshape(NSEQ // SEQS, SEQS)
    single = (rows_within == whole_row).reshape(NSEQ)
    return jnp.where(single[:, None], three_docs, numbers).astype(jnp.int32)


def block_scale(own_key, dims, cuts, least, high):
    loudness, own = 1.0, jax.random.fold_in(own_key, 6)
    for axis_at, shards_of in cuts:
        draws = jnp.exp(jax.random.uniform(jax.random.fold_in(own, axis_at), (shards_of,), jnp.float32, least / len(cuts), high / len(cuts)))
        loudness = loudness * jnp.repeat(draws, dims[axis_at] // shards_of).reshape([-1 if axis == axis_at else 1 for axis in range(len(dims))])
    return loudness


def bell_draw(key, dims, scale, reach, pieces=(), kind=jnp.bfloat16):
    level = block_scale(key, dims, pieces, -0.22, 0.18) if pieces else 1.0
    array = jax.random.normal(key, dims, jnp.float32) * scale * level
    return jnp.minimum(jnp.maximum(array, -reach), reach).astype(kind)


def setup_inputs(seed: int = 0) -> dict:
    seeds = jax.random.split(jax.random.key(seed), 13)
    return {
        "tokens": bell_draw(seeds[0], (NSEQ, LEN, D), 1.0, 6.0, ((0, 4), (1, 8))),
        "segments": draw_segments(jax.random.fold_in(seeds[12], 71), 0),
        "cotangent": bell_draw(seeds[2], (NSEQ, LEN, D), 1.0, 6.0, ((0, 4), (1, 8))),
        "query_weight": bell_draw(seeds[3], (LAYERS, D, D), D ** -0.5, 0.15625, ((1, 32),)),
        "key_weight": bell_draw(seeds[4], (LAYERS, D, KVH * HD), D ** -0.5, 0.15625, ((1, 32),)),
        "value_weight": bell_draw(seeds[5], (LAYERS, D, KVH * HD), D ** -0.5, 0.15625, ((1, 32),)),
        "output_weight": bell_draw(seeds[6], (LAYERS, D, D), (max(D * 16 // LEN, 1)) ** -0.5, 1.25, ((1, 32),)),
        "attention_gain": jnp.clip(1.0 + 0.1 * jax.random.normal(seeds[7], (LAYERS, D), jnp.float32), 0.5, 1.5).astype(jnp.bfloat16),
        "gate_weight": bell_draw(seeds[8], (LAYERS, D, FF), D ** -0.5, 0.15625, ((1, 32),)),
        "up_weight": bell_draw(seeds[9], (LAYERS, D, FF), D ** -0.5, 0.15625, ((1, 32),)),
        "down_weight": bell_draw(seeds[10], (LAYERS, FF, D), FF ** -0.5, 0.09375, ((1, 32),)),
        "feedforward_gain": jnp.clip(1.0 + 0.1 * jax.random.normal(seeds[11], (LAYERS, D), jnp.float32), 0.5, 1.5).astype(jnp.bfloat16),
    }


@jax.custom_vjp
def low(v):
    return lax.optimization_barrier(v.astype(jnp.bfloat16)).astype(jnp.float32)

@jax.custom_vjp
def low_back(v):
    return v

def low_keep(v):
    return (low(v), None)

def low_pass(kept, grad):
    return (grad,)

def back_keep(v):
    return (v, None)

def back_low(kept, grad):
    return (low(grad),)
low.defvjp(low_keep, low_pass)
low_back.defvjp(back_keep, back_low)
EPSILON = 1e-05
THETA = 100000.0
NEGATIVE = -1e+30

def rms_scale(values):
    return lax.rsqrt(lax.optimization_barrier(jnp.mean(values * values, axis=-1, keepdims=True)) + EPSILON)

def rope_tables(positions, head_width):
    frequency = THETA ** (-(jnp.arange(head_width // 2, dtype=jnp.float32) * 2.0 / head_width))
    angles = positions.astype(jnp.float32)[..., None] * frequency
    return (jnp.cos(angles), jnp.sin(angles))

def rotate(vectors, cosine, sine_table):
    half_width = vectors.shape[-1] // 2
    cos_part = cosine[:, :, None, :]
    sin_part = sine_table[:, :, None, :]
    former = vectors[..., :half_width]
    latter = vectors[..., half_width:]
    return jnp.concatenate([former * cos_part - latter * sin_part, latter * cos_part + former * sin_part], axis=-1)

def doc_positions(segments):
    places = jnp.arange(segments.shape[1], dtype=jnp.int32)
    starts_new = jnp.concatenate([jnp.ones((segments.shape[0], 1), dtype=jnp.bool_), segments[:, 1:] != segments[:, :-1]], axis=1)
    starts = lax.cummax(jnp.where(starts_new, places[None, :], 0), axis=1)
    return places[None, :] - starts

def project(values, matrix):
    return jnp.einsum('sla,ab->slb', values, matrix, precision=lax.Precision.HIGHEST)

def attend(members):
    query_rows, key_rows, value_rows, doc_ids = members
    products = jnp.einsum('igd,jd->igj', query_rows, key_rows, precision=lax.Precision.HIGHEST)
    scores = low_back(products) * (1.0 / math.sqrt(query_rows.shape[-1]))
    places = jnp.arange(query_rows.shape[0], dtype=jnp.int32)
    allowed = (places[None, :] <= places[:, None]) & (doc_ids[None, :] == doc_ids[:, None])
    scores = jnp.where(allowed[:, None, :], scores, NEGATIVE)
    highest = lax.optimization_barrier(jnp.max(scores, axis=-1, keepdims=True))
    log_total = highest + jnp.log(lax.optimization_barrier(jnp.sum(jnp.exp(scores - highest), axis=-1, keepdims=True)))
    weights = jnp.exp(scores - log_total)
    return jnp.einsum('igj,jd->igd', low(weights), value_rows, precision=lax.Precision.HIGHEST)

def reference(tokens, segments, cotangent, query_weight, key_weight, value_weight, output_weight, attention_gain, gate_weight, up_weight, down_weight, feedforward_gain):
    sequences, full_len = segments.shape
    group_size = H // KVH
    positions = doc_positions(segments)
    cosine, sine_table = rope_tables(positions, HD)
    repeated = jnp.repeat(segments, KVH, axis=0)

    def attention(queries, keys_rot, values):
        query_items = queries.reshape(sequences, full_len, KVH, group_size, HD).transpose(0, 2, 1, 3, 4).reshape(sequences * KVH, full_len, group_size, HD)
        key_items = keys_rot.reshape(sequences, full_len, KVH, HD).transpose(0, 2, 1, 3).reshape(sequences * KVH, full_len, HD)
        value_items = values.reshape(sequences, full_len, KVH, HD).transpose(0, 2, 1, 3).reshape(sequences * KVH, full_len, HD)
        mixed = lax.map(jax.checkpoint(attend), (query_items, key_items, value_items, repeated))
        return mixed.reshape(sequences, KVH, full_len, group_size, HD).transpose(0, 2, 1, 3, 4).reshape(sequences, full_len, H * HD)

    def forward(residual, query_all, key_all, value_all, output_all, gain_first, gate_all, up_all, down_all, gain_second):
        for layer_number in range(LAYERS):
            hidden = low(residual * rms_scale(residual) * gain_first[layer_number])
            queries = low(rotate(low_back(project(hidden, query_all[layer_number])).reshape(sequences, full_len, H, HD), cosine, sine_table))
            keys_rot = low(rotate(low_back(project(hidden, key_all[layer_number])).reshape(sequences, full_len, KVH, HD), cosine, sine_table))
            values = low(low_back(project(hidden, value_all[layer_number])))
            attended = low(low_back(attention(queries, keys_rot, values)))
            residual = residual + low_back(project(attended, output_all[layer_number]))
            hidden_mid = low(residual * rms_scale(residual) * gain_second[layer_number])
            gate_pre = low_back(project(hidden_mid, gate_all[layer_number]))
            up_pre = low_back(project(hidden_mid, up_all[layer_number]))
            activated = low(jax.nn.silu(gate_pre) * up_pre)
            residual = residual + low_back(project(activated, down_all[layer_number]))
        return residual
    output, pullback = jax.vjp(forward, tokens.astype(jnp.float32), query_weight.astype(jnp.float32), key_weight.astype(jnp.float32), value_weight.astype(jnp.float32), output_weight.astype(jnp.float32), attention_gain.astype(jnp.float32), gate_weight.astype(jnp.float32), up_weight.astype(jnp.float32), down_weight.astype(jnp.float32), feedforward_gain.astype(jnp.float32))
    gradients = pullback(cotangent.astype(jnp.float32))
    return (output.astype(jnp.bfloat16), gradients[0], gradients[1], gradients[2], gradients[3], gradients[4], gradients[5], gradients[6], gradients[7], gradients[8], gradients[9])
```

```python
import functools
import math

import jax
import jax.numpy as jnp
from jax import lax
from jax.experimental import pallas as pl
from jax.experimental.pallas import tpu as pltpu
from jax.sharding import PartitionSpec as P

H = 16
KVH = 8
HD = 96
GROUP = 4

EPSILON = 1e-05
THETA = 100000.0
NEGATIVE = -1e30
AXES = ("seq", "ctx")
MESH = pl.DeviceIdType.MESH
ANY = pl.BlockSpec(memory_space=pl.ANY)
VMEM = pl.BlockSpec(memory_space=pltpu.VMEM)
BF = jnp.bfloat16
F32 = jnp.float32


def params(collective_id=None):
    if collective_id is None:
        return pltpu.CompilerParams(vmem_limit_bytes=48 * 2**20)
    return pltpu.CompilerParams(
        collective_id=collective_id, has_side_effects=True, vmem_limit_bytes=48 * 2**20
    )


def place():
    s = lax.axis_index("seq")
    k = lax.axis_index("ctx")
    return s // 2, s % 2, k // 2, k % 2


def device(x, c, z, y):
    return (x * 2 + c, z * 2 + y)


def remote(src, dst, send, recv, to):
    return pltpu.make_async_remote_copy(
        src_ref=src, dst_ref=dst, send_sem=send, recv_sem=recv, device_id=to, device_id_type=MESH
    )


def greet(partners):
    barrier = pltpu.get_barrier_semaphore()
    for partner in partners:
        pl.semaphore_signal(barrier, inc=1, device_id=partner, device_id_type=MESH)
    pl.semaphore_wait(barrier, len(partners))


def exchange_kernel(n_slab, n_swap, n_pair, *refs):
    count = n_slab + n_swap + n_pair
    ins, outs = refs[:count], refs[count : 2 * count]
    send, recv, local = refs[2 * count :]
    x, c, z, y = place()
    me = x * 2 + y
    others = [(1 - x, y), (x, 1 - y), (1 - x, 1 - y)]
    barrier = pltpu.get_barrier_semaphore()
    for ox, oy in others:
        pl.semaphore_signal(barrier, inc=1, device_id=device(ox, c, z, oy), device_id_type=MESH)
    crossed = device(x, 1 - c, z, 1 - y)
    if n_swap:

        @pl.when(c != y)
        def _():
            pl.semaphore_signal(barrier, inc=1, device_id=crossed, device_id_type=MESH)
            pl.semaphore_wait(barrier, 4)

        @pl.when(c == y)
        def _():
            pl.semaphore_wait(barrier, 3)

    else:
        pl.semaphore_wait(barrier, 3)

    copies = []
    locals_ = []
    for i in range(n_slab):
        for j, (ox, oy) in enumerate(others):
            copies.append(
                remote(
                    ins[i].at[ox * 2 + oy],
                    outs[i].at[me],
                    send.at[i * 3 + j],
                    recv.at[i * 3 + j],
                    device(ox, c, z, oy),
                )
            )
        locals_.append(pltpu.make_async_copy(ins[i].at[me], outs[i].at[me], local.at[i]))
    base = 3 * n_slab
    for i in range(n_pair):
        at = n_slab + n_swap + i
        copies.append(
            remote(
                ins[at], outs[at].at[x], send.at[base + i], recv.at[base + i], device(1 - x, c, z, y)
            )
        )
        locals_.append(pltpu.make_async_copy(ins[at], outs[at].at[x], local.at[n_slab + i]))
    base += n_pair
    for copy in copies + locals_:
        copy.start()
    for i in range(n_swap):
        at = n_slab + i
        cross = remote(ins[at], outs[at], send.at[base + i], recv.at[base + i], crossed)
        stay = pltpu.make_async_copy(ins[at], outs[at], local.at[n_slab + n_pair + i])

        @pl.when(c != y)
        def _(cross=cross):
            cross.start()

        @pl.when(c == y)
        def _(stay=stay):
            stay.start()

    for i in range(n_swap):
        at = n_slab + i
        cross = remote(ins[at], outs[at], send.at[base + i], recv.at[base + i], crossed)
        stay = pltpu.make_async_copy(ins[at], outs[at], local.at[n_slab + n_pair + i])

        @pl.when(c != y)
        def _(cross=cross):
            cross.wait()

        @pl.when(c == y)
        def _(stay=stay):
            stay.wait()

    for copy in copies + locals_:
        copy.wait()


def exchange(slabs, swaps, pairs, collective_id):
    arrays = list(slabs) + list(swaps) + list(pairs)
    shapes = [jax.ShapeDtypeStruct(a.shape, a.dtype) for a in list(slabs) + list(swaps)]
    shapes += [jax.ShapeDtypeStruct((2,) + a.shape, a.dtype) for a in pairs]
    total = 3 * len(slabs) + len(swaps) + len(pairs)
    return pl.pallas_call(
        functools.partial(exchange_kernel, len(slabs), len(swaps), len(pairs)),
        out_shape=shapes,
        in_specs=[ANY] * len(arrays),
        out_specs=[ANY] * len(arrays),
        scratch_shapes=[
            pltpu.SemaphoreType.DMA((total,)),
            pltpu.SemaphoreType.DMA((total,)),
            pltpu.SemaphoreType.DMA((len(arrays),)),
        ],
        compiler_params=params(collective_id),
        name="exchange",
    )(*arrays)


def gather_kernel(rows, own_ref, out_ref, send, recv, local):
    x, c, z, y = place()
    me, at_x, at_y = x * 2 + y, (1 - x) * 2 + y, x * 2 + 1 - y
    to_x, to_y = device(1 - x, c, z, y), device(x, c, z, 1 - y)
    greet([to_x, to_y])
    half = rows // 2
    low, high = pl.ds(0, half), pl.ds(half, half)
    keep = pltpu.make_async_copy(own_ref, out_ref.at[me], local.at[0])
    x_low = remote(own_ref.at[low], out_ref.at[me, low], send.at[0], recv.at[0], to_x)
    y_high = remote(own_ref.at[high], out_ref.at[me, high], send.at[1], recv.at[1], to_y)
    x_high = remote(own_ref.at[high], out_ref.at[me, high], send.at[2], recv.at[2], to_x)
    y_low = remote(own_ref.at[low], out_ref.at[me, low], send.at[3], recv.at[3], to_y)
    x_low.start()
    y_high.start()
    x_high.start()
    y_low.start()
    keep.start()
    on_y = remote(out_ref.at[at_x, low], out_ref.at[at_x, low], send.at[4], recv.at[4], to_y)
    on_x = remote(out_ref.at[at_y, high], out_ref.at[at_y, high], send.at[5], recv.at[5], to_x)
    x_low.wait_recv()
    on_y.start()
    y_high.wait_recv()
    on_x.start()
    x_high.wait_recv()
    y_low.wait_recv()
    on_y.wait_recv()
    on_x.wait_recv()
    for copy in (x_low, y_high, x_high, y_low, on_y, on_x):
        copy.wait_send()
    keep.wait()


def gather_square(own, collective_id):
    rows = own.shape[0]
    return pl.pallas_call(
        functools.partial(gather_kernel, rows),
        out_shape=jax.ShapeDtypeStruct((GROUP,) + own.shape, own.dtype),
        in_specs=[ANY],
        out_specs=ANY,
        scratch_shapes=[
            pltpu.SemaphoreType.DMA((6,)),
            pltpu.SemaphoreType.DMA((6,)),
            pltpu.SemaphoreType.DMA((1,)),
        ],
        compiler_params=params(collective_id),
        name="gather_square",
    )(own)


def scatter_kernel(rows, part_ref, out_ref, diag, sums, from_x, from_y, send, recv):
    x, c, z, y = place()
    me, at_x, at_y, at_xy = x * 2 + y, (1 - x) * 2 + y, x * 2 + 1 - y, (1 - x) * 2 + 1 - y
    to_x, to_y = device(1 - x, c, z, y), device(x, c, z, 1 - y)
    greet([to_x, to_y])
    half = rows // 2
    low, high = pl.ds(0, half), pl.ds(half, half)
    x_diag = remote(part_ref.at[at_xy, low], diag.at[0], send.at[0], recv.at[0], to_x)
    y_diag = remote(part_ref.at[at_xy, high], diag.at[1], send.at[1], recv.at[1], to_y)
    x_one = remote(part_ref.at[at_x, low], from_x.at[low], send.at[2], recv.at[2], to_x)
    y_one = remote(part_ref.at[at_y, high], from_y.at[high], send.at[3], recv.at[3], to_y)
    x_diag.start()
    y_diag.start()
    x_one.start()
    y_one.start()
    x_two = remote(sums.at[0], from_x.at[high], send.at[4], recv.at[4], to_x)
    y_two = remote(sums.at[1], from_y.at[low], send.at[5], recv.at[5], to_y)
    y_diag.wait_recv()
    sums[0] = (part_ref[at_x, high].astype(F32) + diag[1].astype(F32)).astype(BF)
    x_two.start()
    x_diag.wait_recv()
    sums[1] = (part_ref[at_y, low].astype(F32) + diag[0].astype(F32)).astype(BF)
    y_two.start()
    x_one.wait_recv()
    y_one.wait_recv()
    x_two.wait_recv()
    y_two.wait_recv()
    out_ref[...] = part_ref[me].astype(F32) + from_x[...].astype(F32) + from_y[...].astype(F32)
    for copy in (x_diag, y_diag, x_one, y_one, x_two, y_two):
        copy.wait_send()


def scatter_square(parts, collective_id):
    _, rows, width = parts.shape
    return pl.pallas_call(
        functools.partial(scatter_kernel, rows),
        out_shape=jax.ShapeDtypeStruct((rows, width), F32),
        in_specs=[VMEM],
        out_specs=VMEM,
        scratch_shapes=[
            pltpu.VMEM((2, rows // 2, width), BF),
            pltpu.VMEM((2, rows // 2, width), BF),
            pltpu.VMEM((rows, width), BF),
            pltpu.VMEM((rows, width), BF),
            pltpu.SemaphoreType.DMA((6,)),
            pltpu.SemaphoreType.DMA((6,)),
        ],
        compiler_params=params(collective_id),
        name="scatter_square",
    )(parts)


def climb_kernel(levels, own_ref, out_ref, send, recv, local):
    x, c, z, y = place()
    up = device(x, c, lax.rem(z + 1, levels), y)
    down = device(x, c, lax.rem(z + levels - 1, levels), y)
    barrier = pltpu.get_barrier_semaphore()

    @pl.when(z > 0)
    def _():
        pl.semaphore_signal(barrier, inc=1, device_id=down, device_id_type=MESH)

    keep = pltpu.make_async_copy(own_ref, out_ref.at[z], local.at[0])
    keep.start()

    def hop(distance):
        block = lax.rem(z - distance + levels, levels)
        source = own_ref if distance == 0 else out_ref.at[block]
        return remote(source, out_ref.at[block], send.at[distance], recv.at[distance], up)

    @pl.when(z < levels - 1)
    def _():
        pl.semaphore_wait(barrier, 1)
        hop(0).start()

    for distance in range(1, levels):

        @pl.when(z >= distance)
        def _(distance=distance):
            block = lax.rem(z - distance + levels, levels)
            remote(
                out_ref.at[block], out_ref.at[block], send.at[distance - 1], recv.at[distance - 1], up
            ).wait_recv()

            @pl.when(z < levels - 1)
            def _():
                hop(distance).start()

    for distance in range(levels):

        @pl.when((z >= distance) & (z < levels - 1))
        def _(distance=distance):
            hop(distance).wait_send()

    keep.wait()


def climb(own, levels, collective_id):
    return pl.pallas_call(
        functools.partial(climb_kernel, levels),
        out_shape=jax.ShapeDtypeStruct((levels,) + own.shape, own.dtype),
        in_specs=[ANY],
        out_specs=ANY,
        scratch_shapes=[
            pltpu.SemaphoreType.DMA((levels,)),
            pltpu.SemaphoreType.DMA((levels,)),
            pltpu.SemaphoreType.DMA((1,)),
        ],
        compiler_params=params(collective_id),
        name="climb",
    )(own)


def descend_kernel(levels, part_ref, out_ref, came, sums, send, recv):
    x, c, z, y = place()
    up = device(x, c, lax.rem(z + 1, levels), y)
    down = device(x, c, lax.rem(z + levels - 1, levels), y)
    barrier = pltpu.get_barrier_semaphore()

    @pl.when(z < levels - 1)
    def _():
        pl.semaphore_signal(barrier, inc=1, device_id=up, device_id_type=MESH)

    @pl.when(z > 0)
    def _():
        pl.semaphore_wait(barrier, 1)

    def hop(block):
        return remote(sums.at[block], came.at[block], send.at[block], recv.at[block], down)

    for block in range(levels):

        @pl.when(block <= z)
        def _(block=block):
            @pl.when(z < levels - 1)
            def _():
                hop(block).wait_recv()

        @pl.when(block < z)
        def _(block=block):
            @pl.when(z < levels - 1)
            def _():
                sums[block] = (part_ref[block].astype(F32) + came[block].astype(F32)).astype(BF)

            @pl.when(z == levels - 1)
            def _():
                sums[block] = part_ref[block]

            hop(block).start()

        @pl.when(block == z)
        def _(block=block):
            @pl.when(z < levels - 1)
            def _():
                out_ref[...] = part_ref[block].astype(F32) + came[block].astype(F32)

            @pl.when(z == levels - 1)
            def _():
                out_ref[...] = part_ref[block].astype(F32)

    for block in range(levels):

        @pl.when(block < z)
        def _(block=block):
            hop(block).wait_send()


def descend(parts, collective_id):
    levels = parts.shape[0]
    shape = parts.shape[1:]
    return pl.pallas_call(
        functools.partial(descend_kernel, levels),
        out_shape=jax.ShapeDtypeStruct(shape, F32),
        in_specs=[VMEM],
        out_specs=VMEM,
        scratch_shapes=[
            pltpu.VMEM((levels,) + shape, BF),
            pltpu.VMEM((levels,) + shape, BF),
            pltpu.SemaphoreType.DMA((levels,)),
            pltpu.SemaphoreType.DMA((levels,)),
        ],
        compiler_params=params(collective_id),
        name="descend",
    )(parts)


def dot_nt(a, b):
    return lax.dot_general(a, b, (((1,), (1,)), ((), ())), preferred_element_type=F32)


def dot_tn(a, b):
    return lax.dot_general(a, b, (((0,), (0,)), ((), ())), preferred_element_type=F32)


def two_heads(block, j):
    a = block[:, 2 * j * HD : (2 * j + 1) * HD]
    b = block[:, (2 * j + 1) * HD : (2 * j + 2) * HD]
    return jnp.concatenate([a, b], axis=0)


def visible_keys(z, level, span, row_segs, key_segs):
    rows = lax.broadcasted_iota(jnp.int32, (span, span), 0)
    cols = lax.broadcasted_iota(jnp.int32, (span, span), 1)
    mask = (row_segs == key_segs) & ((cols <= rows) | (level < z))
    return jnp.concatenate([mask, mask], axis=0)


def attend_kernel(span, q_ref, kv_ref, row_ref, key_ref, out_ref, lse_ref):
    z = place()[2]
    scaling = 1.0 / math.sqrt(HD)
    for s in range(2):
        rows = pl.ds(s * span, span)
        row_segs = row_ref[s]
        queries = [two_heads(q_ref[rows, :], j) for j in range(2)]

        def step(level, carry):
            block = kv_ref[level, rows, :]
            mask = visible_keys(z, level, span, row_segs, key_ref[level, s])
            after = []
            for j in range(2):
                top, total, accum = carry[3 * j : 3 * j + 3]
                keys = block[:, j * HD : (j + 1) * HD]
                values = block[:, (2 + j) * HD : (3 + j) * HD]
                scores = dot_nt(queries[j], keys) * scaling
                scores = jnp.where(mask, scores, NEGATIVE)
                new = jnp.maximum(top, jnp.max(scores, axis=-1, keepdims=True))
                scale = jnp.exp(top - new)
                weights = jnp.where(mask, jnp.exp(scores - new), 0.0)
                total = total * scale + jnp.sum(weights, axis=-1, keepdims=True)
                accum = accum * scale + jnp.dot(
                    weights.astype(BF), values, preferred_element_type=F32
                )
                after += [new, total, accum]
            return tuple(after)

        start = (
            jnp.full((2 * span, 1), NEGATIVE, F32),
            jnp.zeros((2 * span, 1), F32),
            jnp.zeros((2 * span, HD), F32),
        )
        done = lax.fori_loop(0, z + 1, step, start + start)
        outs, lses = [], []
        for j in range(2):
            top, total, accum = done[3 * j : 3 * j + 3]
            result = (accum / total).astype(BF)
            wide = jnp.broadcast_to(top + jnp.log(total), (2 * span, 32))
            outs += [result[:span], result[span:]]
            lses += [wide[:span], wide[span:]]
        out_ref[rows, :] = jnp.concatenate(outs, axis=1)
        lse_ref[rows, :] = jnp.concatenate(lses, axis=1)


def attend(q, kv, row_segs, key_segs):
    rows, width = q.shape
    return pl.pallas_call(
        functools.partial(attend_kernel, rows // 2),
        out_shape=[
            jax.ShapeDtypeStruct((rows, width), BF),
            jax.ShapeDtypeStruct((rows, 128), F32),
        ],
        in_specs=[VMEM] * 4,
        out_specs=[VMEM] * 2,
        compiler_params=params(),
        name="attend",
    )(q, kv, row_segs, key_segs)


def attend_back_kernel(
    span, q_ref, kv_ref, row_ref, key_ref, out_ref, lse_ref, back_ref, dq_ref, dkv_ref
):
    z = place()[2]
    scaling = 1.0 / math.sqrt(HD)
    for s in range(2):
        rows = pl.ds(s * span, span)
        row_segs = row_ref[s]
        lse_all = lse_ref[rows, :]
        queries = [two_heads(q_ref[rows, :], j) for j in range(2)]
        backs = [two_heads(back_ref[rows, :], j) for j in range(2)]
        outs = [two_heads(out_ref[rows, :], j) for j in range(2)]
        lse = [
            jnp.concatenate(
                [lse_all[:, 64 * j : 64 * j + 1], lse_all[:, 64 * j + 32 : 64 * j + 33]], axis=0
            )
            for j in range(2)
        ]
        delta = [
            jnp.sum(backs[j].astype(F32) * outs[j].astype(F32), axis=-1, keepdims=True)
            for j in range(2)
        ]

        def step(level, carry):
            block = kv_ref[level, rows, :]
            mask = visible_keys(z, level, span, row_segs, key_ref[level, s])
            dks, dvs, sums = [], [], []
            for j in range(2):
                keys = block[:, j * HD : (j + 1) * HD]
                values = block[:, (2 + j) * HD : (3 + j) * HD]
                scores = dot_nt(queries[j], keys) * scaling
                probs = jnp.where(mask, jnp.exp(scores - lse[j]), 0.0)
                dprobs = dot_nt(backs[j], values)
                dscores = (probs * (dprobs - delta[j]) * scaling).astype(BF)
                sums.append(carry[j] + jnp.dot(dscores, keys, preferred_element_type=F32))
                dks.append(dot_tn(dscores, queries[j]).astype(BF))
                dvs.append(dot_tn(probs.astype(BF), backs[j]).astype(BF))
            dkv_ref[level, rows, :] = jnp.concatenate(dks + dvs, axis=1)
            return tuple(sums)

        sums = lax.fori_loop(
            0, z + 1, step, tuple(jnp.zeros((2 * span, HD), F32) for _ in range(2))
        )
        dq_ref[rows, :] = jnp.concatenate(
            [sums[0][:span], sums[0][span:], sums[1][:span], sums[1][span:]], axis=1
        )


def attend_back(q, kv, row_segs, key_segs, out, lse, back):
    rows, width = q.shape
    return pl.pallas_call(
        functools.partial(attend_back_kernel, rows // 2),
        out_shape=[
            jax.ShapeDtypeStruct((rows, width), F32),
            jax.ShapeDtypeStruct(kv.shape, BF),
        ],
        in_specs=[VMEM] * 7,
        out_specs=[VMEM] * 2,
        compiler_params=params(),
        name="attend_back",
    )(q, kv, row_segs, key_segs, out, lse, back)


def rms_scale(values):
    return lax.rsqrt(jnp.mean(values * values, axis=-1, keepdims=True) + EPSILON)


def rope_tables(positions, head_width):
    frequency = THETA ** (-(jnp.arange(head_width // 2, dtype=F32) * 2.0 / head_width))
    angles = positions.astype(F32)[..., None] * frequency
    return (jnp.cos(angles), jnp.sin(angles))


def rotate(flat, cosine, sine):
    tokens = flat.shape[0]
    vectors = flat.reshape(tokens, -1, 2, HD // 2)
    a, b = vectors[:, :, 0], vectors[:, :, 1]
    cosine, sine = cosine[:, None, :], sine[:, None, :]
    return jnp.stack([a * cosine - b * sine, b * cosine + a * sine], axis=2).reshape(flat.shape)


def doc_positions(segments):
    places = jnp.arange(segments.shape[1], dtype=jnp.int32)
    starts_new = jnp.concatenate(
        [jnp.ones((segments.shape[0], 1), dtype=jnp.bool_), segments[:, 1:] != segments[:, :-1]],
        axis=1,
    )
    starts = lax.cummax(jnp.where(starts_new, places[None, :], 0), axis=1)
    return places[None, :] - starts


def on_device(
    levels,
    tokens,
    segments,
    cotangent,
    query_weight,
    key_weight,
    value_weight,
    output_weight,
    attention_gain,
    gate_weight,
    up_weight,
    down_weight,
    feedforward_gain,
):
    _, rows, width = tokens.shape
    full_len = segments.shape[1]
    layers = query_weight.shape[0]
    rb = query_weight.shape[1]
    rbf = down_weight.shape[1]
    kv_width = KVH * HD
    ffn = gate_weight.shape[2]
    qw, kw, fw = width // GROUP, kv_width // GROUP, ffn // GROUP
    span = 2 * rows
    group_rows = GROUP * rows
    x, c, z, y = place()
    n_ctx = 2 * levels
    lines = [
        [(gx * 2 + gc) * n_ctx + gz * 2 + gy for gc in range(2) for gz in range(levels)]
        for gx in range(2)
        for gy in range(2)
    ]

    def gather_line(part):
        return lax.all_gather(part, AXES, axis=0, tiled=True, axis_index_groups=lines)

    def scatter_line(total):
        return lax.psum_scatter(
            total, AXES, scatter_dimension=0, tiled=True, axis_index_groups=lines
        )

    def to_line_order(flat):
        return (
            flat.reshape(-1, 2, 2 * levels, 2 * rb).transpose(0, 2, 1, 3).reshape(flat.shape)
        )

    def from_line_order(flat):
        return (
            flat.reshape(-1, 2 * levels, 2, 2 * rb).transpose(0, 2, 1, 3).reshape(flat.shape)
        )

    gain1 = attention_gain.astype(F32)[:, :, None]
    gain2 = feedforward_gain.astype(F32)[:, :, None]
    attention_slabs, ffn_slabs = [], []
    for l in range(layers):
        cut = lambda w, g, n: (w[l].astype(F32) * g[l]).astype(BF).reshape(rb, GROUP, n)
        slab = jnp.concatenate(
            [cut(query_weight, gain1, qw), cut(key_weight, gain1, kw), cut(value_weight, gain1, kw)],
            axis=2,
        )
        attention_slabs.append(slab.transpose(1, 0, 2))

        def columns(w):
            scaled = (w[l].astype(F32) * gain2[l]).astype(BF)
            return (
                scaled.reshape(rb, GROUP, levels, 2, rbf)
                .transpose(1, 0, 3, 2, 4)
                .reshape(GROUP, rb, fw)
            )

        ffn_slabs.append(jnp.concatenate([columns(gate_weight), columns(up_weight)], axis=2))

    lanes = segments.reshape(full_len // 128, 128)
    first = exchange([attention_slabs[0]], [output_weight[0]], [lanes], 1)
    pair_segments = first[2].reshape(2, full_len)
    rest = exchange(
        [ffn_slabs[0], attention_slabs[1], ffn_slabs[1]],
        [down_weight[0], output_weight[1], down_weight[1]],
        [],
        2,
    )
    qkv_parts = [first[0], rest[1]]
    out_parts = [first[1], rest[4]]
    up_parts = [rest[0], rest[2]]
    down_parts = [rest[3], rest[5]]
    qkv_full, out_full, gu_full, down_full = [], [], [], []
    for l in range(layers):
        qkv_full.append(gather_line(qkv_parts[l].reshape(GROUP * rb, qw + 2 * kw)))
        out_full.append(
            gather_line(out_parts[l])
            .reshape(2, levels, rb, width)
            .transpose(1, 0, 2, 3)
            .reshape(qw, width)
        )
        gu_full.append(gather_line(up_parts[l].reshape(GROUP * rb, 2 * fw)))
        down_full.append(gather_line(down_parts[l]))

    positions = lax.dynamic_slice_in_dim(doc_positions(pair_segments), z * span, span, 1)
    cosine, sine = rope_tables(positions.reshape(group_rows), HD)
    row_segs = lax.dynamic_slice_in_dim(pair_segments, z * span, span, 1)[:, :, None]
    key_segs = pair_segments.reshape(2, levels, 1, span).transpose(1, 0, 2, 3)

    def gather_rows(own):
        return gather_square(own, 3).reshape(group_rows, width)

    def scatter_rows(parts):
        return scatter_square(parts.astype(BF).reshape(GROUP, rows, width), 4)

    dot = functools.partial(jnp.dot, preferred_element_type=F32)

    residual = tokens.astype(F32).reshape(rows, width)
    stored = []
    for l in range(layers):
        scale1 = rms_scale(residual)
        normed = gather_rows(to_line_order((residual * scale1).astype(BF)))
        qkv = dot(normed, qkv_full[l])
        q = rotate(qkv[:, :qw], cosine, sine).astype(BF)
        k = rotate(qkv[:, qw : qw + kw], cosine, sine).astype(BF)
        kv = climb(jnp.concatenate([k, qkv[:, qw + kw :].astype(BF)], axis=1), levels, 5)
        attended, lse = attend(q, kv, row_segs, key_segs)
        middle = residual + scatter_rows(dot(attended, out_full[l]))
        scale2 = rms_scale(middle)
        normed2 = gather_rows(to_line_order((middle * scale2).astype(BF)))
        gu = dot(normed2, gu_full[l])
        gate, up = gu[:, :fw], gu[:, fw:]
        active = (jax.nn.silu(gate) * up).astype(BF)
        stored.append(
            (residual, scale1, normed, q, kv, attended, lse, middle, scale2, normed2, gate, up, active)
        )
        residual = middle + scatter_rows(dot(active, down_full[l]))
    block_output = residual.astype(BF)

    def norm_back(upstream, dnorm, values, scale):
        norm = values * scale
        return upstream + scale * (dnorm - norm * jnp.mean(dnorm * norm, axis=-1, keepdims=True))

    def outer(a, b):
        return lax.dot_general(a, b, (((0,), (0,)), ((), ())), preferred_element_type=F32).astype(BF)

    def dot_t(a, b):
        return lax.dot_general(a, b, (((1,), (1,)), ((), ())), preferred_element_type=F32)

    upstream = cotangent.astype(F32).reshape(rows, width)
    grads = [None] * layers
    for l in reversed(range(layers)):
        (residual, scale1, normed, q, kv, attended, lse, middle, scale2, normed2, gate, up, active) = (
            stored[l]
        )
        up_all = gather_rows(upstream.astype(BF))
        down_grad = scatter_line(outer(active, up_all))
        dactive = dot_t(up_all, down_full[l])
        sig = jax.nn.sigmoid(gate)
        dgate = (dactive * up * sig * (1.0 + gate * (1.0 - sig))).astype(BF)
        dup = (dactive * gate * sig).astype(BF)
        dgu = jnp.concatenate([dgate, dup], axis=1)
        gu_grad = scatter_line(outer(normed2, dgu))
        dnorm2 = from_line_order(scatter_rows(dot_t(dgu, gu_full[l])))
        dmiddle = norm_back(upstream, dnorm2, middle, scale2)
        mid_all = gather_rows(dmiddle.astype(BF))
        dout = outer(attended, mid_all).reshape(levels, 2, rb, width).transpose(1, 0, 2, 3)
        out_grad = scatter_line(dout.reshape(qw, width))
        back = dot_t(mid_all, out_full[l]).astype(BF)
        dq, dkv = attend_back(q, kv, row_segs, key_segs, attended, lse, back)
        dkv = descend(dkv, 6)
        dqkv = jnp.concatenate(
            [
                rotate(dq, cosine, -sine).astype(BF),
                rotate(dkv[:, :kw], cosine, -sine).astype(BF),
                dkv[:, kw:].astype(BF),
            ],
            axis=1,
        )
        qkv_grad = scatter_line(outer(normed, dqkv))
        dnorm1 = from_line_order(scatter_rows(dot_t(dqkv, qkv_full[l])))
        upstream = norm_back(dmiddle, dnorm1, residual, scale1)
        grads[l] = exchange(
            [qkv_grad.reshape(GROUP, rb, qw + 2 * kw), gu_grad.reshape(GROUP, rb, 2 * fw)],
            [out_grad, down_grad],
            [],
            7,
        )

    results = [[] for _ in range(9)]
    for l in range(layers):
        qkv_grad, gu_grad, out_grad, down_grad = grads[l]
        qkv_grad = qkv_grad.astype(F32)
        gu_grad = gu_grad.astype(F32).reshape(GROUP, rb, 2, 2, levels, rbf)
        raw = [
            qkv_grad[:, :, lo:hi].transpose(1, 0, 2).reshape(rb, -1)
            for lo, hi in ((0, qw), (qw, qw + kw), (qw + kw, qw + 2 * kw))
        ]
        raw += [gu_grad[:, :, i].transpose(1, 0, 3, 2, 4).reshape(rb, ffn) for i in range(2)]
        weights = [query_weight, key_weight, value_weight, gate_weight, up_weight]
        sums = [jnp.sum(raw[i] * weights[i][l].astype(F32), axis=1) for i in range(5)]
        results[0].append(raw[0] * gain1[l])
        results[1].append(raw[1] * gain1[l])
        results[2].append(raw[2] * gain1[l])
        results[3].append(out_grad.astype(F32))
        results[4].append(sums[0] + sums[1] + sums[2])
        results[5].append(raw[3] * gain2[l])
        results[6].append(raw[4] * gain2[l])
        results[7].append(down_grad.astype(F32))
        results[8].append(sums[3] + sums[4])
    return (
        block_output.reshape(1, rows, width),
        upstream.reshape(1, rows, width),
    ) + tuple(jnp.stack(r) for r in results)


def solution(mesh):
    levels = mesh.shape["ctx"] // 2
    rows3 = P(None, AXES, None)
    gains = P(None, AXES)
    return jax.shard_map(
        functools.partial(on_device, levels),
        mesh=mesh,
        in_specs=(
            P("seq", "ctx", None),
            P("seq", None),
            P("seq", "ctx", None),
            rows3,
            rows3,
            rows3,
            rows3,
            gains,
            rows3,
            rows3,
            rows3,
            gains,
        ),
        out_specs=(
            P("seq", "ctx", None),
            P("seq", "ctx", None),
            rows3,
            rows3,
            rows3,
            rows3,
            gains,
            rows3,
            rows3,
            rows3,
            gains,
        ),
        check_vma=False,
    )
```

```python
import functools
import math

import jax
import jax.numpy as jnp
from jax import lax
from jax.experimental import pallas as pl
from jax.experimental.pallas import tpu as pltpu
from jax.sharding import PartitionSpec as P

H = 16
KVH = 8
HD = 96
GROUP = 4

EPSILON = 1e-05
THETA = 100000.0
NEGATIVE = -1e30
AXES = ("seq", "ctx")
MESH = pl.DeviceIdType.MESH
ANY = pl.BlockSpec(memory_space=pl.ANY)
VMEM = pl.BlockSpec(memory_space=pltpu.VMEM)
BF = jnp.bfloat16
F32 = jnp.float32


def params(collective_id=None):
    if collective_id is None:
        return pltpu.CompilerParams(vmem_limit_bytes=48 * 2**20)
    return pltpu.CompilerParams(
        collective_id=collective_id, has_side_effects=True, vmem_limit_bytes=48 * 2**20
    )


def place():
    s = lax.axis_index("seq")
    k = lax.axis_index("ctx")
    return s // 2, s % 2, k // 2, k % 2


def device(x, c, z, y):
    return (x * 2 + c, z * 2 + y)


def level_of(c, z, levels):
    return z + c * (levels - 1 - 2 * z)


def remote(src, dst, send, recv, to):
    return pltpu.make_async_remote_copy(
        src_ref=src, dst_ref=dst, send_sem=send, recv_sem=recv, device_id=to, device_id_type=MESH
    )


def greet(partners):
    barrier = pltpu.get_barrier_semaphore()
    for partner in partners:
        pl.semaphore_signal(barrier, inc=1, device_id=partner, device_id_type=MESH)
    pl.semaphore_wait(barrier, len(partners))


def exchange_kernel(levels, n_slab, n_swap, n_pair, n_mirror, *refs):
    count = n_slab + n_swap + n_pair + n_mirror
    ins, outs = refs[:count], refs[count : 2 * count]
    send, recv, local = refs[2 * count :]
    x, c, z, y = place()
    me = x * 2 + y
    others = [(1 - x, y), (x, 1 - y), (1 - x, 1 - y)]
    crossed = device(x, 1 - c, z, 1 - y)
    mirrored = device(x, c, levels - 1 - z, y)
    barrier = pltpu.get_barrier_semaphore()
    expected = 3
    for ox, oy in others:
        pl.semaphore_signal(barrier, inc=1, device_id=device(ox, c, z, oy), device_id_type=MESH)
    if n_swap:
        expected = expected + lax.rem(c + y, 2)

        @pl.when(c != y)
        def _():
            pl.semaphore_signal(barrier, inc=1, device_id=crossed, device_id_type=MESH)

    if n_mirror:
        expected = expected + c

        @pl.when(c == 1)
        def _():
            pl.semaphore_signal(barrier, inc=1, device_id=mirrored, device_id_type=MESH)

    pl.semaphore_wait(barrier, expected)

    copies = []
    locals_ = []
    for i in range(n_slab):
        for j, (ox, oy) in enumerate(others):
            sem = 3 * i + j
            copies.append(
                remote(
                    ins[i].at[ox * 2 + oy],
                    outs[i].at[me],
                    send.at[sem],
                    recv.at[sem],
                    device(ox, c, z, oy),
                )
            )
        locals_.append(pltpu.make_async_copy(ins[i].at[me], outs[i].at[me], local.at[i]))
    for i in range(n_pair):
        at = n_slab + n_swap + i
        sem = 3 * n_slab + n_swap + i
        copies.append(
            remote(ins[at], outs[at].at[x], send.at[sem], recv.at[sem], device(1 - x, c, z, y))
        )
        locals_.append(pltpu.make_async_copy(ins[at], outs[at].at[x], local.at[at]))
    for copy in copies + locals_:
        copy.start()

    def whole(at, to):
        sem = at + 2 * n_slab
        return (
            remote(ins[at], outs[at], send.at[sem], recv.at[sem], to),
            pltpu.make_async_copy(ins[at], outs[at], local.at[at]),
        )

    moves = [(n_slab + i, crossed, c != y) for i in range(n_swap)]
    moves += [(count - n_mirror + i, mirrored, c == 1) for i in range(n_mirror)]
    for at, to, goes in moves:
        cross, stay = whole(at, to)
        pl.when(goes)(cross.start)
        pl.when(jnp.logical_not(goes))(stay.start)
    for at, to, goes in moves:
        cross, stay = whole(at, to)
        pl.when(goes)(cross.wait)
        pl.when(jnp.logical_not(goes))(stay.wait)
    for copy in copies + locals_:
        copy.wait()


def exchange(levels, slabs, swaps, collective_id, pairs=(), mirrors=()):
    arrays = list(slabs) + list(swaps) + list(pairs) + list(mirrors)
    shapes = [jax.ShapeDtypeStruct(a.shape, a.dtype) for a in list(slabs) + list(swaps)]
    shapes += [jax.ShapeDtypeStruct((2,) + a.shape, a.dtype) for a in pairs]
    shapes += [jax.ShapeDtypeStruct(a.shape, a.dtype) for a in mirrors]
    total = 2 * len(slabs) + len(arrays)
    return pl.pallas_call(
        functools.partial(
            exchange_kernel, levels, len(slabs), len(swaps), len(pairs), len(mirrors)
        ),
        out_shape=shapes,
        in_specs=[ANY] * len(arrays),
        out_specs=[ANY] * len(arrays),
        scratch_shapes=[
            pltpu.SemaphoreType.DMA((total,)),
            pltpu.SemaphoreType.DMA((total,)),
            pltpu.SemaphoreType.DMA((len(arrays),)),
        ],
        compiler_params=params(collective_id),
        name="exchange",
    )(*arrays)


def norm_scale(values):
    return lax.rsqrt(jnp.mean(values * values, axis=-1, keepdims=True) + EPSILON)


def line_order(flat, levels):
    n = 2 * levels
    w = flat.shape[1] // (2 * n)
    return jnp.concatenate(
        [flat[:, (i * n + j) * w : (i * n + j + 1) * w] for j in range(n) for i in range(2)], axis=1
    )


def place_order(flat, levels):
    n = 2 * levels
    w = flat.shape[1] // (2 * n)
    return jnp.concatenate(
        [flat[:, (j * 2 + i) * w : (j * 2 + i + 1) * w] for i in range(2) for j in range(n)], axis=1
    )


def square_kernel(mode, levels, n_spread, n_collect, *refs):
    scatters, gathers = mode not in ("first", "plain"), mode not in ("turn", "last")
    refs = list(refs)
    take = lambda n: [refs.pop(0) for _ in range(n)]
    part_ref = take(1)[0] if scatters else None
    rows_in = take(2 if mode in ("backward", "last") else 1)
    spread_in, collect_in = take(n_spread), take(n_collect)
    kept_ref = take(1)[0] if scatters else None
    all_ref = take(1)[0] if gathers else None
    spread_out, collect_out = take(n_spread), take(n_collect)
    if scatters:
        diag, sums, from_x, from_y, rs_send, rs_recv = take(6)
    if gathers:
        ag_send, ag_recv = take(2)
    if n_spread:
        line_send, line_recv, cross_send, cross_recv, keep_sem = take(5)
    if n_collect:
        slots = take(n_collect)
        sum_send, sum_recv = take(2)
    x, c, z, y = place()
    me, at_x, at_y, at_xy = x * 2 + y, (1 - x) * 2 + y, x * 2 + 1 - y, (1 - x) * 2 + 1 - y
    to_x, to_y = device(1 - x, c, z, y), device(x, c, z, 1 - y)
    ahead = [lax.rem(z + d, levels) for d in range(levels)]
    behind = [lax.rem(z - d + levels, levels) for d in range(levels)]
    partners = [to_x, to_y]
    if n_spread or n_collect:
        partners += [device(x, c, ahead[d], y) for d in range(1, levels)]
    to_core = device(x, 1 - c, z, y)
    if n_spread:
        partners += [to_core]
    greet(partners)

    side = []
    for i in range(n_spread):
        block = spread_out[i].at[c, z]
        for d in range(1, levels):
            to = device(x, c, ahead[d], y)
            side.append(remote(spread_in[i], block, line_send.at[i, d], line_recv.at[i, d], to))
        side.append(
            remote(spread_in[i], block, cross_send.at[i, 0], cross_recv.at[i, 0], to_core)
        )
    for i in range(n_collect):
        for d in range(1, levels):
            to = device(x, c, ahead[d], y)
            block = collect_in[i].at[ahead[d]]
            side.append(remote(block, slots[i].at[d], sum_send.at[i, d], sum_recv.at[i, d], to))
    keeps = [
        pltpu.make_async_copy(spread_in[i], spread_out[i].at[c, z], keep_sem.at[i])
        for i in range(n_spread)
    ]

    def start_side():
        for copy in side + keeps:
            copy.start()

    def finish_side():
        onward = []
        for i in range(n_spread):
            for d in range(1, levels):
                block = spread_out[i].at[c, behind[d]]
                remote(block, block, line_send.at[i, d], line_recv.at[i, d], to_core).wait_recv()
                copy = remote(block, block, cross_send.at[i, d], cross_recv.at[i, d], to_core)
                copy.start()
                onward.append(copy)
        for i in range(n_collect):
            total = collect_in[i][z].astype(F32)
            for d in range(1, levels):
                block = slots[i].at[d]
                remote(block, block, sum_send.at[i, d], sum_recv.at[i, d], to_core).wait_recv()
                total = total + slots[i][d].astype(F32)
            collect_out[i][...] = total.astype(BF)
        for i in range(n_spread):
            for d in range(levels):
                block = spread_out[i].at[1 - c, behind[d]]
                remote(
                    block, block, cross_send.at[i, d], cross_recv.at[i, d], to_core
                ).wait_recv()
        for copy in side + onward:
            copy.wait_send()
        for copy in keeps:
            copy.wait()

    rows = rows_in[0].shape[0]
    half = rows // 2
    low, high = pl.ds(0, half), pl.ds(half, half)
    copies = []
    if gathers:
        x_low, y_high, x_high, y_low = [
            remote(all_ref.at[me, part], all_ref.at[me, part], ag_send.at[i], ag_recv.at[i], to)
            for i, (part, to) in enumerate([(low, to_x), (high, to_y), (high, to_x), (low, to_y)])
        ]
        there = all_ref.at[at_x, low]
        on_y = remote(there, there, ag_send.at[4], ag_recv.at[4], to_y)
        there = all_ref.at[at_y, high]
        on_x = remote(there, there, ag_send.at[5], ag_recv.at[5], to_x)
    if not scatters:
        start_side()
    if scatters:
        x_diag = remote(part_ref.at[at_xy, low], diag.at[0], rs_send.at[0], rs_recv.at[0], to_x)
        y_diag = remote(part_ref.at[at_xy, high], diag.at[1], rs_send.at[1], rs_recv.at[1], to_y)
        x_one = remote(part_ref.at[at_x, low], from_x.at[low], rs_send.at[2], rs_recv.at[2], to_x)
        y_one = remote(part_ref.at[at_y, high], from_y.at[high], rs_send.at[3], rs_recv.at[3], to_y)
        x_two = remote(sums.at[0], from_x.at[high], rs_send.at[4], rs_recv.at[4], to_x)
        y_two = remote(sums.at[1], from_y.at[low], rs_send.at[5], rs_recv.at[5], to_y)
        x_diag.start()
        y_diag.start()
        x_one.start()
        y_one.start()
        start_side()
        y_diag.wait_recv()
        sums[0] = (part_ref[at_x, high].astype(F32) + diag[1].astype(F32)).astype(BF)
        x_two.start()
        x_diag.wait_recv()
        sums[1] = (part_ref[at_y, low].astype(F32) + diag[0].astype(F32)).astype(BF)
        y_two.start()
        copies += [x_diag, y_diag, x_one, y_one, x_two, y_two]

    def own_step(part):
        if mode == "plain":
            all_ref[me, part] = rows_in[0][part]
            return
        if mode == "first":
            values = rows_in[0][part].astype(F32)
            all_ref[me, part] = line_order((values * norm_scale(values)).astype(BF), levels)
            return
        total = (
            part_ref[me, part].astype(F32) + from_x[part].astype(F32) + from_y[part].astype(F32)
        )
        if mode == "forward":
            values = rows_in[0][part] + total
            kept_ref[part] = values
            all_ref[me, part] = line_order((values * norm_scale(values)).astype(BF), levels)
        elif mode == "turn":
            kept_ref[part] = (rows_in[0][part] + total).astype(BF)
        else:
            total = place_order(total, levels)
            upstream, values = rows_in[0][part], rows_in[1][part]
            scale = norm_scale(values)
            norm = values * scale
            result = upstream + scale * (
                total - norm * jnp.mean(total * norm, axis=-1, keepdims=True)
            )
            kept_ref[part] = result
            if gathers:
                all_ref[me, part] = result.astype(BF)

    if scatters:
        x_one.wait_recv()
        y_two.wait_recv()
    own_step(low)
    if gathers:
        x_low.start()
        y_low.start()
    if scatters:
        x_two.wait_recv()
        y_one.wait_recv()
    own_step(high)
    if gathers:
        y_high.start()
        x_high.start()
        x_low.wait_recv()
        on_y.start()
        y_high.wait_recv()
        on_x.start()
        x_high.wait_recv()
        y_low.wait_recv()
        on_y.wait_recv()
        on_x.wait_recv()
        copies += [x_low, y_high, x_high, y_low, on_y, on_x]
    for copy in copies:
        copy.wait_send()
    finish_side()


def square(mode, levels, parts, rows_in, collective_id, spread=(), collect=()):
    rows, width = rows_in[0].shape
    scatters, gathers = mode not in ("first", "plain"), mode not in ("turn", "last")
    out_shape, scratch = [], []
    if scatters:
        out_shape.append(jax.ShapeDtypeStruct((rows, width), BF if mode == "turn" else F32))
        scratch += [
            pltpu.VMEM((2, rows // 2, width), BF),
            pltpu.VMEM((2, rows // 2, width), BF),
            pltpu.VMEM((rows, width), BF),
            pltpu.VMEM((rows, width), BF),
            pltpu.SemaphoreType.DMA((6,)),
            pltpu.SemaphoreType.DMA((6,)),
        ]
    if gathers:
        out_shape.append(jax.ShapeDtypeStruct((GROUP, rows, width), BF))
        scratch += [pltpu.SemaphoreType.DMA((6,)), pltpu.SemaphoreType.DMA((6,))]
    operands = ([parts] if scatters else []) + list(rows_in)
    in_specs = [VMEM] * len(operands) + [ANY] * len(spread) + [VMEM] * len(collect)
    out_specs = [VMEM] * len(out_shape) + [ANY] * len(spread) + [VMEM] * len(collect)
    out_shape += [jax.ShapeDtypeStruct((2, levels) + a.shape, a.dtype) for a in spread]
    out_shape += [jax.ShapeDtypeStruct(a.shape[1:], a.dtype) for a in collect]
    operands += list(spread) + list(collect)
    dma = lambda *shape: pltpu.SemaphoreType.DMA(shape)
    if spread:
        n = len(spread)
        scratch += [dma(n, levels), dma(n, levels), dma(n, levels), dma(n, levels), dma(n)]
    if collect:
        n = len(collect)
        scratch += [pltpu.VMEM(a.shape, a.dtype) for a in collect]
        scratch += [dma(n, levels), dma(n, levels)]
    return pl.pallas_call(
        functools.partial(square_kernel, mode, levels, len(spread), len(collect)),
        out_shape=out_shape,
        in_specs=in_specs,
        out_specs=out_specs,
        scratch_shapes=scratch,
        compiler_params=params(collective_id),
        name="square_" + mode,
    )(*operands)


PIECES = 4


def piece_rows(rows):
    return [pl.ds(i * (rows // PIECES), rows // PIECES) for i in range(PIECES)]


def climb_kernel(levels, own_ref, out_ref, send, recv, local):
    x, c, z, y = place()
    up = device(x, c, lax.rem(z + levels + 1 - 2 * c, levels), y)
    down = device(x, c, lax.rem(z + levels - 1 + 2 * c, levels), y)
    z = level_of(c, z, levels)
    pieces = piece_rows(own_ref.shape[0])
    barrier = pltpu.get_barrier_semaphore()

    @pl.when(z > 0)
    def _():
        pl.semaphore_signal(barrier, inc=1, device_id=down, device_id_type=MESH)

    keep = pltpu.make_async_copy(own_ref, out_ref.at[z], local.at[0])
    keep.start()

    def hop(distance, piece):
        block = lax.rem(z - distance + levels, levels)
        source = own_ref.at[pieces[piece]] if distance == 0 else out_ref.at[block, pieces[piece]]
        return remote(
            source,
            out_ref.at[block, pieces[piece]],
            send.at[distance, piece],
            recv.at[distance, piece],
            up,
        )

    def came(distance, piece):
        block = lax.rem(z - distance + levels, levels)
        there = out_ref.at[block, pieces[piece]]
        return remote(there, there, send.at[distance - 1, piece], recv.at[distance - 1, piece], up)

    @pl.when(z < levels - 1)
    def _():
        pl.semaphore_wait(barrier, 1)
        for piece in range(PIECES):
            hop(0, piece).start()

    for distance in range(1, levels):

        @pl.when(z >= distance)
        def _(distance=distance):
            for piece in range(PIECES):
                came(distance, piece).wait_recv()

                @pl.when(z < levels - 1)
                def _(piece=piece):
                    hop(distance, piece).start()

    for distance in range(levels):

        @pl.when((z >= distance) & (z < levels - 1))
        def _(distance=distance):
            for piece in range(PIECES):
                hop(distance, piece).wait_send()

    keep.wait()


def climb(own, levels, collective_id):
    return pl.pallas_call(
        functools.partial(climb_kernel, levels),
        out_shape=jax.ShapeDtypeStruct((levels,) + own.shape, own.dtype),
        in_specs=[ANY],
        out_specs=ANY,
        scratch_shapes=[
            pltpu.SemaphoreType.DMA((levels, PIECES)),
            pltpu.SemaphoreType.DMA((levels, PIECES)),
            pltpu.SemaphoreType.DMA((1,)),
        ],
        compiler_params=params(collective_id),
        name="climb",
    )(own)


def descend_kernel(levels, part_ref, out_ref, came, sums, send, recv):
    x, c, z, y = place()
    up = device(x, c, lax.rem(z + levels + 1 - 2 * c, levels), y)
    down = device(x, c, lax.rem(z + levels - 1 + 2 * c, levels), y)
    z = level_of(c, z, levels)
    pieces = piece_rows(out_ref.shape[0])
    barrier = pltpu.get_barrier_semaphore()

    @pl.when(z < levels - 1)
    def _():
        pl.semaphore_signal(barrier, inc=1, device_id=up, device_id_type=MESH)

    @pl.when(z > 0)
    def _():
        pl.semaphore_wait(barrier, 1)

    def hop(block, piece, source):
        rows = pieces[piece]
        return remote(
            source.at[block, rows],
            came.at[block, rows],
            send.at[block, piece],
            recv.at[block, piece],
            down,
        )

    @pl.when(z == levels - 1)
    def _():
        for block in range(levels - 1):
            for piece in range(PIECES):
                hop(block, piece, part_ref).start()
        out_ref[...] = part_ref[levels - 1].astype(F32)
        for block in range(levels - 1):
            for piece in range(PIECES):
                hop(block, piece, part_ref).wait_send()

    @pl.when(z < levels - 1)
    def _():
        for block in range(levels - 1):

            @pl.when(block < z)
            def _(block=block):
                for piece in range(PIECES):
                    rows = pieces[piece]
                    hop(block, piece, sums).wait_recv()
                    sums[block, rows] = (
                        part_ref[block, rows].astype(F32) + came[block, rows].astype(F32)
                    ).astype(BF)
                    hop(block, piece, sums).start()

            @pl.when(block == z)
            def _(block=block):
                for piece in range(PIECES):
                    rows = pieces[piece]
                    hop(block, piece, sums).wait_recv()
                    out_ref[rows] = part_ref[block, rows].astype(F32) + came[block, rows].astype(
                        F32
                    )

        for block in range(levels - 1):

            @pl.when(block < z)
            def _(block=block):
                for piece in range(PIECES):
                    hop(block, piece, sums).wait_send()


def descend(parts, collective_id):
    levels = parts.shape[0]
    shape = parts.shape[1:]
    return pl.pallas_call(
        functools.partial(descend_kernel, levels),
        out_shape=jax.ShapeDtypeStruct(shape, F32),
        in_specs=[VMEM],
        out_specs=VMEM,
        scratch_shapes=[
            pltpu.VMEM((levels,) + shape, BF),
            pltpu.VMEM((levels,) + shape, BF),
            pltpu.SemaphoreType.DMA((levels, PIECES)),
            pltpu.SemaphoreType.DMA((levels, PIECES)),
        ],
        compiler_params=params(collective_id),
        name="descend",
    )(parts)


def dot_nt(a, b):
    return lax.dot_general(a, b, (((1,), (1,)), ((), ())), preferred_element_type=F32)


def dot_tn(a, b):
    return lax.dot_general(a, b, (((0,), (0,)), ((), ())), preferred_element_type=F32)


def two_heads(block, j):
    a = block[:, 2 * j * HD : (2 * j + 1) * HD]
    b = block[:, (2 * j + 1) * HD : (2 * j + 2) * HD]
    return jnp.concatenate([a, b], axis=0)


def visible_keys(z, level, span, row_segs, key_segs):
    rows = lax.broadcasted_iota(jnp.int32, (span, span), 0)
    cols = lax.broadcasted_iota(jnp.int32, (span, span), 1)
    mask = (row_segs == key_segs) & ((cols <= rows) | (level < z))
    return jnp.concatenate([mask, mask], axis=0)


def attend_kernel(span, q_ref, kv_ref, row_ref, key_ref, out_ref, lse_ref):
    _, c, z, _ = place()
    z = level_of(c, z, kv_ref.shape[0])
    scaling = 1.0 / math.sqrt(HD)
    for s in range(2):
        rows = pl.ds(s * span, span)
        row_segs = row_ref[s]
        queries = [two_heads(q_ref[rows, :], j) for j in range(2)]

        def step(level, carry):
            block = kv_ref[level, rows, :]
            mask = visible_keys(z, level, span, row_segs, key_ref[level, s])
            after = []
            for j in range(2):
                top, total, accum = carry[3 * j : 3 * j + 3]
                keys = block[:, j * HD : (j + 1) * HD]
                values = block[:, (2 + j) * HD : (3 + j) * HD]
                scores = dot_nt(queries[j], keys) * scaling
                scores = jnp.where(mask, scores, NEGATIVE)
                new = jnp.maximum(top, jnp.max(scores, axis=-1, keepdims=True))
                scale = jnp.exp(top - new)
                weights = jnp.where(mask, jnp.exp(scores - new), 0.0)
                total = total * scale + jnp.sum(weights, axis=-1, keepdims=True)
                accum = accum * scale + jnp.dot(
                    weights.astype(BF), values, preferred_element_type=F32
                )
                after += [new, total, accum]
            return tuple(after)

        start = (
            jnp.full((2 * span, 1), NEGATIVE, F32),
            jnp.zeros((2 * span, 1), F32),
            jnp.zeros((2 * span, HD), F32),
        )
        done = lax.fori_loop(0, z + 1, step, start + start)
        outs, lses = [], []
        for j in range(2):
            top, total, accum = done[3 * j : 3 * j + 3]
            result = (accum / total).astype(BF)
            wide = jnp.broadcast_to(top + jnp.log(total), (2 * span, 32))
            outs += [result[:span], result[span:]]
            lses += [wide[:span], wide[span:]]
        out_ref[rows, :] = jnp.concatenate(outs, axis=1)
        lse_ref[rows, :] = jnp.concatenate(lses, axis=1)


def attend(q, kv, row_segs, key_segs):
    rows, width = q.shape
    return pl.pallas_call(
        functools.partial(attend_kernel, rows // 2),
        out_shape=[
            jax.ShapeDtypeStruct((rows, width), BF),
            jax.ShapeDtypeStruct((rows, 128), F32),
        ],
        in_specs=[VMEM] * 4,
        out_specs=[VMEM] * 2,
        compiler_params=params(),
        name="attend",
    )(q, kv, row_segs, key_segs)


def attend_back_kernel(
    span, q_ref, kv_ref, row_ref, key_ref, out_ref, lse_ref, back_ref, dq_ref, dkv_ref
):
    _, c, z, _ = place()
    z = level_of(c, z, kv_ref.shape[0])
    scaling = 1.0 / math.sqrt(HD)
    for s in range(2):
        rows = pl.ds(s * span, span)
        row_segs = row_ref[s]
        lse_all = lse_ref[rows, :]
        queries = [two_heads(q_ref[rows, :], j) for j in range(2)]
        backs = [two_heads(back_ref[rows, :], j) for j in range(2)]
        outs = [two_heads(out_ref[rows, :], j) for j in range(2)]
        lse = [
            jnp.concatenate(
                [lse_all[:, 64 * j : 64 * j + 1], lse_all[:, 64 * j + 32 : 64 * j + 33]], axis=0
            )
            for j in range(2)
        ]
        delta = [
            jnp.sum(backs[j].astype(F32) * outs[j].astype(F32), axis=-1, keepdims=True)
            for j in range(2)
        ]

        def step(level, carry):
            block = kv_ref[level, rows, :]
            mask = visible_keys(z, level, span, row_segs, key_ref[level, s])
            dks, dvs, sums = [], [], []
            for j in range(2):
                keys = block[:, j * HD : (j + 1) * HD]
                values = block[:, (2 + j) * HD : (3 + j) * HD]
                scores = dot_nt(queries[j], keys) * scaling
                probs = jnp.where(mask, jnp.exp(scores - lse[j]), 0.0)
                dprobs = dot_nt(backs[j], values)
                dscores = (probs * (dprobs - delta[j]) * scaling).astype(BF)
                sums.append(carry[j] + jnp.dot(dscores, keys, preferred_element_type=F32))
                dks.append(dot_tn(dscores, queries[j]).astype(BF))
                dvs.append(dot_tn(probs.astype(BF), backs[j]).astype(BF))
            dkv_ref[level, rows, :] = jnp.concatenate(dks + dvs, axis=1)
            return tuple(sums)

        sums = lax.fori_loop(
            0, z + 1, step, tuple(jnp.zeros((2 * span, HD), F32) for _ in range(2))
        )
        dq_ref[rows, :] = jnp.concatenate(
            [sums[0][:span], sums[0][span:], sums[1][:span], sums[1][span:]], axis=1
        )


def attend_back(q, kv, row_segs, key_segs, out, lse, back):
    rows, width = q.shape
    return pl.pallas_call(
        functools.partial(attend_back_kernel, rows // 2),
        out_shape=[
            jax.ShapeDtypeStruct((rows, width), F32),
            jax.ShapeDtypeStruct(kv.shape, BF),
        ],
        in_specs=[VMEM] * 7,
        out_specs=[VMEM] * 2,
        compiler_params=params(),
        name="attend_back",
    )(q, kv, row_segs, key_segs, out, lse, back)


def rope_tables(positions, head_width):
    frequency = THETA ** (-(jnp.arange(head_width // 2, dtype=F32) * 2.0 / head_width))
    angles = positions.astype(F32)[..., None] * frequency
    return (jnp.cos(angles), jnp.sin(angles))


def rotate(flat, cosine, sine):
    tokens = flat.shape[0]
    vectors = flat.reshape(tokens, -1, 2, HD // 2)
    a, b = vectors[:, :, 0], vectors[:, :, 1]
    cosine, sine = cosine[:, None, :], sine[:, None, :]
    return jnp.stack([a * cosine - b * sine, b * cosine + a * sine], axis=2).reshape(flat.shape)


def doc_positions(segments):
    places = jnp.arange(segments.shape[1], dtype=jnp.int32)
    starts_new = jnp.concatenate(
        [jnp.ones((segments.shape[0], 1), dtype=jnp.bool_), segments[:, 1:] != segments[:, :-1]],
        axis=1,
    )
    starts = lax.cummax(jnp.where(starts_new, places[None, :], 0), axis=1)
    return places[None, :] - starts


def on_device(
    levels,
    tokens,
    segments,
    cotangent,
    query_weight,
    key_weight,
    value_weight,
    output_weight,
    attention_gain,
    gate_weight,
    up_weight,
    down_weight,
    feedforward_gain,
):
    _, rows, width = tokens.shape
    full_len = segments.shape[1]
    layers = query_weight.shape[0]
    rb = query_weight.shape[1]
    rbf = down_weight.shape[1]
    kv_width = KVH * HD
    ffn = gate_weight.shape[2]
    qw, kw, fw = width // GROUP, kv_width // GROUP, ffn // GROUP
    span = 2 * rows
    group_rows = GROUP * rows
    _, c, z, _ = place()
    z = level_of(c, z, levels)
    n_ctx = 2 * levels
    lines = [
        [(gx * 2 + gc) * n_ctx + gz * 2 + gy for gc in range(2) for gz in range(levels)]
        for gx in range(2)
        for gy in range(2)
    ]
    core_lines = [
        [gs * n_ctx + gz * 2 + gy for gz in range(levels)] for gs in range(4) for gy in range(2)
    ]
    core_pairs = [
        (gs * n_ctx + gk, (gs ^ 1) * n_ctx + gk) for gs in range(4) for gk in range(n_ctx)
    ]

    def gather_line(part):
        return lax.all_gather(part, AXES, axis=0, tiled=True, axis_index_groups=lines)

    def scatter_line(total):
        return lax.psum_scatter(
            total, AXES, scatter_dimension=0, tiled=True, axis_index_groups=core_lines
        )

    def after(value, *others):
        return lax.optimization_barrier((value,) + others)[0]

    def swap_cores(a):
        return lax.ppermute(a, AXES, core_pairs)

    gain1 = attention_gain.astype(F32)[:, :, None]
    gain2 = feedforward_gain.astype(F32)[:, :, None]
    qkv_slabs, gu_slabs = [], []
    for l in range(layers):
        cut = lambda w, n: (w[l].astype(F32) * gain1[l]).astype(BF).reshape(rb, GROUP, n)
        slab = jnp.concatenate(
            [cut(query_weight, qw), cut(key_weight, kw), cut(value_weight, kw)], axis=2
        )
        qkv_slabs.append(slab.transpose(1, 0, 2))

        def columns(w):
            scaled = (w[l].astype(F32) * gain2[l]).astype(BF)
            return (
                scaled.reshape(rb, GROUP, levels, 2, rbf)
                .transpose(1, 0, 3, 2, 4)
                .reshape(GROUP, rb, fw)
            )

        gu_slabs.append(jnp.concatenate([columns(gate_weight), columns(up_weight)], axis=2))

    lanes = segments.reshape(full_len // 128, 128)
    qkv0, out0, pair_segments, tokens, cotangent = exchange(
        levels,
        [qkv_slabs[0]],
        [output_weight[0]],
        1,
        [lanes],
        [tokens.reshape(rows, width), cotangent.reshape(rows, width)],
    )
    pair_segments = pair_segments.reshape(2, full_len)

    def exchange_ffn(gu, down, *others):
        return exchange(levels, [after(gu, *others)], [down], 2)

    def exchange_attention(qkv, out, *others):
        return exchange(levels, [after(qkv, *others)], [out], 8)

    def all_attention(qkv, out):
        return gather_line(qkv.reshape(GROUP * rb, qw + 2 * kw)), gather_line(out)

    def all_ffn(gu, down):
        return gather_line(gu.reshape(GROUP * rb, 2 * fw)), gather_line(down)

    positions = lax.dynamic_slice_in_dim(doc_positions(pair_segments), z * span, span, 1)
    cosine, sine = rope_tables(positions.reshape(group_rows), HD)
    row_segs = lax.dynamic_slice_in_dim(pair_segments, z * span, span, 1)[:, :, None]
    key_segs = pair_segments.reshape(2, levels, 1, span).transpose(1, 0, 2, 3)

    def in_square(mode, parts, rows_in, collective_id, spread=(), collect=()):
        if parts is not None:
            parts = parts.astype(BF).reshape(GROUP, rows, width)
        out = list(square(mode, levels, parts, rows_in, collective_id, spread, collect))
        if mode not in ("turn", "last"):
            at = 0 if mode in ("first", "plain") else 1
            out[at] = out[at].reshape(group_rows, width)
        return out

    dot = functools.partial(jnp.dot, preferred_element_type=F32)

    residual = tokens
    qkv_full, out_full, gu_full, down_full = [[None] * layers for _ in range(4)]
    qkv_full[0], out_full[0] = all_attention(qkv0, out0)
    (normed,) = in_square("first", None, [residual], 3)
    ffn_own = exchange_ffn(gu_slabs[0], down_weight[0], normed)
    residual = residual.astype(F32)
    stored = []
    for l in range(layers):
        qkv = dot(normed, after(qkv_full[l], normed))
        q = rotate(qkv[:, :qw], cosine, sine).astype(BF)
        k = rotate(qkv[:, qw : qw + kw], cosine, sine).astype(BF)
        kv = climb(jnp.concatenate([k, qkv[:, qw + kw :].astype(BF)], axis=1), levels, 5)
        gu_full[l], down_full[l] = all_ffn(after(ffn_own[0], kv), after(ffn_own[1], kv))
        attended, lse = attend(q, kv, row_segs, key_segs)
        out_full[l] = (
            after(out_full[l], attended)
            .reshape(2, levels, rb, width)
            .transpose(1, 0, 2, 3)
            .reshape(qw, width)
        )
        middle, normed2 = in_square("forward", dot(attended, out_full[l]), [residual], 4)
        if l < layers - 1:
            qkv_own, out_own = exchange_attention(qkv_slabs[l + 1], output_weight[l + 1], normed2)
            ffn_own = exchange_ffn(gu_slabs[l + 1], down_weight[l + 1], qkv_own)
            qkv_full[l + 1], out_full[l + 1] = all_attention(qkv_own, out_own)
        gu = dot(normed2, after(gu_full[l], normed2))
        gate, up = gu[:, :fw], gu[:, fw:]
        active = (jax.nn.silu(gate) * up).astype(BF)
        if l == 0:
            (up_all,) = in_square("plain", None, [after(cotangent, active)], 9)
        stored.append((residual, normed, q, kv, attended, lse, middle, normed2, gate, up, active))
        if l < layers - 1:
            parts = dot(active, after(down_full[l], active))
            residual, normed = in_square("forward", parts, [middle], 4)

    def outer(a, b):
        return lax.dot_general(a, b, (((0,), (0,)), ((), ())), preferred_element_type=F32)

    def core_half(a, core):
        half = a.shape[1] // 2
        return lax.dynamic_slice_in_dim(a, core * half, half, 1)

    def two_core_outer(pick, b):
        theirs = swap_cores(outer(pick(1 - c), b).astype(BF))
        return (outer(pick(c), b) + theirs.astype(F32)).astype(BF)

    def dot_t(a, b):
        return lax.dot_general(a, b, (((1,), (1,)), ((), ())), preferred_element_type=F32)

    upstream = cotangent.astype(F32)
    ffn_grads, attention_grads = [None] * layers, [None] * layers
    for l in reversed(range(layers)):
        residual, normed, q, kv, attended, lse, middle, normed2, gate, up, active = stored[l]
        down_total = two_core_outer(lambda core: core_half(active, core), up_all)
        if l == layers - 1:
            down_full[l] = after(down_full[l], down_total)
            parts = dot(active, down_full[l])
        dactive = dot_t(up_all, down_full[l])
        sig = jax.nn.sigmoid(gate)
        dgate = (dactive * up * sig * (1.0 + gate * (1.0 - sig))).astype(BF)
        dup = (dactive * gate * sig).astype(BF)
        dgu = jnp.concatenate([dgate, dup], axis=1)
        gu_total = two_core_outer(lambda core: core_half(normed2, core), dgu)
        dnorm2 = dot_t(dgu, gu_full[l]).astype(BF)
        down_total, gu_total, dnorm2 = lax.optimization_barrier((down_total, gu_total, dnorm2))
        ffn_grads[l] = [scatter_line(down_total), scatter_line(gu_total)]
        if l == layers - 1:
            (block_output,) = in_square("turn", after(parts, dnorm2), [middle], 13)
            dnorm2 = after(dnorm2, block_output)
        dmiddle, mid_all = in_square("backward", dnorm2, [upstream, middle], 10)
        back = dot_t(mid_all, out_full[l]).astype(BF)
        by_core = attended.reshape(group_rows, levels, 2, rb)
        out_total = two_core_outer(
            lambda core: lax.dynamic_index_in_dim(by_core, core, 2, False).reshape(
                group_rows, qw // 2
            ),
            mid_all,
        )
        out_total = out_total.reshape(levels, rb, width)
        dq, dkv = attend_back(q, kv, row_segs, key_segs, attended, lse, back)
        dkv = descend(dkv, 6)
        dqkv = jnp.concatenate(
            [
                rotate(dq, cosine, -sine).astype(BF),
                rotate(dkv[:, :kw], cosine, -sine).astype(BF),
                dkv[:, kw:].astype(BF),
            ],
            axis=1,
        )
        qkv_total = two_core_outer(lambda core: core_half(normed, core), dqkv)
        qkv_total = qkv_total.reshape(levels, GROUP * rb, qw + 2 * kw)
        dnorm1 = dot_t(dqkv, qkv_full[l]).astype(BF)
        if l > 0:
            upstream, up_all, *attention_grads[l] = in_square(
                "backward", dnorm1, [dmiddle, residual], 14, collect=[qkv_total, out_total]
            )
        else:
            upstream, *attention_grads[l] = in_square(
                "last", dnorm1, [dmiddle, residual], 11, collect=[qkv_total, out_total]
            )

    grads = [None] * layers
    landed = [attention_grads[layers - 1][0]]
    for l in reversed(range(layers)):
        down_grad, gu_grad = ffn_grads[l]
        gu_grad, down_grad = exchange_ffn(gu_grad.reshape(GROUP, rb, 2 * fw), down_grad, *landed)
        qkv_grad, out_grad = attention_grads[l]
        qkv_grad = qkv_grad.reshape(GROUP, rb, qw + 2 * kw)
        if l > 0:
            qkv_grad, out_grad = exchange_attention(qkv_grad, out_grad, gu_grad)
        else:
            qkv_grad, out_grad, block_output, mirrored = exchange(
                levels,
                [after(qkv_grad, gu_grad)],
                [out_grad],
                12,
                mirrors=[block_output, upstream.astype(BF)],
            )
            upstream = jnp.where(c == 1, mirrored.astype(F32), upstream)
        landed = [qkv_grad]
        grads[l] = [qkv_grad, out_grad, gu_grad, down_grad]

    results = [[] for _ in range(9)]
    for l in range(layers):
        qkv_grad, out_grad, gu_grad, down_grad = [g.astype(F32) for g in grads[l]]
        gu_grad = gu_grad.reshape(GROUP, rb, 2, 2, levels, rbf)
        raw = [
            qkv_grad[:, :, lo:hi].transpose(1, 0, 2).reshape(rb, -1)
            for lo, hi in ((0, qw), (qw, qw + kw), (qw + kw, qw + 2 * kw))
        ]
        raw += [gu_grad[:, :, i].transpose(1, 0, 3, 2, 4).reshape(rb, ffn) for i in range(2)]
        weights = [query_weight, key_weight, value_weight, gate_weight, up_weight]
        sums = [jnp.sum(raw[i] * weights[i][l].astype(F32), axis=1) for i in range(5)]
        results[0].append(raw[0] * gain1[l])
        results[1].append(raw[1] * gain1[l])
        results[2].append(raw[2] * gain1[l])
        results[3].append(out_grad)
        results[4].append(sums[0] + sums[1] + sums[2])
        results[5].append(raw[3] * gain2[l])
        results[6].append(raw[4] * gain2[l])
        results[7].append(down_grad)
        results[8].append(sums[3] + sums[4])
    return (
        block_output.reshape(1, rows, width),
        upstream.reshape(1, rows, width),
    ) + tuple(jnp.stack(r) for r in results)


def solution(mesh):
    levels = mesh.shape["ctx"] // 2
    rows3 = P(None, AXES, None)
    gains = P(None, AXES)
    return jax.shard_map(
        functools.partial(on_device, levels),
        mesh=mesh,
        in_specs=(
            P("seq", "ctx", None),
            P("seq", None),
            P("seq", "ctx", None),
            rows3,
            rows3,
            rows3,
            rows3,
            gains,
            rows3,
            rows3,
            rows3,
            gains,
        ),
        out_specs=(
            P("seq", "ctx", None),
            P("seq", "ctx", None),
            rows3,
            rows3,
            rows3,
            rows3,
            gains,
            rows3,
            rows3,
            rows3,
            gains,
        ),
        check_vma=False,
    )
```

```python
import functools
import math

import jax
import jax.numpy as jnp
from jax import lax
from jax.experimental import pallas as pl
from jax.experimental.pallas import tpu as pltpu
from jax.sharding import PartitionSpec as P

H = 16
KVH = 8
HD = 96
GROUP = 4

EPSILON = 1e-05
THETA = 100000.0
NEGATIVE = -1e30
AXES = ("seq", "ctx")
MESH = pl.DeviceIdType.MESH
ANY = pl.BlockSpec(memory_space=pl.ANY)
VMEM = pl.BlockSpec(memory_space=pltpu.VMEM)
BF = jnp.bfloat16
F32 = jnp.float32


def params(collective_id=None):
    if collective_id is None:
        return pltpu.CompilerParams(vmem_limit_bytes=48 * 2**20)
    return pltpu.CompilerParams(
        collective_id=collective_id, has_side_effects=True, vmem_limit_bytes=48 * 2**20
    )


def place():
    s = lax.axis_index("seq")
    k = lax.axis_index("ctx")
    return s // 2, s % 2, k // 2, k % 2


def device(x, c, z, y):
    return (x * 2 + c, z * 2 + y)


def level_of(c, z, levels):
    return z + c * (levels - 1 - 2 * z)


def remote(src, dst, send, recv, to):
    return pltpu.make_async_remote_copy(
        src_ref=src, dst_ref=dst, send_sem=send, recv_sem=recv, device_id=to, device_id_type=MESH
    )


def greet(partners):
    barrier = pltpu.get_barrier_semaphore()
    for partner in partners:
        pl.semaphore_signal(barrier, inc=1, device_id=partner, device_id_type=MESH)
    pl.semaphore_wait(barrier, len(partners))


class Exchange:
    def __init__(self, levels, slabs=(), swaps=(), pairs=(), mirrors=()):
        self.levels = levels
        self.counts = len(slabs), len(swaps), len(pairs), len(mirrors)
        self.arrays = list(slabs) + list(swaps) + list(pairs) + list(mirrors)
        shapes = [jax.ShapeDtypeStruct(a.shape, a.dtype) for a in list(slabs) + list(swaps)]
        shapes += [jax.ShapeDtypeStruct((2,) + a.shape, a.dtype) for a in pairs]
        self.out_shape = shapes + [jax.ShapeDtypeStruct(a.shape, a.dtype) for a in mirrors]
        total = 2 * len(slabs) + len(self.arrays)
        self.scratch = [
            pltpu.SemaphoreType.DMA((total,)),
            pltpu.SemaphoreType.DMA((total,)),
            pltpu.SemaphoreType.DMA((len(self.arrays),)),
        ]

    def bind(self, ins, outs, send, recv, local):
        self.ins, self.outs = ins, outs
        self.send, self.recv, self.local = send, recv, local
        x, c, z, y = place()
        self.where = c, y
        self.others = [(1 - x, y), (x, 1 - y), (1 - x, 1 - y)]
        self.square = [device(ox, c, z, oy) for ox, oy in self.others]
        self.crossed = device(x, 1 - c, z, 1 - y)
        self.mirrored = device(x, c, self.levels - 1 - z, y)
        n_slab, n_swap, n_pair, n_mirror = self.counts
        me = x * 2 + y
        self.copies, self.keeps = [], []
        for i in range(n_slab):
            for j, (ox, oy) in enumerate(self.others):
                sem = 3 * i + j
                self.copies.append(
                    remote(
                        ins[i].at[:, ox * 2 + oy],
                        outs[i].at[:, me],
                        send.at[sem],
                        recv.at[sem],
                        self.square[j],
                    )
                )
            self.keeps.append(
                pltpu.make_async_copy(ins[i].at[:, me], outs[i].at[:, me], local.at[i])
            )
        for i in range(n_pair):
            at = n_slab + n_swap + i
            sem = at + 2 * n_slab
            self.copies.append(
                remote(
                    ins[at], outs[at].at[x], send.at[sem], recv.at[sem], device(1 - x, c, z, y)
                )
            )
            self.keeps.append(pltpu.make_async_copy(ins[at], outs[at].at[x], local.at[at]))
        self.moves = [(n_slab + i, self.crossed, c != y) for i in range(n_swap)]
        first = n_slab + n_swap + n_pair
        self.moves += [(first + i, self.mirrored, c == 1) for i in range(n_mirror)]

    def greet(self, barrier):
        c, y = self.where
        signal = functools.partial(pl.semaphore_signal, barrier, inc=1, device_id_type=MESH)
        for to in self.square:
            signal(device_id=to)
        expected = 3
        if self.counts[1]:
            expected = expected + lax.rem(c + y, 2)
            pl.when(c != y)(lambda: signal(device_id=self.crossed))
        if self.counts[3]:
            expected = expected + c
            pl.when(c == 1)(lambda: signal(device_id=self.mirrored))
        return expected

    def whole(self, at, to):
        sem = at + 2 * self.counts[0]
        return (
            remote(self.ins[at], self.outs[at], self.send.at[sem], self.recv.at[sem], to),
            pltpu.make_async_copy(self.ins[at], self.outs[at], self.local.at[at]),
        )

    def start(self):
        for copy in self.copies + self.keeps:
            copy.start()
        for at, to, goes in self.moves:
            cross, stay = self.whole(at, to)
            pl.when(goes)(cross.start)
            pl.when(jnp.logical_not(goes))(stay.start)

    def wait(self):
        for at, to, goes in self.moves:
            cross, stay = self.whole(at, to)
            pl.when(goes)(cross.wait)
            pl.when(jnp.logical_not(goes))(stay.wait)
        for copy in self.copies + self.keeps:
            copy.wait()


def exchange_kernel(plan, *refs):
    n = len(plan.arrays)
    plan.bind(refs[:n], refs[n : 2 * n], *refs[2 * n :])
    barrier = pltpu.get_barrier_semaphore()
    pl.semaphore_wait(barrier, plan.greet(barrier))
    plan.start()
    plan.wait()


def exchange(levels, slabs, swaps, collective_id, pairs=(), mirrors=()):
    plan = Exchange(levels, slabs, swaps, pairs, mirrors)
    n = len(plan.arrays)
    return pl.pallas_call(
        functools.partial(exchange_kernel, plan),
        out_shape=plan.out_shape,
        in_specs=[ANY] * n,
        out_specs=[ANY] * n,
        scratch_shapes=plan.scratch,
        compiler_params=params(collective_id),
        name="exchange",
    )(*plan.arrays)


def norm_scale(values):
    return lax.rsqrt(jnp.mean(values * values, axis=-1, keepdims=True) + EPSILON)


def line_order(flat, levels):
    n = 2 * levels
    w = flat.shape[1] // (2 * n)
    return jnp.concatenate(
        [flat[:, (i * n + j) * w : (i * n + j + 1) * w] for j in range(n) for i in range(2)], axis=1
    )


def place_order(flat, levels):
    n = 2 * levels
    w = flat.shape[1] // (2 * n)
    return jnp.concatenate(
        [flat[:, (j * 2 + i) * w : (j * 2 + i + 1) * w] for i in range(2) for j in range(n)], axis=1
    )


def square_kernel(mode, levels, n_spread, n_collect, *refs):
    scatters, gathers = mode not in ("first", "plain"), mode not in ("turn", "last")
    refs = list(refs)
    take = lambda n: [refs.pop(0) for _ in range(n)]
    part_ref = take(1)[0] if scatters else None
    rows_in = take(2 if mode in ("backward", "last") else 1)
    spread_in, collect_in = take(n_spread), take(n_collect)
    kept_ref = take(1)[0] if scatters else None
    all_ref = take(1)[0] if gathers else None
    spread_out, collect_out = take(n_spread), take(n_collect)
    if scatters:
        diag, sums, from_x, from_y, rs_send, rs_recv = take(6)
    if gathers:
        ag_send, ag_recv = take(2)
    if n_spread:
        line_send, line_recv, cross_send, cross_recv, keep_sem = take(5)
    if n_collect:
        slots = take(n_collect)
        sum_send, sum_recv = take(2)
    x, c, z, y = place()
    me, at_x, at_y, at_xy = x * 2 + y, (1 - x) * 2 + y, x * 2 + 1 - y, (1 - x) * 2 + 1 - y
    to_x, to_y = device(1 - x, c, z, y), device(x, c, z, 1 - y)
    ahead = [lax.rem(z + d, levels) for d in range(levels)]
    behind = [lax.rem(z - d + levels, levels) for d in range(levels)]
    partners = [to_x, to_y]
    if n_spread or n_collect:
        partners += [device(x, c, ahead[d], y) for d in range(1, levels)]
    to_core = device(x, 1 - c, z, y)
    if n_spread:
        partners += [to_core]
    greet(partners)

    side = []
    for i in range(n_spread):
        block = spread_out[i].at[c, z]
        for d in range(1, levels):
            to = device(x, c, ahead[d], y)
            side.append(remote(spread_in[i], block, line_send.at[i, d], line_recv.at[i, d], to))
        side.append(
            remote(spread_in[i], block, cross_send.at[i, 0], cross_recv.at[i, 0], to_core)
        )
    for i in range(n_collect):
        for d in range(1, levels):
            to = device(x, c, ahead[d], y)
            block = collect_in[i].at[ahead[d]]
            side.append(remote(block, slots[i].at[d], sum_send.at[i, d], sum_recv.at[i, d], to))
    keeps = [
        pltpu.make_async_copy(spread_in[i], spread_out[i].at[c, z], keep_sem.at[i])
        for i in range(n_spread)
    ]

    def start_side():
        for copy in side + keeps:
            copy.start()

    def finish_side():
        onward = []
        for i in range(n_spread):
            for d in range(1, levels):
                block = spread_out[i].at[c, behind[d]]
                remote(block, block, line_send.at[i, d], line_recv.at[i, d], to_core).wait_recv()
                copy = remote(block, block, cross_send.at[i, d], cross_recv.at[i, d], to_core)
                copy.start()
                onward.append(copy)
        for i in range(n_collect):
            total = collect_in[i][z].astype(F32)
            for d in range(1, levels):
                block = slots[i].at[d]
                remote(block, block, sum_send.at[i, d], sum_recv.at[i, d], to_core).wait_recv()
                total = total + slots[i][d].astype(F32)
            collect_out[i][...] = total.astype(BF)
        for i in range(n_spread):
            for d in range(levels):
                block = spread_out[i].at[1 - c, behind[d]]
                remote(
                    block, block, cross_send.at[i, d], cross_recv.at[i, d], to_core
                ).wait_recv()
        for copy in side + onward:
            copy.wait_send()
        for copy in keeps:
            copy.wait()

    rows = rows_in[0].shape[0]
    half = rows // 2
    low, high = pl.ds(0, half), pl.ds(half, half)
    copies = []
    if gathers:
        x_low, y_high, x_high, y_low = [
            remote(all_ref.at[me, part], all_ref.at[me, part], ag_send.at[i], ag_recv.at[i], to)
            for i, (part, to) in enumerate([(low, to_x), (high, to_y), (high, to_x), (low, to_y)])
        ]
        there = all_ref.at[at_x, low]
        on_y = remote(there, there, ag_send.at[4], ag_recv.at[4], to_y)
        there = all_ref.at[at_y, high]
        on_x = remote(there, there, ag_send.at[5], ag_recv.at[5], to_x)
    if not scatters:
        start_side()
    if scatters:
        x_diag = remote(part_ref.at[at_xy, low], diag.at[0], rs_send.at[0], rs_recv.at[0], to_x)
        y_diag = remote(part_ref.at[at_xy, high], diag.at[1], rs_send.at[1], rs_recv.at[1], to_y)
        x_one = remote(part_ref.at[at_x, low], from_x.at[low], rs_send.at[2], rs_recv.at[2], to_x)
        y_one = remote(part_ref.at[at_y, high], from_y.at[high], rs_send.at[3], rs_recv.at[3], to_y)
        x_two = remote(sums.at[0], from_x.at[high], rs_send.at[4], rs_recv.at[4], to_x)
        y_two = remote(sums.at[1], from_y.at[low], rs_send.at[5], rs_recv.at[5], to_y)
        x_diag.start()
        y_diag.start()
        x_one.start()
        y_one.start()
        start_side()
        y_diag.wait_recv()
        sums[0] = (part_ref[at_x, high].astype(F32) + diag[1].astype(F32)).astype(BF)
        x_two.start()
        x_diag.wait_recv()
        sums[1] = (part_ref[at_y, low].astype(F32) + diag[0].astype(F32)).astype(BF)
        y_two.start()
        copies += [x_diag, y_diag, x_one, y_one, x_two, y_two]

    def own_step(part):
        if mode == "plain":
            all_ref[me, part] = rows_in[0][part]
            return
        if mode == "first":
            values = rows_in[0][part].astype(F32)
            all_ref[me, part] = line_order((values * norm_scale(values)).astype(BF), levels)
            return
        total = (
            part_ref[me, part].astype(F32) + from_x[part].astype(F32) + from_y[part].astype(F32)
        )
        if mode == "forward":
            values = rows_in[0][part] + total
            kept_ref[part] = values
            all_ref[me, part] = line_order((values * norm_scale(values)).astype(BF), levels)
        elif mode == "turn":
            kept_ref[part] = (rows_in[0][part] + total).astype(BF)
        else:
            total = place_order(total, levels)
            upstream, values = rows_in[0][part], rows_in[1][part]
            scale = norm_scale(values)
            norm = values * scale
            result = upstream + scale * (
                total - norm * jnp.mean(total * norm, axis=-1, keepdims=True)
            )
            kept_ref[part] = result
            if gathers:
                all_ref[me, part] = result.astype(BF)

    if scatters:
        x_one.wait_recv()
        y_two.wait_recv()
    own_step(low)
    if gathers:
        x_low.start()
        y_low.start()
    if scatters:
        x_two.wait_recv()
        y_one.wait_recv()
    own_step(high)
    if gathers:
        y_high.start()
        x_high.start()
        x_low.wait_recv()
        on_y.start()
        y_high.wait_recv()
        on_x.start()
        x_high.wait_recv()
        y_low.wait_recv()
        on_y.wait_recv()
        on_x.wait_recv()
        copies += [x_low, y_high, x_high, y_low, on_y, on_x]
    for copy in copies:
        copy.wait_send()
    finish_side()


def square(mode, levels, parts, rows_in, collective_id, spread=(), collect=()):
    rows, width = rows_in[0].shape
    scatters, gathers = mode not in ("first", "plain"), mode not in ("turn", "last")
    out_shape, scratch = [], []
    if scatters:
        out_shape.append(jax.ShapeDtypeStruct((rows, width), BF if mode == "turn" else F32))
        scratch += [
            pltpu.VMEM((2, rows // 2, width), BF),
            pltpu.VMEM((2, rows // 2, width), BF),
            pltpu.VMEM((rows, width), BF),
            pltpu.VMEM((rows, width), BF),
            pltpu.SemaphoreType.DMA((6,)),
            pltpu.SemaphoreType.DMA((6,)),
        ]
    if gathers:
        out_shape.append(jax.ShapeDtypeStruct((GROUP, rows, width), BF))
        scratch += [pltpu.SemaphoreType.DMA((6,)), pltpu.SemaphoreType.DMA((6,))]
    operands = ([parts] if scatters else []) + list(rows_in)
    in_specs = [VMEM] * len(operands) + [ANY] * len(spread) + [VMEM] * len(collect)
    out_specs = [VMEM] * len(out_shape) + [ANY] * len(spread) + [VMEM] * len(collect)
    out_shape += [jax.ShapeDtypeStruct((2, levels) + a.shape, a.dtype) for a in spread]
    out_shape += [jax.ShapeDtypeStruct(a.shape[1:], a.dtype) for a in collect]
    operands += list(spread) + list(collect)
    dma = lambda *shape: pltpu.SemaphoreType.DMA(shape)
    if spread:
        n = len(spread)
        scratch += [dma(n, levels), dma(n, levels), dma(n, levels), dma(n, levels), dma(n)]
    if collect:
        n = len(collect)
        scratch += [pltpu.VMEM(a.shape, a.dtype) for a in collect]
        scratch += [dma(n, levels), dma(n, levels)]
    return pl.pallas_call(
        functools.partial(square_kernel, mode, levels, len(spread), len(collect)),
        out_shape=out_shape,
        in_specs=in_specs,
        out_specs=out_specs,
        scratch_shapes=scratch,
        compiler_params=params(collective_id),
        name="square_" + mode,
    )(*operands)


PIECES = 4


def piece_rows(rows):
    return [pl.ds(i * (rows // PIECES), rows // PIECES) for i in range(PIECES)]


def climb_kernel(levels, own_ref, out_ref, send, recv, local):
    x, c, z, y = place()
    up = device(x, c, lax.rem(z + levels + 1 - 2 * c, levels), y)
    down = device(x, c, lax.rem(z + levels - 1 + 2 * c, levels), y)
    z = level_of(c, z, levels)
    pieces = piece_rows(own_ref.shape[0])
    barrier = pltpu.get_barrier_semaphore()

    @pl.when(z > 0)
    def _():
        pl.semaphore_signal(barrier, inc=1, device_id=down, device_id_type=MESH)

    keep = pltpu.make_async_copy(own_ref, out_ref.at[z], local.at[0])
    keep.start()

    def hop(distance, piece):
        block = lax.rem(z - distance + levels, levels)
        source = own_ref.at[pieces[piece]] if distance == 0 else out_ref.at[block, pieces[piece]]
        return remote(
            source,
            out_ref.at[block, pieces[piece]],
            send.at[distance, piece],
            recv.at[distance, piece],
            up,
        )

    def came(distance, piece):
        block = lax.rem(z - distance + levels, levels)
        there = out_ref.at[block, pieces[piece]]
        return remote(there, there, send.at[distance - 1, piece], recv.at[distance - 1, piece], up)

    @pl.when(z < levels - 1)
    def _():
        pl.semaphore_wait(barrier, 1)
        for piece in range(PIECES):
            hop(0, piece).start()

    for distance in range(1, levels):

        @pl.when(z >= distance)
        def _(distance=distance):
            for piece in range(PIECES):
                came(distance, piece).wait_recv()

                @pl.when(z < levels - 1)
                def _(piece=piece):
                    hop(distance, piece).start()

    for distance in range(levels):

        @pl.when((z >= distance) & (z < levels - 1))
        def _(distance=distance):
            for piece in range(PIECES):
                hop(distance, piece).wait_send()

    keep.wait()


def climb(own, levels, collective_id):
    return pl.pallas_call(
        functools.partial(climb_kernel, levels),
        out_shape=jax.ShapeDtypeStruct((levels,) + own.shape, own.dtype),
        in_specs=[ANY],
        out_specs=ANY,
        scratch_shapes=[
            pltpu.SemaphoreType.DMA((levels, PIECES)),
            pltpu.SemaphoreType.DMA((levels, PIECES)),
            pltpu.SemaphoreType.DMA((1,)),
        ],
        compiler_params=params(collective_id),
        name="climb",
    )(own)


def descend_kernel(levels, plan, *refs):
    refs = list(refs)
    n = len(plan.arrays) if plan else 0
    part_ref, side_in = refs[0], refs[1 : 1 + n]
    out_ref, side_out = refs[1 + n], refs[2 + n : 2 + 2 * n]
    came, sums, send, recv = refs[2 + 2 * n : 6 + 2 * n]
    x, c, z, y = place()
    up = device(x, c, lax.rem(z + levels + 1 - 2 * c, levels), y)
    down = device(x, c, lax.rem(z + levels - 1 + 2 * c, levels), y)
    z = level_of(c, z, levels)
    pieces = piece_rows(out_ref.shape[0])
    barrier = pltpu.get_barrier_semaphore()

    @pl.when(z < levels - 1)
    def _():
        pl.semaphore_signal(barrier, inc=1, device_id=up, device_id_type=MESH)

    if plan:
        plan.bind(side_in, side_out, *refs[6 + 2 * n :])
        pl.semaphore_wait(barrier, plan.greet(barrier) + jnp.minimum(z, 1))
        plan.start()
    else:

        @pl.when(z > 0)
        def _():
            pl.semaphore_wait(barrier, 1)

    def hop(block, piece, source):
        rows = pieces[piece]
        return remote(
            source.at[block, rows],
            came.at[block, rows],
            send.at[block, piece],
            recv.at[block, piece],
            down,
        )

    @pl.when(z == levels - 1)
    def _():
        for block in range(levels - 1):
            for piece in range(PIECES):
                hop(block, piece, part_ref).start()
        out_ref[...] = part_ref[levels - 1].astype(F32)
        for block in range(levels - 1):
            for piece in range(PIECES):
                hop(block, piece, part_ref).wait_send()

    @pl.when(z < levels - 1)
    def _():
        for block in range(levels - 1):

            @pl.when(block < z)
            def _(block=block):
                for piece in range(PIECES):
                    rows = pieces[piece]
                    hop(block, piece, sums).wait_recv()
                    sums[block, rows] = (
                        part_ref[block, rows].astype(F32) + came[block, rows].astype(F32)
                    ).astype(BF)
                    hop(block, piece, sums).start()

            @pl.when(block == z)
            def _(block=block):
                for piece in range(PIECES):
                    rows = pieces[piece]
                    hop(block, piece, sums).wait_recv()
                    out_ref[rows] = part_ref[block, rows].astype(F32) + came[block, rows].astype(
                        F32
                    )

        for block in range(levels - 1):

            @pl.when(block < z)
            def _(block=block):
                for piece in range(PIECES):
                    hop(block, piece, sums).wait_send()

    if plan:
        plan.wait()


def descend(parts, collective_id, slabs=(), swaps=()):
    levels = parts.shape[0]
    shape = parts.shape[1:]
    plan = Exchange(levels, slabs, swaps) if slabs else None
    side = plan.arrays if plan else []
    return pl.pallas_call(
        functools.partial(descend_kernel, levels, plan),
        out_shape=[jax.ShapeDtypeStruct(shape, F32)] + (plan.out_shape if plan else []),
        in_specs=[VMEM] + [ANY] * len(side),
        out_specs=[VMEM] + [ANY] * len(side),
        scratch_shapes=[
            pltpu.VMEM((levels,) + shape, BF),
            pltpu.VMEM((levels,) + shape, BF),
            pltpu.SemaphoreType.DMA((levels, PIECES)),
            pltpu.SemaphoreType.DMA((levels, PIECES)),
        ]
        + (plan.scratch if plan else []),
        compiler_params=params(collective_id),
        name="descend",
    )(parts, *side)


CW = 512


def ffn_gradient_kernel(levels, active, up_all, normed, dgu, out, away, came, send, recv):
    x, c, z, y = place()
    other = device(x, 1 - c, z, y)
    greet([other])
    plan = []
    gu_rows = normed.shape[1] // 2 // levels
    down_rows = active.shape[1] // 2 // levels
    chunks = dgu.shape[1] // CW
    for k in range(chunks):
        plan.append((normed, dgu, k, k * gu_rows, gu_rows))
    for k in range(up_all.shape[1] // CW):
        plan.append((active, up_all, k, chunks * gu_rows + k * down_rows, down_rows))

    def turned(ref, core):
        half = ref.shape[1] // 2
        return ref[:, pl.ds(pl.multiple_of(core * half, 128), half)].T

    def move(i):
        rows = pl.ds(plan[i][3], plan[i][4])
        return remote(away.at[:, rows], came.at[:, rows], send.at[i], recv.at[i], other)

    for core, mine in ((1 - c, False), (c, True)):
        left = {}
        for i, (a, b, k, first, n) in enumerate(plan):
            if id(a) not in left:
                left[id(a)] = turned(a, core)
            result = jnp.dot(
                left[id(a)], b[:, pl.ds(k * CW, CW)], preferred_element_type=F32
            )
            rows = pl.ds(first, n)
            if mine:
                move(i).wait_recv()
            for level in range(levels):
                block = result[level * n : (level + 1) * n]
                if mine:
                    out[level, rows] = (block + came[level, rows].astype(F32)).astype(BF)
                else:
                    away[level, rows] = block.astype(BF)
            if not mine:
                move(i).start()
    for i in range(len(plan)):
        move(i).wait_send()


def ffn_gradient(levels, active, up_all, normed, dgu, collective_id):
    rows = normed.shape[1] // 2 // levels * (dgu.shape[1] // CW)
    rows += active.shape[1] // 2 // levels * (up_all.shape[1] // CW)
    shape = (levels, rows, CW)
    chunks = (dgu.shape[1] + up_all.shape[1]) // CW
    return pl.pallas_call(
        functools.partial(ffn_gradient_kernel, levels),
        out_shape=jax.ShapeDtypeStruct(shape, BF),
        in_specs=[VMEM] * 4,
        out_specs=VMEM,
        scratch_shapes=[
            pltpu.VMEM(shape, BF),
            pltpu.VMEM(shape, BF),
            pltpu.SemaphoreType.DMA((chunks,)),
            pltpu.SemaphoreType.DMA((chunks,)),
        ],
        compiler_params=params(collective_id),
        name="ffn_gradient",
    )(active, up_all, normed, dgu)


def finish_kernel(levels, layers, *refs):
    grads = [refs[4 * l : 4 * l + 4] for l in range(layers)]
    weights, gain1, gain2, outs = (
        refs[4 * layers : 4 * layers + 5],
        refs[4 * layers + 5],
        refs[4 * layers + 6],
        refs[4 * layers + 7 :],
    )
    query, key, value, output, gate, up, down, gain1_out, gain2_out = outs
    qw, kw, fw = query.shape[2] // GROUP, key.shape[2] // GROUP, gate.shape[2] // GROUP
    rbf = down.shape[1]
    for l in range(layers):
        qkv, out, gu, dn = grads[l]

        def place_columns(target, weight, gain, pieces, total):
            raw = jnp.concatenate(pieces, axis=1).astype(F32)
            target[l] = raw * gain[l]
            dots = jnp.sum(raw * weight[l].astype(F32), axis=1, keepdims=True)
            return dots if total is None else total + dots

        total = None
        for target, weight, first, n in (
            (query, weights[0], 0, qw),
            (key, weights[1], qw, kw),
            (value, weights[2], qw + kw, kw),
        ):
            pieces = [qkv[0, t, :, first : first + n] for t in range(GROUP)]
            total = place_columns(target, weight, gain1, pieces, total)
        gain1_out[l] = total
        output[l] = out[...].astype(F32)
        total = None
        for target, weight, base in ((gate, weights[3], 0), (up, weights[4], fw)):
            pieces = []
            for t in range(GROUP):
                for level in range(levels):
                    for core in range(2):
                        at = base + (core * levels + level) * rbf
                        pieces.append(gu[at // CW, t, :, at % CW : at % CW + rbf])
            total = place_columns(target, weight, gain2, pieces, total)
        gain2_out[l] = total
        down[l] = jnp.concatenate([dn[k] for k in range(dn.shape[0])], axis=1).astype(F32)


def finish(levels, grads, weights, output_weight, down_weight, gain1, gain2):
    layers, rb, _ = output_weight.shape
    like = lambda a: jax.ShapeDtypeStruct(a.shape, F32)
    query, key, value, gate, up = weights
    column = jax.ShapeDtypeStruct((layers, rb, 1), F32)
    operands = [a for layer in grads for a in layer] + list(weights) + [gain1, gain2]
    out_shape = [like(a) for a in (query, key, value, output_weight, gate, up, down_weight)]
    return pl.pallas_call(
        functools.partial(finish_kernel, levels, layers),
        out_shape=out_shape + [column, column],
        in_specs=[VMEM] * len(operands),
        out_specs=[VMEM] * 9,
        compiler_params=params(),
        name="finish",
    )(*operands)


def dot_nt(a, b):
    return lax.dot_general(a, b, (((1,), (1,)), ((), ())), preferred_element_type=F32)


def dot_tn(a, b):
    return lax.dot_general(a, b, (((0,), (0,)), ((), ())), preferred_element_type=F32)


def two_heads(block, j):
    a = block[:, 2 * j * HD : (2 * j + 1) * HD]
    b = block[:, (2 * j + 1) * HD : (2 * j + 2) * HD]
    return jnp.concatenate([a, b], axis=0)


def visible_keys(z, level, span, row_segs, key_segs):
    rows = lax.broadcasted_iota(jnp.int32, (span, span), 0)
    cols = lax.broadcasted_iota(jnp.int32, (span, span), 1)
    mask = (row_segs == key_segs) & ((cols <= rows) | (level < z))
    return jnp.concatenate([mask, mask], axis=0)


def attend_kernel(span, q_ref, kv_ref, row_ref, key_ref, out_ref, lse_ref):
    _, c, z, _ = place()
    z = level_of(c, z, kv_ref.shape[0])
    scaling = 1.0 / math.sqrt(HD)
    for s in range(2):
        rows = pl.ds(s * span, span)
        row_segs = row_ref[s]
        queries = [two_heads(q_ref[rows, :], j) for j in range(2)]

        def step(level, carry):
            block = kv_ref[level, rows, :]
            mask = visible_keys(z, level, span, row_segs, key_ref[level, s])
            after = []
            for j in range(2):
                top, total, accum = carry[3 * j : 3 * j + 3]
                keys = block[:, j * HD : (j + 1) * HD]
                values = block[:, (2 + j) * HD : (3 + j) * HD]
                scores = dot_nt(queries[j], keys) * scaling
                scores = jnp.where(mask, scores, NEGATIVE)
                new = jnp.maximum(top, jnp.max(scores, axis=-1, keepdims=True))
                scale = jnp.exp(top - new)
                weights = jnp.where(mask, jnp.exp(scores - new), 0.0)
                total = total * scale + jnp.sum(weights, axis=-1, keepdims=True)
                accum = accum * scale + jnp.dot(
                    weights.astype(BF), values, preferred_element_type=F32
                )
                after += [new, total, accum]
            return tuple(after)

        start = (
            jnp.full((2 * span, 1), NEGATIVE, F32),
            jnp.zeros((2 * span, 1), F32),
            jnp.zeros((2 * span, HD), F32),
        )
        done = lax.fori_loop(0, z + 1, step, start + start)
        outs, lses = [], []
        for j in range(2):
            top, total, accum = done[3 * j : 3 * j + 3]
            result = (accum / total).astype(BF)
            wide = jnp.broadcast_to(top + jnp.log(total), (2 * span, 32))
            outs += [result[:span], result[span:]]
            lses += [wide[:span], wide[span:]]
        out_ref[rows, :] = jnp.concatenate(outs, axis=1)
        lse_ref[rows, :] = jnp.concatenate(lses, axis=1)


def attend(q, kv, row_segs, key_segs):
    rows, width = q.shape
    return pl.pallas_call(
        functools.partial(attend_kernel, rows // 2),
        out_shape=[
            jax.ShapeDtypeStruct((rows, width), BF),
            jax.ShapeDtypeStruct((rows, 128), F32),
        ],
        in_specs=[VMEM] * 4,
        out_specs=[VMEM] * 2,
        compiler_params=params(),
        name="attend",
    )(q, kv, row_segs, key_segs)


def attend_back_kernel(
    span, q_ref, kv_ref, row_ref, key_ref, out_ref, lse_ref, back_ref, dq_ref, dkv_ref
):
    _, c, z, _ = place()
    z = level_of(c, z, kv_ref.shape[0])
    scaling = 1.0 / math.sqrt(HD)
    for s in range(2):
        rows = pl.ds(s * span, span)
        row_segs = row_ref[s]
        lse_all = lse_ref[rows, :]
        queries = [two_heads(q_ref[rows, :], j) for j in range(2)]
        backs = [two_heads(back_ref[rows, :], j) for j in range(2)]
        outs = [two_heads(out_ref[rows, :], j) for j in range(2)]
        lse = [
            jnp.concatenate(
                [lse_all[:, 64 * j : 64 * j + 1], lse_all[:, 64 * j + 32 : 64 * j + 33]], axis=0
            )
            for j in range(2)
        ]
        delta = [
            jnp.sum(backs[j].astype(F32) * outs[j].astype(F32), axis=-1, keepdims=True)
            for j in range(2)
        ]

        def step(level, carry):
            block = kv_ref[level, rows, :]
            mask = visible_keys(z, level, span, row_segs, key_ref[level, s])
            dks, dvs, sums = [], [], []
            for j in range(2):
                keys = block[:, j * HD : (j + 1) * HD]
                values = block[:, (2 + j) * HD : (3 + j) * HD]
                scores = dot_nt(queries[j], keys) * scaling
                probs = jnp.where(mask, jnp.exp(scores - lse[j]), 0.0)
                dprobs = dot_nt(backs[j], values)
                dscores = (probs * (dprobs - delta[j]) * scaling).astype(BF)
                sums.append(carry[j] + jnp.dot(dscores, keys, preferred_element_type=F32))
                dks.append(dot_tn(dscores, queries[j]).astype(BF))
                dvs.append(dot_tn(probs.astype(BF), backs[j]).astype(BF))
            dkv_ref[level, rows, :] = jnp.concatenate(dks + dvs, axis=1)
            return tuple(sums)

        sums = lax.fori_loop(
            0, z + 1, step, tuple(jnp.zeros((2 * span, HD), F32) for _ in range(2))
        )
        dq_ref[rows, :] = jnp.concatenate(
            [sums[0][:span], sums[0][span:], sums[1][:span], sums[1][span:]], axis=1
        )


def attend_back(q, kv, row_segs, key_segs, out, lse, back):
    rows, width = q.shape
    return pl.pallas_call(
        functools.partial(attend_back_kernel, rows // 2),
        out_shape=[
            jax.ShapeDtypeStruct((rows, width), F32),
            jax.ShapeDtypeStruct(kv.shape, BF),
        ],
        in_specs=[VMEM] * 7,
        out_specs=[VMEM] * 2,
        compiler_params=params(),
        name="attend_back",
    )(q, kv, row_segs, key_segs, out, lse, back)


def rope_tables(positions, head_width):
    frequency = THETA ** (-(jnp.arange(head_width // 2, dtype=F32) * 2.0 / head_width))
    angles = positions.astype(F32)[..., None] * frequency
    return (jnp.cos(angles), jnp.sin(angles))


def rotate(flat, cosine, sine):
    tokens = flat.shape[0]
    vectors = flat.reshape(tokens, -1, 2, HD // 2)
    a, b = vectors[:, :, 0], vectors[:, :, 1]
    cosine, sine = cosine[:, None, :], sine[:, None, :]
    return jnp.stack([a * cosine - b * sine, b * cosine + a * sine], axis=2).reshape(flat.shape)


def doc_positions(segments):
    places = jnp.arange(segments.shape[1], dtype=jnp.int32)
    starts_new = jnp.concatenate(
        [jnp.ones((segments.shape[0], 1), dtype=jnp.bool_), segments[:, 1:] != segments[:, :-1]],
        axis=1,
    )
    starts = lax.cummax(jnp.where(starts_new, places[None, :], 0), axis=1)
    return places[None, :] - starts


def on_device(
    levels,
    tokens,
    segments,
    cotangent,
    query_weight,
    key_weight,
    value_weight,
    output_weight,
    attention_gain,
    gate_weight,
    up_weight,
    down_weight,
    feedforward_gain,
):
    _, rows, width = tokens.shape
    full_len = segments.shape[1]
    layers = query_weight.shape[0]
    rb = query_weight.shape[1]
    rbf = down_weight.shape[1]
    kv_width = KVH * HD
    ffn = gate_weight.shape[2]
    qw, kw, fw = width // GROUP, kv_width // GROUP, ffn // GROUP
    span = 2 * rows
    group_rows = GROUP * rows
    _, c, z, _ = place()
    z = level_of(c, z, levels)
    n_ctx = 2 * levels
    lines = [
        [(gx * 2 + gc) * n_ctx + gz * 2 + gy for gc in range(2) for gz in range(levels)]
        for gx in range(2)
        for gy in range(2)
    ]
    core_lines = [
        [gs * n_ctx + gz * 2 + gy for gz in range(levels)] for gs in range(4) for gy in range(2)
    ]
    core_pairs = [
        (gs * n_ctx + gk, (gs ^ 1) * n_ctx + gk) for gs in range(4) for gk in range(n_ctx)
    ]

    def gather_line(part):
        return lax.all_gather(part, AXES, axis=0, tiled=True, axis_index_groups=lines)

    def scatter_line(total):
        return lax.psum_scatter(
            total, AXES, scatter_dimension=0, tiled=True, axis_index_groups=core_lines
        )

    def after(value, *others):
        return lax.optimization_barrier((value,) + others)[0]

    def swap_cores(a):
        return lax.ppermute(a, AXES, core_pairs)

    gain1 = attention_gain.astype(F32)[:, :, None]
    gain2 = feedforward_gain.astype(F32)[:, :, None]
    qkv_slabs, gu_slabs = [], []
    for l in range(layers):
        cut = lambda w, n: (w[l].astype(F32) * gain1[l]).astype(BF).reshape(rb, GROUP, n)
        slab = jnp.concatenate(
            [cut(query_weight, qw), cut(key_weight, kw), cut(value_weight, kw)], axis=2
        )
        qkv_slabs.append(slab.transpose(1, 0, 2))

        def columns(w):
            scaled = (w[l].astype(F32) * gain2[l]).astype(BF)
            return (
                scaled.reshape(rb, GROUP, levels, 2, rbf)
                .transpose(1, 0, 3, 2, 4)
                .reshape(GROUP, rb, fw)
            )

        gu_slabs.append(jnp.concatenate([columns(gate_weight), columns(up_weight)], axis=2))

    lanes = segments.reshape(full_len // 128, 128)
    qkv0, out0, pair_segments, tokens, cotangent = exchange(
        levels,
        [qkv_slabs[0][None]],
        [output_weight[0]],
        1,
        [lanes],
        [tokens.reshape(rows, width), cotangent.reshape(rows, width)],
    )
    pair_segments = pair_segments.reshape(2, full_len)

    def exchange_ffn(gu, down, *others):
        return exchange(levels, [after(gu, *others)[None]], [down], 2)

    def exchange_attention(qkv, out, *others):
        return exchange(levels, [after(qkv, *others)[None]], [out], 8)

    def all_attention(qkv, out):
        return gather_line(qkv.reshape(GROUP * rb, qw + 2 * kw)), gather_line(out)

    def all_ffn(gu, down):
        return gather_line(gu.reshape(GROUP * rb, 2 * fw)), gather_line(down)

    positions = lax.dynamic_slice_in_dim(doc_positions(pair_segments), z * span, span, 1)
    cosine, sine = rope_tables(positions.reshape(group_rows), HD)
    row_segs = lax.dynamic_slice_in_dim(pair_segments, z * span, span, 1)[:, :, None]
    key_segs = pair_segments.reshape(2, levels, 1, span).transpose(1, 0, 2, 3)

    def in_square(mode, parts, rows_in, collective_id, spread=(), collect=()):
        if parts is not None:
            parts = parts.astype(BF).reshape(GROUP, rows, width)
        out = list(square(mode, levels, parts, rows_in, collective_id, spread, collect))
        if mode not in ("turn", "last"):
            at = 0 if mode in ("first", "plain") else 1
            out[at] = out[at].reshape(group_rows, width)
        return out

    dot = functools.partial(jnp.dot, preferred_element_type=F32)

    residual = tokens
    qkv_full, out_full, gu_full, down_full = [[None] * layers for _ in range(4)]
    qkv_full[0], out_full[0] = all_attention(qkv0, out0)
    (normed,) = in_square("first", None, [residual], 3)
    ffn_own = exchange_ffn(gu_slabs[0], down_weight[0], normed)
    residual = residual.astype(F32)
    stored = []
    for l in range(layers):
        qkv = dot(normed, after(qkv_full[l], normed))
        q = rotate(qkv[:, :qw], cosine, sine).astype(BF)
        k = rotate(qkv[:, qw : qw + kw], cosine, sine).astype(BF)
        kv = climb(jnp.concatenate([k, qkv[:, qw + kw :].astype(BF)], axis=1), levels, 5)
        gu_full[l], down_full[l] = all_ffn(after(ffn_own[0], kv), after(ffn_own[1], kv))
        attended, lse = attend(q, kv, row_segs, key_segs)
        out_full[l] = (
            after(out_full[l], attended)
            .reshape(2, levels, rb, width)
            .transpose(1, 0, 2, 3)
            .reshape(qw, width)
        )
        middle, normed2 = in_square("forward", dot(attended, out_full[l]), [residual], 4)
        if l < layers - 1:
            qkv_own, out_own = exchange_attention(qkv_slabs[l + 1], output_weight[l + 1], normed2)
            ffn_own = exchange_ffn(gu_slabs[l + 1], down_weight[l + 1], qkv_own)
            qkv_full[l + 1], out_full[l + 1] = all_attention(qkv_own, out_own)
        gu = dot(normed2, after(gu_full[l], normed2))
        gate, up = gu[:, :fw], gu[:, fw:]
        active = (jax.nn.silu(gate) * up).astype(BF)
        if l == 0:
            (up_all,) = in_square("plain", None, [after(cotangent, active)], 9)
        stored.append((residual, normed, q, kv, attended, lse, middle, normed2, gate, up, active))
        if l < layers - 1:
            parts = dot(active, after(down_full[l], active))
            residual, normed = in_square("forward", parts, [middle], 4)

    def outer(a, b):
        return lax.dot_general(a, b, (((0,), (0,)), ((), ())), preferred_element_type=F32)

    def core_half(a, core):
        half = a.shape[1] // 2
        return lax.dynamic_slice_in_dim(a, core * half, half, 1)

    def two_core_outer(pick, b):
        theirs = swap_cores(outer(pick(1 - c), b).astype(BF))
        return (outer(pick(c), b) + theirs.astype(F32)).astype(BF)

    def dot_t(a, b):
        return lax.dot_general(a, b, (((1,), (1,)), ((), ())), preferred_element_type=F32)

    upstream = cotangent.astype(F32)
    ffn_grads, attention_grads, grads = [[None] * layers for _ in range(3)]

    def in_slabs(l):
        qkv_grad, out_grad = attention_grads[l]
        gu_rows = GROUP * rb * (2 * fw // CW)
        gu_grad = ffn_grads[l][:gu_rows].reshape(2 * fw // CW, GROUP, rb, CW)
        down_grad = ffn_grads[l][gu_rows:]
        qkv_grad = qkv_grad.reshape(1, GROUP, rb, qw + 2 * kw)
        return [qkv_grad, gu_grad], [out_grad, down_grad]

    for l in reversed(range(layers)):
        residual, normed, q, kv, attended, lse, middle, normed2, gate, up, active = stored[l]
        if l == layers - 1:
            down_full[l] = after(down_full[l], active)
            parts = dot(active, down_full[l])
        dactive = dot_t(up_all, down_full[l])
        sig = jax.nn.sigmoid(gate)
        dgate = (dactive * up * sig * (1.0 + gate * (1.0 - sig))).astype(BF)
        dup = (dactive * gate * sig).astype(BF)
        dgu = jnp.concatenate([dgate, dup], axis=1)
        ffn_total = ffn_gradient(levels, active, up_all, normed2, dgu, 16)
        ffn_grads[l] = scatter_line(ffn_total.reshape(-1, CW))
        dnorm2 = dot_t(after(dgu, ffn_total), gu_full[l]).astype(BF)
        if l == layers - 1:
            (block_output,) = in_square("turn", after(parts, dnorm2), [middle], 13)
            dnorm2 = after(dnorm2, block_output)
        dmiddle, mid_all = in_square("backward", dnorm2, [upstream, middle], 10)
        back = dot_t(mid_all, out_full[l]).astype(BF)
        by_core = attended.reshape(group_rows, levels, 2, rb)
        out_total = two_core_outer(
            lambda core: lax.dynamic_index_in_dim(by_core, core, 2, False).reshape(
                group_rows, qw // 2
            ),
            mid_all,
        )
        out_total = out_total.reshape(levels, rb, width)
        dq, dkv = attend_back(q, kv, row_segs, key_segs, attended, lse, back)
        if l < layers - 1:
            dkv, *grads[l + 1] = descend(dkv, 15, *in_slabs(l + 1))
        else:
            (dkv,) = descend(dkv, 6)
        dqkv = jnp.concatenate(
            [
                rotate(dq, cosine, -sine).astype(BF),
                rotate(dkv[:, :kw], cosine, -sine).astype(BF),
                dkv[:, kw:].astype(BF),
            ],
            axis=1,
        )
        qkv_total = two_core_outer(lambda core: core_half(normed, core), dqkv)
        qkv_total = qkv_total.reshape(levels, GROUP * rb, qw + 2 * kw)
        dnorm1 = dot_t(dqkv, qkv_full[l]).astype(BF)
        if l > 0:
            upstream, up_all, *attention_grads[l] = in_square(
                "backward", dnorm1, [dmiddle, residual], 14, collect=[qkv_total, out_total]
            )
        else:
            upstream, *attention_grads[l] = in_square(
                "last", dnorm1, [dmiddle, residual], 11, collect=[qkv_total, out_total]
            )

    slabs, swaps = in_slabs(0)
    *grads[0], block_output, mirrored = exchange(
        levels, slabs, swaps, 12, mirrors=[block_output, upstream.astype(BF)]
    )
    upstream = jnp.where(c == 1, mirrored.astype(F32), upstream)
    ordered = [
        [qkv, out, gu, down.reshape(width // CW, rbf, CW)] for qkv, gu, out, down in grads
    ]
    results = finish(
        levels,
        ordered,
        [query_weight, key_weight, value_weight, gate_weight, up_weight],
        output_weight,
        down_weight,
        gain1,
        gain2,
    )
    query, key, value, output, gate, up, down, gain1_grad, gain2_grad = results
    return (
        block_output.reshape(1, rows, width),
        upstream.reshape(1, rows, width),
        query,
        key,
        value,
        output,
        gain1_grad[:, :, 0],
        gate,
        up,
        down,
        gain2_grad[:, :, 0],
    )


def solution(mesh):
    levels = mesh.shape["ctx"] // 2
    rows3 = P(None, AXES, None)
    gains = P(None, AXES)
    return jax.shard_map(
        functools.partial(on_device, levels),
        mesh=mesh,
        in_specs=(
            P("seq", "ctx", None),
            P("seq", None),
            P("seq", "ctx", None),
            rows3,
            rows3,
            rows3,
            rows3,
            gains,
            rows3,
            rows3,
            rows3,
            gains,
        ),
        out_specs=(
            P("seq", "ctx", None),
            P("seq", "ctx", None),
            rows3,
            rows3,
            rows3,
            rows3,
            gains,
            rows3,
            rows3,
            rows3,
            gains,
        ),
        check_vma=False,
    )
```

```python
import functools
import math

import jax
import jax.numpy as jnp
from jax import lax
from jax.experimental import pallas as pl
from jax.experimental.pallas import tpu as pltpu
from jax.sharding import PartitionSpec as P

H = 16
KVH = 8
HD = 96
GROUP = 4

EPSILON = 1e-05
THETA = 100000.0
NEGATIVE = -1e30
AXES = ("seq", "ctx")
MESH = pl.DeviceIdType.MESH
ANY = pl.BlockSpec(memory_space=pl.ANY)
VMEM = pl.BlockSpec(memory_space=pltpu.VMEM)
BF = jnp.bfloat16
F32 = jnp.float32


def params(collective_id=None):
    if collective_id is None:
        return pltpu.CompilerParams(vmem_limit_bytes=48 * 2**20)
    return pltpu.CompilerParams(
        collective_id=collective_id, has_side_effects=True, vmem_limit_bytes=48 * 2**20
    )


def place():
    s = lax.axis_index("seq")
    k = lax.axis_index("ctx")
    return s // 2, s % 2, k // 2, k % 2


def device(x, c, z, y):
    return (x * 2 + c, z * 2 + y)


def sequence_of(z, levels):
    return z // (levels // 4)


def level_of(c, z, levels):
    return lax.rem(z, levels // 4) * 2 + c


def home_of(x, c, z, y, levels):
    block = z * 2 + y
    level = block // GROUP
    place_z = (x * 2 + c) * (levels // 4) + level // 2
    return lax.rem(block, GROUP) // 2, lax.rem(level, 2), place_z, y


def origin_of(x, c, z, y, levels):
    s = sequence_of(z, levels)
    return s // 2, lax.rem(s, 2), 2 * level_of(c, z, levels) + x, y


def chain(x, c, z, y, levels):
    up = device(x, 1 - c, lax.rem(z + c, levels), y)
    down = device(x, 1 - c, lax.rem(z + levels - 1 + c, levels), y)
    return up, down


def remote(src, dst, send, recv, to):
    return pltpu.make_async_remote_copy(
        src_ref=src, dst_ref=dst, send_sem=send, recv_sem=recv, device_id=to, device_id_type=MESH
    )


def greet(partners, plan=None):
    barrier = pltpu.get_barrier_semaphore()
    for partner in partners:
        pl.semaphore_signal(barrier, inc=1, device_id=partner, device_id_type=MESH)
    expected = len(partners)
    if plan:
        expected = expected + plan.greet(barrier)
    pl.semaphore_wait(barrier, expected)


class Exchange:
    def __init__(self, levels, slabs=(), swaps=(), rows=(), tokens=(), back=False):
        self.levels, self.back = levels, back
        self.counts = len(slabs), len(swaps), len(rows), len(tokens)
        self.arrays = list(slabs) + list(swaps) + list(rows) + list(tokens)
        shapes = [jax.ShapeDtypeStruct(a.shape, a.dtype) for a in list(slabs) + list(swaps)]
        shapes += [jax.ShapeDtypeStruct((4,) + a.shape, a.dtype) for a in rows]
        self.out_shape = shapes + [jax.ShapeDtypeStruct(a.shape, a.dtype) for a in tokens]
        total = 2 * (len(slabs) + len(rows)) + len(self.arrays)
        self.scratch = [
            pltpu.SemaphoreType.DMA((total,)),
            pltpu.SemaphoreType.DMA((total,)),
            pltpu.SemaphoreType.DMA((len(self.arrays),)),
        ]

    def bind(self, ins, outs, send, recv, local):
        self.ins, self.outs = ins, outs
        self.send, self.recv, self.local = send, recv, local
        x, c, z, y = place()
        self.where = c, y
        self.others = [(1 - x, y), (x, 1 - y), (1 - x, 1 - y)]
        self.square = [device(ox, c, z, oy) for ox, oy in self.others]
        self.crossed = device(x, 1 - c, z, 1 - y)
        home = home_of(x, c, z, y, self.levels)
        origin = origin_of(x, c, z, y, self.levels)
        self.moves_away = (home[0] != x) | (home[1] != c) | (home[2] != z)
        taker, giver = (origin, home) if self.back else (home, origin)
        self.taker, self.giver = device(*taker), device(*giver)
        self.seq_others = [device(x, 1 - c, z, y), device(1 - x, 1 - c, z, y)]
        n_slab, n_swap, n_rows, n_tokens = self.counts
        me = x * 2 + y
        self.groups = [[] for _ in self.arrays]
        for i in range(n_slab):
            for j, (ox, oy) in enumerate(self.others):
                sem = 3 * i + j
                self.groups[i].append(
                    remote(
                        ins[i].at[:, ox * 2 + oy],
                        outs[i].at[:, me],
                        send.at[sem],
                        recv.at[sem],
                        self.square[j],
                    )
                )
            self.groups[i].append(
                pltpu.make_async_copy(ins[i].at[:, me], outs[i].at[:, me], local.at[i])
            )
        for i in range(n_rows):
            at = n_slab + n_swap + i
            sem = self.semaphore(at)
            mine = outs[at].at[x * 2 + c]
            for j, to in enumerate([self.square[0]] + self.seq_others):
                self.groups[at].append(
                    remote(ins[at], mine, send.at[sem + j], recv.at[sem + j], to)
                )
            self.groups[at].append(pltpu.make_async_copy(ins[at], mine, local.at[at]))
        self.moves = {n_slab + i: (self.crossed, c != y) for i in range(n_swap)}
        first = n_slab + n_swap + n_rows
        for i in range(n_tokens):
            self.moves[first + i] = self.taker, self.moves_away

    def semaphore(self, at):
        n_slab, n_swap, n_rows, _ = self.counts
        rows_before = min(max(at - n_slab - n_swap, 0), n_rows)
        return at + 2 * (n_slab + rows_before)

    def greet(self, barrier):
        c, y = self.where
        signal = functools.partial(pl.semaphore_signal, barrier, inc=1, device_id_type=MESH)
        for to in self.square:
            signal(device_id=to)
        expected = 3
        if self.counts[1]:
            expected = expected + lax.rem(c + y, 2)
            pl.when(c != y)(lambda: signal(device_id=self.crossed))
        if self.counts[2]:
            expected = expected + 2
            for to in self.seq_others:
                signal(device_id=to)
        if self.counts[3]:
            expected = expected + jnp.where(self.moves_away, 1, 0)
            pl.when(self.moves_away)(lambda: signal(device_id=self.giver))
        return expected

    def whole(self, at, to):
        sem = self.semaphore(at)
        return (
            remote(self.ins[at], self.outs[at], self.send.at[sem], self.recv.at[sem], to),
            pltpu.make_async_copy(self.ins[at], self.outs[at], self.local.at[at]),
        )

    def start(self, which=None):
        for at in range(len(self.arrays)) if which is None else which:
            for copy in self.groups[at]:
                copy.start()
            if at in self.moves:
                to, goes = self.moves[at]
                cross, stay = self.whole(at, to)
                pl.when(goes)(cross.start)
                pl.when(jnp.logical_not(goes))(stay.start)

    def wait(self, which=None):
        for at in range(len(self.arrays)) if which is None else which:
            for copy in self.groups[at]:
                copy.wait()
            if at in self.moves:
                to, goes = self.moves[at]
                cross, stay = self.whole(at, to)
                pl.when(goes)(cross.wait)
                pl.when(jnp.logical_not(goes))(stay.wait)


def exchange_kernel(plan, *refs):
    n = len(plan.arrays)
    plan.bind(refs[:n], refs[n : 2 * n], *refs[2 * n :])
    barrier = pltpu.get_barrier_semaphore()
    pl.semaphore_wait(barrier, plan.greet(barrier))
    plan.start()
    plan.wait()


def exchange(levels, slabs, swaps, collective_id, rows=(), tokens=(), back=False):
    plan = Exchange(levels, slabs, swaps, rows, tokens, back)
    n = len(plan.arrays)
    return pl.pallas_call(
        functools.partial(exchange_kernel, plan),
        out_shape=plan.out_shape,
        in_specs=[ANY] * n,
        out_specs=[ANY] * n,
        scratch_shapes=plan.scratch,
        compiler_params=params(collective_id),
        name="exchange",
    )(*plan.arrays)


class CoreSum:
    def __init__(self, levels, pairs, away, came, send, recv):
        self.levels, self.away, self.came = levels, away, came
        self.send, self.recv = send, recv
        x, c, z, y = place()
        self.core, self.other_core = c, device(x, 1 - c, z, y)
        self.width = away.shape[2]
        self.entries, self.turned = [], {}
        first = 0
        for a, b in pairs:
            n = a.shape[1] // 2 // levels
            for k in range(b.shape[1] // self.width):
                self.entries.append((a, b, k, first, n))
                first += n

    def product(self, i, core, mine):
        a, b, k, _, _ = self.entries[i]
        key = (id(a), mine)
        if key not in self.turned:
            half = a.shape[1] // 2
            self.turned[key] = a[:, pl.ds(pl.multiple_of(core * half, 128), half)].T
        columns = pl.ds(k * self.width, self.width)
        return jnp.dot(self.turned[key], b[:, columns], preferred_element_type=F32)

    def move(self, i):
        rows = pl.ds(self.entries[i][3], self.entries[i][4])
        return remote(
            self.away.at[:, rows],
            self.came.at[:, rows],
            self.send.at[i],
            self.recv.at[i],
            self.other_core,
        )

    def give(self, which):
        for i in which:
            result = self.product(i, 1 - self.core, False)
            _, _, _, first, n = self.entries[i]
            for level in range(self.levels):
                self.away[level, pl.ds(first, n)] = result[level * n : (level + 1) * n].astype(BF)
            self.move(i).start()

    def keep(self, which, out):
        for i in which:
            result = self.product(i, self.core, True)
            _, _, _, first, n = self.entries[i]
            rows = pl.ds(first, n)
            self.move(i).wait_recv()
            for level in range(self.levels):
                block = result[level * n : (level + 1) * n]
                out[level, rows] = (block + self.came[level, rows].astype(F32)).astype(BF)

    def end(self):
        for i in range(len(self.entries)):
            self.move(i).wait_send()


def core_sum_shape(levels, pairs, width):
    rows = sum(a.shape[1] // 2 // levels * (b.shape[1] // width) for a, b in pairs)
    return (levels, rows, width)


def core_sum_scratch(levels, pairs, width):
    shape = core_sum_shape(levels, pairs, width)
    chunks = sum(b.shape[1] // width for _, b in pairs)
    return [
        pltpu.VMEM(shape, BF),
        pltpu.VMEM(shape, BF),
        pltpu.SemaphoreType.DMA((chunks,)),
        pltpu.SemaphoreType.DMA((chunks,)),
    ]


CW = 512


def ffn_gradient_kernel(levels, n, *refs):
    pairs = [refs[2 * i : 2 * i + 2] for i in range(n)]
    out = refs[2 * n]
    total = CoreSum(levels, pairs, *refs[2 * n + 1 :])
    greet([total.other_core])
    chunks = range(len(total.entries))
    total.give(chunks)
    total.keep(chunks, out)
    total.end()


def ffn_gradient(levels, pairs, collective_id):
    operands = [a for pair in pairs for a in pair]
    return pl.pallas_call(
        functools.partial(ffn_gradient_kernel, levels, len(pairs)),
        out_shape=jax.ShapeDtypeStruct(core_sum_shape(levels, pairs, CW), BF),
        in_specs=[VMEM] * len(operands),
        out_specs=VMEM,
        scratch_shapes=core_sum_scratch(levels, pairs, CW),
        compiler_params=params(collective_id),
        name="ffn_gradient",
    )(*operands)


def norm_scale(values):
    return lax.rsqrt(jnp.mean(values * values, axis=-1, keepdims=True) + EPSILON)


def line_order(flat, levels):
    n = 2 * levels
    w = flat.shape[1] // (2 * n)
    return jnp.concatenate(
        [flat[:, (i * n + j) * w : (i * n + j + 1) * w] for j in range(n) for i in range(2)], axis=1
    )


def place_order(flat, levels):
    n = 2 * levels
    w = flat.shape[1] // (2 * n)
    return jnp.concatenate(
        [flat[:, (j * 2 + i) * w : (j * 2 + i + 1) * w] for i in range(2) for j in range(n)], axis=1
    )


def square_kernel(mode, levels, n_spread, collects, second, plan, *refs):
    scatters, gathers = mode not in ("first", "plain"), mode != "last"
    refs = list(refs)
    take = lambda n: [refs.pop(0) for _ in range(n)]
    part_ref = take(1)[0] if scatters else None
    rows_in = take({"backward": 2, "last": 2, "first": 0}.get(mode, 1))
    part2_ref, rows2_ref = take(2) if second else (None, None)
    pair_in, ready = take(2 * min(collects, 1)), take(max(collects - 1, 0))
    plan_in = take(len(plan.arrays)) if plan and gathers else None
    kept_ref = take(1)[0] if scatters and gathers else None
    kept2_ref = take(1)[0] if second else None
    all_ref = take(1)[0] if gathers else None
    spread_out, collect_out = take(n_spread), take(collects)
    plan_out = take(len(plan.arrays)) if plan else None
    spread_in = []
    if mode == "first":
        rows_in = [plan_out[3]]
        spread_in = [plan_out[0].at[0]]
    if mode == "last":
        kept_ref = take(1)[0]
        plan_in = [kept_ref]
    scatter_refs = take(6) if scatters else None
    scatter2_refs = take(6) if second else None
    if gathers:
        ag_send, ag_recv = take(2)
    if n_spread:
        line_send, line_recv, cross_send, cross_recv, keep_sem = take(5)
    product = None
    if collects:
        held, *slots = take(1 + collects)
        sum_send, sum_recv = take(2)
        product = CoreSum(levels, [pair_in], *take(4))
    if plan:
        plan.bind(plan_in, plan_out, *take(3))
    x, c, z, y = place()
    me, at_x, at_y, at_xy = x * 2 + y, (1 - x) * 2 + y, x * 2 + 1 - y, (1 - x) * 2 + 1 - y
    to_x, to_y = device(1 - x, c, z, y), device(x, c, z, 1 - y)
    ahead = [lax.rem(z + d, levels) for d in range(levels)]
    behind = [lax.rem(z - d + levels, levels) for d in range(levels)]
    partners = [to_x, to_y]
    if n_spread or collects:
        partners += [device(x, c, ahead[d], y) for d in range(1, levels)]
    to_core = device(x, 1 - c, z, y)
    if n_spread or product:
        partners += [to_core]
    greet(partners, plan)

    side = []
    for i in range(n_spread):
        block = spread_out[i].at[c, z]
        for d in range(1, levels):
            to = device(x, c, ahead[d], y)
            side.append(remote(spread_in[i], block, line_send.at[i, d], line_recv.at[i, d], to))
        side.append(
            remote(spread_in[i], block, cross_send.at[i, 0], cross_recv.at[i, 0], to_core)
        )
    blocks = []
    for i, source in enumerate([held] + ready if collects else []):
        for d in range(1, levels):
            to = device(x, c, ahead[d], y)
            block = source.at[ahead[d]]
            copy = remote(block, slots[i].at[d], sum_send.at[i, d], sum_recv.at[i, d], to)
            (side if i else blocks).append(copy)
    keeps = [
        pltpu.make_async_copy(spread_in[i], spread_out[i].at[c, z], keep_sem.at[i])
        for i in range(n_spread)
    ]

    def start_side():
        for copy in side + keeps:
            copy.start()

    def finish_side():
        onward = []
        for i in range(n_spread):
            for d in range(1, levels):
                block = spread_out[i].at[c, behind[d]]
                remote(block, block, line_send.at[i, d], line_recv.at[i, d], to_core).wait_recv()
                copy = remote(block, block, cross_send.at[i, d], cross_recv.at[i, d], to_core)
                copy.start()
                onward.append(copy)
        for i, source in enumerate([held] + ready if collects else []):
            total = source[z].astype(F32)
            for d in range(1, levels):
                block = slots[i].at[d]
                remote(block, block, sum_send.at[i, d], sum_recv.at[i, d], to_core).wait_recv()
                total = total + slots[i][d].astype(F32)
            collect_out[i][...] = total.astype(BF)
        if collects:
            product.end()
        if plan:
            plan.wait([1, 2] if mode == "first" else None)
        for i in range(n_spread):
            for d in range(levels):
                block = spread_out[i].at[1 - c, behind[d]]
                remote(
                    block, block, cross_send.at[i, d], cross_recv.at[i, d], to_core
                ).wait_recv()
        for copy in side + blocks + onward:
            copy.wait_send()
        for copy in keeps:
            copy.wait()

    rows = rows_in[0].shape[0]
    half = rows // 2
    low, high = pl.ds(0, half), pl.ds(half, half)
    copies = []
    if gathers:
        x_low, y_high, x_high, y_low = [
            remote(all_ref.at[me, part], all_ref.at[me, part], ag_send.at[i], ag_recv.at[i], to)
            for i, (part, to) in enumerate([(low, to_x), (high, to_y), (high, to_x), (low, to_y)])
        ]
        there = all_ref.at[at_x, low]
        on_y = remote(there, there, ag_send.at[4], ag_recv.at[4], to_y)
        there = all_ref.at[at_y, high]
        on_x = remote(there, there, ag_send.at[5], ag_recv.at[5], to_x)
    if mode == "first":
        plan.start([0, 3])
        plan.wait([0])
        start_side()
        plan.wait([3])

    class Scatter:
        def __init__(self, part_ref, diag, sums, from_x, from_y, send, recv):
            self.part_ref, self.diag, self.sums = part_ref, diag, sums
            self.from_x, self.from_y = from_x, from_y
            ends = [
                (part_ref.at[at_xy, low], diag.at[0], to_x),
                (part_ref.at[at_xy, high], diag.at[1], to_y),
                (part_ref.at[at_x, low], from_x.at[low], to_x),
                (part_ref.at[at_y, high], from_y.at[high], to_y),
                (sums.at[0], from_x.at[high], to_x),
                (sums.at[1], from_y.at[low], to_y),
            ]
            self.copies = [
                remote(src, dst, send.at[i], recv.at[i], to) for i, (src, dst, to) in enumerate(ends)
            ]

        def start(self):
            for copy in self.copies[:4]:
                copy.start()

        def relay(self):
            x_diag, y_diag, _, _, x_two, y_two = self.copies
            y_diag.wait_recv()
            self.sums[0] = (
                self.part_ref[at_x, high].astype(F32) + self.diag[1].astype(F32)
            ).astype(BF)
            x_two.start()
            x_diag.wait_recv()
            self.sums[1] = (
                self.part_ref[at_y, low].astype(F32) + self.diag[0].astype(F32)
            ).astype(BF)
            y_two.start()

        def wait_low(self):
            self.copies[2].wait_recv()
            self.copies[5].wait_recv()

        def wait_high(self):
            self.copies[4].wait_recv()
            self.copies[3].wait_recv()

        def total(self, part):
            return (
                self.part_ref[me, part].astype(F32)
                + self.from_x[part].astype(F32)
                + self.from_y[part].astype(F32)
            )

    if scatters:
        scatter = Scatter(part_ref, *scatter_refs)
        scatter.start()
        start_side()
        if second:
            scatter2 = Scatter(part2_ref, *scatter2_refs)
            scatter2.start()
        if product:
            product.give([0])
        scatter.relay()
        copies += scatter.copies
        if product:
            product.keep([0], held)
            for copy in blocks:
                copy.start()

    def own_step(part):
        if mode == "plain":
            all_ref[me, part] = rows_in[0][part]
            return
        if mode == "first":
            values = rows_in[0][part].astype(F32)
            all_ref[me, part] = line_order((values * norm_scale(values)).astype(BF), levels)
            return
        total = scatter.total(part)
        if mode == "forward":
            values = rows_in[0][part] + total
            kept_ref[part] = values
            all_ref[me, part] = line_order((values * norm_scale(values)).astype(BF), levels)
        else:
            total = place_order(total, levels)
            upstream, values = rows_in[0][part], rows_in[1][part]
            scale = norm_scale(values)
            norm = values * scale
            result = upstream + scale * (
                total - norm * jnp.mean(total * norm, axis=-1, keepdims=True)
            )
            kept_ref[part] = result.astype(kept_ref.dtype)
            if gathers:
                all_ref[me, part] = result.astype(BF)

    if scatters:
        scatter.wait_low()
    own_step(low)
    if gathers:
        x_low.start()
        y_low.start()
    if scatters:
        scatter.wait_high()
    own_step(high)
    if mode == "last":
        plan.start()

    def finish_second():
        scatter2.relay()
        scatter2.wait_low()
        scatter2.wait_high()
        kept2_ref[...] = (rows2_ref[...] + scatter2.total(slice(None))).astype(BF)
        copies.extend(scatter2.copies)

    if gathers:
        y_high.start()
        x_high.start()
        if mode == "first":
            plan.start([1, 2])
        x_low.wait_recv()
        on_y.start()
        y_high.wait_recv()
        on_x.start()
        x_high.wait_recv()
        y_low.wait_recv()
        on_y.wait_recv()
        on_x.wait_recv()
        copies += [x_low, y_high, x_high, y_low, on_y, on_x]
    if second:
        finish_second()
    for copy in copies:
        copy.wait_send()
    finish_side()


def square(
    mode, levels, parts, rows_in, collective_id, collect=(), ready=(), second=(), start=None
):
    rows, width = (start[3] if start else rows_in[0]).shape
    scatters, gathers = mode not in ("first", "plain"), mode != "last"
    dma = lambda *shape: pltpu.SemaphoreType.DMA(shape)
    like = lambda kind: jax.ShapeDtypeStruct((rows, width), kind)
    for_scatter = [pltpu.VMEM((2, rows // 2, width), BF)] * 2
    for_scatter += [pltpu.VMEM((rows, width), BF)] * 2 + [dma(6), dma(6)]
    plan = None
    if mode == "last":
        plan = Exchange(levels, tokens=[like(BF)], back=True)
    elif start:
        plan = Exchange(levels, start[:2], start[2:3], (), start[3:])
    spread = [start[0][0]] if start else []
    operands = ([parts] if scatters else []) + list(rows_in) + list(second)
    operands += list(collect) + list(ready)
    in_specs = [VMEM] * len(operands)
    out_shape, scratch = [], []
    if mode == "last":
        scratch.append(pltpu.VMEM((rows, width), BF))
    elif scatters:
        out_shape.append(like(F32))
    if scatters:
        scratch += for_scatter
    if second:
        out_shape.append(like(BF))
        scratch += for_scatter
    if gathers:
        out_shape.append(jax.ShapeDtypeStruct((GROUP, rows, width), BF))
        scratch += [dma(6), dma(6)]
    out_specs = [VMEM] * len(out_shape) + [ANY] * len(spread)
    out_shape += [jax.ShapeDtypeStruct((2, levels) + a.shape, a.dtype) for a in spread]
    if spread:
        n = len(spread)
        scratch += [dma(n, levels), dma(n, levels), dma(n, levels), dma(n, levels), dma(n)]
    collects = 0
    if collect:
        shape = core_sum_shape(levels, [collect], collect[1].shape[1])
        shapes = [shape] + [a.shape for a in ready]
        collects = len(shapes)
        out_specs += [VMEM] * collects
        out_shape += [jax.ShapeDtypeStruct(a[1:], BF) for a in shapes]
        scratch += [pltpu.VMEM(shape, BF)] + [pltpu.VMEM(a, BF) for a in shapes]
        scratch += [dma(collects, levels), dma(collects, levels)]
        scratch += core_sum_scratch(levels, [collect], shape[2])
    if plan:
        if gathers:
            operands += plan.arrays
            in_specs += [ANY] * len(plan.arrays)
        out_specs += [ANY] * (len(plan.arrays) - 1) + [VMEM if start else ANY]
        out_shape += plan.out_shape
        scratch += plan.scratch
    return pl.pallas_call(
        functools.partial(
            square_kernel, mode, levels, len(spread), collects, bool(second), plan
        ),
        out_shape=out_shape,
        in_specs=in_specs,
        out_specs=out_specs,
        scratch_shapes=scratch,
        compiler_params=params(collective_id),
        name="square_" + mode,
    )(*operands)


PIECES = 4


def piece_rows(rows):
    return [pl.ds(i * (rows // PIECES), rows // PIECES) for i in range(PIECES)]


def climb_kernel(planes, levels, own_ref, out_ref, send, recv, local):
    x, c, z, y = place()
    up, down = chain(x, c, z, y, planes)
    z = level_of(c, z, planes)
    pieces = piece_rows(own_ref.shape[0])
    barrier = pltpu.get_barrier_semaphore()

    @pl.when(z > 0)
    def _():
        pl.semaphore_signal(barrier, inc=1, device_id=down, device_id_type=MESH)

    @pl.when(z < levels - 1)
    def _():
        pl.semaphore_wait(barrier, 1)

    keep = pltpu.make_async_copy(own_ref, out_ref.at[z], local.at[0])
    keep.start()

    def hop(distance, piece):
        block = lax.rem(z - distance + levels, levels)
        source = own_ref.at[pieces[piece]] if distance == 0 else out_ref.at[block, pieces[piece]]
        return remote(
            source,
            out_ref.at[block, pieces[piece]],
            send.at[distance, piece],
            recv.at[distance, piece],
            up,
        )

    def came(distance, piece):
        block = lax.rem(z - distance + levels, levels)
        there = out_ref.at[block, pieces[piece]]
        return remote(there, there, send.at[distance - 1, piece], recv.at[distance - 1, piece], up)

    @pl.when(z < levels - 1)
    def _():
        for piece in range(PIECES):
            hop(0, piece).start()

    for distance in range(1, levels):

        @pl.when(z >= distance)
        def _(distance=distance):
            for piece in range(PIECES):
                came(distance, piece).wait_recv()

                @pl.when(z < levels - 1)
                def _(piece=piece):
                    hop(distance, piece).start()

    for distance in range(levels):

        @pl.when((z >= distance) & (z < levels - 1))
        def _(distance=distance):
            for piece in range(PIECES):
                hop(distance, piece).wait_send()

    keep.wait()


def climb(own, planes, collective_id):
    levels = planes // 2
    return pl.pallas_call(
        functools.partial(climb_kernel, planes, levels),
        out_shape=jax.ShapeDtypeStruct((levels,) + own.shape, own.dtype),
        in_specs=[ANY],
        out_specs=ANY,
        scratch_shapes=[
            pltpu.SemaphoreType.DMA((levels, PIECES)),
            pltpu.SemaphoreType.DMA((levels, PIECES)),
            pltpu.SemaphoreType.DMA((1,)),
        ],
        compiler_params=params(collective_id),
        name="climb",
    )(own)


def dot_nt(a, b):
    return lax.dot_general(a, b, (((1,), (1,)), ((), ())), preferred_element_type=F32)


def dot_tn(a, b):
    return lax.dot_general(a, b, (((0,), (0,)), ((), ())), preferred_element_type=F32)


def two_heads(block, j):
    a = block[:, 2 * j * HD : (2 * j + 1) * HD]
    b = block[:, (2 * j + 1) * HD : (2 * j + 2) * HD]
    return jnp.concatenate([a, b], axis=0)


def visible_keys(z, level, span, row_segs, key_segs):
    rows = lax.broadcasted_iota(jnp.int32, (span, span), 0)
    cols = lax.broadcasted_iota(jnp.int32, (span, span), 1)
    mask = (row_segs == key_segs) & ((cols <= rows) | (level < z))
    return jnp.concatenate([mask, mask], axis=0)


def attend_kernel(planes, q_ref, kv_ref, row_ref, key_ref, out_ref, lse_ref):
    _, c, z, _ = place()
    here = level_of(c, z, planes)
    scaling = 1.0 / math.sqrt(HD)
    span = q_ref.shape[0]
    queries = [two_heads(q_ref[...], j) for j in range(2)]

    def step(level, carry):
        block = kv_ref[level]
        mask = visible_keys(here, level, span, row_ref[...], key_ref[level])
        after = []
        for j in range(2):
            top, total, accum = carry[3 * j : 3 * j + 3]
            keys = block[:, j * HD : (j + 1) * HD]
            values = block[:, (2 + j) * HD : (3 + j) * HD]
            scores = dot_nt(queries[j], keys) * scaling
            scores = jnp.where(mask, scores, NEGATIVE)
            new = jnp.maximum(top, jnp.max(scores, axis=-1, keepdims=True))
            scale = jnp.exp(top - new)
            weights = jnp.where(mask, jnp.exp(scores - new), 0.0)
            total = total * scale + jnp.sum(weights, axis=-1, keepdims=True)
            accum = accum * scale + jnp.dot(weights.astype(BF), values, preferred_element_type=F32)
            after += [new, total, accum]
        return tuple(after)

    start = (
        jnp.full((2 * span, 1), NEGATIVE, F32),
        jnp.zeros((2 * span, 1), F32),
        jnp.zeros((2 * span, HD), F32),
    )
    done = lax.fori_loop(0, here + 1, step, start + start)
    outs, lses = [], []
    for j in range(2):
        top, total, accum = done[3 * j : 3 * j + 3]
        result = (accum / total).astype(BF)
        wide = jnp.broadcast_to(top + jnp.log(total), (2 * span, 32))
        outs += [result[:span], result[span:]]
        lses += [wide[:span], wide[span:]]
    out_ref[...] = jnp.concatenate(outs, axis=1)
    lse_ref[...] = jnp.concatenate(lses, axis=1)


def attend(q, kv, row_segs, key_segs, planes):
    rows, width = q.shape
    return pl.pallas_call(
        functools.partial(attend_kernel, planes),
        out_shape=[
            jax.ShapeDtypeStruct((rows, width), BF),
            jax.ShapeDtypeStruct((rows, 128), F32),
        ],
        in_specs=[VMEM] * 4,
        out_specs=[VMEM] * 2,
        compiler_params=params(),
        name="attend",
    )(q, kv, row_segs, key_segs)


def turn_back(block, cosine, sine):
    a, b = block[:, : HD // 2], block[:, HD // 2 :]
    return jnp.concatenate([a * cosine + b * sine, b * cosine - a * sine], axis=1)


def attend_back_kernel(planes, plan, *refs):
    refs = list(refs)
    take = lambda n: [refs.pop(0) for _ in range(n)]
    q_ref, kv_ref, row_ref, key_ref, out_ref, lse_ref, back_ref, cos_ref, sin_ref, mid_ref = take(10)
    side_in = take(len(plan.arrays) if plan else 0)
    dqkv_ref, dout_ref = take(2)
    side_out = take(len(plan.arrays) if plan else 0)
    part, came, sums, heads_q, heads_back, lse4, delta4, dq4, send, recv = take(10)
    own, away, came_out, out_send, out_recv = take(5)
    levels = kv_ref.shape[0]
    x, c, z, y = place()
    up, down = chain(x, c, z, y, planes)
    other_core = device(x, 1 - c, z, y)
    z = level_of(c, z, planes)
    top = levels - 1
    span = q_ref.shape[0]
    scaling = 1.0 / math.sqrt(HD)
    pieces = piece_rows(span)
    barrier = pltpu.get_barrier_semaphore()
    pl.semaphore_signal(barrier, inc=1, device_id=other_core, device_id_type=MESH)

    @pl.when(z < top)
    def _():
        pl.semaphore_signal(barrier, inc=1, device_id=up, device_id_type=MESH)

    expected = 1 + jnp.minimum(z, 1)
    if plan:
        plan.bind(side_in, side_out, *refs)
        expected = expected + plan.greet(barrier)
    pl.semaphore_wait(barrier, expected)
    if plan:
        plan.start()

    def hop(block, piece, source):
        rows = pieces[piece]
        return remote(
            source.at[block, rows],
            came.at[block, rows],
            send.at[block, piece],
            recv.at[block, piece],
            down,
        )

    lse_all = lse_ref[...]
    for j in range(2):
        back = two_heads(back_ref[...], j)
        heads_q[j] = two_heads(q_ref[...], j)
        heads_back[j] = back
        lse4[j] = jnp.concatenate(
            [lse_all[:, 64 * j : 64 * j + 1], lse_all[:, 64 * j + 32 : 64 * j + 33]], axis=0
        )
        out = two_heads(out_ref[...], j)
        delta4[j] = jnp.sum(back.astype(F32) * out.astype(F32), axis=-1, keepdims=True)
        dq4[j] = jnp.zeros((2 * span, HD), F32)

    def one_level(level, nothing):
        block = kv_ref[level]
        mask = visible_keys(z, level, span, row_ref[...], key_ref[level])
        dks, dvs = [], []
        for j in range(2):
            keys = block[:, j * HD : (j + 1) * HD]
            values = block[:, (2 + j) * HD : (3 + j) * HD]
            queries, back = heads_q[j], heads_back[j]
            scores = dot_nt(queries, keys) * scaling
            probs = jnp.where(mask, jnp.exp(scores - lse4[j]), 0.0)
            dprobs = dot_nt(back, values)
            dscores = (probs * (dprobs - delta4[j]) * scaling).astype(BF)
            dq4[j] += jnp.dot(dscores, keys, preferred_element_type=F32)
            dks.append(dot_tn(dscores, queries).astype(BF))
            dvs.append(dot_tn(probs.astype(BF), back).astype(BF))
        part[level] = jnp.concatenate(dks + dvs, axis=1)

        @pl.when((z == top) & (level < top))
        def _():
            for piece in range(PIECES):
                hop(level, piece, part).start()

        return nothing

    lax.fori_loop(0, z + 1, one_level, 0)

    rb = own.shape[1]
    wide = own.shape[2]
    for k in range(wide // CW):
        columns = pl.ds(k * CW, CW)
        product = dot_tn(out_ref[...], mid_ref[:, columns])
        for level in range(planes):
            first = product[2 * level * rb : (2 * level + 1) * rb]
            second = product[(2 * level + 1) * rb : (2 * level + 2) * rb]
            own[level, :, columns] = jnp.where(c == 0, first, second)
            away[level, :, columns] = jnp.where(c == 0, second, first).astype(BF)
    cross = remote(away, came_out, out_send.at[0], out_recv.at[0], other_core)
    cross.start()

    heads = []
    for j in range(2):
        both = dq4[j]
        heads += [
            turn_back(both[:span], cos_ref[...], sin_ref[...]),
            turn_back(both[span:], cos_ref[...], sin_ref[...]),
        ]
    dqkv_ref[:, : 4 * HD] = jnp.concatenate(heads, axis=1).astype(BF)

    def store(total, rows):
        cosine, sine = cos_ref[rows, :], sin_ref[rows, :]
        heads = [turn_back(total[:, j * HD : (j + 1) * HD], cosine, sine) for j in range(2)]
        dqkv_ref[rows, 4 * HD :] = jnp.concatenate(heads + [total[:, 2 * HD :]], axis=1).astype(BF)

    @pl.when(z == top)
    def _():
        for piece in range(PIECES):
            rows = pieces[piece]
            store(part[top, rows].astype(F32), rows)
        for block in range(top):
            for piece in range(PIECES):
                hop(block, piece, part).wait_send()

    @pl.when(z < top)
    def _():
        for block in range(top):

            @pl.when(block < z)
            def _(block=block):
                for piece in range(PIECES):
                    rows = pieces[piece]
                    hop(block, piece, sums).wait_recv()
                    sums[block, rows] = (
                        part[block, rows].astype(F32) + came[block, rows].astype(F32)
                    ).astype(BF)
                    hop(block, piece, sums).start()

            @pl.when(block == z)
            def _(block=block):
                for piece in range(PIECES):
                    rows = pieces[piece]
                    hop(block, piece, sums).wait_recv()
                    store(part[block, rows].astype(F32) + came[block, rows].astype(F32), rows)

        for block in range(top):

            @pl.when(block < z)
            def _(block=block):
                for piece in range(PIECES):
                    hop(block, piece, sums).wait_send()

    cross.wait_recv()
    for level in range(planes):
        dout_ref[level] = (own[level] + came_out[level].astype(F32)).astype(BF)
    cross.wait_send()
    if plan:
        plan.wait()


def attend_back(operands, rb, planes, collective_id, slabs=(), swaps=(), tokens=()):
    q, kv, mid_all = operands[0], operands[1], operands[-1]
    levels = kv.shape[0]
    rows, width = q.shape
    plan = Exchange(planes, slabs, swaps, (), tokens, True) if slabs or swaps else None
    side = plan.arrays if plan else []
    heads = (2, 2 * rows, HD)
    column = (2, 2 * rows, 1)
    dout = (planes, rb, mid_all.shape[1])
    return pl.pallas_call(
        functools.partial(attend_back_kernel, planes, plan),
        out_shape=[jax.ShapeDtypeStruct((rows, 2 * width), BF), jax.ShapeDtypeStruct(dout, BF)]
        + (plan.out_shape if plan else []),
        in_specs=[VMEM] * len(operands) + [ANY] * len(side),
        out_specs=[VMEM] * 2 + [ANY] * len(side),
        scratch_shapes=[
            pltpu.VMEM(kv.shape, BF),
            pltpu.VMEM(kv.shape, BF),
            pltpu.VMEM(kv.shape, BF),
            pltpu.VMEM(heads, BF),
            pltpu.VMEM(heads, BF),
            pltpu.VMEM(column, F32),
            pltpu.VMEM(column, F32),
            pltpu.VMEM(heads, F32),
            pltpu.SemaphoreType.DMA((levels, PIECES)),
            pltpu.SemaphoreType.DMA((levels, PIECES)),
            pltpu.VMEM(dout, F32),
            pltpu.VMEM(dout, BF),
            pltpu.VMEM(dout, BF),
            pltpu.SemaphoreType.DMA((1,)),
            pltpu.SemaphoreType.DMA((1,)),
        ]
        + (plan.scratch if plan else []),
        compiler_params=params(collective_id),
        name="attend_back",
    )(*operands, *side)


def cut_kernel(levels, layers, rbf, *refs):
    query, key, value, gate, up, gain1, gain2 = refs[:7]
    outs = refs[7:]
    qw, kw, fw = query.shape[2] // GROUP, key.shape[2] // GROUP, gate.shape[2] // GROUP
    for l in range(layers):
        q, k, v = [(w[l].astype(F32) * gain1[l]).astype(BF) for w in (query, key, value)]
        g, u = [(w[l].astype(F32) * gain2[l]).astype(BF) for w in (gate, up)]
        for t in range(GROUP):
            outs[2 * l][0, t] = jnp.concatenate(
                [
                    q[:, t * qw : (t + 1) * qw],
                    k[:, t * kw : (t + 1) * kw],
                    v[:, t * kw : (t + 1) * kw],
                ],
                axis=1,
            )
            pieces = []
            for w in (g, u):
                for core in range(2):
                    for level in range(levels):
                        at = t * fw + (2 * level + core) * rbf
                        pieces.append(w[:, at : at + rbf])
            outs[2 * l + 1][0, t] = jnp.concatenate(pieces, axis=1)


def cut(levels, query, key, value, gate, up, gain1, gain2, rbf):
    layers, rb, _ = query.shape
    shapes = []
    for _ in range(layers):
        wide = (query.shape[2] + 2 * key.shape[2]) // GROUP
        shapes.append(jax.ShapeDtypeStruct((1, GROUP, rb, wide), BF))
        shapes.append(jax.ShapeDtypeStruct((1, GROUP, rb, 2 * gate.shape[2] // GROUP), BF))
    out = pl.pallas_call(
        functools.partial(cut_kernel, levels, layers, rbf),
        out_shape=shapes,
        in_specs=[VMEM] * 7,
        out_specs=[VMEM] * len(shapes),
        compiler_params=params(),
        name="cut",
    )(query, key, value, gate, up, gain1, gain2)
    return out[0::2], out[1::2]


def finish_kernel(levels, layers, *refs):
    grads = [refs[4 * l : 4 * l + 4] for l in range(layers)]
    weights, gain1, gain2, outs = (
        refs[4 * layers : 4 * layers + 5],
        refs[4 * layers + 5],
        refs[4 * layers + 6],
        refs[4 * layers + 7 :],
    )
    query, key, value, output, gate, up, down, gain1_out, gain2_out = outs
    qw, kw, fw = query.shape[2] // GROUP, key.shape[2] // GROUP, gate.shape[2] // GROUP
    rbf = down.shape[1]
    for l in range(layers):
        qkv, out, gu, dn = grads[l]

        def place_columns(target, weight, gain, pieces, total):
            raw = jnp.concatenate(pieces, axis=1).astype(F32)
            target[l] = raw * gain[l]
            dots = jnp.sum(raw * weight[l].astype(F32), axis=1, keepdims=True)
            return dots if total is None else total + dots

        total = None
        for target, weight, first, n in (
            (query, weights[0], 0, qw),
            (key, weights[1], qw, kw),
            (value, weights[2], qw + kw, kw),
        ):
            pieces = [qkv[0, t, :, first : first + n] for t in range(GROUP)]
            total = place_columns(target, weight, gain1, pieces, total)
        gain1_out[l] = total
        output[l] = out[...].astype(F32)
        total = None
        for target, weight, base in ((gate, weights[3], 0), (up, weights[4], fw)):
            pieces = []
            for t in range(GROUP):
                for level in range(levels):
                    for core in range(2):
                        at = base + (core * levels + level) * rbf
                        pieces.append(gu[at // CW, t, :, at % CW : at % CW + rbf])
            total = place_columns(target, weight, gain2, pieces, total)
        gain2_out[l] = total
        down[l] = jnp.concatenate([dn[k] for k in range(dn.shape[0])], axis=1).astype(F32)


def finish(levels, grads, weights, output_weight, down_weight, gain1, gain2):
    layers, rb, _ = output_weight.shape
    like = lambda a: jax.ShapeDtypeStruct(a.shape, F32)
    query, key, value, gate, up = weights
    column = jax.ShapeDtypeStruct((layers, rb, 1), F32)
    operands = [a for layer in grads for a in layer] + list(weights) + [gain1, gain2]
    out_shape = [like(a) for a in (query, key, value, output_weight, gate, up, down_weight)]
    return pl.pallas_call(
        functools.partial(finish_kernel, levels, layers),
        out_shape=out_shape + [column, column],
        in_specs=[VMEM] * len(operands),
        out_specs=[VMEM] * 9,
        compiler_params=params(),
        name="finish",
    )(*operands)


def rope_tables(positions, head_width):
    frequency = THETA ** (-(jnp.arange(head_width // 2, dtype=F32) * 2.0 / head_width))
    angles = positions.astype(F32)[..., None] * frequency
    return (jnp.cos(angles), jnp.sin(angles))


def rotate(flat, cosine, sine):
    tokens = flat.shape[0]
    vectors = flat.reshape(tokens, -1, 2, HD // 2)
    a, b = vectors[:, :, 0], vectors[:, :, 1]
    cosine, sine = cosine[:, None, :], sine[:, None, :]
    return jnp.stack([a * cosine - b * sine, b * cosine + a * sine], axis=2).reshape(flat.shape)


def doc_positions(segments):
    places = jnp.arange(segments.shape[1], dtype=jnp.int32)
    starts_new = jnp.concatenate(
        [jnp.ones((segments.shape[0], 1), dtype=jnp.bool_), segments[:, 1:] != segments[:, :-1]],
        axis=1,
    )
    starts = lax.cummax(jnp.where(starts_new, places[None, :], 0), axis=1)
    return places[None, :] - starts


def on_device(
    levels,
    tokens,
    segments,
    cotangent,
    query_weight,
    key_weight,
    value_weight,
    output_weight,
    attention_gain,
    gate_weight,
    up_weight,
    down_weight,
    feedforward_gain,
):
    _, rows, width = tokens.shape
    full_len = segments.shape[1]
    layers = query_weight.shape[0]
    rb = query_weight.shape[1]
    rbf = down_weight.shape[1]
    kv_width = KVH * HD
    ffn = gate_weight.shape[2]
    qw, kw, fw = width // GROUP, kv_width // GROUP, ffn // GROUP
    group_rows = GROUP * rows
    _, c, z, _ = place()
    here = level_of(c, z, levels)
    n_ctx = 2 * levels
    lines = [
        [(gx * 2 + gc) * n_ctx + gz * 2 + gy for gc in range(2) for gz in range(levels)]
        for gx in range(2)
        for gy in range(2)
    ]
    core_lines = [
        [gs * n_ctx + gz * 2 + gy for gz in range(levels)] for gs in range(4) for gy in range(2)
    ]
    def gather_line(part):
        return lax.all_gather(part, AXES, axis=0, tiled=True, axis_index_groups=lines)

    def scatter_line(total):
        return lax.psum_scatter(
            total, AXES, scatter_dimension=0, tiled=True, axis_index_groups=core_lines
        )

    def after(value, *others):
        return lax.optimization_barrier((value,) + others)[0]

    gain1 = attention_gain.astype(F32)[:, :, None]
    gain2 = feedforward_gain.astype(F32)[:, :, None]
    lanes = segments.reshape(full_len // 128, 128)
    out0, all_segments = exchange(levels, [], [output_weight[0]], 1, [lanes])
    qkv_slabs, gu_slabs = cut(
        levels, query_weight, key_weight, value_weight, gate_weight, up_weight, gain1, gain2, rbf
    )

    def all_attention(qkv, out):
        return gather_line(qkv.reshape(GROUP * rb, qw + 2 * kw)), gather_line(out)

    def all_ffn(gu, down):
        return gather_line(gu.reshape(GROUP * rb, 2 * fw)), gather_line(down)

    own_segments = lax.dynamic_index_in_dim(
        all_segments.reshape(4, full_len), sequence_of(z, levels), 0
    )
    first = here * group_rows
    positions = lax.dynamic_slice_in_dim(doc_positions(own_segments)[0], first, group_rows)
    cosine, sine = rope_tables(positions, HD)
    row_segs = lax.dynamic_slice_in_dim(own_segments[0], first, group_rows)[:, None]
    key_segs = own_segments.reshape(levels // 2, 1, group_rows)

    def split(parts):
        return parts.astype(BF).reshape(GROUP, rows, width)

    def in_square(mode, parts, rows_in, collective_id, **more):
        parts = None if parts is None else split(parts)
        out = list(square(mode, levels, parts, rows_in, collective_id, **more))
        if mode != "last":
            at = 0 if mode in ("first", "plain") else 2 if "second" in more else 1
            out[at] = out[at].reshape(group_rows, width)
        return out

    dot = functools.partial(jnp.dot, preferred_element_type=F32)

    qkv_full, out_full, gu_full, down_full = [[None] * layers for _ in range(4)]
    out_full[0] = gather_line(out0)
    tokens = after(tokens.reshape(rows, width), out0)
    normed, qkv_full[0], _, gu_own, down_own, residual = in_square(
        "first", None, [], 3, start=[qkv_slabs[0], gu_slabs[0], down_weight[0], tokens]
    )
    gu_full[0], down_full[0] = all_ffn(gu_own, down_own)
    residual = residual.astype(F32)
    stored = []
    for l in range(layers):
        qkv = dot(normed, after(qkv_full[l].reshape(width, qw + 2 * kw), normed))
        q = rotate(qkv[:, :qw], cosine, sine).astype(BF)
        k = rotate(qkv[:, qw : qw + kw], cosine, sine).astype(BF)
        kv = jnp.concatenate([k, qkv[:, qw + kw :].astype(BF)], axis=1)
        kv = climb(kv, levels, 5)
        attended, lse = attend(q, kv, row_segs, key_segs, levels)
        out_full[l] = (
            after(out_full[l], attended)
            .reshape(2, levels, rb, width)
            .transpose(1, 0, 2, 3)
            .reshape(qw, width)
        )
        if l == layers - 1:
            (up_all,) = in_square("plain", None, [after(cotangent, attended)], 9)
            attended = after(attended, up_all)
        middle, normed2 = in_square("forward", dot(attended, out_full[l]), [residual], 4)
        if l < layers - 1:
            qkv_own, gu_own, out_own, down_own, *moved = exchange(
                levels,
                [after(qkv_slabs[l + 1], normed2), gu_slabs[l + 1]],
                [output_weight[l + 1], down_weight[l + 1]],
                8,
                tokens=[cotangent.reshape(rows, width)] if l == 0 else [],
            )
            cotangent = moved[0] if l == 0 else cotangent
            qkv_full[l + 1], out_full[l + 1] = all_attention(qkv_own, out_own)
            gu_full[l + 1], down_full[l + 1] = all_ffn(gu_own, down_own)
        gu = dot(normed2, after(gu_full[l], normed2))
        gate, up = gu[:, :fw], gu[:, fw:]
        active = (jax.nn.silu(gate) * up).astype(BF)
        stored.append((residual, normed, q, kv, attended, lse, middle, normed2, gate, up, active))
        if l < layers - 1:
            parts = dot(active, after(down_full[l], active))
            residual, normed = in_square("forward", parts, [middle], 4)

    def dot_t(a, b):
        return lax.dot_general(a, b, (((1,), (1,)), ((), ())), preferred_element_type=F32)

    upstream = cotangent.astype(F32)
    ffn_grads, attention_grads, grads = [[None] * layers for _ in range(3)]

    def in_slabs(l):
        qkv_grad, out_grad = attention_grads[l]
        gu_rows = GROUP * rb * (2 * fw // CW)
        gu_grad = ffn_grads[l][0][:gu_rows].reshape(2 * fw // CW, GROUP, rb, CW)
        qkv_grad = qkv_grad.reshape(1, GROUP, rb, qw + 2 * kw)
        if l == layers - 1:
            return [qkv_grad, gu_grad], [out_grad]
        return [qkv_grad, gu_grad], [out_grad, ffn_grads[l][0][gu_rows:]]

    for l in reversed(range(layers)):
        residual, normed, q, kv, attended, lse, middle, normed2, gate, up, active = stored[l]
        if l == layers - 1:
            down_total = ffn_gradient(levels, [(active, up_all)], 13)
            down_full[l] = after(down_full[l], down_total)
            block = split(dot(active, down_full[l])), middle
        dactive = dot_t(up_all, down_full[l])
        sig = jax.nn.sigmoid(gate)
        dgate = (dactive * up * sig * (1.0 + gate * (1.0 - sig))).astype(BF)
        dup = (dactive * gate * sig).astype(BF)
        dgu = jnp.concatenate([dgate, dup], axis=1)
        if l == layers - 1:
            ffn_total = ffn_gradient(levels, [(normed2, dgu)], 16)
            totals = [ffn_total, down_total]
        else:
            ffn_total = ffn_gradient(levels, [(normed2, dgu), (active, up_all)], 17)
            totals = [ffn_total]
        ffn_grads[l] = [scatter_line(total.reshape(-1, CW)) for total in totals]
        dnorm2 = dot_t(after(dgu, ffn_total), gu_full[l]).astype(BF)
        dmiddle, mid_all = in_square("backward", dnorm2, [upstream, middle], 10)
        back = dot_t(mid_all, out_full[l]).astype(BF)
        operands = [q, kv, row_segs, key_segs, attended, lse, back, cosine, sine, mid_all]
        if l < layers - 1:
            slabs, swaps = in_slabs(l + 1)
            moved = [block_output] if l == layers - 2 else []
            dqkv, out_total, *landed = attend_back(
                operands, rb, levels, 15, slabs, swaps, moved
            )
            block_output = landed.pop() if moved else block_output
            grads[l + 1] = landed + [down_grad] if l == layers - 2 else landed
        else:
            down_grad = ffn_grads[l][1]
            dqkv, out_total, down_grad = attend_back(operands, rb, levels, 6, [], [down_grad])
            ffn_grads[l] = [ffn_grads[l][0]]
        dnorm1 = dot_t(dqkv, qkv_full[l].reshape(width, qw + 2 * kw)).astype(BF)
        collect = normed, dqkv
        if l == layers - 1:
            upstream, block_output, up_all, qkv_grad, out_grad = in_square(
                "backward",
                dnorm1,
                [dmiddle, residual],
                14,
                collect=collect,
                ready=[out_total],
                second=block,
            )
        elif l > 0:
            upstream, up_all, qkv_grad, out_grad = in_square(
                "backward", dnorm1, [dmiddle, residual], 18, collect=collect, ready=[out_total]
            )
        else:
            qkv_grad, out_grad, tokens_grad = in_square(
                "last", dnorm1, [dmiddle, residual], 11, collect=collect, ready=[out_total]
            )
        attention_grads[l] = [qkv_grad, out_grad]

    slabs, swaps = in_slabs(0)
    grads[0] = exchange(levels, slabs, swaps, 12)
    ordered = [
        [qkv, out, gu, down.reshape(width // CW, rbf, CW)] for qkv, gu, out, down in grads
    ]
    results = finish(
        levels,
        ordered,
        [query_weight, key_weight, value_weight, gate_weight, up_weight],
        output_weight,
        down_weight,
        gain1,
        gain2,
    )
    query, key, value, output, gate, up, down, gain1_grad, gain2_grad = results
    return (
        block_output.reshape(1, rows, width),
        tokens_grad.astype(F32).reshape(1, rows, width),
        query,
        key,
        value,
        output,
        gain1_grad[:, :, 0],
        gate,
        up,
        down,
        gain2_grad[:, :, 0],
    )


def solution(mesh):
    levels = mesh.shape["ctx"] // 2
    rows3 = P(None, AXES, None)
    gains = P(None, AXES)
    return jax.shard_map(
        functools.partial(on_device, levels),
        mesh=mesh,
        in_specs=(
            P("seq", "ctx", None),
            P("seq", None),
            P("seq", "ctx", None),
            rows3,
            rows3,
            rows3,
            rows3,
            gains,
            rows3,
            rows3,
            rows3,
            gains,
        ),
        out_specs=(
            P("seq", "ctx", None),
            P("seq", "ctx", None),
            rows3,
            rows3,
            rows3,
            rows3,
            gains,
            rows3,
            rows3,
            rows3,
            gains,
        ),
        check_vma=False,
    )
```

```python
import functools
import math

import jax
import jax.numpy as jnp
from jax import lax
from jax.experimental import pallas as pl
from jax.experimental.pallas import tpu as pltpu
from jax.sharding import PartitionSpec as P

H = 16
KVH = 8
HD = 96
GROUP = 4

EPSILON = 1e-05
THETA = 100000.0
NEGATIVE = -1e30
AXES = ("seq", "ctx")
MESH = pl.DeviceIdType.MESH
ANY = pl.BlockSpec(memory_space=pltpu.HBM)
VMEM = pl.BlockSpec(memory_space=pltpu.VMEM)
BF = jnp.bfloat16
F32 = jnp.float32


def params(collective_id=None, mib=48):
    if collective_id is None:
        return pltpu.CompilerParams(vmem_limit_bytes=mib * 2**20)
    return pltpu.CompilerParams(
        collective_id=collective_id, has_side_effects=True, vmem_limit_bytes=mib * 2**20
    )


def place():
    s = lax.axis_index("seq")
    k = lax.axis_index("ctx")
    return s // 2, s % 2, k // 2, k % 2


def device(x, c, z, y):
    return (x * 2 + c, z * 2 + y)


def sequence_of(z, levels):
    return z // (levels // 4)


def level_of(c, z, levels):
    return lax.rem(z, levels // 4) * 2 + c


def home_of(x, c, z, y, levels):
    block = z * 2 + y
    level = block // GROUP
    place_z = (x * 2 + c) * (levels // 4) + level // 2
    return lax.rem(block, GROUP) // 2, lax.rem(level, 2), place_z, y


def origin_of(x, c, z, y, levels):
    s = sequence_of(z, levels)
    return s // 2, lax.rem(s, 2), 2 * level_of(c, z, levels) + x, y


def chain(x, c, z, y, levels):
    up = device(x, 1 - c, lax.rem(z + c, levels), y)
    down = device(x, 1 - c, lax.rem(z + levels - 1 + c, levels), y)
    return up, down


def remote(src, dst, send, recv, to):
    return pltpu.make_async_remote_copy(
        src_ref=src, dst_ref=dst, send_sem=send, recv_sem=recv, device_id=to, device_id_type=MESH
    )


def greet(partners, plan=None):
    barrier = pltpu.get_barrier_semaphore()
    for partner in partners:
        pl.semaphore_signal(barrier, inc=1, device_id=partner, device_id_type=MESH)
    expected = len(partners)
    if plan:
        expected = expected + plan.greet(barrier)
    pl.semaphore_wait(barrier, expected)


class Exchange:
    def __init__(self, levels, slabs=(), swaps=(), rows=(), tokens=(), back=False):
        self.levels, self.back = levels, back
        self.counts = len(slabs), len(swaps), len(rows), len(tokens)
        self.arrays = list(slabs) + list(swaps) + list(rows) + list(tokens)
        shapes = [jax.ShapeDtypeStruct(a.shape, a.dtype) for a in list(slabs) + list(swaps)]
        shapes += [jax.ShapeDtypeStruct((4,) + a.shape, a.dtype) for a in rows]
        self.out_shape = shapes + [jax.ShapeDtypeStruct(a.shape, a.dtype) for a in tokens]
        total = 2 * (len(slabs) + len(rows)) + len(self.arrays)
        self.scratch = [
            pltpu.SemaphoreType.DMA((total,)),
            pltpu.SemaphoreType.DMA((total,)),
            pltpu.SemaphoreType.DMA((len(self.arrays),)),
        ]

    def bind(self, ins, outs, send, recv, local):
        self.ins, self.outs = ins, outs
        self.send, self.recv, self.local = send, recv, local
        x, c, z, y = place()
        self.where = c, y
        self.others = [(1 - x, y), (x, 1 - y), (1 - x, 1 - y)]
        self.square = [device(ox, c, z, oy) for ox, oy in self.others]
        self.crossed = device(x, 1 - c, z, 1 - y)
        home = home_of(x, c, z, y, self.levels)
        origin = origin_of(x, c, z, y, self.levels)
        self.moves_away = (home[0] != x) | (home[1] != c) | (home[2] != z)
        taker, giver = (origin, home) if self.back else (home, origin)
        self.taker, self.giver = device(*taker), device(*giver)
        self.seq_others = [device(x, 1 - c, z, y), device(1 - x, 1 - c, z, y)]
        n_slab, n_swap, n_rows, n_tokens = self.counts
        me = x * 2 + y
        self.groups = [[] for _ in self.arrays]
        for i in range(n_slab):
            for j, (ox, oy) in enumerate(self.others):
                sem = 3 * i + j
                self.groups[i].append(
                    remote(
                        ins[i].at[:, ox * 2 + oy],
                        outs[i].at[:, me],
                        send.at[sem],
                        recv.at[sem],
                        self.square[j],
                    )
                )
            self.groups[i].append(
                pltpu.make_async_copy(ins[i].at[:, me], outs[i].at[:, me], local.at[i])
            )
        for i in range(n_rows):
            at = n_slab + n_swap + i
            sem = self.semaphore(at)
            mine = outs[at].at[x * 2 + c]
            for j, to in enumerate([self.square[0]] + self.seq_others):
                self.groups[at].append(
                    remote(ins[at], mine, send.at[sem + j], recv.at[sem + j], to)
                )
            self.groups[at].append(pltpu.make_async_copy(ins[at], mine, local.at[at]))
        self.moves = {n_slab + i: (self.crossed, c != y) for i in range(n_swap)}
        first = n_slab + n_swap + n_rows
        for i in range(n_tokens):
            self.moves[first + i] = self.taker, self.moves_away

    def semaphore(self, at):
        n_slab, n_swap, n_rows, _ = self.counts
        rows_before = min(max(at - n_slab - n_swap, 0), n_rows)
        return at + 2 * (n_slab + rows_before)

    def greet(self, barrier):
        c, y = self.where
        signal = functools.partial(pl.semaphore_signal, barrier, inc=1, device_id_type=MESH)
        for to in self.square:
            signal(device_id=to)
        expected = 3
        if self.counts[1]:
            expected = expected + lax.rem(c + y, 2)
            pl.when(c != y)(lambda: signal(device_id=self.crossed))
        if self.counts[2]:
            expected = expected + 2
            for to in self.seq_others:
                signal(device_id=to)
        if self.counts[3]:
            expected = expected + jnp.where(self.moves_away, 1, 0)
            pl.when(self.moves_away)(lambda: signal(device_id=self.giver))
        return expected

    def whole(self, at, to):
        sem = self.semaphore(at)
        return (
            remote(self.ins[at], self.outs[at], self.send.at[sem], self.recv.at[sem], to),
            pltpu.make_async_copy(self.ins[at], self.outs[at], self.local.at[at]),
        )

    def start(self, which=None):
        for at in range(len(self.arrays)) if which is None else which:
            for copy in self.groups[at]:
                copy.start()
            if at in self.moves:
                to, goes = self.moves[at]
                cross, stay = self.whole(at, to)
                pl.when(goes)(cross.start)
                pl.when(jnp.logical_not(goes))(stay.start)

    def wait(self, which=None):
        for at in range(len(self.arrays)) if which is None else which:
            for copy in self.groups[at]:
                copy.wait()
            if at in self.moves:
                to, goes = self.moves[at]
                cross, stay = self.whole(at, to)
                pl.when(goes)(cross.wait)
                pl.when(jnp.logical_not(goes))(stay.wait)


def exchange_kernel(plan, n_spread, gathers, *refs):
    n = len(plan.arrays)
    own_ref = all_ref = None
    if gathers:
        refs = list(refs)
        own_ref, all_ref = refs.pop(n), refs.pop(2 * n + n_spread)
    outs = refs[n : 2 * n]
    spread_out = refs[2 * n : 2 * n + n_spread]
    scratch = refs[2 * n + n_spread :]
    plan.bind(refs[:n], outs, *scratch[:3])
    barrier = pltpu.get_barrier_semaphore()
    if not n_spread:
        pl.semaphore_wait(barrier, plan.greet(barrier))
        plan.start()
        plan.wait()
        return
    swap = plan.counts[0]
    line = Line(plan.levels)
    spread = Spread(line, [outs[0].at[0], outs[swap]], spread_out, *scratch[3:8])
    gather = Gather(own_ref, all_ref, *scratch[8:]) if own_ref is not None else None
    greet(line.partners + [line.other_core], plan)
    rest = [at for at in range(n) if at not in (0, swap)]
    plan.start([0, swap])
    plan.start(rest)
    plan.wait([0, swap])
    spread.start()
    if gather:
        gather.start()
    plan.wait(rest)
    if gather:
        gather.finish()
    spread.finish()


class Gather:
    def __init__(self, own, everyone, send, recv, local):
        x, c, z, y = place()
        me, at_x, at_y = x * 2 + y, (1 - x) * 2 + y, x * 2 + 1 - y
        to_x, to_y = device(1 - x, c, z, y), device(x, c, z, 1 - y)
        half = own.shape[0] // 2
        low, high = pl.ds(0, half), pl.ds(half, half)
        ends = [
            (own.at[low], everyone.at[me, low], to_x),
            (own.at[high], everyone.at[me, high], to_y),
            (own.at[high], everyone.at[me, high], to_x),
            (own.at[low], everyone.at[me, low], to_y),
            (everyone.at[at_x, low], everyone.at[at_x, low], to_y),
            (everyone.at[at_y, high], everyone.at[at_y, high], to_x),
        ]
        self.copies = [
            remote(src, dst, send.at[i], recv.at[i], to) for i, (src, dst, to) in enumerate(ends)
        ]
        self.keep = pltpu.make_async_copy(own, everyone.at[me], local.at[0])

    def start(self):
        for copy in self.copies[:4]:
            copy.start()
        self.keep.start()

    def finish(self):
        for i in (0, 1):
            self.copies[i].wait_recv()
            self.copies[4 + i].start()
        for copy in self.copies[2:]:
            copy.wait_recv()
        for copy in self.copies:
            copy.wait_send()
        self.keep.wait()


def exchange(
    levels, slabs, swaps, collective_id, rows=(), tokens=(), back=False, spread=False, own=None
):
    mib = 63 if spread else 48
    plan = Exchange(levels, slabs, swaps, rows, tokens, back)
    n = len(plan.arrays)
    spreads = [slabs[0].shape[1:], swaps[0].shape] if spread else []
    out_shape = plan.out_shape + [
        jax.ShapeDtypeStruct((2, levels) + shape, BF) for shape in spreads
    ]
    scratch = plan.scratch + (spread_scratch(2, levels) if spread else [])
    operands = list(plan.arrays)
    if own is not None:
        operands.append(own)
        out_shape.append(jax.ShapeDtypeStruct((GROUP,) + own.shape, own.dtype))
        scratch += [pltpu.SemaphoreType.DMA((n,)) for n in (6, 6, 1)]
    return pl.pallas_call(
        functools.partial(exchange_kernel, plan, len(spreads), own is not None),
        out_shape=out_shape,
        in_specs=[ANY] * len(operands),
        out_specs=[ANY] * len(out_shape),
        scratch_shapes=scratch,
        compiler_params=params(collective_id, mib),
        name="exchange",
    )(*operands)


class Line:
    def __init__(self, levels):
        x, c, z, y = place()
        self.levels, self.c, self.z = levels, c, z
        self.ahead = [lax.rem(z + d, levels) for d in range(levels)]
        self.behind = [lax.rem(z - d + levels, levels) for d in range(levels)]
        self.device = lambda to: device(x, c, to, y)
        self.other_core = device(x, 1 - c, z, y)
        self.partners = [self.device(self.ahead[d]) for d in range(1, levels)]
        self.near = list(dict.fromkeys([2, levels - 2])) + [
            d for d in range(1, levels) if d not in (2, levels - 2)
        ]
        self.bottom, self.top = z == 0, z == levels - 1
        self.low, self.high = z == 1, z == levels - 2

    def to_far_end(self, d):
        return (self.bottom & (d == self.levels - 1)) | (self.top & (d == 1))

    def by_way_to(self, d):
        return (self.low & (d == self.levels - 2)) | (self.high & (d == 2))

    def from_far_end(self, d):
        return (self.top & (d == self.levels - 1)) | (self.bottom & (d == 1))


class Spread:
    def __init__(self, line, sources, outs, send, recv, cross_send, cross_recv, local):
        self.line, self.sources, self.outs = line, sources, outs
        self.send, self.recv, self.local = send, recv, local
        self.cross_send, self.cross_recv = cross_send, cross_recv
        self.count = range(len(sources))

    def to_line(self, i, d):
        line = self.line
        block = self.outs[i].at[line.c, line.z]
        to = line.device(line.ahead[d])
        return remote(self.sources[i], block, self.send.at[i, d], self.recv.at[i, d], to)

    def to_core(self, i, d):
        line = self.line
        block = self.outs[i].at[line.c, line.behind[d]]
        source = block if d else self.sources[i]
        return remote(
            source, block, self.cross_send.at[i, d], self.cross_recv.at[i, d], line.other_core
        )

    def onward(self, i, d):
        line = self.line
        block = self.outs[i].at[line.c, line.behind[d]]
        end = jnp.where(line.low, 0, line.levels - 1)
        slot = jnp.where(line.low, 1, line.levels - 1)
        return remote(
            block, block, self.send.at[i, 0], self.recv.at[i, slot], line.device(end)
        )

    def passes_on(self, d):
        line = self.line
        return (line.high & (d == line.levels - 2)) | (line.low & (d == 2))

    def keep(self, i):
        line = self.line
        return pltpu.make_async_copy(
            self.sources[i], self.outs[i].at[line.c, line.z], self.local.at[i]
        )

    def start(self):
        for i in self.count:
            for d in self.line.near:
                pl.when(jnp.logical_not(self.line.to_far_end(d)))(self.to_line(i, d).start)
            self.to_core(i, 0).start()
            self.keep(i).start()

    def finish(self):
        line = self.line
        for i in self.count:
            for d in line.near:
                block = self.outs[i].at[line.c, line.behind[d]]
                remote(
                    block, block, self.send.at[i, d], self.recv.at[i, d], line.other_core
                ).wait_recv()
                pl.when(self.passes_on(d))(self.onward(i, d).start)
                self.to_core(i, d).start()
        for i in self.count:
            for d in range(line.levels):
                block = self.outs[i].at[1 - line.c, line.behind[d]]
                remote(
                    block, block, self.cross_send.at[i, d], self.cross_recv.at[i, d], line.other_core
                ).wait_recv()
            for d in line.near:
                pl.when(jnp.logical_not(line.to_far_end(d)))(self.to_line(i, d).wait_send)
                pl.when(self.passes_on(d))(self.onward(i, d).wait_send)
            for d in range(line.levels):
                self.to_core(i, d).wait_send()
            self.keep(i).wait()


def spread_scratch(n, levels):
    dma = lambda *shape: pltpu.SemaphoreType.DMA(shape)
    return [dma(n, levels), dma(n, levels), dma(n, levels), dma(n, levels), dma(n)]


class Collect:
    def __init__(self, line, sources, slots, folds, relays, send, recv, relay_send, relay_recv):
        self.line, self.sources, self.slots = line, sources, slots
        self.folds, self.relays = folds, relays
        self.send, self.recv = send, recv
        self.relay_send, self.relay_recv = relay_send, relay_recv

    def clear(self):
        for slot in self.slots:
            for d in (1, self.line.levels - 1):

                @pl.when(self.line.from_far_end(d))
                def _(slot=slot, d=d):
                    slot[d] = jnp.zeros_like(slot[d])

    def direct(self, i, d):
        line = self.line
        return remote(
            self.sources[i].at[line.ahead[d]],
            self.slots[i].at[d],
            self.send.at[i, d],
            self.recv.at[i, d],
            line.device(line.ahead[d]),
        )

    def goes_direct(self, d):
        return jnp.logical_not(self.line.to_far_end(d) | self.line.by_way_to(d))

    def via(self, i):
        line = self.line
        far = jnp.where(line.bottom, line.levels - 1, 0)
        to = jnp.where(line.bottom, 1, line.levels - 2)
        return remote(
            self.sources[i].at[far],
            self.relays[i],
            self.relay_send.at[i],
            self.relay_recv.at[i],
            line.device(to),
        )

    def folded(self, i):
        line = self.line
        end = jnp.where(line.low, line.levels - 1, 0)
        slot = jnp.where(line.low, line.levels - 2, 2)
        return end, remote(
            self.folds[i],
            self.slots[i].at[slot],
            self.send.at[i, 0],
            self.recv.at[i, slot],
            line.device(end),
        )

    def start(self, i):
        line = self.line
        pl.when(line.bottom | line.top)(self.via(i).start)
        for d in range(1, line.levels):
            pl.when(self.goes_direct(d))(self.direct(i, d).start)

    def relay(self, i):
        line = self.line

        @pl.when(line.low | line.high)
        def _():
            end, copy = self.folded(i)
            self.via(i).wait_recv()
            self.folds[i][...] = (
                self.sources[i][end].astype(F32) + self.relays[i][...].astype(F32)
            ).astype(BF)
            copy.start()

    def finish(self, i, out):
        line = self.line
        total = self.sources[i][line.z].astype(F32)
        for d in range(1, line.levels):
            block = self.slots[i].at[d]
            came = remote(block, block, self.send.at[i, d], self.recv.at[i, d], line.other_core)
            pl.when(jnp.logical_not(line.from_far_end(d)))(came.wait_recv)
            total = total + self.slots[i][d].astype(F32)
        out[...] = total.astype(BF)
        pl.when(line.bottom | line.top)(self.via(i).wait_send)
        pl.when(line.low | line.high)(self.folded(i)[1].wait_send)
        for d in range(1, line.levels):
            pl.when(self.goes_direct(d))(self.direct(i, d).wait_send)


def collect_scratch(shapes):
    dma = lambda *shape: pltpu.SemaphoreType.DMA(shape)
    n, levels = len(shapes), shapes[0][0]
    scratch = [pltpu.VMEM(a, BF) for a in shapes]
    scratch += [pltpu.VMEM(a[1:], BF) for a in shapes] * 2
    return scratch + [dma(n, levels), dma(n, levels), dma(n), dma(n)]


class CoreSum:
    def __init__(self, levels, pairs, away, came, send, recv):
        self.levels, self.away, self.came = levels, away, came
        self.send, self.recv = send, recv
        x, c, z, y = place()
        self.core, self.other_core = c, device(x, 1 - c, z, y)
        self.width = away.shape[2]
        self.entries, self.turned = [], {}
        first = 0
        for a, b in pairs:
            n = a.shape[1] // 2 // levels
            for k in range(b.shape[1] // self.width):
                self.entries.append((a, b, k, first, n))
                first += n

    def product(self, i, core, mine):
        a, b, k, _, _ = self.entries[i]
        key = (id(a), mine)
        if key not in self.turned:
            half = a.shape[1] // 2
            self.turned[key] = a[:, pl.ds(pl.multiple_of(core * half, 128), half)].T
        columns = pl.ds(k * self.width, self.width)
        return jnp.dot(self.turned[key], b[:, columns], preferred_element_type=F32)

    def move(self, i):
        rows = pl.ds(self.entries[i][3], self.entries[i][4])
        return remote(
            self.away.at[:, rows],
            self.came.at[:, rows],
            self.send.at[i],
            self.recv.at[i],
            self.other_core,
        )

    def give(self, which):
        for i in which:
            result = self.product(i, 1 - self.core, False)
            _, _, _, first, n = self.entries[i]
            for level in range(self.levels):
                self.away[level, pl.ds(first, n)] = result[level * n : (level + 1) * n].astype(BF)
            self.move(i).start()

    def keep(self, which, out):
        for i in which:
            result = self.product(i, self.core, True)
            _, _, _, first, n = self.entries[i]
            rows = pl.ds(first, n)
            self.move(i).wait_recv()
            for level in range(self.levels):
                block = result[level * n : (level + 1) * n]
                out[level, rows] = (block + self.came[level, rows].astype(F32)).astype(BF)

    def end(self):
        for i in range(len(self.entries)):
            self.move(i).wait_send()


def core_sum_shape(levels, pairs, width):
    rows = sum(a.shape[1] // 2 // levels * (b.shape[1] // width) for a, b in pairs)
    return (levels, rows, width)


def core_sum_scratch(levels, pairs, width):
    shape = core_sum_shape(levels, pairs, width)
    chunks = sum(b.shape[1] // width for _, b in pairs)
    return [
        pltpu.VMEM(shape, BF),
        pltpu.VMEM(shape, BF),
        pltpu.SemaphoreType.DMA((chunks,)),
        pltpu.SemaphoreType.DMA((chunks,)),
    ]


CW = 512


def ffn_gradient_kernel(levels, n, *refs):
    pairs = [refs[2 * i : 2 * i + 2] for i in range(n)]
    out = refs[2 * n]
    total = CoreSum(levels, pairs, *refs[2 * n + 1 :])
    greet([total.other_core])
    chunks = range(len(total.entries))
    total.give(chunks)
    total.keep(chunks, out)
    total.end()


def ffn_gradient(levels, pairs, collective_id):
    operands = [a for pair in pairs for a in pair]
    return pl.pallas_call(
        functools.partial(ffn_gradient_kernel, levels, len(pairs)),
        out_shape=jax.ShapeDtypeStruct(core_sum_shape(levels, pairs, CW), BF),
        in_specs=[VMEM] * len(operands),
        out_specs=VMEM,
        scratch_shapes=core_sum_scratch(levels, pairs, CW),
        compiler_params=params(collective_id),
        name="ffn_gradient",
    )(*operands)


def norm_scale(values):
    return lax.rsqrt(jnp.mean(values * values, axis=-1, keepdims=True) + EPSILON)


def line_order(flat, levels):
    n = 2 * levels
    w = flat.shape[1] // (2 * n)
    return jnp.concatenate(
        [flat[:, (i * n + j) * w : (i * n + j + 1) * w] for j in range(n) for i in range(2)], axis=1
    )


def place_order(flat, levels):
    n = 2 * levels
    w = flat.shape[1] // (2 * n)
    return jnp.concatenate(
        [flat[:, (j * 2 + i) * w : (j * 2 + i + 1) * w] for i in range(2) for j in range(n)], axis=1
    )


def square_kernel(mode, levels, collects, second, plan, *refs):
    gathers = mode != "last"
    refs = list(refs)
    take = lambda n: [refs.pop(0) for _ in range(n)]
    part_ref = take(1)[0]
    rows_in = take(2 if mode in ("backward", "last") else 1)
    part2_ref, rows2_ref = take(2) if second else (None, None)
    pair_in, ready = take(2 * min(collects, 1)), take(max(collects - 1, 0))
    slab_ref = take(1)[0] if plan else None
    kept_ref = take(1)[0] if gathers else None
    kept2_ref = take(1)[0] if second else None
    all_ref = take(1)[0] if gathers else None
    collect_out = take(collects)
    plan_out = take(len(plan.arrays)) if plan else None
    if mode == "last":
        kept_ref = take(1)[0]
    scatter_refs = take(6)
    scatter2_refs = take(6) if second else None
    if gathers:
        ag_send, ag_recv = take(2)
    line = Line(levels)
    product = collect = None
    if collects:
        held = take(1)[0]
        slots, folds, relays = take(collects), take(collects), take(collects)
        collect = Collect(line, [held] + ready, slots, folds, relays, *take(4))
        product = CoreSum(levels, [pair_in], *take(4))
    if plan:
        plan.bind([slab_ref, kept_ref], plan_out, *take(3))
    x, c, z, y = place()
    me, at_x, at_y, at_xy = x * 2 + y, (1 - x) * 2 + y, x * 2 + 1 - y, (1 - x) * 2 + 1 - y
    to_x, to_y = device(1 - x, c, z, y), device(x, c, z, 1 - y)
    partners = [to_x, to_y]
    if collect:
        partners += line.partners + [line.other_core]
    greet(partners, plan)
    if collect:
        collect.clear()

    def finish_side():
        if collect:
            for i in range(collects):
                collect.finish(i, collect_out[i])
            product.end()
        if plan:
            plan.wait()

    rows = rows_in[0].shape[0]
    half = rows // 2
    low, high = pl.ds(0, half), pl.ds(half, half)
    copies = []
    if gathers:
        x_low, y_high, x_high, y_low = [
            remote(all_ref.at[me, part], all_ref.at[me, part], ag_send.at[i], ag_recv.at[i], to)
            for i, (part, to) in enumerate([(low, to_x), (high, to_y), (high, to_x), (low, to_y)])
        ]
        there = all_ref.at[at_x, low]
        on_y = remote(there, there, ag_send.at[4], ag_recv.at[4], to_y)
        there = all_ref.at[at_y, high]
        on_x = remote(there, there, ag_send.at[5], ag_recv.at[5], to_x)
    class Scatter:
        def __init__(self, part_ref, diag, sums, from_x, from_y, send, recv):
            self.part_ref, self.diag, self.sums = part_ref, diag, sums
            self.from_x, self.from_y = from_x, from_y
            ends = [
                (part_ref.at[at_xy, low], diag.at[0], to_x),
                (part_ref.at[at_xy, high], diag.at[1], to_y),
                (part_ref.at[at_x, low], from_x.at[low], to_x),
                (part_ref.at[at_y, high], from_y.at[high], to_y),
                (sums.at[0], from_x.at[high], to_x),
                (sums.at[1], from_y.at[low], to_y),
            ]
            self.copies = [
                remote(src, dst, send.at[i], recv.at[i], to) for i, (src, dst, to) in enumerate(ends)
            ]

        def start(self):
            for copy in self.copies[:4]:
                copy.start()

        def relay(self):
            x_diag, y_diag, _, _, x_two, y_two = self.copies
            y_diag.wait_recv()
            self.sums[0] = (
                self.part_ref[at_x, high].astype(F32) + self.diag[1].astype(F32)
            ).astype(BF)
            x_two.start()
            x_diag.wait_recv()
            self.sums[1] = (
                self.part_ref[at_y, low].astype(F32) + self.diag[0].astype(F32)
            ).astype(BF)
            y_two.start()

        def wait_low(self):
            self.copies[2].wait_recv()
            self.copies[5].wait_recv()

        def wait_high(self):
            self.copies[4].wait_recv()
            self.copies[3].wait_recv()

        def total(self, part):
            return (
                self.part_ref[me, part].astype(F32)
                + self.from_x[part].astype(F32)
                + self.from_y[part].astype(F32)
            )

    scatter = Scatter(part_ref, *scatter_refs)
    scatter.start()
    if plan:
        plan.start([0])
    for i in range(1, collects):
        collect.start(i)
    if second:
        scatter2 = Scatter(part2_ref, *scatter2_refs)
        scatter2.start()
    if product:
        product.give([0])
    scatter.relay()
    copies += scatter.copies
    if product:
        product.keep([0], held)
        collect.start(0)
        for i in range(1, collects):
            collect.relay(i)

    def own_step(part):
        total = scatter.total(part)
        if mode == "forward":
            values = rows_in[0][part] + total
            kept_ref[part] = values
            all_ref[me, part] = line_order((values * norm_scale(values)).astype(BF), levels)
        else:
            total = place_order(total, levels)
            upstream, values = rows_in[0][part], rows_in[1][part]
            scale = norm_scale(values)
            norm = values * scale
            result = upstream + scale * (
                total - norm * jnp.mean(total * norm, axis=-1, keepdims=True)
            )
            kept_ref[part] = result.astype(kept_ref.dtype)
            if gathers:
                all_ref[me, part] = result.astype(BF)

    scatter.wait_low()
    own_step(low)
    if gathers:
        x_low.start()
        y_low.start()
    scatter.wait_high()
    own_step(high)
    if mode == "last":
        plan.start([1])

    def finish_second():
        scatter2.relay()
        scatter2.wait_low()
        scatter2.wait_high()
        kept2_ref[...] = (rows2_ref[...] + scatter2.total(slice(None))).astype(BF)
        copies.extend(scatter2.copies)

    if gathers:
        y_high.start()
        x_high.start()
        x_low.wait_recv()
        on_y.start()
        y_high.wait_recv()
        on_x.start()
        x_high.wait_recv()
        y_low.wait_recv()
        on_y.wait_recv()
        on_x.wait_recv()
        copies += [x_low, y_high, x_high, y_low, on_y, on_x]
    if collect:
        collect.relay(0)
    if second:
        finish_second()
    for copy in copies:
        copy.wait_send()
    finish_side()


def square(
    mode, levels, parts, rows_in, collective_id, collect=(), ready=(), second=(), slab=None
):
    rows, width = rows_in[0].shape
    gathers = mode != "last"
    dma = lambda *shape: pltpu.SemaphoreType.DMA(shape)
    like = lambda kind: jax.ShapeDtypeStruct((rows, width), kind)
    for_scatter = [pltpu.VMEM((2, rows // 2, width), BF)] * 2
    for_scatter += [pltpu.VMEM((rows, width), BF)] * 2 + [dma(6), dma(6)]
    plan = None
    if mode == "last":
        plan = Exchange(levels, [slab], tokens=[like(BF)], back=True)
    operands = [parts] + list(rows_in) + list(second)
    operands += list(collect) + list(ready)
    in_specs = [VMEM] * len(operands)
    out_shape, scratch = [], []
    if mode == "last":
        scratch.append(pltpu.VMEM((rows, width), BF))
    else:
        out_shape.append(like(F32))
    scratch += for_scatter
    if second:
        out_shape.append(like(BF))
        scratch += for_scatter
    if gathers:
        out_shape.append(jax.ShapeDtypeStruct((GROUP, rows, width), BF))
        scratch += [dma(6), dma(6)]
    out_specs = [VMEM] * len(out_shape)
    collects = 0
    if collect:
        shape = core_sum_shape(levels, [collect], collect[1].shape[1])
        shapes = [shape] + [a.shape for a in ready]
        collects = len(shapes)
        out_specs += [VMEM] * collects
        out_shape += [jax.ShapeDtypeStruct(a[1:], BF) for a in shapes]
        scratch += [pltpu.VMEM(shape, BF)] + collect_scratch(shapes)
        scratch += core_sum_scratch(levels, [collect], shape[2])
    if plan:
        operands.append(slab)
        in_specs.append(ANY)
        out_specs += [ANY] * len(plan.arrays)
        out_shape += plan.out_shape
        scratch += plan.scratch
    return pl.pallas_call(
        functools.partial(
            square_kernel, mode, levels, collects, bool(second), plan
        ),
        out_shape=out_shape,
        in_specs=in_specs,
        out_specs=out_specs,
        scratch_shapes=scratch,
        compiler_params=params(collective_id),
        name="square_" + mode,
    )(*operands)


PIECES = 4


def piece_rows(rows):
    return [pl.ds(i * (rows // PIECES), rows // PIECES) for i in range(PIECES)]


def climb_kernel(planes, levels, own_ref, out_ref, send, recv, local):
    x, c, z, y = place()
    up, down = chain(x, c, z, y, planes)
    z = level_of(c, z, planes)
    pieces = piece_rows(own_ref.shape[0])
    barrier = pltpu.get_barrier_semaphore()

    @pl.when(z > 0)
    def _():
        pl.semaphore_signal(barrier, inc=1, device_id=down, device_id_type=MESH)

    @pl.when(z < levels - 1)
    def _():
        pl.semaphore_wait(barrier, 1)

    keep = pltpu.make_async_copy(own_ref, out_ref.at[z], local.at[0])
    keep.start()

    def hop(distance, piece):
        block = lax.rem(z - distance + levels, levels)
        source = own_ref.at[pieces[piece]] if distance == 0 else out_ref.at[block, pieces[piece]]
        return remote(
            source,
            out_ref.at[block, pieces[piece]],
            send.at[distance, piece],
            recv.at[distance, piece],
            up,
        )

    def came(distance, piece):
        block = lax.rem(z - distance + levels, levels)
        there = out_ref.at[block, pieces[piece]]
        return remote(there, there, send.at[distance - 1, piece], recv.at[distance - 1, piece], up)

    @pl.when(z < levels - 1)
    def _():
        for piece in range(PIECES):
            hop(0, piece).start()

    for distance in range(1, levels):

        @pl.when(z >= distance)
        def _(distance=distance):
            for piece in range(PIECES):
                came(distance, piece).wait_recv()

                @pl.when(z < levels - 1)
                def _(piece=piece):
                    hop(distance, piece).start()

    for distance in range(levels):

        @pl.when((z >= distance) & (z < levels - 1))
        def _(distance=distance):
            for piece in range(PIECES):
                hop(distance, piece).wait_send()

    keep.wait()


def climb(own, planes, collective_id):
    levels = planes // 2
    return pl.pallas_call(
        functools.partial(climb_kernel, planes, levels),
        out_shape=jax.ShapeDtypeStruct((levels,) + own.shape, own.dtype),
        in_specs=[ANY],
        out_specs=ANY,
        scratch_shapes=[
            pltpu.SemaphoreType.DMA((levels, PIECES)),
            pltpu.SemaphoreType.DMA((levels, PIECES)),
            pltpu.SemaphoreType.DMA((1,)),
        ],
        compiler_params=params(collective_id),
        name="climb",
    )(own)


def dot_nt(a, b):
    return lax.dot_general(a, b, (((1,), (1,)), ((), ())), preferred_element_type=F32)


def dot_tn(a, b):
    return lax.dot_general(a, b, (((0,), (0,)), ((), ())), preferred_element_type=F32)


def two_heads(block, j):
    a = block[:, 2 * j * HD : (2 * j + 1) * HD]
    b = block[:, (2 * j + 1) * HD : (2 * j + 2) * HD]
    return jnp.concatenate([a, b], axis=0)


def visible_keys(z, level, span, row_segs, key_segs):
    rows = lax.broadcasted_iota(jnp.int32, (span, span), 0)
    cols = lax.broadcasted_iota(jnp.int32, (span, span), 1)
    mask = (row_segs == key_segs) & ((cols <= rows) | (level < z))
    return jnp.concatenate([mask, mask], axis=0)


def attend_kernel(planes, q_ref, kv_ref, row_ref, key_ref, out_ref, lse_ref):
    _, c, z, _ = place()
    here = level_of(c, z, planes)
    scaling = 1.0 / math.sqrt(HD)
    span = q_ref.shape[0]
    queries = [two_heads(q_ref[...], j) for j in range(2)]

    def step(level, carry):
        block = kv_ref[level]
        mask = visible_keys(here, level, span, row_ref[...], key_ref[level])
        after = []
        for j in range(2):
            top, total, accum = carry[3 * j : 3 * j + 3]
            keys = block[:, j * HD : (j + 1) * HD]
            values = block[:, (2 + j) * HD : (3 + j) * HD]
            scores = dot_nt(queries[j], keys) * scaling
            scores = jnp.where(mask, scores, NEGATIVE)
            new = jnp.maximum(top, jnp.max(scores, axis=-1, keepdims=True))
            scale = jnp.exp(top - new)
            weights = jnp.where(mask, jnp.exp(scores - new), 0.0)
            total = total * scale + jnp.sum(weights, axis=-1, keepdims=True)
            accum = accum * scale + jnp.dot(weights.astype(BF), values, preferred_element_type=F32)
            after += [new, total, accum]
        return tuple(after)

    start = (
        jnp.full((2 * span, 1), NEGATIVE, F32),
        jnp.zeros((2 * span, 1), F32),
        jnp.zeros((2 * span, HD), F32),
    )
    done = lax.fori_loop(0, here + 1, step, start + start)
    outs, lses = [], []
    for j in range(2):
        top, total, accum = done[3 * j : 3 * j + 3]
        result = (accum / total).astype(BF)
        wide = jnp.broadcast_to(top + jnp.log(total), (2 * span, 32))
        outs += [result[:span], result[span:]]
        lses += [wide[:span], wide[span:]]
    out_ref[...] = jnp.concatenate(outs, axis=1)
    lse_ref[...] = jnp.concatenate(lses, axis=1)


def attend(q, kv, row_segs, key_segs, planes):
    rows, width = q.shape
    return pl.pallas_call(
        functools.partial(attend_kernel, planes),
        out_shape=[
            jax.ShapeDtypeStruct((rows, width), BF),
            jax.ShapeDtypeStruct((rows, 128), F32),
        ],
        in_specs=[VMEM] * 4,
        out_specs=[VMEM] * 2,
        compiler_params=params(),
        name="attend",
    )(q, kv, row_segs, key_segs)


def turn_back(block, cosine, sine):
    a, b = block[:, : HD // 2], block[:, HD // 2 :]
    return jnp.concatenate([a * cosine + b * sine, b * cosine - a * sine], axis=1)


def attend_back_kernel(planes, plan, *refs):
    refs = list(refs)
    take = lambda n: [refs.pop(0) for _ in range(n)]
    q_ref, kv_ref, row_ref, key_ref, out_ref, lse_ref, back_ref, cos_ref, sin_ref, mid_ref = take(10)
    side_in = take(len(plan.arrays) if plan else 0)
    dqkv_ref, dout_ref = take(2)
    side_out = take(len(plan.arrays) if plan else 0)
    part, came, sums, heads_q, heads_back, lse4, delta4, dq4, send, recv = take(10)
    own, away, came_out, out_send, out_recv = take(5)
    levels = kv_ref.shape[0]
    x, c, z, y = place()
    up, down = chain(x, c, z, y, planes)
    other_core = device(x, 1 - c, z, y)
    z = level_of(c, z, planes)
    top = levels - 1
    span = q_ref.shape[0]
    scaling = 1.0 / math.sqrt(HD)
    pieces = piece_rows(span)
    barrier = pltpu.get_barrier_semaphore()
    pl.semaphore_signal(barrier, inc=1, device_id=other_core, device_id_type=MESH)

    @pl.when(z < top)
    def _():
        pl.semaphore_signal(barrier, inc=1, device_id=up, device_id_type=MESH)

    expected = 1 + jnp.minimum(z, 1)
    if plan:
        plan.bind(side_in, side_out, *refs)
        expected = expected + plan.greet(barrier)
    pl.semaphore_wait(barrier, expected)
    if plan:
        plan.start()

    def hop(block, piece, source):
        rows = pieces[piece]
        return remote(
            source.at[block, rows],
            came.at[block, rows],
            send.at[block, piece],
            recv.at[block, piece],
            down,
        )

    lse_all = lse_ref[...]
    for j in range(2):
        back = two_heads(back_ref[...], j)
        heads_q[j] = two_heads(q_ref[...], j)
        heads_back[j] = back
        lse4[j] = jnp.concatenate(
            [lse_all[:, 64 * j : 64 * j + 1], lse_all[:, 64 * j + 32 : 64 * j + 33]], axis=0
        )
        out = two_heads(out_ref[...], j)
        delta4[j] = jnp.sum(back.astype(F32) * out.astype(F32), axis=-1, keepdims=True)
        dq4[j] = jnp.zeros((2 * span, HD), F32)

    def one_level(level, nothing):
        block = kv_ref[level]
        mask = visible_keys(z, level, span, row_ref[...], key_ref[level])
        dks, dvs = [], []
        for j in range(2):
            keys = block[:, j * HD : (j + 1) * HD]
            values = block[:, (2 + j) * HD : (3 + j) * HD]
            queries, back = heads_q[j], heads_back[j]
            scores = dot_nt(queries, keys) * scaling
            probs = jnp.where(mask, jnp.exp(scores - lse4[j]), 0.0)
            dprobs = dot_nt(back, values)
            dscores = (probs * (dprobs - delta4[j]) * scaling).astype(BF)
            dq4[j] += jnp.dot(dscores, keys, preferred_element_type=F32)
            dks.append(dot_tn(dscores, queries).astype(BF))
            dvs.append(dot_tn(probs.astype(BF), back).astype(BF))
        part[level] = jnp.concatenate(dks + dvs, axis=1)

        @pl.when((z == top) & (level < top))
        def _():
            for piece in range(PIECES):
                hop(level, piece, part).start()

        return nothing

    lax.fori_loop(0, z + 1, one_level, 0)

    rb = own.shape[1]
    wide = own.shape[2]
    for k in range(wide // CW):
        columns = pl.ds(k * CW, CW)
        product = dot_tn(out_ref[...], mid_ref[:, columns])
        for level in range(planes):
            first = product[2 * level * rb : (2 * level + 1) * rb]
            second = product[(2 * level + 1) * rb : (2 * level + 2) * rb]
            own[level, :, columns] = jnp.where(c == 0, first, second)
            away[level, :, columns] = jnp.where(c == 0, second, first).astype(BF)
    cross = remote(away, came_out, out_send.at[0], out_recv.at[0], other_core)
    cross.start()

    heads = []
    for j in range(2):
        both = dq4[j]
        heads += [
            turn_back(both[:span], cos_ref[...], sin_ref[...]),
            turn_back(both[span:], cos_ref[...], sin_ref[...]),
        ]
    dqkv_ref[:, : 4 * HD] = jnp.concatenate(heads, axis=1).astype(BF)

    def store(total, rows):
        cosine, sine = cos_ref[rows, :], sin_ref[rows, :]
        heads = [turn_back(total[:, j * HD : (j + 1) * HD], cosine, sine) for j in range(2)]
        dqkv_ref[rows, 4 * HD :] = jnp.concatenate(heads + [total[:, 2 * HD :]], axis=1).astype(BF)

    @pl.when(z == top)
    def _():
        for piece in range(PIECES):
            rows = pieces[piece]
            store(part[top, rows].astype(F32), rows)
        for block in range(top):
            for piece in range(PIECES):
                hop(block, piece, part).wait_send()

    @pl.when(z < top)
    def _():
        for block in range(top):

            @pl.when(block < z)
            def _(block=block):
                for piece in range(PIECES):
                    rows = pieces[piece]
                    hop(block, piece, sums).wait_recv()
                    sums[block, rows] = (
                        part[block, rows].astype(F32) + came[block, rows].astype(F32)
                    ).astype(BF)
                    hop(block, piece, sums).start()

            @pl.when(block == z)
            def _(block=block):
                for piece in range(PIECES):
                    rows = pieces[piece]
                    hop(block, piece, sums).wait_recv()
                    store(part[block, rows].astype(F32) + came[block, rows].astype(F32), rows)

        for block in range(top):

            @pl.when(block < z)
            def _(block=block):
                for piece in range(PIECES):
                    hop(block, piece, sums).wait_send()

    cross.wait_recv()
    for level in range(planes):
        dout_ref[level] = (own[level] + came_out[level].astype(F32)).astype(BF)
    cross.wait_send()
    if plan:
        plan.wait()


def attend_back(operands, rb, planes, collective_id, slabs=(), swaps=(), tokens=()):
    q, kv, mid_all = operands[0], operands[1], operands[-1]
    levels = kv.shape[0]
    rows, width = q.shape
    plan = Exchange(planes, slabs, swaps, (), tokens, True) if slabs or swaps else None
    side = plan.arrays if plan else []
    heads = (2, 2 * rows, HD)
    column = (2, 2 * rows, 1)
    dout = (planes, rb, mid_all.shape[1])
    return pl.pallas_call(
        functools.partial(attend_back_kernel, planes, plan),
        out_shape=[jax.ShapeDtypeStruct((rows, 2 * width), BF), jax.ShapeDtypeStruct(dout, BF)]
        + (plan.out_shape if plan else []),
        in_specs=[VMEM] * len(operands) + [ANY] * len(side),
        out_specs=[VMEM] * 2 + [ANY] * len(side),
        scratch_shapes=[
            pltpu.VMEM(kv.shape, BF),
            pltpu.VMEM(kv.shape, BF),
            pltpu.VMEM(kv.shape, BF),
            pltpu.VMEM(heads, BF),
            pltpu.VMEM(heads, BF),
            pltpu.VMEM(column, F32),
            pltpu.VMEM(column, F32),
            pltpu.VMEM(heads, F32),
            pltpu.SemaphoreType.DMA((levels, PIECES)),
            pltpu.SemaphoreType.DMA((levels, PIECES)),
            pltpu.VMEM(dout, F32),
            pltpu.VMEM(dout, BF),
            pltpu.VMEM(dout, BF),
            pltpu.SemaphoreType.DMA((1,)),
            pltpu.SemaphoreType.DMA((1,)),
        ]
        + (plan.scratch if plan else []),
        compiler_params=params(collective_id),
        name="attend_back",
    )(*operands, *side)


def cut_weights(levels, l, rbf, weights, gains, qkv_out, gu_out):
    query, key, value, gate, up = weights
    qw, kw, fw = query.shape[2] // GROUP, key.shape[2] // GROUP, gate.shape[2] // GROUP
    q, k, v = [(w[l].astype(F32) * gains[0][l]).astype(BF) for w in (query, key, value)]
    for t in range(GROUP):
        qkv_out[0, t] = jnp.concatenate(
            [
                q[:, t * qw : (t + 1) * qw],
                k[:, t * kw : (t + 1) * kw],
                v[:, t * kw : (t + 1) * kw],
            ],
            axis=1,
        )

    def feed_forward():
        g, u = [(w[l].astype(F32) * gains[1][l]).astype(BF) for w in (gate, up)]
        for t in range(GROUP):
            pieces = []
            for w in (g, u):
                for core in range(2):
                    for level in range(levels):
                        at = t * fw + (2 * level + core) * rbf
                        pieces.append(w[:, at : at + rbf])
            gu_out[0, t] = jnp.concatenate(pieces, axis=1)

    return feed_forward


def start_kernel(levels, layers, rbf, plan, *refs):
    refs = list(refs)
    take = lambda n: [refs.pop(0) for _ in range(n)]
    sources, gains = take(5), take(2)
    out_weight, down_weight, lanes, tokens, cotangent = take(5)
    all_ref = take(1)[0]
    spread_out = take(2)
    cuts = [take(2) for _ in range(layers - 1)]
    plan_out = take(7)
    weights = take(5)
    qkv_cut, gu_cut, normed = take(3)
    load = take(1)[0]
    plan_sems, gather_sems, spread_sems = take(3), take(3), take(5)
    loads = [pltpu.make_async_copy(a, b, load.at[i]) for i, (a, b) in enumerate(zip(sources, weights))]
    for copy in loads:
        copy.start()
    ins = [qkv_cut, gu_cut, out_weight.at[0], down_weight.at[0], lanes, tokens, cotangent]
    plan.bind(ins, plan_out, *plan_sems)
    line = Line(levels)
    greet(line.partners + [line.other_core], plan)
    spread = Spread(line, [plan_out[0].at[0], plan_out[2]], spread_out, *spread_sems)
    gather = Gather(normed, all_ref, *gather_sems)
    plan.start([5])
    plan.start([2, 4])
    for copy in loads:
        copy.wait()
    feed_forward = cut_weights(levels, 0, rbf, weights, gains, qkv_cut, gu_cut)
    plan.start([0])
    feed_forward()
    plan.wait([0, 2])
    spread.start()
    plan.wait([5])
    values = plan_out[5][...].astype(F32)
    normed[...] = line_order((values * norm_scale(values)).astype(BF), levels)
    gather.start()
    plan.start([1, 3])
    plan.start([6])
    for l in range(1, layers):
        cut_weights(levels, l, rbf, weights, gains, *cuts[l - 1])()
    gather.finish()
    spread.finish()
    plan.wait([1, 3, 4, 6])


def start(levels, weights, gains, out_weight, down_weight, lanes, tokens, cotangent, collective_id):
    query, key, _, gate, _ = weights
    layers, rb, _ = query.shape
    rbf = down_weight.shape[1]
    rows, width = tokens.shape
    wide = (query.shape[2] + 2 * key.shape[2]) // GROUP
    shape = jax.ShapeDtypeStruct
    qkv_cut = shape((1, GROUP, rb, wide), BF)
    gu_cut = shape((1, GROUP, rb, 2 * gate.shape[2] // GROUP), BF)
    one = lambda a: shape(a.shape[1:], a.dtype)
    plan = Exchange(
        levels,
        [qkv_cut, gu_cut],
        [one(out_weight), one(down_weight)],
        [lanes],
        [tokens, cotangent],
    )
    spreads = [qkv_cut.shape[1:], out_weight.shape[1:]]
    out_shape = [shape((GROUP, rows, width), BF)]
    out_shape += [shape((2, levels) + a, BF) for a in spreads]
    out_shape += [qkv_cut, gu_cut] * (layers - 1) + plan.out_shape
    out_specs = [VMEM] + [ANY] * 2 + [VMEM] * (2 * layers - 2) + [ANY] * 5 + [VMEM, ANY]
    dma = lambda n: pltpu.SemaphoreType.DMA((n,))
    return pl.pallas_call(
        functools.partial(start_kernel, levels, layers, rbf, plan),
        out_shape=out_shape,
        in_specs=[ANY] * 5 + [VMEM] * 2 + [ANY] * 5,
        out_specs=out_specs,
        scratch_shapes=[pltpu.VMEM(a.shape, BF) for a in weights]
        + [pltpu.VMEM(a.shape, BF) for a in (qkv_cut, gu_cut, tokens)]
        + [dma(5)]
        + plan.scratch
        + [dma(6), dma(6), dma(1)]
        + spread_scratch(2, levels),
        compiler_params=params(collective_id, 63),
        name="start",
    )(*weights, *gains, out_weight, down_weight, lanes, tokens, cotangent)


def finish_kernel(levels, layers, *refs):
    grads = [refs[4 * l : 4 * l + 4] for l in range(layers)]
    weights, gain1, gain2, outs = (
        refs[4 * layers : 4 * layers + 5],
        refs[4 * layers + 5],
        refs[4 * layers + 6],
        refs[4 * layers + 7 :],
    )
    query, key, value, output, gate, up, down, gain1_out, gain2_out = outs
    qw, kw, fw = query.shape[2] // GROUP, key.shape[2] // GROUP, gate.shape[2] // GROUP
    rbf = down.shape[1]
    for l in range(layers):
        qkv, out, gu, dn = grads[l]

        def place_columns(target, weight, gain, pieces, total):
            raw = jnp.concatenate(pieces, axis=1).astype(F32)
            target[l] = raw * gain[l]
            dots = jnp.sum(raw * weight[l].astype(F32), axis=1, keepdims=True)
            return dots if total is None else total + dots

        total = None
        for target, weight, first, n in (
            (query, weights[0], 0, qw),
            (key, weights[1], qw, kw),
            (value, weights[2], qw + kw, kw),
        ):
            pieces = [qkv[0, t, :, first : first + n] for t in range(GROUP)]
            total = place_columns(target, weight, gain1, pieces, total)
        gain1_out[l] = total
        output[l] = out[...].astype(F32)
        total = None
        for target, weight, base in ((gate, weights[3], 0), (up, weights[4], fw)):
            pieces = []
            for t in range(GROUP):
                for level in range(levels):
                    for core in range(2):
                        at = base + (core * levels + level) * rbf
                        pieces.append(gu[at // CW, t, :, at % CW : at % CW + rbf])
            total = place_columns(target, weight, gain2, pieces, total)
        gain2_out[l] = total
        down[l] = jnp.concatenate([dn[k] for k in range(dn.shape[0])], axis=1).astype(F32)


def finish(levels, grads, weights, output_weight, down_weight, gain1, gain2):
    layers, rb, _ = output_weight.shape
    like = lambda a: jax.ShapeDtypeStruct(a.shape, F32)
    query, key, value, gate, up = weights
    column = jax.ShapeDtypeStruct((layers, rb, 1), F32)
    operands = [a for layer in grads for a in layer] + list(weights) + [gain1, gain2]
    out_shape = [like(a) for a in (query, key, value, output_weight, gate, up, down_weight)]
    return pl.pallas_call(
        functools.partial(finish_kernel, levels, layers),
        out_shape=out_shape + [column, column],
        in_specs=[VMEM] * len(operands),
        out_specs=[VMEM] * 9,
        compiler_params=params(),
        name="finish",
    )(*operands)


def rope_tables(positions, head_width):
    frequency = THETA ** (-(jnp.arange(head_width // 2, dtype=F32) * 2.0 / head_width))
    angles = positions.astype(F32)[..., None] * frequency
    return (jnp.cos(angles), jnp.sin(angles))


def rotate(flat, cosine, sine):
    tokens = flat.shape[0]
    vectors = flat.reshape(tokens, -1, 2, HD // 2)
    a, b = vectors[:, :, 0], vectors[:, :, 1]
    cosine, sine = cosine[:, None, :], sine[:, None, :]
    return jnp.stack([a * cosine - b * sine, b * cosine + a * sine], axis=2).reshape(flat.shape)


def doc_positions(segments):
    places = jnp.arange(segments.shape[1], dtype=jnp.int32)
    starts_new = jnp.concatenate(
        [jnp.ones((segments.shape[0], 1), dtype=jnp.bool_), segments[:, 1:] != segments[:, :-1]],
        axis=1,
    )
    starts = lax.cummax(jnp.where(starts_new, places[None, :], 0), axis=1)
    return places[None, :] - starts


def on_device(
    levels,
    tokens,
    segments,
    cotangent,
    query_weight,
    key_weight,
    value_weight,
    output_weight,
    attention_gain,
    gate_weight,
    up_weight,
    down_weight,
    feedforward_gain,
):
    _, rows, width = tokens.shape
    full_len = segments.shape[1]
    layers = query_weight.shape[0]
    rb = query_weight.shape[1]
    rbf = down_weight.shape[1]
    kv_width = KVH * HD
    ffn = gate_weight.shape[2]
    qw, kw, fw = width // GROUP, kv_width // GROUP, ffn // GROUP
    group_rows = GROUP * rows
    _, c, z, _ = place()
    here = level_of(c, z, levels)
    n_ctx = 2 * levels
    lines = [
        [(gx * 2 + gc) * n_ctx + gz * 2 + gy for gc in range(2) for gz in range(levels)]
        for gx in range(2)
        for gy in range(2)
    ]
    core_lines = [
        [gs * n_ctx + gz * 2 + gy for gz in range(levels)] for gs in range(4) for gy in range(2)
    ]
    def gather_line(part):
        return lax.all_gather(part, AXES, axis=0, tiled=True, axis_index_groups=lines)

    def scatter_line(total):
        return lax.psum_scatter(
            total, AXES, scatter_dimension=0, tiled=True, axis_index_groups=core_lines
        )

    def after(value, *others):
        return lax.optimization_barrier((value,) + others)[0]

    gain1 = attention_gain.astype(F32)[:, :, None]
    gain2 = feedforward_gain.astype(F32)[:, :, None]
    lanes = segments.reshape(full_len // 128, 128)
    normed, qkv0, out0, *cuts = start(
        levels,
        [query_weight, key_weight, value_weight, gate_weight, up_weight],
        [gain1, gain2],
        output_weight,
        down_weight,
        lanes,
        tokens.reshape(rows, width),
        cotangent.reshape(rows, width),
        1,
    )
    cuts, (_, gu_own, _, down_own, all_segments, residual, cotangent) = cuts[:-7], cuts[-7:]
    qkv_slabs, gu_slabs = [None] + cuts[0::2], [None] + cuts[1::2]
    normed = normed.reshape(group_rows, width)

    def all_ffn(gu, down):
        return gather_line(gu.reshape(GROUP * rb, 2 * fw)), gather_line(down)

    own_segments = lax.dynamic_index_in_dim(
        all_segments.reshape(4, full_len), sequence_of(z, levels), 0
    )
    first = here * group_rows
    positions = lax.dynamic_slice_in_dim(doc_positions(own_segments)[0], first, group_rows)
    cosine, sine = rope_tables(positions, HD)
    row_segs = lax.dynamic_slice_in_dim(own_segments[0], first, group_rows)[:, None]
    key_segs = own_segments.reshape(levels // 2, 1, group_rows)

    def split(parts):
        return parts.astype(BF).reshape(GROUP, rows, width)

    def in_square(mode, parts, rows_in, collective_id, **more):
        out = list(square(mode, levels, split(parts), rows_in, collective_id, **more))
        if mode != "last":
            at = 2 if "second" in more else 1
            out[at] = out[at].reshape(group_rows, width)
        return out

    dot = functools.partial(jnp.dot, preferred_element_type=F32)

    qkv_full, out_full, gu_full, down_full = [[None] * layers for _ in range(4)]
    qkv_full[0], out_full[0] = qkv0, out0
    gu_full[0], down_full[0] = all_ffn(gu_own, down_own)
    residual = residual.astype(F32)
    stored = []
    for l in range(layers):
        qkv = dot(normed, after(qkv_full[l].reshape(width, qw + 2 * kw), normed))
        q = rotate(qkv[:, :qw], cosine, sine).astype(BF)
        k = rotate(qkv[:, qw : qw + kw], cosine, sine).astype(BF)
        kv = jnp.concatenate([k, qkv[:, qw + kw :].astype(BF)], axis=1)
        kv = climb(kv, levels, 5)
        attended, lse = attend(q, kv, row_segs, key_segs, levels)
        out_full[l] = (
            after(out_full[l], attended)
            .reshape(2, levels, rb, width)
            .transpose(1, 0, 2, 3)
            .reshape(qw, width)
        )
        middle, normed2 = in_square("forward", dot(attended, out_full[l]), [residual], 4)
        if l < layers - 1:
            _, gu_own, _, down_own, qkv_full[l + 1], out_full[l + 1], *gathered = exchange(
                levels,
                [after(qkv_slabs[l + 1], normed2), gu_slabs[l + 1]],
                [output_weight[l + 1], down_weight[l + 1]],
                8,
                spread=True,
                own=cotangent if l == 0 else None,
            )
            up_all = gathered[0].reshape(group_rows, width) if l == 0 else up_all
            gu_full[l + 1], down_full[l + 1] = all_ffn(gu_own, down_own)
        gu = dot(normed2, after(gu_full[l], normed2))
        gate, up = gu[:, :fw], gu[:, fw:]
        active = (jax.nn.silu(gate) * up).astype(BF)
        stored.append((residual, normed, q, kv, attended, lse, middle, normed2, gate, up, active))
        if l < layers - 1:
            parts = dot(active, after(down_full[l], active))
            residual, normed = in_square("forward", parts, [middle], 4)

    def dot_t(a, b):
        return lax.dot_general(a, b, (((1,), (1,)), ((), ())), preferred_element_type=F32)

    upstream = cotangent.astype(F32)
    ffn_grads, attention_grads, down_grads, grads = [[None] * layers for _ in range(4)]

    def in_slabs(l):
        qkv_grad, out_grad = attention_grads[l]
        gu_grad = ffn_grads[l][0].reshape(2 * fw // CW, GROUP, rb, CW)
        qkv_grad = qkv_grad.reshape(1, GROUP, rb, qw + 2 * kw)
        return [qkv_grad, gu_grad], [out_grad]

    for l in reversed(range(layers)):
        residual, normed, q, kv, attended, lse, middle, normed2, gate, up, active = stored[l]
        down_total = ffn_gradient(levels, [(active, up_all)], 13)
        down_full[l] = after(down_full[l], down_total)
        if l == layers - 1:
            block = split(dot(active, down_full[l])), middle
        dactive = dot_t(up_all, down_full[l])
        sig = jax.nn.sigmoid(gate)
        dgate = (dactive * up * sig * (1.0 + gate * (1.0 - sig))).astype(BF)
        dup = (dactive * gate * sig).astype(BF)
        dgu = jnp.concatenate([dgate, dup], axis=1)
        ffn_total = ffn_gradient(levels, [(normed2, dgu)], 16)
        ffn_grads[l] = [scatter_line(total.reshape(-1, CW)) for total in (ffn_total, down_total)]
        dnorm2 = dot_t(after(dgu, ffn_total), gu_full[l]).astype(BF)
        dmiddle, mid_all = in_square("backward", dnorm2, [upstream, middle], 10)
        back = dot_t(mid_all, out_full[l]).astype(BF)
        operands = [q, kv, row_segs, key_segs, attended, lse, back, cosine, sine, mid_all]
        if l < layers - 1:
            slabs, swaps = in_slabs(l + 1)
            moved = [block_output] if l == layers - 2 else []
            swaps = [ffn_grads[l][1]] + swaps
            dqkv, out_total, *landed = attend_back(
                operands, rb, levels, 15, slabs, swaps, moved
            )
            block_output = landed.pop() if moved else block_output
            down_grads[l] = landed.pop(len(slabs))
            grads[l + 1] = landed + [down_grads[l + 1]]
        else:
            dqkv, out_total, down_grads[l] = attend_back(
                operands, rb, levels, 6, [], [ffn_grads[l][1]]
            )
        dnorm1 = dot_t(dqkv, qkv_full[l].reshape(width, qw + 2 * kw)).astype(BF)
        collect = normed, dqkv
        if l == layers - 1:
            upstream, block_output, up_all, qkv_grad, out_grad = in_square(
                "backward",
                dnorm1,
                [dmiddle, residual],
                14,
                collect=collect,
                ready=[out_total],
                second=block,
            )
        elif l > 0:
            upstream, up_all, qkv_grad, out_grad = in_square(
                "backward", dnorm1, [dmiddle, residual], 18, collect=collect, ready=[out_total]
            )
        else:
            qkv_grad, out_grad, gu_grad, tokens_grad = in_square(
                "last",
                dnorm1,
                [dmiddle, residual],
                11,
                collect=collect,
                ready=[out_total],
                slab=ffn_grads[l][0].reshape(2 * fw // CW, GROUP, rb, CW),
            )
        attention_grads[l] = [qkv_grad, out_grad]

    qkv_grad, out_grad = exchange(
        levels, [qkv_grad.reshape(1, GROUP, rb, qw + 2 * kw)], [out_grad], 12
    )
    grads[0] = [qkv_grad, gu_grad, out_grad, down_grads[0]]
    ordered = [
        [qkv, out, gu, down.reshape(width // CW, rbf, CW)] for qkv, gu, out, down in grads
    ]
    results = finish(
        levels,
        ordered,
        [query_weight, key_weight, value_weight, gate_weight, up_weight],
        output_weight,
        down_weight,
        gain1,
        gain2,
    )
    query, key, value, output, gate, up, down, gain1_grad, gain2_grad = results
    return (
        block_output.reshape(1, rows, width),
        tokens_grad.astype(F32).reshape(1, rows, width),
        query,
        key,
        value,
        output,
        gain1_grad[:, :, 0],
        gate,
        up,
        down,
        gain2_grad[:, :, 0],
    )


def solution(mesh):
    levels = mesh.shape["ctx"] // 2
    rows3 = P(None, AXES, None)
    gains = P(None, AXES)
    return jax.shard_map(
        functools.partial(on_device, levels),
        mesh=mesh,
        in_specs=(
            P("seq", "ctx", None),
            P("seq", None),
            P("seq", "ctx", None),
            rows3,
            rows3,
            rows3,
            rows3,
            gains,
            rows3,
            rows3,
            rows3,
            gains,
        ),
        out_specs=(
            P("seq", "ctx", None),
            P("seq", "ctx", None),
            rows3,
            rows3,
            rows3,
            rows3,
            gains,
            rows3,
            rows3,
            rows3,
            gains,
        ),
        check_vma=False,
    )
```

```python
import functools
import math

import jax
import jax.numpy as jnp
from jax import lax
from jax.experimental import pallas as pl
from jax.experimental.pallas import tpu as pltpu
from jax.sharding import PartitionSpec as P

H = 16
KVH = 8
HD = 96
GROUP = 4

EPSILON = 1e-05
THETA = 100000.0
NEGATIVE = -1e30
AXES = ("seq", "ctx")
MESH = pl.DeviceIdType.MESH
ANY = pl.BlockSpec(memory_space=pltpu.HBM)
VMEM = pl.BlockSpec(memory_space=pltpu.VMEM)
BF = jnp.bfloat16
F32 = jnp.float32


def params(collective_id=None, mib=48):
    if collective_id is None:
        return pltpu.CompilerParams(vmem_limit_bytes=mib * 2**20)
    return pltpu.CompilerParams(
        collective_id=collective_id, has_side_effects=True, vmem_limit_bytes=mib * 2**20
    )


def place():
    s = lax.axis_index("seq")
    k = lax.axis_index("ctx")
    return s // 2, s % 2, k // 2, k % 2


def device(x, c, z, y):
    return (x * 2 + c, z * 2 + y)


def sequence_of(z, levels):
    return z // (levels // 4)


def level_of(c, z, levels):
    return lax.rem(z, levels // 4) * 2 + c


def home_of(x, c, z, y, levels):
    block = z * 2 + y
    level = block // GROUP
    place_z = (x * 2 + c) * (levels // 4) + level // 2
    return lax.rem(block, GROUP) // 2, lax.rem(level, 2), place_z, y


def origin_of(x, c, z, y, levels):
    s = sequence_of(z, levels)
    return s // 2, lax.rem(s, 2), 2 * level_of(c, z, levels) + x, y


def chain(x, c, z, y, levels):
    up = device(x, 1 - c, lax.rem(z + c, levels), y)
    down = device(x, 1 - c, lax.rem(z + levels - 1 + c, levels), y)
    return up, down


def remote(src, dst, send, recv, to):
    return pltpu.make_async_remote_copy(
        src_ref=src, dst_ref=dst, send_sem=send, recv_sem=recv, device_id=to, device_id_type=MESH
    )


def greet(partners, plan=None):
    barrier = pltpu.get_barrier_semaphore()
    for partner in partners:
        pl.semaphore_signal(barrier, inc=1, device_id=partner, device_id_type=MESH)
    expected = len(partners)
    if plan:
        expected = expected + plan.greet(barrier)
    pl.semaphore_wait(barrier, expected)


class Exchange:
    def __init__(self, levels, slabs=(), swaps=(), rows=(), tokens=(), back=False):
        self.levels, self.back = levels, back
        self.counts = len(slabs), len(swaps), len(rows), len(tokens)
        self.arrays = list(slabs) + list(swaps) + list(rows) + list(tokens)
        shapes = [jax.ShapeDtypeStruct(a.shape, a.dtype) for a in list(slabs) + list(swaps)]
        shapes += [jax.ShapeDtypeStruct((4,) + a.shape, a.dtype) for a in rows]
        self.out_shape = shapes + [jax.ShapeDtypeStruct(a.shape, a.dtype) for a in tokens]
        total = 2 * (len(slabs) + len(rows)) + len(self.arrays)
        self.scratch = [
            pltpu.SemaphoreType.DMA((total,)),
            pltpu.SemaphoreType.DMA((total,)),
            pltpu.SemaphoreType.DMA((len(self.arrays),)),
        ]

    def bind(self, ins, outs, send, recv, local):
        self.ins, self.outs = ins, outs
        self.send, self.recv, self.local = send, recv, local
        x, c, z, y = place()
        self.where = c, y
        self.others = [(1 - x, y), (x, 1 - y), (1 - x, 1 - y)]
        self.square = [device(ox, c, z, oy) for ox, oy in self.others]
        self.crossed = device(x, 1 - c, z, 1 - y)
        home = home_of(x, c, z, y, self.levels)
        origin = origin_of(x, c, z, y, self.levels)
        self.moves_away = (home[0] != x) | (home[1] != c) | (home[2] != z)
        taker, giver = (origin, home) if self.back else (home, origin)
        self.taker, self.giver = device(*taker), device(*giver)
        self.seq_others = [device(x, 1 - c, z, y), device(1 - x, 1 - c, z, y)]
        n_slab, n_swap, n_rows, n_tokens = self.counts
        me = x * 2 + y
        self.groups = [[] for _ in self.arrays]
        for i in range(n_slab):
            for j, (ox, oy) in enumerate(self.others):
                sem = 3 * i + j
                self.groups[i].append(
                    remote(
                        ins[i].at[:, ox * 2 + oy],
                        outs[i].at[:, me],
                        send.at[sem],
                        recv.at[sem],
                        self.square[j],
                    )
                )
            self.groups[i].append(
                pltpu.make_async_copy(ins[i].at[:, me], outs[i].at[:, me], local.at[i])
            )
        for i in range(n_rows):
            at = n_slab + n_swap + i
            sem = self.semaphore(at)
            mine = outs[at].at[x * 2 + c]
            for j, to in enumerate([self.square[0]] + self.seq_others):
                self.groups[at].append(
                    remote(ins[at], mine, send.at[sem + j], recv.at[sem + j], to)
                )
            self.groups[at].append(pltpu.make_async_copy(ins[at], mine, local.at[at]))
        self.moves = {n_slab + i: (self.crossed, c != y) for i in range(n_swap)}
        first = n_slab + n_swap + n_rows
        for i in range(n_tokens):
            self.moves[first + i] = self.taker, self.moves_away

    def semaphore(self, at):
        n_slab, n_swap, n_rows, _ = self.counts
        rows_before = min(max(at - n_slab - n_swap, 0), n_rows)
        return at + 2 * (n_slab + rows_before)

    def greet(self, barrier):
        c, y = self.where
        signal = functools.partial(pl.semaphore_signal, barrier, inc=1, device_id_type=MESH)
        for to in self.square:
            signal(device_id=to)
        expected = 3
        if self.counts[1]:
            expected = expected + lax.rem(c + y, 2)
            pl.when(c != y)(lambda: signal(device_id=self.crossed))
        if self.counts[2]:
            expected = expected + 2
            for to in self.seq_others:
                signal(device_id=to)
        if self.counts[3]:
            expected = expected + jnp.where(self.moves_away, 1, 0)
            pl.when(self.moves_away)(lambda: signal(device_id=self.giver))
        return expected

    def whole(self, at, to):
        sem = self.semaphore(at)
        return (
            remote(self.ins[at], self.outs[at], self.send.at[sem], self.recv.at[sem], to),
            pltpu.make_async_copy(self.ins[at], self.outs[at], self.local.at[at]),
        )

    def start(self, which=None):
        for at in range(len(self.arrays)) if which is None else which:
            for copy in self.groups[at]:
                copy.start()
            if at in self.moves:
                to, goes = self.moves[at]
                cross, stay = self.whole(at, to)
                pl.when(goes)(cross.start)
                pl.when(jnp.logical_not(goes))(stay.start)

    def wait(self, which=None):
        for at in range(len(self.arrays)) if which is None else which:
            for copy in self.groups[at]:
                copy.wait()
            if at in self.moves:
                to, goes = self.moves[at]
                cross, stay = self.whole(at, to)
                pl.when(goes)(cross.wait)
                pl.when(jnp.logical_not(goes))(stay.wait)


def exchange_kernel(plan, n_spread, gathers, *refs):
    n = len(plan.arrays)
    own_ref = all_ref = None
    if gathers:
        refs = list(refs)
        own_ref, all_ref = refs.pop(n), refs.pop(2 * n + n_spread)
    outs = refs[n : 2 * n]
    spread_out = refs[2 * n : 2 * n + n_spread]
    scratch = refs[2 * n + n_spread :]
    plan.bind(refs[:n], outs, *scratch[:3])
    barrier = pltpu.get_barrier_semaphore()
    if not n_spread:
        pl.semaphore_wait(barrier, plan.greet(barrier))
        plan.start()
        plan.wait()
        return
    swap = plan.counts[0]
    line = Line(plan.levels)
    spread = Spread(line, [outs[0].at[0], outs[swap]], spread_out, *scratch[3:8])
    gather = Gather(own_ref, all_ref, *scratch[8:]) if own_ref is not None else None
    greet(line.partners + [line.other_core], plan)
    rest = [at for at in range(n) if at not in (0, swap)]
    plan.start([0, swap])
    plan.start(rest)
    plan.wait([0, swap])
    spread.start()
    if gather:
        gather.start()
    spread.relay()
    plan.wait(rest)
    if gather:
        gather.relay()
        gather.finish()
    spread.finish()


class Gather:
    def __init__(self, own, everyone, send, recv, local):
        x, c, z, y = place()
        me, at_x, at_y = x * 2 + y, (1 - x) * 2 + y, x * 2 + 1 - y
        to_x, to_y = device(1 - x, c, z, y), device(x, c, z, 1 - y)
        half = own.shape[0] // 2
        low, high = pl.ds(0, half), pl.ds(half, half)
        ends = [
            (own.at[low], everyone.at[me, low], to_x),
            (own.at[high], everyone.at[me, high], to_y),
            (own.at[high], everyone.at[me, high], to_x),
            (own.at[low], everyone.at[me, low], to_y),
            (everyone.at[at_x, low], everyone.at[at_x, low], to_y),
            (everyone.at[at_y, high], everyone.at[at_y, high], to_x),
        ]
        self.copies = [
            remote(src, dst, send.at[i], recv.at[i], to) for i, (src, dst, to) in enumerate(ends)
        ]
        self.keep = pltpu.make_async_copy(own, everyone.at[me], local.at[0])

    def start(self):
        for copy in self.copies[:4]:
            copy.start()
        self.keep.start()

    def relay(self):
        for i in (0, 1):
            self.copies[i].wait_recv()
            self.copies[4 + i].start()

    def finish(self):
        for copy in self.copies[2:]:
            copy.wait_recv()
        for copy in self.copies:
            copy.wait_send()
        self.keep.wait()


def exchange(
    levels, slabs, swaps, collective_id, rows=(), tokens=(), back=False, spread=False, own=None
):
    mib = 63 if spread else 48
    plan = Exchange(levels, slabs, swaps, rows, tokens, back)
    n = len(plan.arrays)
    spreads = [slabs[0].shape[1:], swaps[0].shape] if spread else []
    out_shape = plan.out_shape + [
        jax.ShapeDtypeStruct((2, levels) + shape, BF) for shape in spreads
    ]
    scratch = plan.scratch + (spread_scratch(2, levels) if spread else [])
    operands = list(plan.arrays)
    if own is not None:
        operands.append(own)
        out_shape.append(jax.ShapeDtypeStruct((GROUP,) + own.shape, own.dtype))
        scratch += [pltpu.SemaphoreType.DMA((n,)) for n in (6, 6, 1)]
    return pl.pallas_call(
        functools.partial(exchange_kernel, plan, len(spreads), own is not None),
        out_shape=out_shape,
        in_specs=[ANY] * len(operands),
        out_specs=[ANY] * len(out_shape),
        scratch_shapes=scratch,
        compiler_params=params(collective_id, mib),
        name="exchange",
    )(*operands)


class Line:
    def __init__(self, levels):
        x, c, z, y = place()
        self.levels, self.c, self.z = levels, c, z
        self.ahead = [lax.rem(z + d, levels) for d in range(levels)]
        self.behind = [lax.rem(z - d + levels, levels) for d in range(levels)]
        self.device = lambda to: device(x, c, to, y)
        self.other_core = device(x, 1 - c, z, y)
        self.partners = [self.device(self.ahead[d]) for d in range(1, levels)]
        self.near = list(dict.fromkeys([2, levels - 2])) + [
            d for d in range(1, levels) if d not in (2, levels - 2)
        ]
        self.bottom, self.top = z == 0, z == levels - 1
        self.low, self.high = z == 1, z == levels - 2

    def to_far_end(self, d):
        return (self.bottom & (d == self.levels - 1)) | (self.top & (d == 1))

    def by_way_to(self, d):
        return (self.low & (d == self.levels - 2)) | (self.high & (d == 2))

    def from_far_end(self, d):
        return (self.top & (d == self.levels - 1)) | (self.bottom & (d == 1))


class Spread:
    def __init__(self, line, sources, outs, send, recv, cross_send, cross_recv, local):
        self.line, self.sources, self.outs = line, sources, outs
        self.send, self.recv, self.local = send, recv, local
        self.cross_send, self.cross_recv = cross_send, cross_recv
        self.count = range(len(sources))

    def to_line(self, i, d):
        line = self.line
        block = self.outs[i].at[line.c, line.z]
        to = line.device(line.ahead[d])
        return remote(self.sources[i], block, self.send.at[i, d], self.recv.at[i, d], to)

    def to_core(self, i, d):
        line = self.line
        block = self.outs[i].at[line.c, line.behind[d]]
        source = block if d else self.sources[i]
        return remote(
            source, block, self.cross_send.at[i, d], self.cross_recv.at[i, d], line.other_core
        )

    def onward(self, i, d):
        line = self.line
        block = self.outs[i].at[line.c, line.behind[d]]
        end = jnp.where(line.low, 0, line.levels - 1)
        slot = jnp.where(line.low, 1, line.levels - 1)
        return remote(
            block, block, self.send.at[i, 0], self.recv.at[i, slot], line.device(end)
        )

    def passes_on(self, d):
        line = self.line
        return (line.high & (d == line.levels - 2)) | (line.low & (d == 2))

    def keep(self, i):
        line = self.line
        return pltpu.make_async_copy(
            self.sources[i], self.outs[i].at[line.c, line.z], self.local.at[i]
        )

    def start(self):
        for i in self.count:
            for d in self.line.near:
                pl.when(jnp.logical_not(self.line.to_far_end(d)))(self.to_line(i, d).start)
            self.to_core(i, 0).start()
            self.keep(i).start()

    def relay(self, first=True):
        line = self.line
        firsts = len(dict.fromkeys([2, line.levels - 2]))
        for i in self.count:
            for d in line.near[:firsts] if first else line.near[firsts:]:
                block = self.outs[i].at[line.c, line.behind[d]]
                remote(
                    block, block, self.send.at[i, d], self.recv.at[i, d], line.other_core
                ).wait_recv()
                pl.when(self.passes_on(d))(self.onward(i, d).start)
                self.to_core(i, d).start()

    def finish(self):
        line = self.line
        self.relay(False)
        for i in self.count:
            for d in range(line.levels):
                block = self.outs[i].at[1 - line.c, line.behind[d]]
                remote(
                    block, block, self.cross_send.at[i, d], self.cross_recv.at[i, d], line.other_core
                ).wait_recv()
            for d in line.near:
                pl.when(jnp.logical_not(line.to_far_end(d)))(self.to_line(i, d).wait_send)
                pl.when(self.passes_on(d))(self.onward(i, d).wait_send)
            for d in range(line.levels):
                self.to_core(i, d).wait_send()
            self.keep(i).wait()


def spread_scratch(n, levels):
    dma = lambda *shape: pltpu.SemaphoreType.DMA(shape)
    return [dma(n, levels), dma(n, levels), dma(n, levels), dma(n, levels), dma(n)]


class Collect:
    def __init__(self, line, sources, slots, folds, relays, send, recv, relay_send, relay_recv):
        self.line, self.sources, self.slots = line, sources, slots
        self.folds, self.relays = folds, relays
        self.send, self.recv = send, recv
        self.relay_send, self.relay_recv = relay_send, relay_recv

    def clear(self):
        for slot in self.slots:
            for d in (1, self.line.levels - 1):

                @pl.when(self.line.from_far_end(d))
                def _(slot=slot, d=d):
                    slot[d] = jnp.zeros_like(slot[d])

    def direct(self, i, d):
        line = self.line
        return remote(
            self.sources[i].at[line.ahead[d]],
            self.slots[i].at[d],
            self.send.at[i, d],
            self.recv.at[i, d],
            line.device(line.ahead[d]),
        )

    def goes_direct(self, d):
        return jnp.logical_not(self.line.to_far_end(d) | self.line.by_way_to(d))

    def via(self, i):
        line = self.line
        far = jnp.where(line.bottom, line.levels - 1, 0)
        to = jnp.where(line.bottom, 1, line.levels - 2)
        return remote(
            self.sources[i].at[far],
            self.relays[i],
            self.relay_send.at[i],
            self.relay_recv.at[i],
            line.device(to),
        )

    def folded(self, i):
        line = self.line
        end = jnp.where(line.low, line.levels - 1, 0)
        slot = jnp.where(line.low, line.levels - 2, 2)
        return end, remote(
            self.folds[i],
            self.slots[i].at[slot],
            self.send.at[i, 0],
            self.recv.at[i, slot],
            line.device(end),
        )

    def start(self, i):
        line = self.line
        pl.when(line.bottom | line.top)(self.via(i).start)
        for d in range(1, line.levels):
            pl.when(self.goes_direct(d))(self.direct(i, d).start)

    def relay(self, i):
        line = self.line

        @pl.when(line.low | line.high)
        def _():
            end, copy = self.folded(i)
            self.via(i).wait_recv()
            self.folds[i][...] = (
                self.sources[i][end].astype(F32) + self.relays[i][...].astype(F32)
            ).astype(BF)
            copy.start()

    def finish(self, i, out):
        line = self.line
        total = self.sources[i][line.z].astype(F32)
        for d in range(1, line.levels):
            block = self.slots[i].at[d]
            came = remote(block, block, self.send.at[i, d], self.recv.at[i, d], line.other_core)
            pl.when(jnp.logical_not(line.from_far_end(d)))(came.wait_recv)
            total = total + self.slots[i][d].astype(F32)
        out[...] = total.astype(BF)
        pl.when(line.bottom | line.top)(self.via(i).wait_send)
        pl.when(line.low | line.high)(self.folded(i)[1].wait_send)
        for d in range(1, line.levels):
            pl.when(self.goes_direct(d))(self.direct(i, d).wait_send)


def collect_scratch(shapes):
    dma = lambda *shape: pltpu.SemaphoreType.DMA(shape)
    n, levels = len(shapes), shapes[0][0]
    scratch = [pltpu.VMEM(a, BF) for a in shapes]
    scratch += [pltpu.VMEM(a[1:], BF) for a in shapes] * 2
    return scratch + [dma(n, levels), dma(n, levels), dma(n), dma(n)]


class CoreSum:
    def __init__(self, levels, pairs, away, came, send, recv):
        self.levels, self.away, self.came = levels, away, came
        self.send, self.recv = send, recv
        x, c, z, y = place()
        self.core, self.other_core = c, device(x, 1 - c, z, y)
        self.width = away.shape[2]
        self.entries, self.turned = [], {}
        first = 0
        for a, b in pairs:
            n = a.shape[1] // 2 // levels
            for k in range(b.shape[1] // self.width):
                self.entries.append((a, b, k, first, n))
                first += n

    def product(self, i, core, mine):
        a, b, k, _, _ = self.entries[i]
        key = (id(a), mine)
        if key not in self.turned:
            half = a.shape[1] // 2
            self.turned[key] = a[:, pl.ds(pl.multiple_of(core * half, 128), half)].T
        columns = pl.ds(k * self.width, self.width)
        return jnp.dot(self.turned[key], b[:, columns], preferred_element_type=F32)

    def move(self, i):
        rows = pl.ds(self.entries[i][3], self.entries[i][4])
        return remote(
            self.away.at[:, rows],
            self.came.at[:, rows],
            self.send.at[i],
            self.recv.at[i],
            self.other_core,
        )

    def give(self, which):
        for i in which:
            result = self.product(i, 1 - self.core, False)
            _, _, _, first, n = self.entries[i]
            for level in range(self.levels):
                self.away[level, pl.ds(first, n)] = result[level * n : (level + 1) * n].astype(BF)
            self.move(i).start()

    def keep(self, which, out):
        for i in which:
            result = self.product(i, self.core, True)
            _, _, _, first, n = self.entries[i]
            rows = pl.ds(first, n)
            self.move(i).wait_recv()
            for level in range(self.levels):
                block = result[level * n : (level + 1) * n]
                out[level, rows] = (block + self.came[level, rows].astype(F32)).astype(BF)

    def end(self):
        for i in range(len(self.entries)):
            self.move(i).wait_send()


def core_sum_shape(levels, pairs, width):
    rows = sum(a.shape[1] // 2 // levels * (b.shape[1] // width) for a, b in pairs)
    return (levels, rows, width)


def core_sum_scratch(levels, pairs, width):
    shape = core_sum_shape(levels, pairs, width)
    chunks = sum(b.shape[1] // width for _, b in pairs)
    return [
        pltpu.VMEM(shape, BF),
        pltpu.VMEM(shape, BF),
        pltpu.SemaphoreType.DMA((chunks,)),
        pltpu.SemaphoreType.DMA((chunks,)),
    ]


CW = 512


def ffn_gradient_kernel(levels, n, *refs):
    pairs = [refs[2 * i : 2 * i + 2] for i in range(n)]
    out = refs[2 * n]
    total = CoreSum(levels, pairs, *refs[2 * n + 1 :])
    greet([total.other_core])
    chunks = range(len(total.entries))
    total.give(chunks)
    total.keep(chunks, out)
    total.end()


def ffn_gradient(levels, pairs, collective_id):
    operands = [a for pair in pairs for a in pair]
    return pl.pallas_call(
        functools.partial(ffn_gradient_kernel, levels, len(pairs)),
        out_shape=jax.ShapeDtypeStruct(core_sum_shape(levels, pairs, CW), BF),
        in_specs=[VMEM] * len(operands),
        out_specs=VMEM,
        scratch_shapes=core_sum_scratch(levels, pairs, CW),
        compiler_params=params(collective_id),
        name="ffn_gradient",
    )(*operands)


def norm_scale(values):
    return lax.rsqrt(jnp.mean(values * values, axis=-1, keepdims=True) + EPSILON)


def line_order(flat, levels):
    n = 2 * levels
    w = flat.shape[1] // (2 * n)
    return jnp.concatenate(
        [flat[:, (i * n + j) * w : (i * n + j + 1) * w] for j in range(n) for i in range(2)], axis=1
    )


def place_order(flat, levels):
    n = 2 * levels
    w = flat.shape[1] // (2 * n)
    return jnp.concatenate(
        [flat[:, (j * 2 + i) * w : (j * 2 + i + 1) * w] for i in range(2) for j in range(n)], axis=1
    )


def square_kernel(mode, levels, collects, second, plan, *refs):
    gathers = mode != "last"
    refs = list(refs)
    take = lambda n: [refs.pop(0) for _ in range(n)]
    part_ref = take(1)[0]
    rows_in = take(2 if mode in ("backward", "last") else 1)
    part2_ref, rows2_ref = take(2) if second else (None, None)
    pair_in, ready = take(2 * min(collects, 1)), take(max(collects - 1, 0))
    slab_ref = take(1)[0] if plan else None
    kept_ref = take(1)[0] if gathers else None
    kept2_ref = take(1)[0] if second else None
    all_ref = take(1)[0] if gathers else None
    collect_out = take(collects)
    plan_out = take(len(plan.arrays)) if plan else None
    if mode == "last":
        kept_ref = take(1)[0]
    scatter_refs = take(6)
    scatter2_refs = take(6) if second else None
    if gathers:
        ag_send, ag_recv = take(2)
    line = Line(levels)
    product = collect = None
    if collects:
        held = take(1)[0]
        slots, folds, relays = take(collects), take(collects), take(collects)
        collect = Collect(line, [held] + ready, slots, folds, relays, *take(4))
        product = CoreSum(levels, [pair_in], *take(4))
    if plan:
        plan.bind([slab_ref, kept_ref], plan_out, *take(3))
    x, c, z, y = place()
    me, at_x, at_y, at_xy = x * 2 + y, (1 - x) * 2 + y, x * 2 + 1 - y, (1 - x) * 2 + 1 - y
    to_x, to_y = device(1 - x, c, z, y), device(x, c, z, 1 - y)
    partners = [to_x, to_y]
    if collect:
        partners += line.partners + [line.other_core]
    greet(partners, plan)
    if collect:
        collect.clear()

    def finish_side():
        if collect:
            for i in range(collects):
                collect.finish(i, collect_out[i])
            product.end()
        if plan:
            plan.wait()

    rows = rows_in[0].shape[0]
    half = rows // 2
    low, high = pl.ds(0, half), pl.ds(half, half)
    copies = []
    if gathers:
        x_low, y_high, x_high, y_low = [
            remote(all_ref.at[me, part], all_ref.at[me, part], ag_send.at[i], ag_recv.at[i], to)
            for i, (part, to) in enumerate([(low, to_x), (high, to_y), (high, to_x), (low, to_y)])
        ]
        there = all_ref.at[at_x, low]
        on_y = remote(there, there, ag_send.at[4], ag_recv.at[4], to_y)
        there = all_ref.at[at_y, high]
        on_x = remote(there, there, ag_send.at[5], ag_recv.at[5], to_x)
    class Scatter:
        def __init__(self, part_ref, diag, sums, from_x, from_y, send, recv):
            self.part_ref, self.diag, self.sums = part_ref, diag, sums
            self.from_x, self.from_y = from_x, from_y
            ends = [
                (part_ref.at[at_xy, low], diag.at[0], to_x),
                (part_ref.at[at_xy, high], diag.at[1], to_y),
                (part_ref.at[at_x, low], from_x.at[low], to_x),
                (part_ref.at[at_y, high], from_y.at[high], to_y),
                (sums.at[0], from_x.at[high], to_x),
                (sums.at[1], from_y.at[low], to_y),
            ]
            self.copies = [
                remote(src, dst, send.at[i], recv.at[i], to) for i, (src, dst, to) in enumerate(ends)
            ]

        def start(self):
            for copy in self.copies[:4]:
                copy.start()

        def relay(self):
            x_diag, y_diag, _, _, x_two, y_two = self.copies
            y_diag.wait_recv()
            self.sums[0] = (
                self.part_ref[at_x, high].astype(F32) + self.diag[1].astype(F32)
            ).astype(BF)
            x_two.start()
            x_diag.wait_recv()
            self.sums[1] = (
                self.part_ref[at_y, low].astype(F32) + self.diag[0].astype(F32)
            ).astype(BF)
            y_two.start()

        def wait_low(self):
            self.copies[2].wait_recv()
            self.copies[5].wait_recv()

        def wait_high(self):
            self.copies[4].wait_recv()
            self.copies[3].wait_recv()

        def total(self, part):
            return (
                self.part_ref[me, part].astype(F32)
                + self.from_x[part].astype(F32)
                + self.from_y[part].astype(F32)
            )

    scatter = Scatter(part_ref, *scatter_refs)
    scatter.start()
    if plan:
        plan.start([0])
    for i in range(1, collects):
        collect.start(i)
    if second:
        scatter2 = Scatter(part2_ref, *scatter2_refs)
        scatter2.start()
    if product:
        product.give([0])
    scatter.relay()
    copies += scatter.copies
    if product:
        product.keep([0], held)
        collect.start(0)
        for i in range(1, collects):
            collect.relay(i)

    def own_step(part):
        total = scatter.total(part)
        if mode == "forward":
            values = rows_in[0][part] + total
            kept_ref[part] = values
            all_ref[me, part] = line_order((values * norm_scale(values)).astype(BF), levels)
        else:
            total = place_order(total, levels)
            upstream, values = rows_in[0][part], rows_in[1][part]
            scale = norm_scale(values)
            norm = values * scale
            result = upstream + scale * (
                total - norm * jnp.mean(total * norm, axis=-1, keepdims=True)
            )
            kept_ref[part] = result.astype(kept_ref.dtype)
            if gathers:
                all_ref[me, part] = result.astype(BF)

    scatter.wait_low()
    own_step(low)
    if gathers:
        x_low.start()
        y_low.start()
    scatter.wait_high()
    own_step(high)
    if mode == "last":
        plan.start([1])

    def finish_second():
        scatter2.relay()
        scatter2.wait_low()
        scatter2.wait_high()
        kept2_ref[...] = (rows2_ref[...] + scatter2.total(slice(None))).astype(BF)
        copies.extend(scatter2.copies)

    if gathers:
        y_high.start()
        x_high.start()
        x_low.wait_recv()
        on_y.start()
        y_high.wait_recv()
        on_x.start()
        if collect:
            collect.relay(0)
        x_high.wait_recv()
        y_low.wait_recv()
        on_y.wait_recv()
        on_x.wait_recv()
        copies += [x_low, y_high, x_high, y_low, on_y, on_x]
    if collect and not gathers:
        collect.relay(0)
    if second:
        finish_second()
    for copy in copies:
        copy.wait_send()
    finish_side()


def square(
    mode, levels, parts, rows_in, collective_id, collect=(), ready=(), second=(), slab=None
):
    rows, width = rows_in[0].shape
    gathers = mode != "last"
    dma = lambda *shape: pltpu.SemaphoreType.DMA(shape)
    like = lambda kind: jax.ShapeDtypeStruct((rows, width), kind)
    for_scatter = [pltpu.VMEM((2, rows // 2, width), BF)] * 2
    for_scatter += [pltpu.VMEM((rows, width), BF)] * 2 + [dma(6), dma(6)]
    plan = None
    if mode == "last":
        plan = Exchange(levels, [slab], tokens=[like(BF)], back=True)
    operands = [parts] + list(rows_in) + list(second)
    operands += list(collect) + list(ready)
    in_specs = [VMEM] * len(operands)
    out_shape, scratch = [], []
    if mode == "last":
        scratch.append(pltpu.VMEM((rows, width), BF))
    else:
        out_shape.append(like(F32))
    scratch += for_scatter
    if second:
        out_shape.append(like(BF))
        scratch += for_scatter
    if gathers:
        out_shape.append(jax.ShapeDtypeStruct((GROUP, rows, width), BF))
        scratch += [dma(6), dma(6)]
    out_specs = [VMEM] * len(out_shape)
    collects = 0
    if collect:
        shape = core_sum_shape(levels, [collect], collect[1].shape[1])
        shapes = [shape] + [a.shape for a in ready]
        collects = len(shapes)
        out_specs += [VMEM] * collects
        out_shape += [jax.ShapeDtypeStruct(a[1:], BF) for a in shapes]
        scratch += [pltpu.VMEM(shape, BF)] + collect_scratch(shapes)
        scratch += core_sum_scratch(levels, [collect], shape[2])
    if plan:
        operands.append(slab)
        in_specs.append(ANY)
        out_specs += [ANY] * len(plan.arrays)
        out_shape += plan.out_shape
        scratch += plan.scratch
    return pl.pallas_call(
        functools.partial(
            square_kernel, mode, levels, collects, bool(second), plan
        ),
        out_shape=out_shape,
        in_specs=in_specs,
        out_specs=out_specs,
        scratch_shapes=scratch,
        compiler_params=params(collective_id),
        name="square_" + mode,
    )(*operands)


PIECES = 4


def piece_rows(rows):
    return [pl.ds(i * (rows // PIECES), rows // PIECES) for i in range(PIECES)]


def dot_nt(a, b):
    return lax.dot_general(a, b, (((1,), (1,)), ((), ())), preferred_element_type=F32)


def dot_tn(a, b):
    return lax.dot_general(a, b, (((0,), (0,)), ((), ())), preferred_element_type=F32)


def two_heads(block, j):
    a = block[:, 2 * j * HD : (2 * j + 1) * HD]
    b = block[:, (2 * j + 1) * HD : (2 * j + 2) * HD]
    return jnp.concatenate([a, b], axis=0)


def visible_keys(z, level, span, row_segs, key_segs):
    rows = lax.broadcasted_iota(jnp.int32, (span, span), 0)
    cols = lax.broadcasted_iota(jnp.int32, (span, span), 1)
    mask = (row_segs == key_segs) & ((cols <= rows) | (level < z))
    return jnp.concatenate([mask, mask], axis=0)


def turn(block, cosine, sine):
    a, b = block[:, : HD // 2], block[:, HD // 2 :]
    return jnp.concatenate([a * cosine - b * sine, b * cosine + a * sine], axis=1)


def attend_kernel(planes, *refs):
    normed_ref, weight_ref, cos_ref, sin_ref, row_ref, key_ref = refs[:6]
    q_ref, kv_ref, out_ref, lse_ref = refs[6:10]
    send, recv = refs[10:]
    levels, span = kv_ref.shape[:2]
    x, c, z, y = place()
    up, down = chain(x, c, z, y, planes)
    here = level_of(c, z, planes)
    top = levels - 1
    scaling = 1.0 / math.sqrt(HD)
    barrier = pltpu.get_barrier_semaphore()

    @pl.when(here > 0)
    def _():
        pl.semaphore_signal(barrier, inc=1, device_id=down, device_id_type=MESH)

    cosine, sine = cos_ref[...], sin_ref[...]
    heads = lambda flat, n: [turn(flat[:, j * HD : (j + 1) * HD], cosine, sine) for j in range(n)]
    wide = q_ref.shape[1]
    own = jnp.dot(normed_ref[...], weight_ref[:, wide:], preferred_element_type=F32)
    half = own.shape[1] // 2
    kv_ref[here] = jnp.concatenate(heads(own[:, :half], 2) + [own[:, half:]], axis=1).astype(BF)

    def hop(distance):
        block = kv_ref.at[lax.rem(here - distance + levels, levels)]
        return remote(block, block, send.at[distance], recv.at[distance], up)

    @pl.when(here < top)
    def _():
        pl.semaphore_wait(barrier, 1)
        hop(0).start()

    own = jnp.dot(normed_ref[...], weight_ref[:, :wide], preferred_element_type=F32)
    q_ref[...] = jnp.concatenate(heads(own, 4), axis=1).astype(BF)
    queries = [two_heads(q_ref[...], j) for j in range(2)]

    def step(distance, carry):
        level = here - distance

        @pl.when(distance > 0)
        def _():
            block = kv_ref.at[level]
            remote(block, block, send.at[distance - 1], recv.at[distance - 1], up).wait_recv()

            @pl.when(here < top)
            def _():
                hop(distance).start()

        block = kv_ref[level]
        mask = visible_keys(here, level, span, row_ref[...], key_ref[level])
        after = []
        for j in range(2):
            top_old, total, accum = carry[3 * j : 3 * j + 3]
            keys = block[:, j * HD : (j + 1) * HD]
            values = block[:, (2 + j) * HD : (3 + j) * HD]
            scores = dot_nt(queries[j], keys) * scaling
            scores = jnp.where(mask, scores, NEGATIVE)
            new = jnp.maximum(top_old, jnp.max(scores, axis=-1, keepdims=True))
            scale = jnp.exp(top_old - new)
            weights = jnp.where(mask, jnp.exp(scores - new), 0.0)
            total = total * scale + jnp.sum(weights, axis=-1, keepdims=True)
            accum = accum * scale + jnp.dot(weights.astype(BF), values, preferred_element_type=F32)
            after += [new, total, accum]
        return tuple(after)

    start = (
        jnp.full((2 * span, 1), NEGATIVE, F32),
        jnp.zeros((2 * span, 1), F32),
        jnp.zeros((2 * span, HD), F32),
    )
    done = lax.fori_loop(0, here + 1, step, start + start)
    outs, lses = [], []
    for j in range(2):
        top_all, total, accum = done[3 * j : 3 * j + 3]
        result = (accum / total).astype(BF)
        lse = jnp.broadcast_to(top_all + jnp.log(total), (2 * span, 32))
        outs += [result[:span], result[span:]]
        lses += [lse[:span], lse[span:]]
    out_ref[...] = jnp.concatenate(outs, axis=1)
    lse_ref[...] = jnp.concatenate(lses, axis=1)

    @pl.when(here < top)
    def _():
        def sent(distance, nothing):
            hop(distance).wait_send()
            return nothing

        lax.fori_loop(0, here + 1, sent, 0)


def attend(operands, planes, collective_id):
    normed, weight = operands[:2]
    rows, levels = normed.shape[0], planes // 2
    wide = weight.shape[1] // 2
    shape = jax.ShapeDtypeStruct
    return pl.pallas_call(
        functools.partial(attend_kernel, planes),
        out_shape=[
            shape((rows, wide), BF),
            shape((levels, rows, wide), BF),
            shape((rows, wide), BF),
            shape((rows, 128), F32),
        ],
        in_specs=[VMEM] * len(operands),
        out_specs=[VMEM] * 4,
        scratch_shapes=[pltpu.SemaphoreType.DMA((levels,)), pltpu.SemaphoreType.DMA((levels,))],
        compiler_params=params(collective_id),
        name="attend",
    )(*operands)


def turn_back(block, cosine, sine):
    a, b = block[:, : HD // 2], block[:, HD // 2 :]
    return jnp.concatenate([a * cosine + b * sine, b * cosine - a * sine], axis=1)


def attend_back_kernel(planes, plan, *refs):
    refs = list(refs)
    take = lambda n: [refs.pop(0) for _ in range(n)]
    q_ref, kv_ref, row_ref, key_ref, out_ref, lse_ref, back_ref, cos_ref, sin_ref, mid_ref = take(10)
    side_in = take(len(plan.arrays) if plan else 0)
    dqkv_ref, dout_ref = take(2)
    side_out = take(len(plan.arrays) if plan else 0)
    part, came, sums, heads_q, heads_back, lse4, delta4, dq4, send, recv = take(10)
    own, away, came_out, out_send, out_recv = take(5)
    levels = kv_ref.shape[0]
    x, c, z, y = place()
    up, down = chain(x, c, z, y, planes)
    other_core = device(x, 1 - c, z, y)
    z = level_of(c, z, planes)
    top = levels - 1
    span = q_ref.shape[0]
    scaling = 1.0 / math.sqrt(HD)
    pieces = piece_rows(span)
    barrier = pltpu.get_barrier_semaphore()
    pl.semaphore_signal(barrier, inc=1, device_id=other_core, device_id_type=MESH)

    @pl.when(z < top)
    def _():
        pl.semaphore_signal(barrier, inc=1, device_id=up, device_id_type=MESH)

    expected = 1 + jnp.minimum(z, 1)
    if plan:
        plan.bind(side_in, side_out, *refs)
        expected = expected + plan.greet(barrier)
    pl.semaphore_wait(barrier, expected)
    if plan:
        plan.start()

    def hop(block, piece, source):
        rows = pieces[piece]
        return remote(
            source.at[block, rows],
            came.at[block, rows],
            send.at[block, piece],
            recv.at[block, piece],
            down,
        )

    lse_all = lse_ref[...]
    for j in range(2):
        back = two_heads(back_ref[...], j)
        heads_q[j] = two_heads(q_ref[...], j)
        heads_back[j] = back
        lse4[j] = jnp.concatenate(
            [lse_all[:, 64 * j : 64 * j + 1], lse_all[:, 64 * j + 32 : 64 * j + 33]], axis=0
        )
        out = two_heads(out_ref[...], j)
        delta4[j] = jnp.sum(back.astype(F32) * out.astype(F32), axis=-1, keepdims=True)
        dq4[j] = jnp.zeros((2 * span, HD), F32)

    def one_level(level, nothing):
        block = kv_ref[level]
        mask = visible_keys(z, level, span, row_ref[...], key_ref[level])
        dks, dvs = [], []
        for j in range(2):
            keys = block[:, j * HD : (j + 1) * HD]
            values = block[:, (2 + j) * HD : (3 + j) * HD]
            queries, back = heads_q[j], heads_back[j]
            scores = dot_nt(queries, keys) * scaling
            probs = jnp.where(mask, jnp.exp(scores - lse4[j]), 0.0)
            dprobs = dot_nt(back, values)
            dscores = (probs * (dprobs - delta4[j]) * scaling).astype(BF)
            dq4[j] += jnp.dot(dscores, keys, preferred_element_type=F32)
            dks.append(dot_tn(dscores, queries).astype(BF))
            dvs.append(dot_tn(probs.astype(BF), back).astype(BF))
        part[level] = jnp.concatenate(dks + dvs, axis=1)

        @pl.when((z == top) & (level < top))
        def _():
            for piece in range(PIECES):
                hop(level, piece, part).start()

        return nothing

    lax.fori_loop(0, z + 1, one_level, 0)

    rb = own.shape[1]
    wide = own.shape[2]
    for k in range(wide // CW):
        columns = pl.ds(k * CW, CW)
        product = dot_tn(out_ref[...], mid_ref[:, columns])
        for level in range(planes):
            first = product[2 * level * rb : (2 * level + 1) * rb]
            second = product[(2 * level + 1) * rb : (2 * level + 2) * rb]
            own[level, :, columns] = jnp.where(c == 0, first, second)
            away[level, :, columns] = jnp.where(c == 0, second, first).astype(BF)
    cross = remote(away, came_out, out_send.at[0], out_recv.at[0], other_core)
    cross.start()

    heads = []
    for j in range(2):
        both = dq4[j]
        heads += [
            turn_back(both[:span], cos_ref[...], sin_ref[...]),
            turn_back(both[span:], cos_ref[...], sin_ref[...]),
        ]
    dqkv_ref[:, : 4 * HD] = jnp.concatenate(heads, axis=1).astype(BF)

    def store(total, rows):
        cosine, sine = cos_ref[rows, :], sin_ref[rows, :]
        heads = [turn_back(total[:, j * HD : (j + 1) * HD], cosine, sine) for j in range(2)]
        dqkv_ref[rows, 4 * HD :] = jnp.concatenate(heads + [total[:, 2 * HD :]], axis=1).astype(BF)

    @pl.when(z == top)
    def _():
        for piece in range(PIECES):
            rows = pieces[piece]
            store(part[top, rows].astype(F32), rows)
        for block in range(top):
            for piece in range(PIECES):
                hop(block, piece, part).wait_send()

    @pl.when(z < top)
    def _():
        for block in range(top):

            @pl.when(block < z)
            def _(block=block):
                for piece in range(PIECES):
                    rows = pieces[piece]
                    hop(block, piece, sums).wait_recv()
                    sums[block, rows] = (
                        part[block, rows].astype(F32) + came[block, rows].astype(F32)
                    ).astype(BF)
                    hop(block, piece, sums).start()

            @pl.when(block == z)
            def _(block=block):
                for piece in range(PIECES):
                    rows = pieces[piece]
                    hop(block, piece, sums).wait_recv()
                    store(part[block, rows].astype(F32) + came[block, rows].astype(F32), rows)

        for block in range(top):

            @pl.when(block < z)
            def _(block=block):
                for piece in range(PIECES):
                    hop(block, piece, sums).wait_send()

    cross.wait_recv()
    for level in range(planes):
        dout_ref[level] = (own[level] + came_out[level].astype(F32)).astype(BF)
    cross.wait_send()
    if plan:
        plan.wait()


def attend_back(operands, rb, planes, collective_id, slabs=(), swaps=(), tokens=()):
    q, kv, mid_all = operands[0], operands[1], operands[-1]
    levels = kv.shape[0]
    rows, width = q.shape
    plan = Exchange(planes, slabs, swaps, (), tokens, True) if slabs or swaps else None
    side = plan.arrays if plan else []
    heads = (2, 2 * rows, HD)
    column = (2, 2 * rows, 1)
    dout = (planes, rb, mid_all.shape[1])
    return pl.pallas_call(
        functools.partial(attend_back_kernel, planes, plan),
        out_shape=[jax.ShapeDtypeStruct((rows, 2 * width), BF), jax.ShapeDtypeStruct(dout, BF)]
        + (plan.out_shape if plan else []),
        in_specs=[VMEM] * len(operands) + [ANY] * len(side),
        out_specs=[VMEM] * 2 + [ANY] * len(side),
        scratch_shapes=[
            pltpu.VMEM(kv.shape, BF),
            pltpu.VMEM(kv.shape, BF),
            pltpu.VMEM(kv.shape, BF),
            pltpu.VMEM(heads, BF),
            pltpu.VMEM(heads, BF),
            pltpu.VMEM(column, F32),
            pltpu.VMEM(column, F32),
            pltpu.VMEM(heads, F32),
            pltpu.SemaphoreType.DMA((levels, PIECES)),
            pltpu.SemaphoreType.DMA((levels, PIECES)),
            pltpu.VMEM(dout, F32),
            pltpu.VMEM(dout, BF),
            pltpu.VMEM(dout, BF),
            pltpu.SemaphoreType.DMA((1,)),
            pltpu.SemaphoreType.DMA((1,)),
        ]
        + (plan.scratch if plan else []),
        compiler_params=params(collective_id),
        name="attend_back",
    )(*operands, *side)


def cut_weights(levels, l, rbf, weights, gains, qkv_out, gu_out):
    query, key, value, gate, up = weights
    qw, kw, fw = query.shape[2] // GROUP, key.shape[2] // GROUP, gate.shape[2] // GROUP
    q, k, v = [(w[l].astype(F32) * gains[0][l]).astype(BF) for w in (query, key, value)]
    for t in range(GROUP):
        qkv_out[0, t] = jnp.concatenate(
            [
                q[:, t * qw : (t + 1) * qw],
                k[:, t * kw : (t + 1) * kw],
                v[:, t * kw : (t + 1) * kw],
            ],
            axis=1,
        )

    def feed_forward():
        g, u = [(w[l].astype(F32) * gains[1][l]).astype(BF) for w in (gate, up)]
        for t in range(GROUP):
            pieces = []
            for w in (g, u):
                for core in range(2):
                    for level in range(levels):
                        at = t * fw + (2 * level + core) * rbf
                        pieces.append(w[:, at : at + rbf])
            gu_out[0, t] = jnp.concatenate(pieces, axis=1)

    return feed_forward


def start_kernel(levels, layers, rbf, plan, *refs):
    refs = list(refs)
    take = lambda n: [refs.pop(0) for _ in range(n)]
    sources, gains = take(5), take(2)
    out_weight, down_weight, lanes, tokens, cotangent = take(5)
    all_ref = take(1)[0]
    spread_out = take(2)
    cuts = [take(2) for _ in range(layers - 1)]
    plan_out = take(7)
    weights = take(5)
    qkv_cut, gu_cut, normed = take(3)
    load = take(1)[0]
    plan_sems, gather_sems, spread_sems = take(3), take(3), take(5)
    loads = [pltpu.make_async_copy(a, b, load.at[i]) for i, (a, b) in enumerate(zip(sources, weights))]
    for copy in loads:
        copy.start()
    ins = [qkv_cut, gu_cut, out_weight.at[0], down_weight.at[0], lanes, tokens, cotangent]
    plan.bind(ins, plan_out, *plan_sems)
    line = Line(levels)
    greet(line.partners + [line.other_core], plan)
    spread = Spread(line, [plan_out[0].at[0], plan_out[2]], spread_out, *spread_sems)
    gather = Gather(normed, all_ref, *gather_sems)
    plan.start([5])
    plan.start([2, 4])
    for copy in loads:
        copy.wait()
    feed_forward = cut_weights(levels, 0, rbf, weights, gains, qkv_cut, gu_cut)
    plan.start([0])
    feed_forward()
    plan.wait([0, 2])
    spread.start()
    plan.wait([5])
    values = plan_out[5][...].astype(F32)
    normed[...] = line_order((values * norm_scale(values)).astype(BF), levels)
    gather.start()
    plan.start([1, 3])
    plan.start([6])
    for l in range(1, layers):
        cut_weights(levels, l, rbf, weights, gains, *cuts[l - 1])()
    gather.relay()
    spread.relay()
    gather.finish()
    spread.finish()
    plan.wait([1, 3, 4, 6])


def start(levels, weights, gains, out_weight, down_weight, lanes, tokens, cotangent, collective_id):
    query, key, _, gate, _ = weights
    layers, rb, _ = query.shape
    rbf = down_weight.shape[1]
    rows, width = tokens.shape
    wide = (query.shape[2] + 2 * key.shape[2]) // GROUP
    shape = jax.ShapeDtypeStruct
    qkv_cut = shape((1, GROUP, rb, wide), BF)
    gu_cut = shape((1, GROUP, rb, 2 * gate.shape[2] // GROUP), BF)
    one = lambda a: shape(a.shape[1:], a.dtype)
    plan = Exchange(
        levels,
        [qkv_cut, gu_cut],
        [one(out_weight), one(down_weight)],
        [lanes],
        [tokens, cotangent],
    )
    spreads = [qkv_cut.shape[1:], out_weight.shape[1:]]
    out_shape = [shape((GROUP, rows, width), BF)]
    out_shape += [shape((2, levels) + a, BF) for a in spreads]
    out_shape += [qkv_cut, gu_cut] * (layers - 1) + plan.out_shape
    out_specs = [VMEM] + [ANY] * 2 + [VMEM] * (2 * layers - 2) + [ANY] * 5 + [VMEM, ANY]
    dma = lambda n: pltpu.SemaphoreType.DMA((n,))
    return pl.pallas_call(
        functools.partial(start_kernel, levels, layers, rbf, plan),
        out_shape=out_shape,
        in_specs=[ANY] * 5 + [VMEM] * 2 + [ANY] * 5,
        out_specs=out_specs,
        scratch_shapes=[pltpu.VMEM(a.shape, BF) for a in weights]
        + [pltpu.VMEM(a.shape, BF) for a in (qkv_cut, gu_cut, tokens)]
        + [dma(5)]
        + plan.scratch
        + [dma(6), dma(6), dma(1)]
        + spread_scratch(2, levels),
        compiler_params=params(collective_id, 63),
        name="start",
    )(*weights, *gains, out_weight, down_weight, lanes, tokens, cotangent)


def finish_kernel(levels, layers, *refs):
    grads = [refs[4 * l : 4 * l + 4] for l in range(layers)]
    weights, gain1, gain2, outs = (
        refs[4 * layers : 4 * layers + 5],
        refs[4 * layers + 5],
        refs[4 * layers + 6],
        refs[4 * layers + 7 :],
    )
    query, key, value, output, gate, up, down, gain1_out, gain2_out = outs
    qw, kw, fw = query.shape[2] // GROUP, key.shape[2] // GROUP, gate.shape[2] // GROUP
    rbf = down.shape[1]
    for l in range(layers):
        qkv, out, gu, dn = grads[l]

        def place_columns(target, weight, gain, pieces, total):
            raw = jnp.concatenate(pieces, axis=1).astype(F32)
            target[l] = raw * gain[l]
            dots = jnp.sum(raw * weight[l].astype(F32), axis=1, keepdims=True)
            return dots if total is None else total + dots

        total = None
        for target, weight, first, n in (
            (query, weights[0], 0, qw),
            (key, weights[1], qw, kw),
            (value, weights[2], qw + kw, kw),
        ):
            pieces = [qkv[0, t, :, first : first + n] for t in range(GROUP)]
            total = place_columns(target, weight, gain1, pieces, total)
        gain1_out[l] = total
        output[l] = out[...].astype(F32)
        total = None
        for target, weight, base in ((gate, weights[3], 0), (up, weights[4], fw)):
            pieces = []
            for t in range(GROUP):
                for level in range(levels):
                    for core in range(2):
                        at = base + (core * levels + level) * rbf
                        pieces.append(gu[at // CW, t, :, at % CW : at % CW + rbf])
            total = place_columns(target, weight, gain2, pieces, total)
        gain2_out[l] = total
        down[l] = jnp.concatenate([dn[k] for k in range(dn.shape[0])], axis=1).astype(F32)


def finish(levels, grads, weights, output_weight, down_weight, gain1, gain2):
    layers, rb, _ = output_weight.shape
    like = lambda a: jax.ShapeDtypeStruct(a.shape, F32)
    query, key, value, gate, up = weights
    column = jax.ShapeDtypeStruct((layers, rb, 1), F32)
    operands = [a for layer in grads for a in layer] + list(weights) + [gain1, gain2]
    out_shape = [like(a) for a in (query, key, value, output_weight, gate, up, down_weight)]
    return pl.pallas_call(
        functools.partial(finish_kernel, levels, layers),
        out_shape=out_shape + [column, column],
        in_specs=[VMEM] * len(operands),
        out_specs=[VMEM] * 9,
        compiler_params=params(),
        name="finish",
    )(*operands)


def rope_tables(positions, head_width):
    frequency = THETA ** (-(jnp.arange(head_width // 2, dtype=F32) * 2.0 / head_width))
    angles = positions.astype(F32)[..., None] * frequency
    return (jnp.cos(angles), jnp.sin(angles))


def doc_positions(segments):
    places = jnp.arange(segments.shape[1], dtype=jnp.int32)
    starts_new = jnp.concatenate(
        [jnp.ones((segments.shape[0], 1), dtype=jnp.bool_), segments[:, 1:] != segments[:, :-1]],
        axis=1,
    )
    starts = lax.cummax(jnp.where(starts_new, places[None, :], 0), axis=1)
    return places[None, :] - starts


def on_device(
    levels,
    tokens,
    segments,
    cotangent,
    query_weight,
    key_weight,
    value_weight,
    output_weight,
    attention_gain,
    gate_weight,
    up_weight,
    down_weight,
    feedforward_gain,
):
    _, rows, width = tokens.shape
    full_len = segments.shape[1]
    layers = query_weight.shape[0]
    rb = query_weight.shape[1]
    rbf = down_weight.shape[1]
    kv_width = KVH * HD
    ffn = gate_weight.shape[2]
    qw, kw, fw = width // GROUP, kv_width // GROUP, ffn // GROUP
    group_rows = GROUP * rows
    _, c, z, _ = place()
    here = level_of(c, z, levels)
    n_ctx = 2 * levels
    lines = [
        [(gx * 2 + gc) * n_ctx + gz * 2 + gy for gc in range(2) for gz in range(levels)]
        for gx in range(2)
        for gy in range(2)
    ]
    core_lines = [
        [gs * n_ctx + gz * 2 + gy for gz in range(levels)] for gs in range(4) for gy in range(2)
    ]
    def gather_line(part):
        return lax.all_gather(part, AXES, axis=0, tiled=True, axis_index_groups=lines)

    def scatter_line(total):
        return lax.psum_scatter(
            total, AXES, scatter_dimension=0, tiled=True, axis_index_groups=core_lines
        )

    def after(value, *others):
        return lax.optimization_barrier((value,) + others)[0]

    gain1 = attention_gain.astype(F32)[:, :, None]
    gain2 = feedforward_gain.astype(F32)[:, :, None]
    lanes = segments.reshape(full_len // 128, 128)
    normed, qkv0, out0, *cuts = start(
        levels,
        [query_weight, key_weight, value_weight, gate_weight, up_weight],
        [gain1, gain2],
        output_weight,
        down_weight,
        lanes,
        tokens.reshape(rows, width),
        cotangent.reshape(rows, width),
        1,
    )
    cuts, (_, gu_own, _, down_own, all_segments, residual, cotangent) = cuts[:-7], cuts[-7:]
    qkv_slabs, gu_slabs = [None] + cuts[0::2], [None] + cuts[1::2]
    normed = normed.reshape(group_rows, width)

    def all_ffn(gu, down):
        return gather_line(gu.reshape(GROUP * rb, 2 * fw)), gather_line(down)

    own_segments = lax.dynamic_index_in_dim(
        all_segments.reshape(4, full_len), sequence_of(z, levels), 0
    )
    first = here * group_rows
    positions = lax.dynamic_slice_in_dim(doc_positions(own_segments)[0], first, group_rows)
    cosine, sine = rope_tables(positions, HD)
    row_segs = lax.dynamic_slice_in_dim(own_segments[0], first, group_rows)[:, None]
    key_segs = own_segments.reshape(levels // 2, 1, group_rows)

    def split(parts):
        return parts.astype(BF).reshape(GROUP, rows, width)

    def in_square(mode, parts, rows_in, collective_id, **more):
        out = list(square(mode, levels, split(parts), rows_in, collective_id, **more))
        if mode != "last":
            at = 2 if "second" in more else 1
            out[at] = out[at].reshape(group_rows, width)
        return out

    dot = functools.partial(jnp.dot, preferred_element_type=F32)

    qkv_full, out_full, gu_full, down_full = [[None] * layers for _ in range(4)]
    qkv_full[0], out_full[0] = qkv0, out0
    gu_full[0], down_full[0] = all_ffn(gu_own, down_own)
    residual = residual.astype(F32)
    stored = []
    for l in range(layers):
        weight = after(qkv_full[l].reshape(width, qw + 2 * kw), normed)
        q, kv, attended, lse = attend(
            [normed, weight, cosine, sine, row_segs, key_segs], levels, 5
        )
        out_full[l] = (
            after(out_full[l], attended)
            .reshape(2, levels, rb, width)
            .transpose(1, 0, 2, 3)
            .reshape(qw, width)
        )
        middle, normed2 = in_square("forward", dot(attended, out_full[l]), [residual], 4)
        if l < layers - 1:
            _, gu_own, _, down_own, qkv_full[l + 1], out_full[l + 1], *gathered = exchange(
                levels,
                [after(qkv_slabs[l + 1], normed2), gu_slabs[l + 1]],
                [output_weight[l + 1], down_weight[l + 1]],
                8,
                spread=True,
                own=cotangent if l == 0 else None,
            )
            up_all = gathered[0].reshape(group_rows, width) if l == 0 else up_all
            gu_full[l + 1], down_full[l + 1] = all_ffn(gu_own, down_own)
        gu = dot(normed2, after(gu_full[l], normed2))
        gate, up = gu[:, :fw], gu[:, fw:]
        active = (jax.nn.silu(gate) * up).astype(BF)
        stored.append((residual, normed, q, kv, attended, lse, middle, normed2, gate, up, active))
        if l < layers - 1:
            parts = dot(active, after(down_full[l], active))
            residual, normed = in_square("forward", parts, [middle], 4)

    def dot_t(a, b):
        return lax.dot_general(a, b, (((1,), (1,)), ((), ())), preferred_element_type=F32)

    upstream = cotangent.astype(F32)
    ffn_grads, attention_grads, down_grads, grads = [[None] * layers for _ in range(4)]

    def in_slabs(l):
        qkv_grad, out_grad = attention_grads[l]
        gu_grad = ffn_grads[l][0].reshape(2 * fw // CW, GROUP, rb, CW)
        qkv_grad = qkv_grad.reshape(1, GROUP, rb, qw + 2 * kw)
        return [qkv_grad, gu_grad], [out_grad]

    for l in reversed(range(layers)):
        residual, normed, q, kv, attended, lse, middle, normed2, gate, up, active = stored[l]
        down_total = ffn_gradient(levels, [(active, up_all)], 13)
        down_full[l] = after(down_full[l], down_total)
        if l == layers - 1:
            block = split(dot(active, down_full[l])), middle
        dactive = dot_t(up_all, down_full[l])
        sig = jax.nn.sigmoid(gate)
        dgate = (dactive * up * sig * (1.0 + gate * (1.0 - sig))).astype(BF)
        dup = (dactive * gate * sig).astype(BF)
        dgu = jnp.concatenate([dgate, dup], axis=1)
        ffn_total = ffn_gradient(levels, [(normed2, dgu)], 16)
        ffn_grads[l] = [scatter_line(total.reshape(-1, CW)) for total in (ffn_total, down_total)]
        dnorm2 = dot_t(after(dgu, ffn_total), gu_full[l]).astype(BF)
        dmiddle, mid_all = in_square("backward", dnorm2, [upstream, middle], 10)
        back = dot_t(mid_all, out_full[l]).astype(BF)
        operands = [q, kv, row_segs, key_segs, attended, lse, back, cosine, sine, mid_all]
        if l < layers - 1:
            slabs, swaps = in_slabs(l + 1)
            moved = [block_output] if l == layers - 2 else []
            swaps = [ffn_grads[l][1]] + swaps
            dqkv, out_total, *landed = attend_back(
                operands, rb, levels, 15, slabs, swaps, moved
            )
            block_output = landed.pop() if moved else block_output
            down_grads[l] = landed.pop(len(slabs))
            grads[l + 1] = landed + [down_grads[l + 1]]
        else:
            dqkv, out_total, down_grads[l] = attend_back(
                operands, rb, levels, 6, [], [ffn_grads[l][1]]
            )
        dnorm1 = dot_t(dqkv, qkv_full[l].reshape(width, qw + 2 * kw)).astype(BF)
        collect = normed, dqkv
        if l == layers - 1:
            upstream, block_output, up_all, qkv_grad, out_grad = in_square(
                "backward",
                dnorm1,
                [dmiddle, residual],
                14,
                collect=collect,
                ready=[out_total],
                second=block,
            )
        elif l > 0:
            upstream, up_all, qkv_grad, out_grad = in_square(
                "backward", dnorm1, [dmiddle, residual], 18, collect=collect, ready=[out_total]
            )
        else:
            qkv_grad, out_grad, gu_grad, tokens_grad = in_square(
                "last",
                dnorm1,
                [dmiddle, residual],
                11,
                collect=collect,
                ready=[out_total],
                slab=ffn_grads[l][0].reshape(2 * fw // CW, GROUP, rb, CW),
            )
        attention_grads[l] = [qkv_grad, out_grad]

    qkv_grad, out_grad = exchange(
        levels, [qkv_grad.reshape(1, GROUP, rb, qw + 2 * kw)], [out_grad], 12
    )
    grads[0] = [qkv_grad, gu_grad, out_grad, down_grads[0]]
    ordered = [
        [qkv, out, gu, down.reshape(width // CW, rbf, CW)] for qkv, gu, out, down in grads
    ]
    results = finish(
        levels,
        ordered,
        [query_weight, key_weight, value_weight, gate_weight, up_weight],
        output_weight,
        down_weight,
        gain1,
        gain2,
    )
    query, key, value, output, gate, up, down, gain1_grad, gain2_grad = results
    return (
        block_output.reshape(1, rows, width),
        tokens_grad.astype(F32).reshape(1, rows, width),
        query,
        key,
        value,
        output,
        gain1_grad[:, :, 0],
        gate,
        up,
        down,
        gain2_grad[:, :, 0],
    )


def solution(mesh):
    levels = mesh.shape["ctx"] // 2
    rows3 = P(None, AXES, None)
    gains = P(None, AXES)
    return jax.shard_map(
        functools.partial(on_device, levels),
        mesh=mesh,
        in_specs=(
            P("seq", "ctx", None),
            P("seq", None),
            P("seq", "ctx", None),
            rows3,
            rows3,
            rows3,
            rows3,
            gains,
            rows3,
            rows3,
            rows3,
            gains,
        ),
        out_specs=(
            P("seq", "ctx", None),
            P("seq", "ctx", None),
            rows3,
            rows3,
            rows3,
            rows3,
            gains,
            rows3,
            rows3,
            rows3,
            gains,
        ),
        check_vma=False,
    )
```

```python
import functools
import math

import jax
import jax.numpy as jnp
from jax import lax
from jax.experimental import pallas as pl
from jax.experimental.pallas import tpu as pltpu
from jax.sharding import PartitionSpec as P

H = 16
KVH = 8
HD = 96
GROUP = 4

EPSILON = 1e-05
THETA = 100000.0
NEGATIVE = -1e30
AXES = ("seq", "ctx")
MESH = pl.DeviceIdType.MESH
ANY = pl.BlockSpec(memory_space=pltpu.HBM)
VMEM = pl.BlockSpec(memory_space=pltpu.VMEM)
BF = jnp.bfloat16
F32 = jnp.float32


def params(collective_id=None, mib=48):
    if collective_id is None:
        return pltpu.CompilerParams(vmem_limit_bytes=mib * 2**20)
    return pltpu.CompilerParams(
        collective_id=collective_id, has_side_effects=True, vmem_limit_bytes=mib * 2**20
    )


def place():
    s = lax.axis_index("seq")
    k = lax.axis_index("ctx")
    return s // 2, s % 2, k // 2, k % 2


def device(x, c, z, y):
    return (x * 2 + c, z * 2 + y)


def sequence_of(z, levels):
    return z // (levels // 4)


def level_of(c, z, levels):
    return lax.rem(z, levels // 4) * 2 + c


def home_of(x, c, z, y, levels):
    block = z * 2 + y
    level = block // GROUP
    place_z = (x * 2 + c) * (levels // 4) + level // 2
    return lax.rem(block, GROUP) // 2, lax.rem(level, 2), place_z, y


def origin_of(x, c, z, y, levels):
    s = sequence_of(z, levels)
    return s // 2, lax.rem(s, 2), 2 * level_of(c, z, levels) + x, y


def chain(x, c, z, y, levels):
    up = device(x, 1 - c, lax.rem(z + c, levels), y)
    down = device(x, 1 - c, lax.rem(z + levels - 1 + c, levels), y)
    return up, down


def remote(src, dst, send, recv, to):
    return pltpu.make_async_remote_copy(
        src_ref=src, dst_ref=dst, send_sem=send, recv_sem=recv, device_id=to, device_id_type=MESH
    )


def greet(partners, plan=None):
    barrier = pltpu.get_barrier_semaphore()
    for partner in partners:
        pl.semaphore_signal(barrier, inc=1, device_id=partner, device_id_type=MESH)
    expected = len(partners)
    if plan:
        expected = expected + plan.greet(barrier)
    pl.semaphore_wait(barrier, expected)


class Exchange:
    def __init__(self, levels, slabs=(), swaps=(), rows=(), tokens=(), back=False):
        self.levels, self.back = levels, back
        self.counts = len(slabs), len(swaps), len(rows), len(tokens)
        self.arrays = list(slabs) + list(swaps) + list(rows) + list(tokens)
        shapes = [jax.ShapeDtypeStruct(a.shape, a.dtype) for a in list(slabs) + list(swaps)]
        shapes += [jax.ShapeDtypeStruct((4,) + a.shape, a.dtype) for a in rows]
        self.out_shape = shapes + [jax.ShapeDtypeStruct(a.shape, a.dtype) for a in tokens]
        total = 2 * (len(slabs) + len(rows)) + len(self.arrays)
        self.scratch = [
            pltpu.SemaphoreType.DMA((total,)),
            pltpu.SemaphoreType.DMA((total,)),
            pltpu.SemaphoreType.DMA((len(self.arrays),)),
        ]

    def bind(self, ins, outs, send, recv, local):
        self.ins, self.outs = ins, outs
        self.send, self.recv, self.local = send, recv, local
        x, c, z, y = place()
        self.where = c, y
        self.others = [(1 - x, y), (x, 1 - y), (1 - x, 1 - y)]
        self.square = [device(ox, c, z, oy) for ox, oy in self.others]
        self.crossed = device(x, 1 - c, z, 1 - y)
        home = home_of(x, c, z, y, self.levels)
        origin = origin_of(x, c, z, y, self.levels)
        self.moves_away = (home[0] != x) | (home[1] != c) | (home[2] != z)
        taker, giver = (origin, home) if self.back else (home, origin)
        self.taker, self.giver = device(*taker), device(*giver)
        self.seq_others = [device(x, 1 - c, z, y), device(1 - x, 1 - c, z, y)]
        n_slab, n_swap, n_rows, n_tokens = self.counts
        me = x * 2 + y
        self.groups = [[] for _ in self.arrays]
        for i in range(n_slab):
            for j, (ox, oy) in enumerate(self.others):
                sem = 3 * i + j
                self.groups[i].append(
                    remote(
                        ins[i].at[:, ox * 2 + oy],
                        outs[i].at[:, me],
                        send.at[sem],
                        recv.at[sem],
                        self.square[j],
                    )
                )
            self.groups[i].append(
                pltpu.make_async_copy(ins[i].at[:, me], outs[i].at[:, me], local.at[i])
            )
        for i in range(n_rows):
            at = n_slab + n_swap + i
            sem = self.semaphore(at)
            mine = outs[at].at[x * 2 + c]
            for j, to in enumerate([self.square[0]] + self.seq_others):
                self.groups[at].append(
                    remote(ins[at], mine, send.at[sem + j], recv.at[sem + j], to)
                )
            self.groups[at].append(pltpu.make_async_copy(ins[at], mine, local.at[at]))
        self.moves = {n_slab + i: (self.crossed, c != y) for i in range(n_swap)}
        first = n_slab + n_swap + n_rows
        for i in range(n_tokens):
            self.moves[first + i] = self.taker, self.moves_away

    def semaphore(self, at):
        n_slab, n_swap, n_rows, _ = self.counts
        rows_before = min(max(at - n_slab - n_swap, 0), n_rows)
        return at + 2 * (n_slab + rows_before)

    def greet(self, barrier):
        c, y = self.where
        signal = functools.partial(pl.semaphore_signal, barrier, inc=1, device_id_type=MESH)
        for to in self.square:
            signal(device_id=to)
        expected = 3
        if self.counts[1]:
            expected = expected + lax.rem(c + y, 2)
            pl.when(c != y)(lambda: signal(device_id=self.crossed))
        if self.counts[2]:
            expected = expected + 2
            for to in self.seq_others:
                signal(device_id=to)
        if self.counts[3]:
            expected = expected + jnp.where(self.moves_away, 1, 0)
            pl.when(self.moves_away)(lambda: signal(device_id=self.giver))
        return expected

    def whole(self, at, to):
        sem = self.semaphore(at)
        return (
            remote(self.ins[at], self.outs[at], self.send.at[sem], self.recv.at[sem], to),
            pltpu.make_async_copy(self.ins[at], self.outs[at], self.local.at[at]),
        )

    def start(self, which=None):
        for at in range(len(self.arrays)) if which is None else which:
            for copy in self.groups[at]:
                copy.start()
            if at in self.moves:
                to, goes = self.moves[at]
                cross, stay = self.whole(at, to)
                pl.when(goes)(cross.start)
                pl.when(jnp.logical_not(goes))(stay.start)

    def wait(self, which=None):
        for at in range(len(self.arrays)) if which is None else which:
            for copy in self.groups[at]:
                copy.wait()
            if at in self.moves:
                to, goes = self.moves[at]
                cross, stay = self.whole(at, to)
                pl.when(goes)(cross.wait)
                pl.when(jnp.logical_not(goes))(stay.wait)


def exchange_kernel(plan, n_spread, gathers, *refs):
    n = len(plan.arrays)
    own_ref = all_ref = None
    if gathers:
        refs = list(refs)
        own_ref, all_ref = refs.pop(n), refs.pop(2 * n + n_spread)
    outs = refs[n : 2 * n]
    spread_out = refs[2 * n : 2 * n + n_spread]
    scratch = refs[2 * n + n_spread :]
    plan.bind(refs[:n], outs, *scratch[:3])
    barrier = pltpu.get_barrier_semaphore()
    if not n_spread:
        pl.semaphore_wait(barrier, plan.greet(barrier))
        plan.start()
        plan.wait()
        return
    swap = plan.counts[0]
    line = Line(plan.levels)
    spread = Spread(line, False, [outs[0].at[0], outs[swap]], spread_out, *scratch[3:9])
    gather = Gather(own_ref, all_ref, *scratch[9:]) if own_ref is not None else None
    greet(line.partners + [line.other_core], plan)
    rest = [at for at in range(n) if at not in (0, swap)]
    plan.start([0, swap])
    plan.start(rest)
    plan.wait([0, swap])
    spread.start()
    if gather:
        gather.start()
    spread.relay(others=False)
    plan.wait(rest)
    if gather:
        gather.relay()
        gather.finish()
    spread.relay(ends=False)
    spread.finish()


class Gather:
    def __init__(self, own, everyone, send, recv, local):
        x, c, z, y = place()
        me, at_x, at_y = x * 2 + y, (1 - x) * 2 + y, x * 2 + 1 - y
        to_x, to_y = device(1 - x, c, z, y), device(x, c, z, 1 - y)
        half = own.shape[0] // 2
        low, high = pl.ds(0, half), pl.ds(half, half)
        ends = [
            (own.at[low], everyone.at[me, low], to_x),
            (own.at[high], everyone.at[me, high], to_y),
            (own.at[high], everyone.at[me, high], to_x),
            (own.at[low], everyone.at[me, low], to_y),
            (everyone.at[at_x, low], everyone.at[at_x, low], to_y),
            (everyone.at[at_y, high], everyone.at[at_y, high], to_x),
        ]
        self.copies = [
            remote(src, dst, send.at[i], recv.at[i], to) for i, (src, dst, to) in enumerate(ends)
        ]
        self.keep = pltpu.make_async_copy(own, everyone.at[me], local.at[0])

    def start(self):
        for copy in self.copies[:4]:
            copy.start()
        self.keep.start()

    def relay(self):
        for i in (0, 1):
            self.copies[i].wait_recv()
            self.copies[4 + i].start()

    def finish(self):
        for copy in self.copies[2:]:
            copy.wait_recv()
        for copy in self.copies:
            copy.wait_send()
        self.keep.wait()


def exchange(
    levels, slabs, swaps, collective_id, rows=(), tokens=(), back=False, spread=False, own=None
):
    mib = 63 if spread else 48
    plan = Exchange(levels, slabs, swaps, rows, tokens, back)
    n = len(plan.arrays)
    spreads = [slabs[0].shape[1:], swaps[0].shape] if spread else []
    out_shape = plan.out_shape + [
        jax.ShapeDtypeStruct((2, levels) + shape, BF) for shape in spreads
    ]
    scratch = plan.scratch + (spread_scratch(2, levels) if spread else [])
    operands = list(plan.arrays)
    if own is not None:
        operands.append(own)
        out_shape.append(jax.ShapeDtypeStruct((GROUP,) + own.shape, own.dtype))
        scratch += [pltpu.SemaphoreType.DMA((n,)) for n in (6, 6, 1)]
    return pl.pallas_call(
        functools.partial(exchange_kernel, plan, len(spreads), own is not None),
        out_shape=out_shape,
        in_specs=[ANY] * len(operands),
        out_specs=[ANY] * len(out_shape),
        scratch_shapes=scratch,
        compiler_params=params(collective_id, mib),
        name="exchange",
    )(*operands)


class Line:
    def __init__(self, levels):
        x, c, z, y = place()
        self.levels, self.c, self.z = levels, c, z
        self.ahead = [lax.rem(z + d, levels) for d in range(levels)]
        self.behind = [lax.rem(z - d + levels, levels) for d in range(levels)]
        self.device = lambda to: device(x, c, to, y)
        self.other_core = device(x, 1 - c, z, y)
        self.partners = [self.device(self.ahead[d]) for d in range(1, levels)]
        self.near = list(dict.fromkeys([2, levels - 2])) + [
            d for d in range(1, levels) if d not in (2, levels - 2)
        ]
        self.bottom, self.top = z == 0, z == levels - 1
        self.low, self.high = z == 1, z == levels - 2

    def to_far_end(self, d):
        return (self.bottom & (d == self.levels - 1)) | (self.top & (d == 1))

    def by_way_to(self, d):
        return (self.low & (d == self.levels - 2)) | (self.high & (d == 2))

    def from_far_end(self, d):
        return (self.top & (d == self.levels - 1)) | (self.bottom & (d == 1))


class Spread:
    def __init__(
        self, line, hops, sources, outs, send, recv, cross_send, cross_recv, local, onward_send
    ):
        self.hops, self.onward_send = hops, onward_send
        self.line, self.sources, self.outs = line, sources, outs
        self.send, self.recv, self.local = send, recv, local
        self.cross_send, self.cross_recv = cross_send, cross_recv
        self.count = range(len(sources))

    def to_line(self, i, d):
        line = self.line
        block = self.outs[i].at[line.c, line.z]
        to = line.device(line.ahead[d])
        return remote(self.sources[i], block, self.send.at[i, d], self.recv.at[i, d], to)

    def to_core(self, i, d):
        line = self.line
        block = self.outs[i].at[line.c, line.behind[d]]
        source = block if d else self.sources[i]
        return remote(
            source, block, self.cross_send.at[i, d], self.cross_recv.at[i, d], line.other_core
        )

    def goes_direct(self, d):
        line = self.line
        if not self.hops:
            return jnp.logical_not(line.to_far_end(d))
        to_end = (line.ahead[d] == 0) & (line.z != 1)
        to_end = to_end | ((line.ahead[d] == line.levels - 1) & (line.z != line.levels - 2))
        return jnp.logical_not(to_end)

    def onward(self, i, d):
        line = self.line
        block = self.outs[i].at[line.c, line.behind[d]]
        end = jnp.where(line.low, 0, line.levels - 1)
        slot = jnp.where(line.low, d - 1, d + 1)
        return remote(
            block, block, self.onward_send.at[i, d], self.recv.at[i, slot], line.device(end)
        )

    def passes_on(self, d):
        line = self.line
        if not self.hops:
            far = jnp.where(line.low, line.levels - 1, 0)
            return (line.low | line.high) & (line.behind[d] == far)
        up = line.high & (line.behind[d] < line.levels - 2)
        return up | (line.low & (line.behind[d] > 1))

    def keep(self, i):
        line = self.line
        return pltpu.make_async_copy(
            self.sources[i], self.outs[i].at[line.c, line.z], self.local.at[i]
        )

    def start(self):
        for i in self.count:
            for d in self.line.near:
                pl.when(self.goes_direct(d))(self.to_line(i, d).start)
            self.to_core(i, 0).start()
            self.keep(i).start()

    def relay(self, ends=True, others=True):
        line = self.line
        firsts = len(dict.fromkeys([2, line.levels - 2]))
        which = (line.near[:firsts] if ends else []) + (line.near[firsts:] if others else [])
        for i in self.count:
            for d in which:
                block = self.outs[i].at[line.c, line.behind[d]]
                remote(
                    block, block, self.send.at[i, d], self.recv.at[i, d], line.other_core
                ).wait_recv()
                pl.when(self.passes_on(d))(self.onward(i, d).start)
                self.to_core(i, d).start()

    def finish(self):
        line = self.line
        for i in self.count:
            for d in range(line.levels):
                block = self.outs[i].at[1 - line.c, line.behind[d]]
                remote(
                    block, block, self.cross_send.at[i, d], self.cross_recv.at[i, d], line.other_core
                ).wait_recv()
            for d in line.near:
                pl.when(self.goes_direct(d))(self.to_line(i, d).wait_send)
                pl.when(self.passes_on(d))(self.onward(i, d).wait_send)
            for d in range(line.levels):
                self.to_core(i, d).wait_send()
            self.keep(i).wait()


def spread_scratch(n, levels):
    dma = lambda *shape: pltpu.SemaphoreType.DMA(shape)
    return [dma(n, levels), dma(n, levels), dma(n, levels), dma(n, levels), dma(n), dma(n, levels)]


class Collect:
    def __init__(self, line, sources, slots, folds, relays, send, recv, relay_send, relay_recv):
        self.line, self.sources, self.slots = line, sources, slots
        self.folds, self.relays = folds, relays
        self.send, self.recv = send, recv
        self.relay_send, self.relay_recv = relay_send, relay_recv

    def clear(self):
        for slot in self.slots:
            for d in (1, self.line.levels - 1):

                @pl.when(self.line.from_far_end(d))
                def _(slot=slot, d=d):
                    slot[d] = jnp.zeros_like(slot[d])

    def direct(self, i, d):
        line = self.line
        return remote(
            self.sources[i].at[line.ahead[d]],
            self.slots[i].at[d],
            self.send.at[i, d],
            self.recv.at[i, d],
            line.device(line.ahead[d]),
        )

    def goes_direct(self, d):
        return jnp.logical_not(self.line.to_far_end(d) | self.line.by_way_to(d))

    def via(self, i):
        line = self.line
        far = jnp.where(line.bottom, line.levels - 1, 0)
        to = jnp.where(line.bottom, 1, line.levels - 2)
        return remote(
            self.sources[i].at[far],
            self.relays[i],
            self.relay_send.at[i],
            self.relay_recv.at[i],
            line.device(to),
        )

    def folded(self, i):
        line = self.line
        end = jnp.where(line.low, line.levels - 1, 0)
        slot = jnp.where(line.low, line.levels - 2, 2)
        return end, remote(
            self.folds[i],
            self.slots[i].at[slot],
            self.send.at[i, 0],
            self.recv.at[i, slot],
            line.device(end),
        )

    def start(self, i):
        line = self.line
        pl.when(line.bottom | line.top)(self.via(i).start)
        for d in range(1, line.levels):
            pl.when(self.goes_direct(d))(self.direct(i, d).start)

    def relay(self, i):
        line = self.line

        @pl.when(line.low | line.high)
        def _():
            end, copy = self.folded(i)
            self.via(i).wait_recv()
            self.folds[i][...] = (
                self.sources[i][end].astype(F32) + self.relays[i][...].astype(F32)
            ).astype(BF)
            copy.start()

    def total(self, i):
        line = self.line
        total = self.sources[i][line.z].astype(F32)
        for d in range(1, line.levels):
            block = self.slots[i].at[d]
            came = remote(block, block, self.send.at[i, d], self.recv.at[i, d], line.other_core)
            pl.when(jnp.logical_not(line.from_far_end(d)))(came.wait_recv)
            total = total + self.slots[i][d].astype(F32)
        return total.astype(BF)

    def end(self, i):
        line = self.line
        pl.when(line.bottom | line.top)(self.via(i).wait_send)
        pl.when(line.low | line.high)(self.folded(i)[1].wait_send)
        for d in range(1, line.levels):
            pl.when(self.goes_direct(d))(self.direct(i, d).wait_send)


def collect_scratch(shapes):
    dma = lambda *shape: pltpu.SemaphoreType.DMA(shape)
    n, levels = len(shapes), shapes[0][0]
    scratch = [pltpu.VMEM(a, BF) for a in shapes]
    scratch += [pltpu.VMEM(a[1:], BF) for a in shapes] * 2
    return scratch + [dma(n, levels), dma(n, levels), dma(n), dma(n)]


class CoreSum:
    def __init__(self, levels, pairs, away, came, send, recv):
        self.levels, self.away, self.came = levels, away, came
        self.send, self.recv = send, recv
        x, c, z, y = place()
        self.core, self.other_core = c, device(x, 1 - c, z, y)
        self.width = away.shape[2]
        self.entries, self.turned = [], {}
        first = 0
        for a, b in pairs:
            n = a.shape[1] // 2 // levels
            for k in range(b.shape[1] // self.width):
                self.entries.append((a, b, k, first, n))
                first += n

    def product(self, i, core, mine):
        a, b, k, _, _ = self.entries[i]
        key = (id(a), mine)
        if key not in self.turned:
            half = a.shape[1] // 2
            self.turned[key] = a[:, pl.ds(pl.multiple_of(core * half, 128), half)].T
        columns = pl.ds(k * self.width, self.width)
        return jnp.dot(self.turned[key], b[:, columns], preferred_element_type=F32)

    def move(self, i):
        rows = pl.ds(self.entries[i][3], self.entries[i][4])
        return remote(
            self.away.at[:, rows],
            self.came.at[:, rows],
            self.send.at[i],
            self.recv.at[i],
            self.other_core,
        )

    def give(self, which):
        for i in which:
            result = self.product(i, 1 - self.core, False)
            _, _, _, first, n = self.entries[i]
            for level in range(self.levels):
                self.away[level, pl.ds(first, n)] = result[level * n : (level + 1) * n].astype(BF)
            self.move(i).start()

    def keep(self, which, out):
        for i in which:
            result = self.product(i, self.core, True)
            _, _, _, first, n = self.entries[i]
            rows = pl.ds(first, n)
            self.move(i).wait_recv()
            for level in range(self.levels):
                block = result[level * n : (level + 1) * n]
                out[level, rows] = (block + self.came[level, rows].astype(F32)).astype(BF)

    def end(self):
        for i in range(len(self.entries)):
            self.move(i).wait_send()


class Gathered:
    def __init__(self, ref):
        self.ref = ref
        self.shape = (ref.shape[0] * ref.shape[1], ref.shape[2])

    def __getitem__(self, at):
        return jnp.concatenate([self.ref[t, :, at[1]] for t in range(GROUP)], axis=0)


def core_sum_shape(levels, pairs, width):
    rows = sum(a.shape[1] // 2 // levels * (b.shape[1] // width) for a, b in pairs)
    return (levels, rows, width)


def core_sum_scratch(levels, pairs, width):
    shape = core_sum_shape(levels, pairs, width)
    chunks = sum(b.shape[1] // width for _, b in pairs)
    return [
        pltpu.VMEM(shape, BF),
        pltpu.VMEM(shape, BF),
        pltpu.SemaphoreType.DMA((chunks,)),
        pltpu.SemaphoreType.DMA((chunks,)),
    ]


CW = 512


def ffn_gradient_kernel(levels, n, *refs):
    pairs = [refs[2 * i : 2 * i + 2] for i in range(n)]
    out = refs[2 * n]
    total = CoreSum(levels, pairs, *refs[2 * n + 1 :])
    greet([total.other_core])
    chunks = range(len(total.entries))
    total.give(chunks)
    total.keep(chunks, out)
    total.end()


def ffn_gradient(levels, pairs, collective_id):
    operands = [a for pair in pairs for a in pair]
    return pl.pallas_call(
        functools.partial(ffn_gradient_kernel, levels, len(pairs)),
        out_shape=jax.ShapeDtypeStruct(core_sum_shape(levels, pairs, CW), BF),
        in_specs=[VMEM] * len(operands),
        out_specs=VMEM,
        scratch_shapes=core_sum_scratch(levels, pairs, CW),
        compiler_params=params(collective_id),
        name="ffn_gradient",
    )(*operands)


def norm_scale(values):
    return lax.rsqrt(jnp.mean(values * values, axis=-1, keepdims=True) + EPSILON)


def line_order(flat, levels):
    n = 2 * levels
    w = flat.shape[1] // (2 * n)
    return jnp.concatenate(
        [flat[:, (i * n + j) * w : (i * n + j + 1) * w] for j in range(n) for i in range(2)], axis=1
    )


def place_order(flat, levels):
    n = 2 * levels
    w = flat.shape[1] // (2 * n)
    return jnp.concatenate(
        [flat[:, (j * 2 + i) * w : (j * 2 + i + 1) * w] for i in range(2) for j in range(n)], axis=1
    )


def square_kernel(mode, levels, collects, second, plan, follows, *refs):
    gathers = mode != "last"
    refs = list(refs)
    take = lambda n: [refs.pop(0) for _ in range(n)]
    part_ref = take(1)[0]
    rows_in = take(2 if mode in ("backward", "last") else 1)
    part2_ref, rows2_ref = take(2) if second else (None, None)
    pair_in, ready = take(2 * min(collects, 1)), take(max(collects - 1, 0))
    slab_ref = take(1)[0] if plan else None
    left_ref = take(1)[0] if follows else None
    kept_ref = take(1)[0] if gathers else None
    kept2_ref = take(1)[0] if second else None
    all_ref = take(1)[0] if gathers else None
    collect_out = take(collects) if gathers else None
    follow_out = take(1)[0] if follows else None
    plan_out = take(len(plan.arrays)) if plan else None
    if mode == "last":
        kept_ref, qkv_ref, sum_ref = take(3)
    scatter_refs = take(6)
    scatter2_refs = take(6) if second else None
    if gathers:
        ag_send, ag_recv = take(2)
    line = Line(levels)
    product = collect = None
    if collects:
        held = take(1)[0]
        slots, folds, relays = take(collects), take(collects), take(collects)
        collect = Collect(line, [held] + ready, slots, folds, relays, *take(4))
        product = CoreSum(levels, [pair_in], *take(4))
    follow = CoreSum(levels, [(left_ref, Gathered(all_ref))], *take(4)) if follows else None
    if plan:
        plan.bind([slab_ref, qkv_ref, sum_ref, kept_ref], plan_out, *take(3))
    x, c, z, y = place()
    me, at_x, at_y, at_xy = x * 2 + y, (1 - x) * 2 + y, x * 2 + 1 - y, (1 - x) * 2 + 1 - y
    to_x, to_y = device(1 - x, c, z, y), device(x, c, z, 1 - y)
    partners = [to_x, to_y]
    if collect:
        partners += line.partners + [line.other_core]
    greet(partners, plan)
    if collect:
        collect.clear()

    def finish_side():
        if collect and gathers:
            for i in range(collects):
                collect_out[i][...] = collect.total(i)
        elif collect:
            sum_ref[...] = collect.total(1)
            plan.start([2])
            total = collect.total(0)
            n = qkv_ref.shape[2]
            for t in range(GROUP):
                qkv_ref[0, t] = total[t * n : (t + 1) * n]
            plan.start([1])
        if collect:
            for i in range(collects):
                collect.end(i)
            product.end()
        if follow:
            follow.end()
        if plan:
            plan.wait()

    rows = rows_in[0].shape[0]
    half = rows // 2
    low, high = pl.ds(0, half), pl.ds(half, half)
    copies = []
    if gathers:
        x_low, y_high, x_high, y_low = [
            remote(all_ref.at[me, part], all_ref.at[me, part], ag_send.at[i], ag_recv.at[i], to)
            for i, (part, to) in enumerate([(low, to_x), (high, to_y), (high, to_x), (low, to_y)])
        ]
        there = all_ref.at[at_x, low]
        on_y = remote(there, there, ag_send.at[4], ag_recv.at[4], to_y)
        there = all_ref.at[at_y, high]
        on_x = remote(there, there, ag_send.at[5], ag_recv.at[5], to_x)
    class Scatter:
        def __init__(self, part_ref, diag, sums, from_x, from_y, send, recv):
            self.part_ref, self.diag, self.sums = part_ref, diag, sums
            self.from_x, self.from_y = from_x, from_y
            ends = [
                (part_ref.at[at_xy, low], diag.at[0], to_x),
                (part_ref.at[at_xy, high], diag.at[1], to_y),
                (part_ref.at[at_x, low], from_x.at[low], to_x),
                (part_ref.at[at_y, high], from_y.at[high], to_y),
                (sums.at[0], from_x.at[high], to_x),
                (sums.at[1], from_y.at[low], to_y),
            ]
            self.copies = [
                remote(src, dst, send.at[i], recv.at[i], to) for i, (src, dst, to) in enumerate(ends)
            ]

        def start(self):
            for copy in self.copies[:4]:
                copy.start()

        def relay(self):
            x_diag, y_diag, _, _, x_two, y_two = self.copies
            y_diag.wait_recv()
            self.sums[0] = (
                self.part_ref[at_x, high].astype(F32) + self.diag[1].astype(F32)
            ).astype(BF)
            x_two.start()
            x_diag.wait_recv()
            self.sums[1] = (
                self.part_ref[at_y, low].astype(F32) + self.diag[0].astype(F32)
            ).astype(BF)
            y_two.start()

        def wait_low(self):
            self.copies[2].wait_recv()
            self.copies[5].wait_recv()

        def wait_high(self):
            self.copies[4].wait_recv()
            self.copies[3].wait_recv()

        def total(self, part):
            return (
                self.part_ref[me, part].astype(F32)
                + self.from_x[part].astype(F32)
                + self.from_y[part].astype(F32)
            )

    scatter = Scatter(part_ref, *scatter_refs)
    scatter.start()
    if plan:
        plan.start([0])
    for i in range(1, collects):
        collect.start(i)
    if second:
        scatter2 = Scatter(part2_ref, *scatter2_refs)
        scatter2.start()
    if product:
        product.give([0])
    scatter.relay()
    copies += scatter.copies
    if product:
        product.keep([0], held)
        collect.start(0)
        for i in range(1, collects):
            collect.relay(i)

    def own_step(part):
        total = scatter.total(part)
        if mode == "forward":
            values = rows_in[0][part] + total
            kept_ref[part] = values
            all_ref[me, part] = line_order((values * norm_scale(values)).astype(BF), levels)
        else:
            total = place_order(total, levels)
            upstream, values = rows_in[0][part], rows_in[1][part]
            scale = norm_scale(values)
            norm = values * scale
            result = upstream + scale * (
                total - norm * jnp.mean(total * norm, axis=-1, keepdims=True)
            )
            kept_ref[part] = result.astype(kept_ref.dtype)
            if gathers:
                all_ref[me, part] = result.astype(BF)

    scatter.wait_low()
    own_step(low)
    if gathers:
        x_low.start()
        y_low.start()
    scatter.wait_high()
    own_step(high)
    if mode == "last":
        plan.start([3])

    def finish_second():
        scatter2.relay()
        scatter2.wait_low()
        scatter2.wait_high()
        kept2_ref[...] = (rows2_ref[...] + scatter2.total(slice(None))).astype(BF)
        copies.extend(scatter2.copies)

    if gathers:
        y_high.start()
        x_high.start()
        x_low.wait_recv()
        on_y.start()
        y_high.wait_recv()
        on_x.start()
        if collect:
            collect.relay(0)
        x_high.wait_recv()
        y_low.wait_recv()
        on_y.wait_recv()
        on_x.wait_recv()
        copies += [x_low, y_high, x_high, y_low, on_y, on_x]
    if follow:
        chunks = range(len(follow.entries))
        follow.give(chunks)
        follow.keep(chunks, follow_out)
    if collect and not gathers:
        collect.relay(0)
    if second:
        finish_second()
    for copy in copies:
        copy.wait_send()
    finish_side()


def square(
    mode, levels, parts, rows_in, collective_id, collect=(), ready=(), second=(), slab=None, left=None
):
    rows, width = rows_in[0].shape
    gathers = mode != "last"
    dma = lambda *shape: pltpu.SemaphoreType.DMA(shape)
    like = lambda kind: jax.ShapeDtypeStruct((rows, width), kind)
    for_scatter = [pltpu.VMEM((2, rows // 2, width), BF)] * 2
    for_scatter += [pltpu.VMEM((rows, width), BF)] * 2 + [dma(6), dma(6)]
    plan = None
    if mode == "last":
        n = collect[1].shape[1]
        qkv = jax.ShapeDtypeStruct((1, GROUP, collect[0].shape[1] // 2 // levels // GROUP, n), BF)
        out = jax.ShapeDtypeStruct(ready[0].shape[1:], BF)
        plan = Exchange(levels, [slab, qkv], [out], tokens=[like(BF)], back=True)
    operands = [parts] + list(rows_in) + list(second)
    operands += list(collect) + list(ready)
    in_specs = [VMEM] * len(operands)
    out_shape, scratch = [], []
    if mode == "last":
        scratch += [pltpu.VMEM(a.shape, BF) for a in (like(BF), qkv, out)]
    else:
        out_shape.append(like(F32))
    scratch += for_scatter
    if second:
        out_shape.append(like(BF))
        scratch += for_scatter
    if gathers:
        out_shape.append(jax.ShapeDtypeStruct((GROUP, rows, width), BF))
        scratch += [dma(6), dma(6)]
    out_specs = [VMEM] * len(out_shape)
    collects = 0
    if collect:
        shape = core_sum_shape(levels, [collect], collect[1].shape[1])
        shapes = [shape] + [a.shape for a in ready]
        collects = len(shapes)
        if gathers:
            out_specs += [VMEM] * collects
            out_shape += [jax.ShapeDtypeStruct(a[1:], BF) for a in shapes]
        scratch += [pltpu.VMEM(shape, BF)] + collect_scratch(shapes)
        scratch += core_sum_scratch(levels, [collect], shape[2])
    if left is not None:
        pairs = [(left, jax.ShapeDtypeStruct((GROUP * rows, width), BF))]
        operands.append(left)
        in_specs.append(VMEM)
        out_specs.append(VMEM)
        out_shape.append(jax.ShapeDtypeStruct(core_sum_shape(levels, pairs, CW), BF))
        scratch += core_sum_scratch(levels, pairs, CW)
    if plan:
        operands.append(slab)
        in_specs.append(ANY)
        out_specs += [ANY] * len(plan.arrays)
        out_shape += plan.out_shape
        scratch += plan.scratch
    return pl.pallas_call(
        functools.partial(
            square_kernel, mode, levels, collects, bool(second), plan, left is not None
        ),
        out_shape=out_shape,
        in_specs=in_specs,
        out_specs=out_specs,
        scratch_shapes=scratch,
        compiler_params=params(collective_id),
        name="square_" + mode,
    )(*operands)


PIECES = 4


def piece_rows(rows):
    return [pl.ds(i * (rows // PIECES), rows // PIECES) for i in range(PIECES)]


def dot_nt(a, b):
    return lax.dot_general(a, b, (((1,), (1,)), ((), ())), preferred_element_type=F32)


def dot_tn(a, b):
    return lax.dot_general(a, b, (((0,), (0,)), ((), ())), preferred_element_type=F32)


def two_heads(block, j):
    a = block[:, 2 * j * HD : (2 * j + 1) * HD]
    b = block[:, (2 * j + 1) * HD : (2 * j + 2) * HD]
    return jnp.concatenate([a, b], axis=0)


def visible_keys(z, level, span, row_segs, key_segs):
    rows = lax.broadcasted_iota(jnp.int32, (span, span), 0)
    cols = lax.broadcasted_iota(jnp.int32, (span, span), 1)
    mask = (row_segs == key_segs) & ((cols <= rows) | (level < z))
    return jnp.concatenate([mask, mask], axis=0)


def turn(block, cosine, sine):
    a, b = block[:, : HD // 2], block[:, HD // 2 :]
    return jnp.concatenate([a * cosine - b * sine, b * cosine + a * sine], axis=1)


def attend_kernel(planes, *refs):
    normed_ref, weight_ref, cos_ref, sin_ref, row_ref, key_ref = refs[:6]
    q_ref, kv_ref, out_ref, lse_ref = refs[6:10]
    send, recv = refs[10:]
    levels, span = kv_ref.shape[:2]
    x, c, z, y = place()
    up, down = chain(x, c, z, y, planes)
    here = level_of(c, z, planes)
    top = levels - 1
    scaling = 1.0 / math.sqrt(HD)
    barrier = pltpu.get_barrier_semaphore()

    @pl.when(here > 0)
    def _():
        pl.semaphore_signal(barrier, inc=1, device_id=down, device_id_type=MESH)

    cosine, sine = cos_ref[...], sin_ref[...]
    heads = lambda flat, n: [turn(flat[:, j * HD : (j + 1) * HD], cosine, sine) for j in range(n)]
    wide = q_ref.shape[1]
    own = jnp.dot(normed_ref[...], weight_ref[:, wide:], preferred_element_type=F32)
    half = own.shape[1] // 2
    kv_ref[here] = jnp.concatenate(heads(own[:, :half], 2) + [own[:, half:]], axis=1).astype(BF)

    def hop(distance):
        block = kv_ref.at[lax.rem(here - distance + levels, levels)]
        return remote(block, block, send.at[distance], recv.at[distance], up)

    @pl.when(here < top)
    def _():
        pl.semaphore_wait(barrier, 1)
        hop(0).start()

    own = jnp.dot(normed_ref[...], weight_ref[:, :wide], preferred_element_type=F32)
    q_ref[...] = jnp.concatenate(heads(own, 4), axis=1).astype(BF)
    queries = [two_heads(q_ref[...], j) for j in range(2)]

    def step(distance, carry):
        level = here - distance

        @pl.when(distance > 0)
        def _():
            block = kv_ref.at[level]
            remote(block, block, send.at[distance - 1], recv.at[distance - 1], up).wait_recv()

            @pl.when(here < top)
            def _():
                hop(distance).start()

        block = kv_ref[level]
        mask = visible_keys(here, level, span, row_ref[...], key_ref[level])
        after = []
        for j in range(2):
            top_old, total, accum = carry[3 * j : 3 * j + 3]
            keys = block[:, j * HD : (j + 1) * HD]
            values = block[:, (2 + j) * HD : (3 + j) * HD]
            scores = dot_nt(queries[j], keys) * scaling
            scores = jnp.where(mask, scores, NEGATIVE)
            new = jnp.maximum(top_old, jnp.max(scores, axis=-1, keepdims=True))
            scale = jnp.exp(top_old - new)
            weights = jnp.where(mask, jnp.exp(scores - new), 0.0)
            total = total * scale + jnp.sum(weights, axis=-1, keepdims=True)
            accum = accum * scale + jnp.dot(weights.astype(BF), values, preferred_element_type=F32)
            after += [new, total, accum]
        return tuple(after)

    start = (
        jnp.full((2 * span, 1), NEGATIVE, F32),
        jnp.zeros((2 * span, 1), F32),
        jnp.zeros((2 * span, HD), F32),
    )
    done = lax.fori_loop(0, here + 1, step, start + start)
    outs, lses = [], []
    for j in range(2):
        top_all, total, accum = done[3 * j : 3 * j + 3]
        result = (accum / total).astype(BF)
        lse = jnp.broadcast_to(top_all + jnp.log(total), (2 * span, 32))
        outs += [result[:span], result[span:]]
        lses += [lse[:span], lse[span:]]
    out_ref[...] = jnp.concatenate(outs, axis=1)
    lse_ref[...] = jnp.concatenate(lses, axis=1)

    @pl.when(here < top)
    def _():
        def sent(distance, nothing):
            hop(distance).wait_send()
            return nothing

        lax.fori_loop(0, here + 1, sent, 0)


def attend(operands, planes, collective_id):
    normed, weight = operands[:2]
    rows, levels = normed.shape[0], planes // 2
    wide = weight.shape[1] // 2
    shape = jax.ShapeDtypeStruct
    return pl.pallas_call(
        functools.partial(attend_kernel, planes),
        out_shape=[
            shape((rows, wide), BF),
            shape((levels, rows, wide), BF),
            shape((rows, wide), BF),
            shape((rows, 128), F32),
        ],
        in_specs=[VMEM] * len(operands),
        out_specs=[VMEM] * 4,
        scratch_shapes=[pltpu.SemaphoreType.DMA((levels,)), pltpu.SemaphoreType.DMA((levels,))],
        compiler_params=params(collective_id),
        name="attend",
    )(*operands)


def turn_back(block, cosine, sine):
    a, b = block[:, : HD // 2], block[:, HD // 2 :]
    return jnp.concatenate([a * cosine + b * sine, b * cosine - a * sine], axis=1)


def attend_back_kernel(planes, plan, *refs):
    refs = list(refs)
    take = lambda n: [refs.pop(0) for _ in range(n)]
    q_ref, kv_ref, row_ref, key_ref, out_ref, lse_ref, back_ref, cos_ref, sin_ref, mid_ref = take(10)
    side_in = take(len(plan.arrays) if plan else 0)
    dqkv_ref, dout_ref = take(2)
    side_out = take(len(plan.arrays) if plan else 0)
    part, came, sums, heads_q, heads_back, lse4, delta4, dq4, send, recv = take(10)
    own, away, came_out, out_send, out_recv = take(5)
    levels = kv_ref.shape[0]
    x, c, z, y = place()
    up, down = chain(x, c, z, y, planes)
    other_core = device(x, 1 - c, z, y)
    z = level_of(c, z, planes)
    top = levels - 1
    span = q_ref.shape[0]
    scaling = 1.0 / math.sqrt(HD)
    pieces = piece_rows(span)
    barrier = pltpu.get_barrier_semaphore()
    pl.semaphore_signal(barrier, inc=1, device_id=other_core, device_id_type=MESH)

    @pl.when(z < top)
    def _():
        pl.semaphore_signal(barrier, inc=1, device_id=up, device_id_type=MESH)

    expected = 1 + jnp.minimum(z, 1)
    if plan:
        plan.bind(side_in, side_out, *refs)
        expected = expected + plan.greet(barrier)
    pl.semaphore_wait(barrier, expected)
    if plan:
        plan.start()

    def hop(block, piece, source):
        rows = pieces[piece]
        return remote(
            source.at[block, rows],
            came.at[block, rows],
            send.at[block, piece],
            recv.at[block, piece],
            down,
        )

    lse_all = lse_ref[...]
    for j in range(2):
        back = two_heads(back_ref[...], j)
        heads_q[j] = two_heads(q_ref[...], j)
        heads_back[j] = back
        lse4[j] = jnp.concatenate(
            [lse_all[:, 64 * j : 64 * j + 1], lse_all[:, 64 * j + 32 : 64 * j + 33]], axis=0
        )
        out = two_heads(out_ref[...], j)
        delta4[j] = jnp.sum(back.astype(F32) * out.astype(F32), axis=-1, keepdims=True)
        dq4[j] = jnp.zeros((2 * span, HD), F32)

    def one_level(level, nothing):
        block = kv_ref[level]
        mask = visible_keys(z, level, span, row_ref[...], key_ref[level])
        dks, dvs = [], []
        for j in range(2):
            keys = block[:, j * HD : (j + 1) * HD]
            values = block[:, (2 + j) * HD : (3 + j) * HD]
            queries, back = heads_q[j], heads_back[j]
            scores = dot_nt(queries, keys) * scaling
            probs = jnp.where(mask, jnp.exp(scores - lse4[j]), 0.0)
            dprobs = dot_nt(back, values)
            dscores = (probs * (dprobs - delta4[j]) * scaling).astype(BF)
            dq4[j] += jnp.dot(dscores, keys, preferred_element_type=F32)
            dks.append(dot_tn(dscores, queries).astype(BF))
            dvs.append(dot_tn(probs.astype(BF), back).astype(BF))
        part[level] = jnp.concatenate(dks + dvs, axis=1)

        @pl.when((z == top) & (level < top))
        def _():
            for piece in range(PIECES):
                hop(level, piece, part).start()

        return nothing

    lax.fori_loop(0, z + 1, one_level, 0)

    rb = own.shape[1]
    wide = own.shape[2]
    for k in range(wide // CW):
        columns = pl.ds(k * CW, CW)
        product = dot_tn(out_ref[...], mid_ref[:, columns])
        for level in range(planes):
            first = product[2 * level * rb : (2 * level + 1) * rb]
            second = product[(2 * level + 1) * rb : (2 * level + 2) * rb]
            own[level, :, columns] = jnp.where(c == 0, first, second)
            away[level, :, columns] = jnp.where(c == 0, second, first).astype(BF)
    cross = remote(away, came_out, out_send.at[0], out_recv.at[0], other_core)
    cross.start()

    heads = []
    for j in range(2):
        both = dq4[j]
        heads += [
            turn_back(both[:span], cos_ref[...], sin_ref[...]),
            turn_back(both[span:], cos_ref[...], sin_ref[...]),
        ]
    dqkv_ref[:, : 4 * HD] = jnp.concatenate(heads, axis=1).astype(BF)

    def store(total, rows):
        cosine, sine = cos_ref[rows, :], sin_ref[rows, :]
        heads = [turn_back(total[:, j * HD : (j + 1) * HD], cosine, sine) for j in range(2)]
        dqkv_ref[rows, 4 * HD :] = jnp.concatenate(heads + [total[:, 2 * HD :]], axis=1).astype(BF)

    @pl.when(z == top)
    def _():
        for piece in range(PIECES):
            rows = pieces[piece]
            store(part[top, rows].astype(F32), rows)
        for block in range(top):
            for piece in range(PIECES):
                hop(block, piece, part).wait_send()

    @pl.when(z < top)
    def _():
        for block in range(top):

            @pl.when(block < z)
            def _(block=block):
                for piece in range(PIECES):
                    rows = pieces[piece]
                    hop(block, piece, sums).wait_recv()
                    sums[block, rows] = (
                        part[block, rows].astype(F32) + came[block, rows].astype(F32)
                    ).astype(BF)
                    hop(block, piece, sums).start()

            @pl.when(block == z)
            def _(block=block):
                for piece in range(PIECES):
                    rows = pieces[piece]
                    hop(block, piece, sums).wait_recv()
                    store(part[block, rows].astype(F32) + came[block, rows].astype(F32), rows)

        for block in range(top):

            @pl.when(block < z)
            def _(block=block):
                for piece in range(PIECES):
                    hop(block, piece, sums).wait_send()

    cross.wait_recv()
    for level in range(planes):
        dout_ref[level] = (own[level] + came_out[level].astype(F32)).astype(BF)
    cross.wait_send()
    if plan:
        plan.wait()


def attend_back(operands, rb, planes, collective_id, slabs=(), swaps=(), tokens=()):
    q, kv, mid_all = operands[0], operands[1], operands[-1]
    levels = kv.shape[0]
    rows, width = q.shape
    plan = Exchange(planes, slabs, swaps, (), tokens, True) if slabs or swaps else None
    side = plan.arrays if plan else []
    heads = (2, 2 * rows, HD)
    column = (2, 2 * rows, 1)
    dout = (planes, rb, mid_all.shape[1])
    return pl.pallas_call(
        functools.partial(attend_back_kernel, planes, plan),
        out_shape=[jax.ShapeDtypeStruct((rows, 2 * width), BF), jax.ShapeDtypeStruct(dout, BF)]
        + (plan.out_shape if plan else []),
        in_specs=[VMEM] * len(operands) + [ANY] * len(side),
        out_specs=[VMEM] * 2 + [ANY] * len(side),
        scratch_shapes=[
            pltpu.VMEM(kv.shape, BF),
            pltpu.VMEM(kv.shape, BF),
            pltpu.VMEM(kv.shape, BF),
            pltpu.VMEM(heads, BF),
            pltpu.VMEM(heads, BF),
            pltpu.VMEM(column, F32),
            pltpu.VMEM(column, F32),
            pltpu.VMEM(heads, F32),
            pltpu.SemaphoreType.DMA((levels, PIECES)),
            pltpu.SemaphoreType.DMA((levels, PIECES)),
            pltpu.VMEM(dout, F32),
            pltpu.VMEM(dout, BF),
            pltpu.VMEM(dout, BF),
            pltpu.SemaphoreType.DMA((1,)),
            pltpu.SemaphoreType.DMA((1,)),
        ]
        + (plan.scratch if plan else []),
        compiler_params=params(collective_id),
        name="attend_back",
    )(*operands, *side)


def cut_weights(levels, l, rbf, weights, gains, qkv_out, gu_out):
    query, key, value, gate, up = weights
    qw, kw, fw = query.shape[2] // GROUP, key.shape[2] // GROUP, gate.shape[2] // GROUP
    q, k, v = [(w[l].astype(F32) * gains[0][l]).astype(BF) for w in (query, key, value)]
    for t in range(GROUP):
        qkv_out[0, t] = jnp.concatenate(
            [
                q[:, t * qw : (t + 1) * qw],
                k[:, t * kw : (t + 1) * kw],
                v[:, t * kw : (t + 1) * kw],
            ],
            axis=1,
        )

    def feed_forward():
        g, u = [(w[l].astype(F32) * gains[1][l]).astype(BF) for w in (gate, up)]
        for t in range(GROUP):
            pieces = []
            for w in (g, u):
                for core in range(2):
                    for level in range(levels):
                        at = t * fw + (2 * level + core) * rbf
                        pieces.append(w[:, at : at + rbf])
            gu_out[0, t] = jnp.concatenate(pieces, axis=1)

    return feed_forward


def start_kernel(levels, layers, rbf, plan, *refs):
    refs = list(refs)
    take = lambda n: [refs.pop(0) for _ in range(n)]
    sources, gains = take(5), take(2)
    out_weight, down_weight, lanes, tokens, cotangent = take(5)
    all_ref = take(1)[0]
    spread_out = take(2)
    cuts = [take(2) for _ in range(layers - 1)]
    plan_out = take(7)
    weights = take(5)
    qkv_cut, gu_cut, normed = take(3)
    load = take(1)[0]
    plan_sems, gather_sems, spread_sems = take(3), take(3), take(6)
    loads = [pltpu.make_async_copy(a, b, load.at[i]) for i, (a, b) in enumerate(zip(sources, weights))]
    for copy in loads:
        copy.start()
    ins = [qkv_cut, gu_cut, out_weight.at[0], down_weight.at[0], lanes, tokens, cotangent]
    plan.bind(ins, plan_out, *plan_sems)
    line = Line(levels)
    greet(line.partners + [line.other_core], plan)
    spread = Spread(line, False, [plan_out[0].at[0], plan_out[2]], spread_out, *spread_sems)
    gather = Gather(normed, all_ref, *gather_sems)
    plan.start([5])
    plan.start([2, 4])
    for copy in loads:
        copy.wait()
    feed_forward = cut_weights(levels, 0, rbf, weights, gains, qkv_cut, gu_cut)
    plan.start([0])
    feed_forward()
    plan.wait([0, 2])
    spread.start()
    plan.wait([5])
    values = plan_out[5][...].astype(F32)
    normed[...] = line_order((values * norm_scale(values)).astype(BF), levels)
    gather.start()
    plan.start([1, 3])
    plan.start([6])
    for l in range(1, layers):
        cut_weights(levels, l, rbf, weights, gains, *cuts[l - 1])()
    gather.relay()
    spread.relay(others=False)
    gather.finish()
    spread.relay(ends=False)
    spread.finish()
    plan.wait([1, 3, 4, 6])


def start(levels, weights, gains, out_weight, down_weight, lanes, tokens, cotangent, collective_id):
    query, key, _, gate, _ = weights
    layers, rb, _ = query.shape
    rbf = down_weight.shape[1]
    rows, width = tokens.shape
    wide = (query.shape[2] + 2 * key.shape[2]) // GROUP
    shape = jax.ShapeDtypeStruct
    qkv_cut = shape((1, GROUP, rb, wide), BF)
    gu_cut = shape((1, GROUP, rb, 2 * gate.shape[2] // GROUP), BF)
    one = lambda a: shape(a.shape[1:], a.dtype)
    plan = Exchange(
        levels,
        [qkv_cut, gu_cut],
        [one(out_weight), one(down_weight)],
        [lanes],
        [tokens, cotangent],
    )
    spreads = [qkv_cut.shape[1:], out_weight.shape[1:]]
    out_shape = [shape((GROUP, rows, width), BF)]
    out_shape += [shape((2, levels) + a, BF) for a in spreads]
    out_shape += [qkv_cut, gu_cut] * (layers - 1) + plan.out_shape
    out_specs = [VMEM] + [ANY] * 2 + [VMEM] * (2 * layers - 2) + [ANY] * 5 + [VMEM, ANY]
    dma = lambda n: pltpu.SemaphoreType.DMA((n,))
    return pl.pallas_call(
        functools.partial(start_kernel, levels, layers, rbf, plan),
        out_shape=out_shape,
        in_specs=[ANY] * 5 + [VMEM] * 2 + [ANY] * 5,
        out_specs=out_specs,
        scratch_shapes=[pltpu.VMEM(a.shape, BF) for a in weights]
        + [pltpu.VMEM(a.shape, BF) for a in (qkv_cut, gu_cut, tokens)]
        + [dma(5)]
        + plan.scratch
        + [dma(6), dma(6), dma(1)]
        + spread_scratch(2, levels),
        compiler_params=params(collective_id, 63),
        name="start",
    )(*weights, *gains, out_weight, down_weight, lanes, tokens, cotangent)


def finish_kernel(levels, layers, *refs):
    grads = [refs[4 * l : 4 * l + 4] for l in range(layers)]
    weights, gain1, gain2, outs = (
        refs[4 * layers : 4 * layers + 5],
        refs[4 * layers + 5],
        refs[4 * layers + 6],
        refs[4 * layers + 7 :],
    )
    query, key, value, output, gate, up, down, gain1_out, gain2_out = outs
    qw, kw, fw = query.shape[2] // GROUP, key.shape[2] // GROUP, gate.shape[2] // GROUP
    rbf = down.shape[1]
    for l in range(layers):
        qkv, out, gu, dn = grads[l]

        def place_columns(target, weight, gain, pieces, total):
            raw = jnp.concatenate(pieces, axis=1).astype(F32)
            target[l] = raw * gain[l]
            dots = jnp.sum(raw * weight[l].astype(F32), axis=1, keepdims=True)
            return dots if total is None else total + dots

        total = None
        for target, weight, first, n in (
            (query, weights[0], 0, qw),
            (key, weights[1], qw, kw),
            (value, weights[2], qw + kw, kw),
        ):
            pieces = [qkv[0, t, :, first : first + n] for t in range(GROUP)]
            total = place_columns(target, weight, gain1, pieces, total)
        gain1_out[l] = total
        output[l] = out[...].astype(F32)
        total = None
        for target, weight, base in ((gate, weights[3], 0), (up, weights[4], fw)):
            pieces = []
            for t in range(GROUP):
                for level in range(levels):
                    for core in range(2):
                        at = base + (core * levels + level) * rbf
                        pieces.append(gu[at // CW, t, :, at % CW : at % CW + rbf])
            total = place_columns(target, weight, gain2, pieces, total)
        gain2_out[l] = total
        down[l] = jnp.concatenate([dn[k] for k in range(dn.shape[0])], axis=1).astype(F32)


def finish(levels, grads, weights, output_weight, down_weight, gain1, gain2):
    layers, rb, _ = output_weight.shape
    like = lambda a: jax.ShapeDtypeStruct(a.shape, F32)
    query, key, value, gate, up = weights
    column = jax.ShapeDtypeStruct((layers, rb, 1), F32)
    operands = [a for layer in grads for a in layer] + list(weights) + [gain1, gain2]
    out_shape = [like(a) for a in (query, key, value, output_weight, gate, up, down_weight)]
    return pl.pallas_call(
        functools.partial(finish_kernel, levels, layers),
        out_shape=out_shape + [column, column],
        in_specs=[VMEM] * len(operands),
        out_specs=[VMEM] * 9,
        compiler_params=params(),
        name="finish",
    )(*operands)


def feed_forward_kernel(normed, gu, down, gate, up, active, parts, gu_here, down_here, arrived):
    wide = gate.shape[1]
    halves = wide // CW
    copies = []
    for h in range(halves):
        for first in (h * CW, wide + h * CW):
            columns = pl.ds(first, CW)
            copies.append((gu.at[:, columns], gu_here.at[:, columns]))
        rows = pl.ds(h * CW, CW)
        copies.append((down.at[rows], down_here.at[rows]))
    copies = [pltpu.make_async_copy(a, b, arrived.at[i]) for i, (a, b) in enumerate(copies)]
    for copy in copies:
        copy.start()
    total = None
    for h in range(halves):
        columns = pl.ds(h * CW, CW)
        copies[3 * h].wait()
        g = jnp.dot(normed[...], gu_here[:, columns], preferred_element_type=F32)
        copies[3 * h + 1].wait()
        u = jnp.dot(
            normed[...], gu_here[:, pl.ds(wide + h * CW, CW)], preferred_element_type=F32
        )
        gate[:, columns] = g
        up[:, columns] = u
        a = (g / (1.0 + jnp.exp(-g)) * u).astype(BF)
        active[:, columns] = a
        copies[3 * h + 2].wait()
        part = jnp.dot(a, down_here[columns], preferred_element_type=F32)
        total = part if total is None else total + part
    parts[...] = total.astype(BF)


def feed_forward(normed, gu, down):
    rows, width = normed.shape
    wide = down.shape[0]
    shape = jax.ShapeDtypeStruct
    return pl.pallas_call(
        feed_forward_kernel,
        out_shape=[
            shape((rows, wide), F32),
            shape((rows, wide), F32),
            shape((rows, wide), BF),
            shape((rows, width), BF),
        ],
        in_specs=[VMEM, ANY, ANY],
        out_specs=[VMEM] * 4,
        scratch_shapes=[
            pltpu.VMEM(gu.shape, BF),
            pltpu.VMEM(down.shape, BF),
            pltpu.SemaphoreType.DMA((3 * (wide // CW),)),
        ],
        compiler_params=params(),
        name="feed_forward",
    )(normed, gu, down)


def rope_tables(positions, head_width):
    frequency = THETA ** (-(jnp.arange(head_width // 2, dtype=F32) * 2.0 / head_width))
    angles = positions.astype(F32)[..., None] * frequency
    return (jnp.cos(angles), jnp.sin(angles))


def doc_positions(segments):
    places = jnp.arange(segments.shape[1], dtype=jnp.int32)
    starts_new = jnp.concatenate(
        [jnp.ones((segments.shape[0], 1), dtype=jnp.bool_), segments[:, 1:] != segments[:, :-1]],
        axis=1,
    )
    starts = lax.cummax(jnp.where(starts_new, places[None, :], 0), axis=1)
    return places[None, :] - starts


def on_device(
    levels,
    tokens,
    segments,
    cotangent,
    query_weight,
    key_weight,
    value_weight,
    output_weight,
    attention_gain,
    gate_weight,
    up_weight,
    down_weight,
    feedforward_gain,
):
    _, rows, width = tokens.shape
    full_len = segments.shape[1]
    layers = query_weight.shape[0]
    rb = query_weight.shape[1]
    rbf = down_weight.shape[1]
    kv_width = KVH * HD
    ffn = gate_weight.shape[2]
    qw, kw, fw = width // GROUP, kv_width // GROUP, ffn // GROUP
    group_rows = GROUP * rows
    _, c, z, _ = place()
    here = level_of(c, z, levels)
    n_ctx = 2 * levels
    lines = [
        [(gx * 2 + gc) * n_ctx + gz * 2 + gy for gc in range(2) for gz in range(levels)]
        for gx in range(2)
        for gy in range(2)
    ]
    core_lines = [
        [gs * n_ctx + gz * 2 + gy for gz in range(levels)] for gs in range(4) for gy in range(2)
    ]
    def gather_line(part):
        return lax.all_gather(part, AXES, axis=0, tiled=True, axis_index_groups=lines)

    def scatter_line(total):
        return lax.psum_scatter(
            total, AXES, scatter_dimension=0, tiled=True, axis_index_groups=core_lines
        )

    def after(value, *others):
        return lax.optimization_barrier((value,) + others)[0]

    gain1 = attention_gain.astype(F32)[:, :, None]
    gain2 = feedforward_gain.astype(F32)[:, :, None]
    lanes = segments.reshape(full_len // 128, 128)
    normed, qkv0, out0, *cuts = start(
        levels,
        [query_weight, key_weight, value_weight, gate_weight, up_weight],
        [gain1, gain2],
        output_weight,
        down_weight,
        lanes,
        tokens.reshape(rows, width),
        cotangent.reshape(rows, width),
        1,
    )
    cuts, (_, gu_own, _, down_own, all_segments, residual, cotangent) = cuts[:-7], cuts[-7:]
    qkv_slabs, gu_slabs = [None] + cuts[0::2], [None] + cuts[1::2]
    normed = normed.reshape(group_rows, width)

    def all_ffn(gu, down):
        return gather_line(gu.reshape(GROUP * rb, 2 * fw)), gather_line(down)

    own_segments = lax.dynamic_index_in_dim(
        all_segments.reshape(4, full_len), sequence_of(z, levels), 0
    )
    first = here * group_rows
    positions = lax.dynamic_slice_in_dim(doc_positions(own_segments)[0], first, group_rows)
    cosine, sine = rope_tables(positions, HD)
    row_segs = lax.dynamic_slice_in_dim(own_segments[0], first, group_rows)[:, None]
    key_segs = own_segments.reshape(levels // 2, 1, group_rows)

    def split(parts):
        return parts.astype(BF).reshape(GROUP, rows, width)

    def in_square(mode, parts, rows_in, collective_id, **more):
        out = list(square(mode, levels, split(parts), rows_in, collective_id, **more))
        if mode != "last":
            at = 2 if "second" in more else 1
            out[at] = out[at].reshape(group_rows, width)
        return out

    dot = functools.partial(jnp.dot, preferred_element_type=F32)

    qkv_full, out_full, gu_full, down_full = [[None] * layers for _ in range(4)]
    qkv_full[0], out_full[0] = qkv0, out0
    gu_full[0], down_full[0] = all_ffn(gu_own, down_own)
    residual = residual.astype(F32)
    stored = []
    for l in range(layers):
        weight = after(qkv_full[l].reshape(width, qw + 2 * kw), normed)
        q, kv, attended, lse = attend(
            [normed, weight, cosine, sine, row_segs, key_segs], levels, 5
        )
        out_full[l] = (
            after(out_full[l], attended)
            .reshape(2, levels, rb, width)
            .transpose(1, 0, 2, 3)
            .reshape(qw, width)
        )
        middle, normed2 = in_square("forward", dot(attended, out_full[l]), [residual], 4)
        if l < layers - 1:
            _, gu_own, _, down_own, qkv_full[l + 1], out_full[l + 1], *gathered = exchange(
                levels,
                [after(qkv_slabs[l + 1], normed2), gu_slabs[l + 1]],
                [output_weight[l + 1], down_weight[l + 1]],
                8,
                spread=True,
                own=cotangent if l == 0 else None,
            )
            up_all = gathered[0].reshape(group_rows, width) if l == 0 else up_all
            gu_full[l + 1], down_full[l + 1] = all_ffn(gu_own, down_own)
        if l < layers - 1:
            gu = after(gu_full[l], normed2)
            gate, up, active, parts = feed_forward(normed2, gu, after(down_full[l], gu))
        else:
            gu = dot(normed2, after(gu_full[l], normed2))
            gate, up = gu[:, :fw], gu[:, fw:]
            active = (jax.nn.silu(gate) * up).astype(BF)
        stored.append((residual, normed, q, kv, attended, lse, middle, normed2, gate, up, active))
        if l < layers - 1:
            residual, normed = in_square("forward", parts, [middle], 4)

    def dot_t(a, b):
        return lax.dot_general(a, b, (((1,), (1,)), ((), ())), preferred_element_type=F32)

    upstream = cotangent.astype(F32)
    ffn_grads, attention_grads, down_grads, grads = [[None] * layers for _ in range(4)]

    def in_slabs(l):
        qkv_grad, out_grad = attention_grads[l]
        gu_grad = ffn_grads[l][0].reshape(2 * fw // CW, GROUP, rb, CW)
        qkv_grad = qkv_grad.reshape(1, GROUP, rb, qw + 2 * kw)
        return [qkv_grad, gu_grad], [out_grad]

    for l in reversed(range(layers)):
        residual, normed, q, kv, attended, lse, middle, normed2, gate, up, active = stored[l]
        if l == layers - 1:
            down_total = ffn_gradient(levels, [(active, up_all)], 13)
        down_full[l] = after(down_full[l], down_total)
        if l == layers - 1:
            block = split(dot(active, down_full[l])), middle
        dactive = dot_t(up_all, down_full[l])
        sig = jax.nn.sigmoid(gate)
        dgate = (dactive * up * sig * (1.0 + gate * (1.0 - sig))).astype(BF)
        dup = (dactive * gate * sig).astype(BF)
        dgu = jnp.concatenate([dgate, dup], axis=1)
        ffn_total = ffn_gradient(levels, [(normed2, dgu)], 16)
        ffn_grads[l] = [scatter_line(total.reshape(-1, CW)) for total in (ffn_total, down_total)]
        dnorm2 = dot_t(after(dgu, ffn_total), gu_full[l]).astype(BF)
        dmiddle, mid_all = in_square("backward", dnorm2, [upstream, middle], 10)
        back = dot_t(mid_all, out_full[l]).astype(BF)
        operands = [q, kv, row_segs, key_segs, attended, lse, back, cosine, sine, mid_all]
        if l < layers - 1:
            slabs, swaps = in_slabs(l + 1)
            moved = [block_output] if l == layers - 2 else []
            swaps = [ffn_grads[l][1]] + swaps
            dqkv, out_total, *landed = attend_back(
                operands, rb, levels, 15, slabs, swaps, moved
            )
            block_output = landed.pop() if moved else block_output
            down_grads[l] = landed.pop(len(slabs))
            grads[l + 1] = landed + [down_grads[l + 1]]
        else:
            dqkv, out_total, down_grads[l] = attend_back(
                operands, rb, levels, 6, [], [ffn_grads[l][1]]
            )
        dnorm1 = dot_t(dqkv, qkv_full[l].reshape(width, qw + 2 * kw)).astype(BF)
        collect = normed, dqkv
        if l == layers - 1:
            upstream, block_output, up_all, qkv_grad, out_grad, down_total = in_square(
                "backward",
                dnorm1,
                [dmiddle, residual],
                14,
                collect=collect,
                ready=[out_total],
                second=block,
                left=stored[l - 1][-1],
            )
        elif l > 0:
            upstream, up_all, qkv_grad, out_grad, down_total = in_square(
                "backward",
                dnorm1,
                [dmiddle, residual],
                18,
                collect=collect,
                ready=[out_total],
                left=stored[l - 1][-1],
            )
        else:
            gu_grad, qkv_grad, out_grad, tokens_grad = in_square(
                "last",
                dnorm1,
                [dmiddle, residual],
                11,
                collect=collect,
                ready=[out_total],
                slab=ffn_grads[l][0].reshape(2 * fw // CW, GROUP, rb, CW),
            )
        attention_grads[l] = [qkv_grad, out_grad]

    grads[0] = [qkv_grad, gu_grad, out_grad, down_grads[0]]
    ordered = [
        [qkv, out, gu, down.reshape(width // CW, rbf, CW)] for qkv, gu, out, down in grads
    ]
    results = finish(
        levels,
        ordered,
        [query_weight, key_weight, value_weight, gate_weight, up_weight],
        output_weight,
        down_weight,
        gain1,
        gain2,
    )
    query, key, value, output, gate, up, down, gain1_grad, gain2_grad = results
    return (
        block_output.reshape(1, rows, width),
        tokens_grad.astype(F32).reshape(1, rows, width),
        query,
        key,
        value,
        output,
        gain1_grad[:, :, 0],
        gate,
        up,
        down,
        gain2_grad[:, :, 0],
    )


def solution(mesh):
    levels = mesh.shape["ctx"] // 2
    rows3 = P(None, AXES, None)
    gains = P(None, AXES)
    return jax.shard_map(
        functools.partial(on_device, levels),
        mesh=mesh,
        in_specs=(
            P("seq", "ctx", None),
            P("seq", None),
            P("seq", "ctx", None),
            rows3,
            rows3,
            rows3,
            rows3,
            gains,
            rows3,
            rows3,
            rows3,
            gains,
        ),
        out_specs=(
            P("seq", "ctx", None),
            P("seq", "ctx", None),
            rows3,
            rows3,
            rows3,
            rows3,
            gains,
            rows3,
            rows3,
            rows3,
            gains,
        ),
        check_vma=False,
    )
```

```python
import functools
import math

import jax
import jax.numpy as jnp
from jax import lax
from jax.experimental import pallas as pl
from jax.experimental.pallas import tpu as pltpu
from jax.sharding import PartitionSpec as P

H = 16
KVH = 8
HD = 96
GROUP = 4

EPSILON = 1e-05
THETA = 100000.0
NEGATIVE = -1e30
AXES = ("seq", "ctx")
MESH = pl.DeviceIdType.MESH
ANY = pl.BlockSpec(memory_space=pltpu.HBM)
VMEM = pl.BlockSpec(memory_space=pltpu.VMEM)
BF = jnp.bfloat16
F32 = jnp.float32


def params(collective_id=None, mib=48):
    if collective_id is None:
        return pltpu.CompilerParams(vmem_limit_bytes=mib * 2**20)
    return pltpu.CompilerParams(
        collective_id=collective_id, has_side_effects=True, vmem_limit_bytes=mib * 2**20
    )


def place():
    s = lax.axis_index("seq")
    k = lax.axis_index("ctx")
    return s // 2, s % 2, k // 2, k % 2


def device(x, c, z, y):
    return (x * 2 + c, z * 2 + y)


def sequence_of(z, levels):
    return z // (levels // 4)


def level_of(c, z, levels):
    return lax.rem(z, levels // 4) * 2 + c


def home_of(x, c, z, y, levels):
    block = z * 2 + y
    level = block // GROUP
    place_z = (x * 2 + c) * (levels // 4) + level // 2
    return lax.rem(block, GROUP) // 2, lax.rem(level, 2), place_z, y


def origin_of(x, c, z, y, levels):
    s = sequence_of(z, levels)
    return s // 2, lax.rem(s, 2), 2 * level_of(c, z, levels) + x, y


def chain(x, c, z, y, levels):
    up = device(x, 1 - c, lax.rem(z + c, levels), y)
    down = device(x, 1 - c, lax.rem(z + levels - 1 + c, levels), y)
    return up, down


def remote(src, dst, send, recv, to):
    return pltpu.make_async_remote_copy(
        src_ref=src, dst_ref=dst, send_sem=send, recv_sem=recv, device_id=to, device_id_type=MESH
    )


def greet(partners, plan=None):
    barrier = pltpu.get_barrier_semaphore()
    for partner in partners:
        pl.semaphore_signal(barrier, inc=1, device_id=partner, device_id_type=MESH)
    expected = len(partners)
    if plan:
        expected = expected + plan.greet(barrier)
    pl.semaphore_wait(barrier, expected)


class Exchange:
    def __init__(self, levels, slabs=(), swaps=(), rows=(), tokens=(), back=False):
        self.levels, self.back = levels, back
        self.counts = len(slabs), len(swaps), len(rows), len(tokens)
        self.picks = {len(slabs) + i: a[1] for i, a in enumerate(swaps) if isinstance(a, tuple)}
        shapes = [jax.ShapeDtypeStruct(a.shape, a.dtype) for a in slabs]
        for a in swaps:
            shape = a[0].shape[1:] if isinstance(a, tuple) else a.shape
            shapes.append(jax.ShapeDtypeStruct(shape, BF))
        swaps = [a[0] if isinstance(a, tuple) else a for a in swaps]
        self.arrays = list(slabs) + swaps + list(rows) + list(tokens)
        shapes += [jax.ShapeDtypeStruct((4,) + a.shape, a.dtype) for a in rows]
        self.out_shape = shapes + [jax.ShapeDtypeStruct(a.shape, a.dtype) for a in tokens]
        total = 2 * (len(slabs) + len(rows)) + len(self.arrays)
        self.scratch = [
            pltpu.SemaphoreType.DMA((total,)),
            pltpu.SemaphoreType.DMA((total,)),
            pltpu.SemaphoreType.DMA((len(self.arrays),)),
        ]

    def bind(self, ins, outs, send, recv, local):
        ins = [a.at[self.picks[i]] if i in self.picks else a for i, a in enumerate(ins)]
        self.ins, self.outs = ins, outs
        self.send, self.recv, self.local = send, recv, local
        x, c, z, y = place()
        self.where = c, y
        self.others = [(1 - x, y), (x, 1 - y), (1 - x, 1 - y)]
        self.square = [device(ox, c, z, oy) for ox, oy in self.others]
        self.crossed = device(x, 1 - c, z, 1 - y)
        home = home_of(x, c, z, y, self.levels)
        origin = origin_of(x, c, z, y, self.levels)
        self.moves_away = (home[0] != x) | (home[1] != c) | (home[2] != z)
        taker, giver = (origin, home) if self.back else (home, origin)
        self.taker, self.giver = device(*taker), device(*giver)
        self.seq_others = [device(x, 1 - c, z, y), device(1 - x, 1 - c, z, y)]
        n_slab, n_swap, n_rows, n_tokens = self.counts
        me = x * 2 + y
        self.groups = [[] for _ in self.arrays]
        for i in range(n_slab):
            for j, (ox, oy) in enumerate(self.others):
                sem = 3 * i + j
                self.groups[i].append(
                    remote(
                        ins[i].at[:, ox * 2 + oy],
                        outs[i].at[:, me],
                        send.at[sem],
                        recv.at[sem],
                        self.square[j],
                    )
                )
            self.groups[i].append(
                pltpu.make_async_copy(ins[i].at[:, me], outs[i].at[:, me], local.at[i])
            )
        for i in range(n_rows):
            at = n_slab + n_swap + i
            sem = self.semaphore(at)
            mine = outs[at].at[x * 2 + c]
            for j, to in enumerate([self.square[0]] + self.seq_others):
                self.groups[at].append(
                    remote(ins[at], mine, send.at[sem + j], recv.at[sem + j], to)
                )
            self.groups[at].append(pltpu.make_async_copy(ins[at], mine, local.at[at]))
        self.moves = {n_slab + i: (self.crossed, c != y) for i in range(n_swap)}
        first = n_slab + n_swap + n_rows
        for i in range(n_tokens):
            self.moves[first + i] = self.taker, self.moves_away

    def semaphore(self, at):
        n_slab, n_swap, n_rows, _ = self.counts
        rows_before = min(max(at - n_slab - n_swap, 0), n_rows)
        return at + 2 * (n_slab + rows_before)

    def greet(self, barrier):
        c, y = self.where
        signal = functools.partial(pl.semaphore_signal, barrier, inc=1, device_id_type=MESH)
        for to in self.square:
            signal(device_id=to)
        expected = 3
        if self.counts[1]:
            expected = expected + lax.rem(c + y, 2)
            pl.when(c != y)(lambda: signal(device_id=self.crossed))
        if self.counts[2]:
            expected = expected + 2
            for to in self.seq_others:
                signal(device_id=to)
        if self.counts[3]:
            expected = expected + jnp.where(self.moves_away, 1, 0)
            pl.when(self.moves_away)(lambda: signal(device_id=self.giver))
        return expected

    def whole(self, at, to):
        sem = self.semaphore(at)
        return (
            remote(self.ins[at], self.outs[at], self.send.at[sem], self.recv.at[sem], to),
            pltpu.make_async_copy(self.ins[at], self.outs[at], self.local.at[at]),
        )

    def start(self, which=None):
        for at in range(len(self.arrays)) if which is None else which:
            for copy in self.groups[at]:
                copy.start()
            if at in self.moves:
                to, goes = self.moves[at]
                cross, stay = self.whole(at, to)
                pl.when(goes)(cross.start)
                pl.when(jnp.logical_not(goes))(stay.start)

    def wait(self, which=None):
        for at in range(len(self.arrays)) if which is None else which:
            for copy in self.groups[at]:
                copy.wait()
            if at in self.moves:
                to, goes = self.moves[at]
                cross, stay = self.whole(at, to)
                pl.when(goes)(cross.wait)
                pl.when(jnp.logical_not(goes))(stay.wait)


def exchange_kernel(plan, n_spread, gathers, *refs):
    n = len(plan.arrays)
    own_ref = all_ref = None
    if gathers:
        refs = list(refs)
        own_ref, all_ref = refs.pop(n), refs.pop(2 * n + n_spread)
    outs = refs[n : 2 * n]
    spread_out = refs[2 * n : 2 * n + n_spread]
    scratch = refs[2 * n + n_spread :]
    plan.bind(refs[:n], outs, *scratch[:3])
    barrier = pltpu.get_barrier_semaphore()
    if not n_spread:
        pl.semaphore_wait(barrier, plan.greet(barrier))
        plan.start()
        plan.wait()
        return
    swap = plan.counts[0]
    line = Line(plan.levels)
    spread = Spread(line, False, [outs[0].at[0], outs[swap]], spread_out, *scratch[3:9])
    gather = Gather(own_ref, all_ref, *scratch[9:]) if own_ref is not None else None
    greet(line.partners + [line.other_core], plan)
    rest = [at for at in range(n) if at not in (0, swap)]
    plan.start([0, swap])
    plan.start(rest)
    plan.wait([0, swap])
    spread.start()
    if gather:
        gather.start()
    spread.relay(others=False)
    plan.wait(rest)
    if gather:
        gather.relay()
        gather.finish()
    spread.relay(ends=False)
    spread.finish()


class Gather:
    def __init__(self, own, everyone, send, recv, local):
        x, c, z, y = place()
        me, at_x, at_y = x * 2 + y, (1 - x) * 2 + y, x * 2 + 1 - y
        to_x, to_y = device(1 - x, c, z, y), device(x, c, z, 1 - y)
        half = own.shape[0] // 2
        low, high = pl.ds(0, half), pl.ds(half, half)
        ends = [
            (own.at[low], everyone.at[me, low], to_x),
            (own.at[high], everyone.at[me, high], to_y),
            (own.at[high], everyone.at[me, high], to_x),
            (own.at[low], everyone.at[me, low], to_y),
            (everyone.at[at_x, low], everyone.at[at_x, low], to_y),
            (everyone.at[at_y, high], everyone.at[at_y, high], to_x),
        ]
        self.copies = [
            remote(src, dst, send.at[i], recv.at[i], to) for i, (src, dst, to) in enumerate(ends)
        ]
        self.keep = pltpu.make_async_copy(own, everyone.at[me], local.at[0])

    def start(self):
        for copy in self.copies[:4]:
            copy.start()
        self.keep.start()

    def relay(self):
        for i in (0, 1):
            self.copies[i].wait_recv()
            self.copies[4 + i].start()

    def finish(self):
        for copy in self.copies[2:]:
            copy.wait_recv()
        for copy in self.copies:
            copy.wait_send()
        self.keep.wait()


def exchange(
    levels, slabs, swaps, collective_id, rows=(), tokens=(), back=False, spread=False, own=None
):
    mib = 63 if spread else 48
    plan = Exchange(levels, slabs, swaps, rows, tokens, back)
    n = len(plan.arrays)
    spreads = [slabs[0].shape[1:], plan.out_shape[len(slabs)].shape] if spread else []
    out_shape = plan.out_shape + [
        jax.ShapeDtypeStruct((2, levels) + shape, BF) for shape in spreads
    ]
    scratch = plan.scratch + (spread_scratch(2, levels) if spread else [])
    operands = list(plan.arrays)
    if own is not None:
        operands.append(own)
        out_shape.append(jax.ShapeDtypeStruct((GROUP,) + own.shape, own.dtype))
        scratch += [pltpu.SemaphoreType.DMA((n,)) for n in (6, 6, 1)]
    return pl.pallas_call(
        functools.partial(exchange_kernel, plan, len(spreads), own is not None),
        out_shape=out_shape,
        in_specs=[ANY] * len(operands),
        out_specs=[ANY] * len(out_shape),
        scratch_shapes=scratch,
        compiler_params=params(collective_id, mib),
        name="exchange",
    )(*operands)


class Line:
    def __init__(self, levels):
        x, c, z, y = place()
        self.levels, self.c, self.z = levels, c, z
        self.ahead = [lax.rem(z + d, levels) for d in range(levels)]
        self.behind = [lax.rem(z - d + levels, levels) for d in range(levels)]
        self.device = lambda to: device(x, c, to, y)
        self.other_core = device(x, 1 - c, z, y)
        self.partners = [self.device(self.ahead[d]) for d in range(1, levels)]
        self.near = list(dict.fromkeys([2, levels - 2])) + [
            d for d in range(1, levels) if d not in (2, levels - 2)
        ]
        self.bottom, self.top = z == 0, z == levels - 1
        self.low, self.high = z == 1, z == levels - 2

    def to_far_end(self, d):
        return (self.bottom & (d == self.levels - 1)) | (self.top & (d == 1))

    def by_way_to(self, d):
        return (self.low & (d == self.levels - 2)) | (self.high & (d == 2))

    def from_far_end(self, d):
        return (self.top & (d == self.levels - 1)) | (self.bottom & (d == 1))


class Spread:
    def __init__(
        self, line, hops, sources, outs, send, recv, cross_send, cross_recv, local, onward_send
    ):
        self.hops, self.onward_send = hops, onward_send
        self.line, self.sources, self.outs = line, sources, outs
        self.send, self.recv, self.local = send, recv, local
        self.cross_send, self.cross_recv = cross_send, cross_recv
        self.count = range(len(sources))

    def to_line(self, i, d):
        line = self.line
        block = self.outs[i].at[line.c, line.z]
        to = line.device(line.ahead[d])
        return remote(self.sources[i], block, self.send.at[i, d], self.recv.at[i, d], to)

    def to_core(self, i, d):
        line = self.line
        block = self.outs[i].at[line.c, line.behind[d]]
        source = block if d else self.sources[i]
        return remote(
            source, block, self.cross_send.at[i, d], self.cross_recv.at[i, d], line.other_core
        )

    def goes_direct(self, d):
        line = self.line
        if not self.hops:
            return jnp.logical_not(line.to_far_end(d))
        to_end = (line.ahead[d] == 0) & (line.z != 1)
        to_end = to_end | ((line.ahead[d] == line.levels - 1) & (line.z != line.levels - 2))
        return jnp.logical_not(to_end)

    def onward(self, i, d):
        line = self.line
        block = self.outs[i].at[line.c, line.behind[d]]
        end = jnp.where(line.low, 0, line.levels - 1)
        slot = jnp.where(line.low, d - 1, d + 1)
        return remote(
            block, block, self.onward_send.at[i, d], self.recv.at[i, slot], line.device(end)
        )

    def passes_on(self, d):
        line = self.line
        if not self.hops:
            far = jnp.where(line.low, line.levels - 1, 0)
            return (line.low | line.high) & (line.behind[d] == far)
        up = line.high & (line.behind[d] < line.levels - 2)
        return up | (line.low & (line.behind[d] > 1))

    def keep(self, i):
        line = self.line
        return pltpu.make_async_copy(
            self.sources[i], self.outs[i].at[line.c, line.z], self.local.at[i]
        )

    def start(self):
        for i in self.count:
            for d in self.line.near:
                pl.when(self.goes_direct(d))(self.to_line(i, d).start)
            self.to_core(i, 0).start()
            self.keep(i).start()

    def relay(self, ends=True, others=True):
        line = self.line
        firsts = len(dict.fromkeys([2, line.levels - 2]))
        which = (line.near[:firsts] if ends else []) + (line.near[firsts:] if others else [])
        for i in self.count:
            for d in which:
                block = self.outs[i].at[line.c, line.behind[d]]
                remote(
                    block, block, self.send.at[i, d], self.recv.at[i, d], line.other_core
                ).wait_recv()
                pl.when(self.passes_on(d))(self.onward(i, d).start)
                self.to_core(i, d).start()

    def finish(self):
        line = self.line
        for i in self.count:
            for d in range(line.levels):
                block = self.outs[i].at[1 - line.c, line.behind[d]]
                remote(
                    block, block, self.cross_send.at[i, d], self.cross_recv.at[i, d], line.other_core
                ).wait_recv()
            for d in line.near:
                pl.when(self.goes_direct(d))(self.to_line(i, d).wait_send)
                pl.when(self.passes_on(d))(self.onward(i, d).wait_send)
            for d in range(line.levels):
                self.to_core(i, d).wait_send()
            self.keep(i).wait()


def spread_scratch(n, levels):
    dma = lambda *shape: pltpu.SemaphoreType.DMA(shape)
    return [dma(n, levels), dma(n, levels), dma(n, levels), dma(n, levels), dma(n), dma(n, levels)]


class Collect:
    def __init__(self, line, sources, slots, folds, relays, send, recv, relay_send, relay_recv):
        self.line, self.sources, self.slots = line, sources, slots
        self.folds, self.relays = folds, relays
        self.send, self.recv = send, recv
        self.relay_send, self.relay_recv = relay_send, relay_recv

    def clear(self):
        for slot in self.slots:
            for d in (1, self.line.levels - 1):

                @pl.when(self.line.from_far_end(d))
                def _(slot=slot, d=d):
                    slot[d] = jnp.zeros_like(slot[d])

    def direct(self, i, d):
        line = self.line
        return remote(
            self.sources[i].at[line.ahead[d]],
            self.slots[i].at[d],
            self.send.at[i, d],
            self.recv.at[i, d],
            line.device(line.ahead[d]),
        )

    def goes_direct(self, d):
        return jnp.logical_not(self.line.to_far_end(d) | self.line.by_way_to(d))

    def via(self, i):
        line = self.line
        far = jnp.where(line.bottom, line.levels - 1, 0)
        to = jnp.where(line.bottom, 1, line.levels - 2)
        return remote(
            self.sources[i].at[far],
            self.relays[i],
            self.relay_send.at[i],
            self.relay_recv.at[i],
            line.device(to),
        )

    def folded(self, i):
        line = self.line
        end = jnp.where(line.low, line.levels - 1, 0)
        slot = jnp.where(line.low, line.levels - 2, 2)
        return end, remote(
            self.folds[i],
            self.slots[i].at[slot],
            self.send.at[i, 0],
            self.recv.at[i, slot],
            line.device(end),
        )

    def start(self, i):
        line = self.line
        pl.when(line.bottom | line.top)(self.via(i).start)
        for d in range(1, line.levels):
            pl.when(self.goes_direct(d))(self.direct(i, d).start)

    def relay(self, i):
        line = self.line

        @pl.when(line.low | line.high)
        def _():
            end, copy = self.folded(i)
            self.via(i).wait_recv()
            self.folds[i][...] = (
                self.sources[i][end].astype(F32) + self.relays[i][...].astype(F32)
            ).astype(BF)
            copy.start()

    def total(self, i):
        line = self.line
        total = self.sources[i][line.z].astype(F32)
        for d in range(1, line.levels):
            block = self.slots[i].at[d]
            came = remote(block, block, self.send.at[i, d], self.recv.at[i, d], line.other_core)
            pl.when(jnp.logical_not(line.from_far_end(d)))(came.wait_recv)
            total = total + self.slots[i][d].astype(F32)
        return total.astype(BF)

    def end(self, i):
        line = self.line
        pl.when(line.bottom | line.top)(self.via(i).wait_send)
        pl.when(line.low | line.high)(self.folded(i)[1].wait_send)
        for d in range(1, line.levels):
            pl.when(self.goes_direct(d))(self.direct(i, d).wait_send)


def collect_scratch(shapes):
    dma = lambda *shape: pltpu.SemaphoreType.DMA(shape)
    n, levels = len(shapes), shapes[0][0]
    scratch = [pltpu.VMEM(a, BF) for a in shapes]
    scratch += [pltpu.VMEM(a[1:], BF) for a in shapes] * 2
    return scratch + [dma(n, levels), dma(n, levels), dma(n), dma(n)]


class CoreSum:
    def __init__(self, levels, pairs, away, came, send, recv):
        self.levels, self.away, self.came = levels, away, came
        self.send, self.recv = send, recv
        x, c, z, y = place()
        self.core, self.other_core = c, device(x, 1 - c, z, y)
        self.width = away.shape[2]
        self.entries, self.turned = [], {}
        first = 0
        for a, b in pairs:
            n = a.shape[1] // 2 // levels
            for k in range(b.shape[1] // self.width):
                self.entries.append((a, b, k, first, n))
                first += n

    def product(self, i, core, mine):
        a, b, k, _, _ = self.entries[i]
        key = (id(a), mine)
        if key not in self.turned:
            half = a.shape[1] // 2
            self.turned[key] = a[:, pl.ds(pl.multiple_of(core * half, 128), half)].T
        columns = pl.ds(k * self.width, self.width)
        return jnp.dot(self.turned[key], b[:, columns], preferred_element_type=F32)

    def move(self, i):
        rows = pl.ds(self.entries[i][3], self.entries[i][4])
        return remote(
            self.away.at[:, rows],
            self.came.at[:, rows],
            self.send.at[i],
            self.recv.at[i],
            self.other_core,
        )

    def give(self, which):
        for i in which:
            result = self.product(i, 1 - self.core, False)
            _, _, _, first, n = self.entries[i]
            for level in range(self.levels):
                self.away[level, pl.ds(first, n)] = result[level * n : (level + 1) * n].astype(BF)
            self.move(i).start()

    def keep(self, which, out):
        for i in which:
            result = self.product(i, self.core, True)
            _, _, _, first, n = self.entries[i]
            rows = pl.ds(first, n)
            self.move(i).wait_recv()
            for level in range(self.levels):
                block = result[level * n : (level + 1) * n]
                out[level, rows] = (block + self.came[level, rows].astype(F32)).astype(BF)

    def end(self):
        for i in range(len(self.entries)):
            self.move(i).wait_send()


class Gathered:
    def __init__(self, ref):
        self.ref = ref
        self.shape = (ref.shape[0] * ref.shape[1], ref.shape[2])

    def __getitem__(self, at):
        return jnp.concatenate([self.ref[t, :, at[1]] for t in range(GROUP)], axis=0)


def core_sum_shape(levels, pairs, width):
    rows = sum(a.shape[1] // 2 // levels * (b.shape[1] // width) for a, b in pairs)
    return (levels, rows, width)


def core_sum_scratch(levels, pairs, width):
    shape = core_sum_shape(levels, pairs, width)
    chunks = sum(b.shape[1] // width for _, b in pairs)
    return [
        pltpu.VMEM(shape, BF),
        pltpu.VMEM(shape, BF),
        pltpu.SemaphoreType.DMA((chunks,)),
        pltpu.SemaphoreType.DMA((chunks,)),
    ]


CW = 512


def ffn_gradient_kernel(levels, n, *refs):
    pairs = [refs[2 * i : 2 * i + 2] for i in range(n)]
    out = refs[2 * n]
    total = CoreSum(levels, pairs, *refs[2 * n + 1 :])
    greet([total.other_core])
    chunks = range(len(total.entries))
    total.give(chunks)
    total.keep(chunks, out)
    total.end()


def ffn_gradient(levels, pairs, collective_id):
    operands = [a for pair in pairs for a in pair]
    return pl.pallas_call(
        functools.partial(ffn_gradient_kernel, levels, len(pairs)),
        out_shape=jax.ShapeDtypeStruct(core_sum_shape(levels, pairs, CW), BF),
        in_specs=[VMEM] * len(operands),
        out_specs=VMEM,
        scratch_shapes=core_sum_scratch(levels, pairs, CW),
        compiler_params=params(collective_id),
        name="ffn_gradient",
    )(*operands)


def norm_scale(values):
    return lax.rsqrt(jnp.mean(values * values, axis=-1, keepdims=True) + EPSILON)


def line_order(flat, levels):
    n = 2 * levels
    w = flat.shape[1] // (2 * n)
    return jnp.concatenate(
        [flat[:, (i * n + j) * w : (i * n + j + 1) * w] for j in range(n) for i in range(2)], axis=1
    )


def place_order(flat, levels):
    n = 2 * levels
    w = flat.shape[1] // (2 * n)
    return jnp.concatenate(
        [flat[:, (j * 2 + i) * w : (j * 2 + i + 1) * w] for i in range(2) for j in range(n)], axis=1
    )


def square_kernel(mode, levels, collects, second, plan, follows, *refs):
    gathers = mode != "last"
    refs = list(refs)
    take = lambda n: [refs.pop(0) for _ in range(n)]
    part_ref = take(1)[0]
    rows_in = take(2 if mode in ("backward", "last") else 1)
    part2_ref, rows2_ref = take(2) if second else (None, None)
    pair_in, ready = take(2 * min(collects, 1)), take(max(collects - 1, 0))
    slab_ref = take(1)[0] if plan else None
    left_ref = take(1)[0] if follows else None
    kept_ref = take(1)[0] if gathers else None
    kept2_ref = take(1)[0] if second else None
    all_ref = take(1)[0] if gathers else None
    collect_out = take(collects) if gathers else None
    follow_out = take(1)[0] if follows else None
    plan_out = take(len(plan.arrays)) if plan else None
    if mode == "last":
        kept_ref, qkv_ref, sum_ref = take(3)
    scatter_refs = take(6)
    scatter2_refs = take(6) if second else None
    if gathers:
        ag_send, ag_recv = take(2)
    line = Line(levels)
    product = collect = None
    if collects:
        held = take(1)[0]
        slots, folds, relays = take(collects), take(collects), take(collects)
        collect = Collect(line, [held] + ready, slots, folds, relays, *take(4))
        product = CoreSum(levels, [pair_in], *take(4))
    follow = CoreSum(levels, [(left_ref, Gathered(all_ref))], *take(4)) if follows else None
    if plan:
        plan.bind([slab_ref, qkv_ref, sum_ref, kept_ref], plan_out, *take(3))
    x, c, z, y = place()
    me, at_x, at_y, at_xy = x * 2 + y, (1 - x) * 2 + y, x * 2 + 1 - y, (1 - x) * 2 + 1 - y
    to_x, to_y = device(1 - x, c, z, y), device(x, c, z, 1 - y)
    partners = [to_x, to_y]
    if collect:
        partners += line.partners + [line.other_core]
    greet(partners, plan)
    if collect:
        collect.clear()

    def finish_side():
        if collect and gathers:
            for i in range(collects):
                collect_out[i][...] = collect.total(i)
        elif collect:
            sum_ref[...] = collect.total(1)
            plan.start([2])
            total = collect.total(0)
            n = qkv_ref.shape[2]
            for t in range(GROUP):
                qkv_ref[0, t] = total[t * n : (t + 1) * n]
            plan.start([1])
        if collect:
            for i in range(collects):
                collect.end(i)
            product.end()
        if follow:
            follow.end()
        if plan:
            plan.wait()

    rows = rows_in[0].shape[0]
    half = rows // 2
    low, high = pl.ds(0, half), pl.ds(half, half)
    copies = []
    if gathers:
        x_low, y_high, x_high, y_low = [
            remote(all_ref.at[me, part], all_ref.at[me, part], ag_send.at[i], ag_recv.at[i], to)
            for i, (part, to) in enumerate([(low, to_x), (high, to_y), (high, to_x), (low, to_y)])
        ]
        there = all_ref.at[at_x, low]
        on_y = remote(there, there, ag_send.at[4], ag_recv.at[4], to_y)
        there = all_ref.at[at_y, high]
        on_x = remote(there, there, ag_send.at[5], ag_recv.at[5], to_x)
    class Scatter:
        def __init__(self, part_ref, diag, sums, from_x, from_y, send, recv):
            self.part_ref, self.diag, self.sums = part_ref, diag, sums
            self.from_x, self.from_y = from_x, from_y
            ends = [
                (part_ref.at[at_xy, low], diag.at[0], to_x),
                (part_ref.at[at_xy, high], diag.at[1], to_y),
                (part_ref.at[at_x, low], from_x.at[low], to_x),
                (part_ref.at[at_y, high], from_y.at[high], to_y),
                (sums.at[0], from_x.at[high], to_x),
                (sums.at[1], from_y.at[low], to_y),
            ]
            self.copies = [
                remote(src, dst, send.at[i], recv.at[i], to) for i, (src, dst, to) in enumerate(ends)
            ]

        def start(self):
            for copy in self.copies[:4]:
                copy.start()

        def relay(self):
            x_diag, y_diag, _, _, x_two, y_two = self.copies
            y_diag.wait_recv()
            self.sums[0] = (
                self.part_ref[at_x, high].astype(F32) + self.diag[1].astype(F32)
            ).astype(BF)
            x_two.start()
            x_diag.wait_recv()
            self.sums[1] = (
                self.part_ref[at_y, low].astype(F32) + self.diag[0].astype(F32)
            ).astype(BF)
            y_two.start()

        def wait_low(self):
            self.copies[2].wait_recv()
            self.copies[5].wait_recv()

        def wait_high(self):
            self.copies[4].wait_recv()
            self.copies[3].wait_recv()

        def total(self, part):
            return (
                self.part_ref[me, part].astype(F32)
                + self.from_x[part].astype(F32)
                + self.from_y[part].astype(F32)
            )

    scatter = Scatter(part_ref, *scatter_refs)
    scatter.start()
    if plan:
        plan.start([0])
    for i in range(1, collects):
        collect.start(i)
    if second:
        scatter2 = Scatter(part2_ref, *scatter2_refs)
        scatter2.start()
    if product:
        product.give([0])
    scatter.relay()
    copies += scatter.copies
    if product:
        product.keep([0], held)
        collect.start(0)
        for i in range(1, collects):
            collect.relay(i)

    def own_step(part):
        total = scatter.total(part)
        if mode == "forward":
            values = rows_in[0][part] + total
            kept_ref[part] = values
            all_ref[me, part] = line_order((values * norm_scale(values)).astype(BF), levels)
        else:
            total = place_order(total, levels)
            upstream, values = rows_in[0][part], rows_in[1][part]
            scale = norm_scale(values)
            norm = values * scale
            result = upstream + scale * (
                total - norm * jnp.mean(total * norm, axis=-1, keepdims=True)
            )
            kept_ref[part] = result.astype(kept_ref.dtype)
            if gathers:
                all_ref[me, part] = result.astype(BF)

    scatter.wait_low()
    own_step(low)
    if gathers:
        x_low.start()
        y_low.start()
    scatter.wait_high()
    own_step(high)
    if mode == "last":
        plan.start([3])

    def finish_second():
        scatter2.relay()
        scatter2.wait_low()
        scatter2.wait_high()
        kept2_ref[...] = (rows2_ref[...] + scatter2.total(slice(None))).astype(BF)
        copies.extend(scatter2.copies)

    if gathers:
        y_high.start()
        x_high.start()
        x_low.wait_recv()
        on_y.start()
        y_high.wait_recv()
        on_x.start()
        if collect:
            collect.relay(0)
        x_high.wait_recv()
        y_low.wait_recv()
        on_y.wait_recv()
        on_x.wait_recv()
        copies += [x_low, y_high, x_high, y_low, on_y, on_x]
    if follow:
        chunks = range(len(follow.entries))
        follow.give(chunks)
        follow.keep(chunks, follow_out)
    if collect and not gathers:
        collect.relay(0)
    if second:
        finish_second()
    for copy in copies:
        copy.wait_send()
    finish_side()


def square(
    mode, levels, parts, rows_in, collective_id, collect=(), ready=(), second=(), slab=None, left=None
):
    rows, width = rows_in[0].shape
    gathers = mode != "last"
    dma = lambda *shape: pltpu.SemaphoreType.DMA(shape)
    like = lambda kind: jax.ShapeDtypeStruct((rows, width), kind)
    for_scatter = [pltpu.VMEM((2, rows // 2, width), BF)] * 2
    for_scatter += [pltpu.VMEM((rows, width), BF)] * 2 + [dma(6), dma(6)]
    plan = None
    if mode == "last":
        n = collect[1].shape[1]
        qkv = jax.ShapeDtypeStruct((1, GROUP, collect[0].shape[1] // 2 // levels // GROUP, n), BF)
        out = jax.ShapeDtypeStruct(ready[0].shape[1:], BF)
        plan = Exchange(levels, [slab, qkv], [out], tokens=[like(BF)], back=True)
    operands = [parts] + list(rows_in) + list(second)
    operands += list(collect) + list(ready)
    in_specs = [VMEM] * len(operands)
    out_shape, scratch = [], []
    if mode == "last":
        scratch += [pltpu.VMEM(a.shape, BF) for a in (like(BF), qkv, out)]
    else:
        out_shape.append(like(F32))
    scratch += for_scatter
    if second:
        out_shape.append(like(BF))
        scratch += for_scatter
    if gathers:
        out_shape.append(jax.ShapeDtypeStruct((GROUP, rows, width), BF))
        scratch += [dma(6), dma(6)]
    out_specs = [VMEM] * len(out_shape)
    collects = 0
    if collect:
        shape = core_sum_shape(levels, [collect], collect[1].shape[1])
        shapes = [shape] + [a.shape for a in ready]
        collects = len(shapes)
        if gathers:
            out_specs += [VMEM] * collects
            out_shape += [jax.ShapeDtypeStruct(a[1:], BF) for a in shapes]
        scratch += [pltpu.VMEM(shape, BF)] + collect_scratch(shapes)
        scratch += core_sum_scratch(levels, [collect], shape[2])
    if left is not None:
        pairs = [(left, jax.ShapeDtypeStruct((GROUP * rows, width), BF))]
        operands.append(left)
        in_specs.append(VMEM)
        out_specs.append(VMEM)
        out_shape.append(jax.ShapeDtypeStruct(core_sum_shape(levels, pairs, CW), BF))
        scratch += core_sum_scratch(levels, pairs, CW)
    if plan:
        operands.append(slab)
        in_specs.append(ANY)
        out_specs += [ANY] * len(plan.arrays)
        out_shape += plan.out_shape
        scratch += plan.scratch
    return pl.pallas_call(
        functools.partial(
            square_kernel, mode, levels, collects, bool(second), plan, left is not None
        ),
        out_shape=out_shape,
        in_specs=in_specs,
        out_specs=out_specs,
        scratch_shapes=scratch,
        compiler_params=params(collective_id),
        name="square_" + mode,
    )(*operands)


PIECES = 4


def piece_rows(rows):
    return [pl.ds(i * (rows // PIECES), rows // PIECES) for i in range(PIECES)]


def dot_nt(a, b):
    return lax.dot_general(a, b, (((1,), (1,)), ((), ())), preferred_element_type=F32)


def dot_tn(a, b):
    return lax.dot_general(a, b, (((0,), (0,)), ((), ())), preferred_element_type=F32)


def two_heads(block, j):
    a = block[:, 2 * j * HD : (2 * j + 1) * HD]
    b = block[:, (2 * j + 1) * HD : (2 * j + 2) * HD]
    return jnp.concatenate([a, b], axis=0)


def visible_keys(z, level, span, row_segs, key_segs):
    rows = lax.broadcasted_iota(jnp.int32, (span, span), 0)
    cols = lax.broadcasted_iota(jnp.int32, (span, span), 1)
    mask = (row_segs == key_segs) & ((cols <= rows) | (level < z))
    return jnp.concatenate([mask, mask], axis=0)


def turn(block, cosine, sine):
    a, b = block[:, : HD // 2], block[:, HD // 2 :]
    return jnp.concatenate([a * cosine - b * sine, b * cosine + a * sine], axis=1)


def attend_kernel(planes, *refs):
    normed_ref, weight_ref, cos_ref, sin_ref, row_ref, key_ref = refs[:6]
    q_ref, kv_ref, out_ref, lse_ref = refs[6:10]
    send, recv = refs[10:]
    levels, span = kv_ref.shape[:2]
    x, c, z, y = place()
    up, down = chain(x, c, z, y, planes)
    here = level_of(c, z, planes)
    top = levels - 1
    scaling = 1.0 / math.sqrt(HD)
    barrier = pltpu.get_barrier_semaphore()

    @pl.when(here > 0)
    def _():
        pl.semaphore_signal(barrier, inc=1, device_id=down, device_id_type=MESH)

    cosine, sine = cos_ref[...], sin_ref[...]
    heads = lambda flat, n: [turn(flat[:, j * HD : (j + 1) * HD], cosine, sine) for j in range(n)]
    wide = q_ref.shape[1]
    own = jnp.dot(normed_ref[...], weight_ref[:, wide:], preferred_element_type=F32)
    half = own.shape[1] // 2
    kv_ref[here] = jnp.concatenate(heads(own[:, :half], 2) + [own[:, half:]], axis=1).astype(BF)

    def hop(distance):
        block = kv_ref.at[lax.rem(here - distance + levels, levels)]
        return remote(block, block, send.at[distance], recv.at[distance], up)

    @pl.when(here < top)
    def _():
        pl.semaphore_wait(barrier, 1)
        hop(0).start()

    own = jnp.dot(normed_ref[...], weight_ref[:, :wide], preferred_element_type=F32)
    q_ref[...] = jnp.concatenate(heads(own, 4), axis=1).astype(BF)
    queries = [two_heads(q_ref[...], j) for j in range(2)]

    def step(distance, carry):
        level = here - distance

        @pl.when(distance > 0)
        def _():
            block = kv_ref.at[level]
            remote(block, block, send.at[distance - 1], recv.at[distance - 1], up).wait_recv()

            @pl.when(here < top)
            def _():
                hop(distance).start()

        block = kv_ref[level]
        mask = visible_keys(here, level, span, row_ref[...], key_ref[level])
        after = []
        for j in range(2):
            top_old, total, accum = carry[3 * j : 3 * j + 3]
            keys = block[:, j * HD : (j + 1) * HD]
            values = block[:, (2 + j) * HD : (3 + j) * HD]
            scores = dot_nt(queries[j], keys) * scaling
            scores = jnp.where(mask, scores, NEGATIVE)
            new = jnp.maximum(top_old, jnp.max(scores, axis=-1, keepdims=True))
            scale = jnp.exp(top_old - new)
            weights = jnp.where(mask, jnp.exp(scores - new), 0.0)
            total = total * scale + jnp.sum(weights, axis=-1, keepdims=True)
            accum = accum * scale + jnp.dot(weights.astype(BF), values, preferred_element_type=F32)
            after += [new, total, accum]
        return tuple(after)

    start = (
        jnp.full((2 * span, 1), NEGATIVE, F32),
        jnp.zeros((2 * span, 1), F32),
        jnp.zeros((2 * span, HD), F32),
    )
    done = lax.fori_loop(0, here + 1, step, start + start)
    outs, lses = [], []
    for j in range(2):
        top_all, total, accum = done[3 * j : 3 * j + 3]
        result = (accum / total).astype(BF)
        lse = jnp.broadcast_to(top_all + jnp.log(total), (2 * span, 32))
        outs += [result[:span], result[span:]]
        lses += [lse[:span], lse[span:]]
    out_ref[...] = jnp.concatenate(outs, axis=1)
    lse_ref[...] = jnp.concatenate(lses, axis=1)

    @pl.when(here < top)
    def _():
        def sent(distance, nothing):
            hop(distance).wait_send()
            return nothing

        lax.fori_loop(0, here + 1, sent, 0)


def attend(operands, planes, collective_id):
    normed, weight = operands[:2]
    rows, levels = normed.shape[0], planes // 2
    wide = weight.shape[1] // 2
    shape = jax.ShapeDtypeStruct
    return pl.pallas_call(
        functools.partial(attend_kernel, planes),
        out_shape=[
            shape((rows, wide), BF),
            shape((levels, rows, wide), BF),
            shape((rows, wide), BF),
            shape((rows, 128), F32),
        ],
        in_specs=[VMEM] * len(operands),
        out_specs=[VMEM] * 4,
        scratch_shapes=[pltpu.SemaphoreType.DMA((levels,)), pltpu.SemaphoreType.DMA((levels,))],
        compiler_params=params(collective_id),
        name="attend",
    )(*operands)


def turn_back(block, cosine, sine):
    a, b = block[:, : HD // 2], block[:, HD // 2 :]
    return jnp.concatenate([a * cosine + b * sine, b * cosine - a * sine], axis=1)


def attend_back_kernel(planes, plan, *refs):
    refs = list(refs)
    take = lambda n: [refs.pop(0) for _ in range(n)]
    q_ref, kv_ref, row_ref, key_ref, out_ref, lse_ref, back_ref, cos_ref, sin_ref, mid_ref = take(10)
    side_in = take(len(plan.arrays) if plan else 0)
    dqkv_ref, dout_ref = take(2)
    side_out = take(len(plan.arrays) if plan else 0)
    part, came, sums, heads_q, heads_back, lse4, delta4, dq4, send, recv = take(10)
    own, away, came_out, out_send, out_recv = take(5)
    levels = kv_ref.shape[0]
    x, c, z, y = place()
    up, down = chain(x, c, z, y, planes)
    other_core = device(x, 1 - c, z, y)
    z = level_of(c, z, planes)
    top = levels - 1
    span = q_ref.shape[0]
    scaling = 1.0 / math.sqrt(HD)
    pieces = piece_rows(span)
    barrier = pltpu.get_barrier_semaphore()
    pl.semaphore_signal(barrier, inc=1, device_id=other_core, device_id_type=MESH)

    @pl.when(z < top)
    def _():
        pl.semaphore_signal(barrier, inc=1, device_id=up, device_id_type=MESH)

    expected = 1 + jnp.minimum(z, 1)
    if plan:
        plan.bind(side_in, side_out, *refs)
        expected = expected + plan.greet(barrier)
    pl.semaphore_wait(barrier, expected)
    if plan:
        plan.start()

    def hop(block, piece, source):
        rows = pieces[piece]
        return remote(
            source.at[block, rows],
            came.at[block, rows],
            send.at[block, piece],
            recv.at[block, piece],
            down,
        )

    lse_all = lse_ref[...]
    for j in range(2):
        back = two_heads(back_ref[...], j)
        heads_q[j] = two_heads(q_ref[...], j)
        heads_back[j] = back
        lse4[j] = jnp.concatenate(
            [lse_all[:, 64 * j : 64 * j + 1], lse_all[:, 64 * j + 32 : 64 * j + 33]], axis=0
        )
        out = two_heads(out_ref[...], j)
        delta4[j] = jnp.sum(back.astype(F32) * out.astype(F32), axis=-1, keepdims=True)
        dq4[j] = jnp.zeros((2 * span, HD), F32)

    def one_level(level, nothing):
        block = kv_ref[level]
        mask = visible_keys(z, level, span, row_ref[...], key_ref[level])
        dks, dvs = [], []
        for j in range(2):
            keys = block[:, j * HD : (j + 1) * HD]
            values = block[:, (2 + j) * HD : (3 + j) * HD]
            queries, back = heads_q[j], heads_back[j]
            scores = dot_nt(queries, keys) * scaling
            probs = jnp.where(mask, jnp.exp(scores - lse4[j]), 0.0)
            dprobs = dot_nt(back, values)
            dscores = (probs * (dprobs - delta4[j]) * scaling).astype(BF)
            dq4[j] += jnp.dot(dscores, keys, preferred_element_type=F32)
            dks.append(dot_tn(dscores, queries).astype(BF))
            dvs.append(dot_tn(probs.astype(BF), back).astype(BF))
        part[level] = jnp.concatenate(dks + dvs, axis=1)

        @pl.when((z == top) & (level < top))
        def _():
            for piece in range(PIECES):
                hop(level, piece, part).start()

        return nothing

    lax.fori_loop(0, z + 1, one_level, 0)

    rb = own.shape[1]
    wide = own.shape[2]
    for k in range(wide // CW):
        columns = pl.ds(k * CW, CW)
        product = dot_tn(out_ref[...], mid_ref[:, columns])
        for level in range(planes):
            first = product[2 * level * rb : (2 * level + 1) * rb]
            second = product[(2 * level + 1) * rb : (2 * level + 2) * rb]
            own[level, :, columns] = jnp.where(c == 0, first, second)
            away[level, :, columns] = jnp.where(c == 0, second, first).astype(BF)
    cross = remote(away, came_out, out_send.at[0], out_recv.at[0], other_core)
    cross.start()

    heads = []
    for j in range(2):
        both = dq4[j]
        heads += [
            turn_back(both[:span], cos_ref[...], sin_ref[...]),
            turn_back(both[span:], cos_ref[...], sin_ref[...]),
        ]
    dqkv_ref[:, : 4 * HD] = jnp.concatenate(heads, axis=1).astype(BF)

    def store(total, rows):
        cosine, sine = cos_ref[rows, :], sin_ref[rows, :]
        heads = [turn_back(total[:, j * HD : (j + 1) * HD], cosine, sine) for j in range(2)]
        dqkv_ref[rows, 4 * HD :] = jnp.concatenate(heads + [total[:, 2 * HD :]], axis=1).astype(BF)

    @pl.when(z == top)
    def _():
        for piece in range(PIECES):
            rows = pieces[piece]
            store(part[top, rows].astype(F32), rows)
        for block in range(top):
            for piece in range(PIECES):
                hop(block, piece, part).wait_send()

    @pl.when(z < top)
    def _():
        for block in range(top):

            @pl.when(block < z)
            def _(block=block):
                for piece in range(PIECES):
                    rows = pieces[piece]
                    hop(block, piece, sums).wait_recv()
                    sums[block, rows] = (
                        part[block, rows].astype(F32) + came[block, rows].astype(F32)
                    ).astype(BF)
                    hop(block, piece, sums).start()

            @pl.when(block == z)
            def _(block=block):
                for piece in range(PIECES):
                    rows = pieces[piece]
                    hop(block, piece, sums).wait_recv()
                    store(part[block, rows].astype(F32) + came[block, rows].astype(F32), rows)

        for block in range(top):

            @pl.when(block < z)
            def _(block=block):
                for piece in range(PIECES):
                    hop(block, piece, sums).wait_send()

    cross.wait_recv()
    for level in range(planes):
        dout_ref[level] = (own[level] + came_out[level].astype(F32)).astype(BF)
    cross.wait_send()
    if plan:
        plan.wait()


def attend_back(operands, rb, planes, collective_id, slabs=(), swaps=(), tokens=()):
    q, kv, mid_all = operands[0], operands[1], operands[-1]
    levels = kv.shape[0]
    rows, width = q.shape
    plan = Exchange(planes, slabs, swaps, (), tokens, True) if slabs or swaps else None
    side = plan.arrays if plan else []
    heads = (2, 2 * rows, HD)
    column = (2, 2 * rows, 1)
    dout = (planes, rb, mid_all.shape[1])
    return pl.pallas_call(
        functools.partial(attend_back_kernel, planes, plan),
        out_shape=[jax.ShapeDtypeStruct((rows, 2 * width), BF), jax.ShapeDtypeStruct(dout, BF)]
        + (plan.out_shape if plan else []),
        in_specs=[VMEM] * len(operands) + [ANY] * len(side),
        out_specs=[VMEM] * 2 + [ANY] * len(side),
        scratch_shapes=[
            pltpu.VMEM(kv.shape, BF),
            pltpu.VMEM(kv.shape, BF),
            pltpu.VMEM(kv.shape, BF),
            pltpu.VMEM(heads, BF),
            pltpu.VMEM(heads, BF),
            pltpu.VMEM(column, F32),
            pltpu.VMEM(column, F32),
            pltpu.VMEM(heads, F32),
            pltpu.SemaphoreType.DMA((levels, PIECES)),
            pltpu.SemaphoreType.DMA((levels, PIECES)),
            pltpu.VMEM(dout, F32),
            pltpu.VMEM(dout, BF),
            pltpu.VMEM(dout, BF),
            pltpu.SemaphoreType.DMA((1,)),
            pltpu.SemaphoreType.DMA((1,)),
        ]
        + (plan.scratch if plan else []),
        compiler_params=params(collective_id),
        name="attend_back",
    )(*operands, *side)


def cut_weights(levels, l, rbf, weights, gains, qkv_out, gu_out):
    query, key, value, gate, up = weights
    qw, kw, fw = query.shape[2] // GROUP, key.shape[2] // GROUP, gate.shape[2] // GROUP
    q, k, v = [(w[l].astype(F32) * gains[0][l]).astype(BF) for w in (query, key, value)]
    for t in range(GROUP):
        qkv_out[0, t] = jnp.concatenate(
            [
                q[:, t * qw : (t + 1) * qw],
                k[:, t * kw : (t + 1) * kw],
                v[:, t * kw : (t + 1) * kw],
            ],
            axis=1,
        )

    def feed_forward():
        g, u = [(w[l].astype(F32) * gains[1][l]).astype(BF) for w in (gate, up)]
        for t in range(GROUP):
            pieces = []
            for w in (g, u):
                for core in range(2):
                    for level in range(levels):
                        at = t * fw + (2 * level + core) * rbf
                        pieces.append(w[:, at : at + rbf])
            gu_out[0, t] = jnp.concatenate(pieces, axis=1)

    return feed_forward


def start_kernel(levels, layers, rbf, plan, *refs):
    refs = list(refs)
    take = lambda n: [refs.pop(0) for _ in range(n)]
    sources, gains = take(5), take(2)
    out_weight, down_weight, lanes, tokens, cotangent = take(5)
    all_ref = take(1)[0]
    spread_out = take(2)
    cuts = [take(2) for _ in range(layers - 1)]
    plan_out = take(7)
    weights = take(5)
    qkv_cut, gu_cut, normed = take(3)
    load = take(1)[0]
    plan_sems, gather_sems, spread_sems = take(3), take(3), take(6)
    loads = [pltpu.make_async_copy(a, b, load.at[i]) for i, (a, b) in enumerate(zip(sources, weights))]
    for copy in loads:
        copy.start()
    ins = [qkv_cut, gu_cut, out_weight.at[0], down_weight.at[0], lanes, tokens, cotangent]
    plan.bind(ins, plan_out, *plan_sems)
    line = Line(levels)
    greet(line.partners + [line.other_core], plan)
    spread = Spread(line, False, [plan_out[0].at[0], plan_out[2]], spread_out, *spread_sems)
    gather = Gather(normed, all_ref, *gather_sems)
    plan.start([5])
    plan.start([2, 4])
    for copy in loads:
        copy.wait()
    columns = [g[...].astype(F32).T for g in gains]
    gains = [[g[:, l : l + 1] for l in range(layers)] for g in columns]
    feed_forward = cut_weights(levels, 0, rbf, weights, gains, qkv_cut, gu_cut)
    plan.start([0])
    feed_forward()
    plan.wait([0, 2])
    spread.start()
    plan.wait([5])
    values = plan_out[5][...].astype(F32)
    normed[...] = line_order((values * norm_scale(values)).astype(BF), levels)
    gather.start()
    plan.start([1, 3])
    plan.start([6])
    for l in range(1, layers):
        cut_weights(levels, l, rbf, weights, gains, *cuts[l - 1])()
    gather.relay()
    spread.relay(others=False)
    gather.finish()
    spread.relay(ends=False)
    spread.finish()
    plan.wait([1, 3, 4, 6])


def start(levels, weights, gains, out_weight, down_weight, lanes, tokens, cotangent, collective_id):
    query, key, _, gate, _ = weights
    layers, rb, _ = query.shape
    rbf = down_weight.shape[1]
    rows, width = tokens.shape
    wide = (query.shape[2] + 2 * key.shape[2]) // GROUP
    shape = jax.ShapeDtypeStruct
    qkv_cut = shape((1, GROUP, rb, wide), BF)
    gu_cut = shape((1, GROUP, rb, 2 * gate.shape[2] // GROUP), BF)
    one = lambda a: shape(a.shape[1:], a.dtype)
    plan = Exchange(
        levels,
        [qkv_cut, gu_cut],
        [one(out_weight), one(down_weight)],
        [lanes],
        [tokens, cotangent],
    )
    spreads = [qkv_cut.shape[1:], out_weight.shape[1:]]
    out_shape = [shape((GROUP, rows, width), BF)]
    out_shape += [shape((2, levels) + a, BF) for a in spreads]
    out_shape += [qkv_cut, gu_cut] * (layers - 1) + plan.out_shape
    out_specs = [VMEM] + [ANY] * 2 + [VMEM] * (2 * layers - 2) + [ANY] * 5 + [VMEM, ANY]
    dma = lambda n: pltpu.SemaphoreType.DMA((n,))
    return pl.pallas_call(
        functools.partial(start_kernel, levels, layers, rbf, plan),
        out_shape=out_shape,
        in_specs=[ANY] * 5 + [VMEM] * 2 + [ANY] * 5,
        out_specs=out_specs,
        scratch_shapes=[pltpu.VMEM(a.shape, BF) for a in weights]
        + [pltpu.VMEM(a.shape, BF) for a in (qkv_cut, gu_cut, tokens)]
        + [dma(5)]
        + plan.scratch
        + [dma(6), dma(6), dma(1)]
        + spread_scratch(2, levels),
        compiler_params=params(collective_id, 63),
        name="start",
    )(*weights, *gains, out_weight, down_weight, lanes, tokens, cotangent)


def finish_kernel(levels, layers, *refs):
    grads = [refs[4 * l : 4 * l + 4] for l in range(layers)]
    weights, gain1, gain2, outs = (
        refs[4 * layers : 4 * layers + 5],
        refs[4 * layers + 5],
        refs[4 * layers + 6],
        refs[4 * layers + 7 :],
    )
    query, key, value, output, gate, up, down, gain1_out, gain2_out = outs
    qw, kw, fw = query.shape[2] // GROUP, key.shape[2] // GROUP, gate.shape[2] // GROUP
    rbf = down.shape[1]
    for l in range(layers):
        qkv, out, gu, dn = grads[l]

        def place_columns(target, weight, gain, pieces, total):
            raw = jnp.concatenate(pieces, axis=1).astype(F32)
            target[l] = raw * gain[l]
            dots = jnp.sum(raw * weight[l].astype(F32), axis=1, keepdims=True)
            return dots if total is None else total + dots

        total = None
        for target, weight, first, n in (
            (query, weights[0], 0, qw),
            (key, weights[1], qw, kw),
            (value, weights[2], qw + kw, kw),
        ):
            pieces = [qkv[0, t, :, first : first + n] for t in range(GROUP)]
            total = place_columns(target, weight, gain1, pieces, total)
        gain1_out[l] = total
        output[l] = out[...].astype(F32)
        total = None
        for target, weight, base in ((gate, weights[3], 0), (up, weights[4], fw)):
            pieces = []
            for t in range(GROUP):
                for level in range(levels):
                    for core in range(2):
                        at = base + (core * levels + level) * rbf
                        pieces.append(gu[at // CW, t, :, at % CW : at % CW + rbf])
            total = place_columns(target, weight, gain2, pieces, total)
        gain2_out[l] = total
        down[l] = jnp.concatenate([dn[k] for k in range(dn.shape[0])], axis=1).astype(F32)


def finish(levels, grads, weights, output_weight, down_weight, gain1, gain2):
    layers, rb, _ = output_weight.shape
    like = lambda a: jax.ShapeDtypeStruct(a.shape, F32)
    query, key, value, gate, up = weights
    column = jax.ShapeDtypeStruct((layers, rb, 1), F32)
    operands = [a for layer in grads for a in layer] + list(weights) + [gain1, gain2]
    out_shape = [like(a) for a in (query, key, value, output_weight, gate, up, down_weight)]
    return pl.pallas_call(
        functools.partial(finish_kernel, levels, layers),
        out_shape=out_shape + [column, column],
        in_specs=[VMEM] * len(operands),
        out_specs=[VMEM] * 9,
        compiler_params=params(),
        name="finish",
    )(*operands)


def feed_forward_kernel(normed, gu, down, gate, up, active, parts, gu_here, down_here, arrived):
    wide = gate.shape[1]
    halves = wide // CW
    copies = []
    for h in range(halves):
        for first in (h * CW, wide + h * CW):
            columns = pl.ds(first, CW)
            copies.append((gu.at[:, columns], gu_here.at[:, columns]))
        rows = pl.ds(h * CW, CW)
        copies.append((down.at[rows], down_here.at[rows]))
    copies = [pltpu.make_async_copy(a, b, arrived.at[i]) for i, (a, b) in enumerate(copies)]
    for copy in copies:
        copy.start()
    total = None
    for h in range(halves):
        columns = pl.ds(h * CW, CW)
        copies[3 * h].wait()
        g = jnp.dot(normed[...], gu_here[:, columns], preferred_element_type=F32)
        copies[3 * h + 1].wait()
        u = jnp.dot(
            normed[...], gu_here[:, pl.ds(wide + h * CW, CW)], preferred_element_type=F32
        )
        gate[:, columns] = g
        up[:, columns] = u
        a = (g / (1.0 + jnp.exp(-g)) * u).astype(BF)
        active[:, columns] = a
        copies[3 * h + 2].wait()
        part = jnp.dot(a, down_here[columns], preferred_element_type=F32)
        total = part if total is None else total + part
    parts[...] = total.astype(BF)


def feed_forward(normed, gu, down):
    rows, width = normed.shape
    wide = down.shape[0]
    shape = jax.ShapeDtypeStruct
    return pl.pallas_call(
        feed_forward_kernel,
        out_shape=[
            shape((rows, wide), F32),
            shape((rows, wide), F32),
            shape((rows, wide), BF),
            shape((rows, width), BF),
        ],
        in_specs=[VMEM, ANY, ANY],
        out_specs=[VMEM] * 4,
        scratch_shapes=[
            pltpu.VMEM(gu.shape, BF),
            pltpu.VMEM(down.shape, BF),
            pltpu.SemaphoreType.DMA((3 * (wide // CW),)),
        ],
        compiler_params=params(),
        name="feed_forward",
    )(normed, gu, down)


def rope_tables(positions, head_width):
    frequency = THETA ** (-(jnp.arange(head_width // 2, dtype=F32) * 2.0 / head_width))
    angles = positions.astype(F32)[..., None] * frequency
    return (jnp.cos(angles), jnp.sin(angles))


def doc_positions(segments):
    places = jnp.arange(segments.shape[1], dtype=jnp.int32)
    starts_new = jnp.concatenate(
        [jnp.ones((segments.shape[0], 1), dtype=jnp.bool_), segments[:, 1:] != segments[:, :-1]],
        axis=1,
    )
    starts = lax.cummax(jnp.where(starts_new, places[None, :], 0), axis=1)
    return places[None, :] - starts


def on_device(
    levels,
    tokens,
    segments,
    cotangent,
    query_weight,
    key_weight,
    value_weight,
    output_weight,
    attention_gain,
    gate_weight,
    up_weight,
    down_weight,
    feedforward_gain,
):
    _, rows, width = tokens.shape
    full_len = segments.shape[1]
    layers = query_weight.shape[0]
    rb = query_weight.shape[1]
    rbf = down_weight.shape[1]
    kv_width = KVH * HD
    ffn = gate_weight.shape[2]
    qw, kw, fw = width // GROUP, kv_width // GROUP, ffn // GROUP
    group_rows = GROUP * rows
    _, c, z, _ = place()
    here = level_of(c, z, levels)
    n_ctx = 2 * levels
    lines = [
        [(gx * 2 + gc) * n_ctx + gz * 2 + gy for gc in range(2) for gz in range(levels)]
        for gx in range(2)
        for gy in range(2)
    ]
    core_lines = [
        [gs * n_ctx + gz * 2 + gy for gz in range(levels)] for gs in range(4) for gy in range(2)
    ]
    def gather_line(part):
        return lax.all_gather(part, AXES, axis=0, tiled=True, axis_index_groups=lines)

    def scatter_line(total):
        return lax.psum_scatter(
            total, AXES, scatter_dimension=0, tiled=True, axis_index_groups=core_lines
        )

    def after(value, *others):
        return lax.optimization_barrier((value,) + others)[0]

    gain1 = attention_gain.astype(F32)[:, :, None]
    gain2 = feedforward_gain.astype(F32)[:, :, None]
    lanes = segments.reshape(full_len // 128, 128)
    normed, qkv0, out0, *cuts = start(
        levels,
        [query_weight, key_weight, value_weight, gate_weight, up_weight],
        [attention_gain, feedforward_gain],
        output_weight,
        down_weight,
        lanes,
        tokens.reshape(rows, width),
        cotangent.reshape(rows, width),
        1,
    )
    cuts, (_, gu_own, _, down_own, all_segments, residual, cotangent) = cuts[:-7], cuts[-7:]
    qkv_slabs, gu_slabs = [None] + cuts[0::2], [None] + cuts[1::2]
    normed = normed.reshape(group_rows, width)

    def all_ffn(gu, down):
        return gather_line(gu.reshape(GROUP * rb, 2 * fw)), gather_line(down)

    own_segments = lax.dynamic_index_in_dim(
        all_segments.reshape(4, full_len), sequence_of(z, levels), 0
    )
    first = here * group_rows
    positions = lax.dynamic_slice_in_dim(doc_positions(own_segments)[0], first, group_rows)
    cosine, sine = rope_tables(positions, HD)
    row_segs = lax.dynamic_slice_in_dim(own_segments[0], first, group_rows)[:, None]
    key_segs = own_segments.reshape(levels // 2, 1, group_rows)

    def split(parts):
        return parts.astype(BF).reshape(GROUP, rows, width)

    def in_square(mode, parts, rows_in, collective_id, **more):
        out = list(square(mode, levels, split(parts), rows_in, collective_id, **more))
        if mode != "last":
            at = 2 if "second" in more else 1
            out[at] = out[at].reshape(group_rows, width)
        return out

    dot = functools.partial(jnp.dot, preferred_element_type=F32)

    qkv_full, out_full, gu_full, down_full = [[None] * layers for _ in range(4)]
    qkv_full[0], out_full[0] = qkv0, out0
    gu_full[0], down_full[0] = all_ffn(gu_own, down_own)
    residual = residual.astype(F32)
    stored = []
    for l in range(layers):
        weight = after(qkv_full[l].reshape(width, qw + 2 * kw), normed)
        q, kv, attended, lse = attend(
            [normed, weight, cosine, sine, row_segs, key_segs], levels, 5
        )
        out_full[l] = (
            after(out_full[l], attended)
            .reshape(2, levels, rb, width)
            .transpose(1, 0, 2, 3)
            .reshape(qw, width)
        )
        middle, normed2 = in_square("forward", dot(attended, out_full[l]), [residual], 4)
        if l < layers - 1:
            _, gu_own, _, down_own, qkv_full[l + 1], out_full[l + 1], *gathered = exchange(
                levels,
                [after(qkv_slabs[l + 1], normed2), gu_slabs[l + 1]],
                [(output_weight, l + 1), (down_weight, l + 1)],
                8,
                spread=True,
                own=cotangent if l == 0 else None,
            )
            up_all = gathered[0].reshape(group_rows, width) if l == 0 else up_all
            gu_full[l + 1], down_full[l + 1] = all_ffn(gu_own, down_own)
        if l < layers - 1:
            gu = after(gu_full[l], normed2)
            gate, up, active, parts = feed_forward(normed2, gu, after(down_full[l], gu))
        else:
            gu = dot(normed2, after(gu_full[l], normed2))
            gate, up = gu[:, :fw], gu[:, fw:]
            active = (jax.nn.silu(gate) * up).astype(BF)
        stored.append((residual, normed, q, kv, attended, lse, middle, normed2, gate, up, active))
        if l < layers - 1:
            residual, normed = in_square("forward", parts, [middle], 4)

    def dot_t(a, b):
        return lax.dot_general(a, b, (((1,), (1,)), ((), ())), preferred_element_type=F32)

    upstream = cotangent.astype(F32)
    ffn_grads, attention_grads, down_grads, grads = [[None] * layers for _ in range(4)]

    def in_slabs(l):
        qkv_grad, out_grad = attention_grads[l]
        gu_grad = ffn_grads[l][0].reshape(2 * fw // CW, GROUP, rb, CW)
        qkv_grad = qkv_grad.reshape(1, GROUP, rb, qw + 2 * kw)
        return [qkv_grad, gu_grad], [out_grad]

    for l in reversed(range(layers)):
        residual, normed, q, kv, attended, lse, middle, normed2, gate, up, active = stored[l]
        if l == layers - 1:
            down_total = ffn_gradient(levels, [(active, up_all)], 13)
        down_full[l] = after(down_full[l], down_total)
        if l == layers - 1:
            block = split(dot(active, down_full[l])), middle
        dactive = dot_t(up_all, down_full[l])
        sig = jax.nn.sigmoid(gate)
        dgate = (dactive * up * sig * (1.0 + gate * (1.0 - sig))).astype(BF)
        dup = (dactive * gate * sig).astype(BF)
        dgu = jnp.concatenate([dgate, dup], axis=1)
        ffn_total = ffn_gradient(levels, [(normed2, dgu)], 16)
        ffn_grads[l] = [scatter_line(total.reshape(-1, CW)) for total in (ffn_total, down_total)]
        dnorm2 = dot_t(after(dgu, ffn_total), gu_full[l]).astype(BF)
        dmiddle, mid_all = in_square("backward", dnorm2, [upstream, middle], 10)
        back = dot_t(mid_all, out_full[l]).astype(BF)
        operands = [q, kv, row_segs, key_segs, attended, lse, back, cosine, sine, mid_all]
        if l < layers - 1:
            slabs, swaps = in_slabs(l + 1)
            moved = [block_output] if l == layers - 2 else []
            swaps = [ffn_grads[l][1]] + swaps
            dqkv, out_total, *landed = attend_back(
                operands, rb, levels, 15, slabs, swaps, moved
            )
            block_output = landed.pop() if moved else block_output
            down_grads[l] = landed.pop(len(slabs))
            grads[l + 1] = landed + [down_grads[l + 1]]
        else:
            dqkv, out_total, down_grads[l] = attend_back(
                operands, rb, levels, 6, [], [ffn_grads[l][1]]
            )
        dnorm1 = dot_t(dqkv, qkv_full[l].reshape(width, qw + 2 * kw)).astype(BF)
        collect = normed, dqkv
        if l == layers - 1:
            upstream, block_output, up_all, qkv_grad, out_grad, down_total = in_square(
                "backward",
                dnorm1,
                [dmiddle, residual],
                14,
                collect=collect,
                ready=[out_total],
                second=block,
                left=stored[l - 1][-1],
            )
        elif l > 0:
            upstream, up_all, qkv_grad, out_grad, down_total = in_square(
                "backward",
                dnorm1,
                [dmiddle, residual],
                18,
                collect=collect,
                ready=[out_total],
                left=stored[l - 1][-1],
            )
        else:
            gu_grad, qkv_grad, out_grad, tokens_grad = in_square(
                "last",
                dnorm1,
                [dmiddle, residual],
                11,
                collect=collect,
                ready=[out_total],
                slab=ffn_grads[l][0].reshape(2 * fw // CW, GROUP, rb, CW),
            )
        attention_grads[l] = [qkv_grad, out_grad]

    grads[0] = [qkv_grad, gu_grad, out_grad, down_grads[0]]
    ordered = [
        [qkv, out, gu, down.reshape(width // CW, rbf, CW)] for qkv, gu, out, down in grads
    ]
    results = finish(
        levels,
        ordered,
        [query_weight, key_weight, value_weight, gate_weight, up_weight],
        output_weight,
        down_weight,
        gain1,
        gain2,
    )
    query, key, value, output, gate, up, down, gain1_grad, gain2_grad = results
    return (
        block_output.reshape(1, rows, width),
        tokens_grad.astype(F32).reshape(1, rows, width),
        query,
        key,
        value,
        output,
        gain1_grad[:, :, 0],
        gate,
        up,
        down,
        gain2_grad[:, :, 0],
    )


def solution(mesh):
    levels = mesh.shape["ctx"] // 2
    rows3 = P(None, AXES, None)
    gains = P(None, AXES)
    return jax.shard_map(
        functools.partial(on_device, levels),
        mesh=mesh,
        in_specs=(
            P("seq", "ctx", None),
            P("seq", None),
            P("seq", "ctx", None),
            rows3,
            rows3,
            rows3,
            rows3,
            gains,
            rows3,
            rows3,
            rows3,
            gains,
        ),
        out_specs=(
            P("seq", "ctx", None),
            P("seq", "ctx", None),
            rows3,
            rows3,
            rows3,
            rows3,
            gains,
            rows3,
            rows3,
            rows3,
            gains,
        ),
        check_vma=False,
    )
```

```python
import functools
import math

import jax
import jax.numpy as jnp
from jax import lax
from jax.experimental import pallas as pl
from jax.experimental.pallas import tpu as pltpu
from jax.sharding import PartitionSpec as P

H = 16
KVH = 8
HD = 96
GROUP = 4

EPSILON = 1e-05
THETA = 100000.0
NEGATIVE = -1e30
AXES = ("seq", "ctx")
MESH = pl.DeviceIdType.MESH
ANY = pl.BlockSpec(memory_space=pltpu.HBM)
VMEM = pl.BlockSpec(memory_space=pltpu.VMEM)
BF = jnp.bfloat16
F32 = jnp.float32


def params(collective_id=None, mib=48):
    if collective_id is None:
        return pltpu.CompilerParams(vmem_limit_bytes=mib * 2**20)
    return pltpu.CompilerParams(
        collective_id=collective_id, has_side_effects=True, vmem_limit_bytes=mib * 2**20
    )


def place():
    s = lax.axis_index("seq")
    k = lax.axis_index("ctx")
    return s // 2, s % 2, k // 2, k % 2


def device(x, c, z, y):
    return (x * 2 + c, z * 2 + y)


def sequence_of(z, levels):
    return z // (levels // 4)


def level_of(c, z, levels):
    return lax.rem(z, levels // 4) * 2 + c


def home_of(x, c, z, y, levels):
    block = z * 2 + y
    level = block // GROUP
    place_z = (x * 2 + c) * (levels // 4) + level // 2
    return lax.rem(block, GROUP) // 2, lax.rem(level, 2), place_z, y


def origin_of(x, c, z, y, levels):
    s = sequence_of(z, levels)
    return s // 2, lax.rem(s, 2), 2 * level_of(c, z, levels) + x, y


def chain(x, c, z, y, levels):
    up = device(x, 1 - c, lax.rem(z + c, levels), y)
    down = device(x, 1 - c, lax.rem(z + levels - 1 + c, levels), y)
    return up, down


def remote(src, dst, send, recv, to):
    return pltpu.make_async_remote_copy(
        src_ref=src, dst_ref=dst, send_sem=send, recv_sem=recv, device_id=to, device_id_type=MESH
    )


def greet(partners, plan=None):
    barrier = pltpu.get_barrier_semaphore()
    for partner in partners:
        pl.semaphore_signal(barrier, inc=1, device_id=partner, device_id_type=MESH)
    expected = len(partners)
    if plan:
        expected = expected + plan.greet(barrier)
    pl.semaphore_wait(barrier, expected)


class Exchange:
    def __init__(self, levels, slabs=(), swaps=(), rows=(), tokens=(), back=False):
        self.levels, self.back = levels, back
        self.counts = len(slabs), len(swaps), len(rows), len(tokens)
        self.picks = {len(slabs) + i: a[1] for i, a in enumerate(swaps) if isinstance(a, tuple)}
        shapes = [jax.ShapeDtypeStruct(a.shape, a.dtype) for a in slabs]
        for a in swaps:
            shape = a[0].shape[1:] if isinstance(a, tuple) else a.shape
            shapes.append(jax.ShapeDtypeStruct(shape, BF))
        swaps = [a[0] if isinstance(a, tuple) else a for a in swaps]
        self.arrays = list(slabs) + swaps + list(rows) + list(tokens)
        shapes += [jax.ShapeDtypeStruct((4,) + a.shape, a.dtype) for a in rows]
        self.out_shape = shapes + [jax.ShapeDtypeStruct(a.shape, a.dtype) for a in tokens]
        total = 2 * (len(slabs) + len(rows)) + len(self.arrays)
        self.scratch = [
            pltpu.SemaphoreType.DMA((total,)),
            pltpu.SemaphoreType.DMA((total,)),
            pltpu.SemaphoreType.DMA((len(self.arrays),)),
        ]

    def bind(self, ins, outs, send, recv, local):
        ins = [a.at[self.picks[i]] if i in self.picks else a for i, a in enumerate(ins)]
        self.ins, self.outs = ins, outs
        self.send, self.recv, self.local = send, recv, local
        x, c, z, y = place()
        self.where = c, y
        self.others = [(1 - x, y), (x, 1 - y), (1 - x, 1 - y)]
        self.square = [device(ox, c, z, oy) for ox, oy in self.others]
        self.crossed = device(x, 1 - c, z, 1 - y)
        home = home_of(x, c, z, y, self.levels)
        origin = origin_of(x, c, z, y, self.levels)
        self.moves_away = (home[0] != x) | (home[1] != c) | (home[2] != z)
        taker, giver = (origin, home) if self.back else (home, origin)
        self.taker, self.giver = device(*taker), device(*giver)
        self.seq_others = [device(x, 1 - c, z, y), device(1 - x, 1 - c, z, y)]
        n_slab, n_swap, n_rows, n_tokens = self.counts
        me = x * 2 + y
        self.groups = [[] for _ in self.arrays]
        for i in range(n_slab):
            for j, (ox, oy) in enumerate(self.others):
                sem = 3 * i + j
                self.groups[i].append(
                    remote(
                        ins[i].at[:, ox * 2 + oy],
                        outs[i].at[:, me],
                        send.at[sem],
                        recv.at[sem],
                        self.square[j],
                    )
                )
            self.groups[i].append(
                pltpu.make_async_copy(ins[i].at[:, me], outs[i].at[:, me], local.at[i])
            )
        for i in range(n_rows):
            at = n_slab + n_swap + i
            sem = self.semaphore(at)
            mine = outs[at].at[x * 2 + c]
            for j, to in enumerate([self.square[0]] + self.seq_others):
                self.groups[at].append(
                    remote(ins[at], mine, send.at[sem + j], recv.at[sem + j], to)
                )
            self.groups[at].append(pltpu.make_async_copy(ins[at], mine, local.at[at]))
        self.moves = {n_slab + i: (self.crossed, c != y) for i in range(n_swap)}
        first = n_slab + n_swap + n_rows
        for i in range(n_tokens):
            self.moves[first + i] = self.taker, self.moves_away

    def semaphore(self, at):
        n_slab, n_swap, n_rows, _ = self.counts
        rows_before = min(max(at - n_slab - n_swap, 0), n_rows)
        return at + 2 * (n_slab + rows_before)

    def greet(self, barrier):
        c, y = self.where
        signal = functools.partial(pl.semaphore_signal, barrier, inc=1, device_id_type=MESH)
        for to in self.square:
            signal(device_id=to)
        expected = 3
        if self.counts[1]:
            expected = expected + lax.rem(c + y, 2)
            pl.when(c != y)(lambda: signal(device_id=self.crossed))
        if self.counts[2]:
            expected = expected + 2
            for to in self.seq_others:
                signal(device_id=to)
        if self.counts[3]:
            expected = expected + jnp.where(self.moves_away, 1, 0)
            pl.when(self.moves_away)(lambda: signal(device_id=self.giver))
        return expected

    def whole(self, at, to):
        sem = self.semaphore(at)
        return (
            remote(self.ins[at], self.outs[at], self.send.at[sem], self.recv.at[sem], to),
            pltpu.make_async_copy(self.ins[at], self.outs[at], self.local.at[at]),
        )

    def start(self, which=None):
        for at in range(len(self.arrays)) if which is None else which:
            for copy in self.groups[at]:
                copy.start()
            if at in self.moves:
                to, goes = self.moves[at]
                cross, stay = self.whole(at, to)
                pl.when(goes)(cross.start)
                pl.when(jnp.logical_not(goes))(stay.start)

    def wait(self, which=None):
        for at in range(len(self.arrays)) if which is None else which:
            for copy in self.groups[at]:
                copy.wait()
            if at in self.moves:
                to, goes = self.moves[at]
                cross, stay = self.whole(at, to)
                pl.when(goes)(cross.wait)
                pl.when(jnp.logical_not(goes))(stay.wait)


def exchange_kernel(plan, n_spread, gathers, *refs):
    n = len(plan.arrays)
    own_ref = all_ref = None
    if gathers:
        refs = list(refs)
        own_ref, all_ref = refs.pop(n), refs.pop(2 * n + n_spread)
    outs = refs[n : 2 * n]
    spread_out = refs[2 * n : 2 * n + n_spread]
    scratch = refs[2 * n + n_spread :]
    plan.bind(refs[:n], outs, *scratch[:3])
    barrier = pltpu.get_barrier_semaphore()
    if not n_spread:
        pl.semaphore_wait(barrier, plan.greet(barrier))
        plan.start()
        plan.wait()
        return
    swap = plan.counts[0]
    line = Line(plan.levels)
    spread = Spread(line, False, [outs[0].at[0], outs[swap]], spread_out, *scratch[3:9])
    gather = Gather(own_ref, all_ref, *scratch[9:]) if own_ref is not None else None
    greet(line.partners + [line.other_core], plan)
    rest = [at for at in range(n) if at not in (0, swap)]
    plan.start([0, swap])
    plan.start(rest)
    plan.wait([0, swap])
    spread.start()
    if gather:
        gather.start()
    spread.relay(others=False)
    plan.wait(rest)
    if gather:
        gather.relay()
        gather.finish()
    spread.relay(ends=False)
    spread.finish()


class Gather:
    def __init__(self, own, everyone, send, recv, local):
        x, c, z, y = place()
        me, at_x, at_y = x * 2 + y, (1 - x) * 2 + y, x * 2 + 1 - y
        to_x, to_y = device(1 - x, c, z, y), device(x, c, z, 1 - y)
        half = own.shape[0] // 2
        low, high = pl.ds(0, half), pl.ds(half, half)
        ends = [
            (own.at[low], everyone.at[me, low], to_x),
            (own.at[high], everyone.at[me, high], to_y),
            (own.at[high], everyone.at[me, high], to_x),
            (own.at[low], everyone.at[me, low], to_y),
            (everyone.at[at_x, low], everyone.at[at_x, low], to_y),
            (everyone.at[at_y, high], everyone.at[at_y, high], to_x),
        ]
        self.copies = [
            remote(src, dst, send.at[i], recv.at[i], to) for i, (src, dst, to) in enumerate(ends)
        ]
        self.keep = pltpu.make_async_copy(own, everyone.at[me], local.at[0])

    def start(self):
        for copy in self.copies[:4]:
            copy.start()
        self.keep.start()

    def relay(self):
        for i in (0, 1):
            self.copies[i].wait_recv()
            self.copies[4 + i].start()

    def finish(self):
        for copy in self.copies[2:]:
            copy.wait_recv()
        for copy in self.copies:
            copy.wait_send()
        self.keep.wait()


def exchange(
    levels, slabs, swaps, collective_id, rows=(), tokens=(), back=False, spread=False, own=None
):
    mib = 63 if spread else 48
    plan = Exchange(levels, slabs, swaps, rows, tokens, back)
    n = len(plan.arrays)
    spreads = [slabs[0].shape[1:], plan.out_shape[len(slabs)].shape] if spread else []
    out_shape = plan.out_shape + [
        jax.ShapeDtypeStruct((2, levels) + shape, BF) for shape in spreads
    ]
    scratch = plan.scratch + (spread_scratch(2, levels) if spread else [])
    operands = list(plan.arrays)
    if own is not None:
        operands.append(own)
        out_shape.append(jax.ShapeDtypeStruct((GROUP,) + own.shape, own.dtype))
        scratch += [pltpu.SemaphoreType.DMA((n,)) for n in (6, 6, 1)]
    return pl.pallas_call(
        functools.partial(exchange_kernel, plan, len(spreads), own is not None),
        out_shape=out_shape,
        in_specs=[ANY] * len(operands),
        out_specs=[ANY] * len(out_shape),
        scratch_shapes=scratch,
        compiler_params=params(collective_id, mib),
        name="exchange",
    )(*operands)


class Line:
    def __init__(self, levels):
        x, c, z, y = place()
        self.levels, self.c, self.z = levels, c, z
        self.ahead = [lax.rem(z + d, levels) for d in range(levels)]
        self.behind = [lax.rem(z - d + levels, levels) for d in range(levels)]
        self.device = lambda to: device(x, c, to, y)
        self.other_core = device(x, 1 - c, z, y)
        self.partners = [self.device(self.ahead[d]) for d in range(1, levels)]
        self.near = list(dict.fromkeys([2, levels - 2])) + [
            d for d in range(1, levels) if d not in (2, levels - 2)
        ]
        self.bottom, self.top = z == 0, z == levels - 1
        self.low, self.high = z == 1, z == levels - 2

    def to_far_end(self, d):
        return (self.bottom & (d == self.levels - 1)) | (self.top & (d == 1))

    def by_way_to(self, d):
        return (self.low & (d == self.levels - 2)) | (self.high & (d == 2))

    def from_far_end(self, d):
        return (self.top & (d == self.levels - 1)) | (self.bottom & (d == 1))


class Spread:
    def __init__(
        self, line, hops, sources, outs, send, recv, cross_send, cross_recv, local, onward_send
    ):
        self.hops, self.onward_send = hops, onward_send
        self.line, self.sources, self.outs = line, sources, outs
        self.send, self.recv, self.local = send, recv, local
        self.cross_send, self.cross_recv = cross_send, cross_recv
        self.count = range(len(sources))

    def to_line(self, i, d):
        line = self.line
        block = self.outs[i].at[line.c, line.z]
        to = line.device(line.ahead[d])
        return remote(self.sources[i], block, self.send.at[i, d], self.recv.at[i, d], to)

    def to_core(self, i, d):
        line = self.line
        block = self.outs[i].at[line.c, line.behind[d]]
        source = block if d else self.sources[i]
        return remote(
            source, block, self.cross_send.at[i, d], self.cross_recv.at[i, d], line.other_core
        )

    def goes_direct(self, d):
        line = self.line
        if not self.hops:
            return jnp.logical_not(line.to_far_end(d))
        to_end = (line.ahead[d] == 0) & (line.z != 1)
        to_end = to_end | ((line.ahead[d] == line.levels - 1) & (line.z != line.levels - 2))
        return jnp.logical_not(to_end)

    def onward(self, i, d):
        line = self.line
        block = self.outs[i].at[line.c, line.behind[d]]
        end = jnp.where(line.low, 0, line.levels - 1)
        slot = jnp.where(line.low, d - 1, d + 1)
        return remote(
            block, block, self.onward_send.at[i, d], self.recv.at[i, slot], line.device(end)
        )

    def passes_on(self, d):
        line = self.line
        if not self.hops:
            far = jnp.where(line.low, line.levels - 1, 0)
            return (line.low | line.high) & (line.behind[d] == far)
        up = line.high & (line.behind[d] < line.levels - 2)
        return up | (line.low & (line.behind[d] > 1))

    def keep(self, i):
        line = self.line
        return pltpu.make_async_copy(
            self.sources[i], self.outs[i].at[line.c, line.z], self.local.at[i]
        )

    def start(self):
        for i in self.count:
            for d in self.line.near:
                pl.when(self.goes_direct(d))(self.to_line(i, d).start)
            self.to_core(i, 0).start()
            self.keep(i).start()

    def relay(self, ends=True, others=True):
        line = self.line
        firsts = len(dict.fromkeys([2, line.levels - 2]))
        which = (line.near[:firsts] if ends else []) + (line.near[firsts:] if others else [])
        for i in self.count:
            for d in which:
                block = self.outs[i].at[line.c, line.behind[d]]
                remote(
                    block, block, self.send.at[i, d], self.recv.at[i, d], line.other_core
                ).wait_recv()
                pl.when(self.passes_on(d))(self.onward(i, d).start)
                self.to_core(i, d).start()

    def finish(self):
        line = self.line
        for i in self.count:
            for d in range(line.levels):
                block = self.outs[i].at[1 - line.c, line.behind[d]]
                remote(
                    block, block, self.cross_send.at[i, d], self.cross_recv.at[i, d], line.other_core
                ).wait_recv()
            for d in line.near:
                pl.when(self.goes_direct(d))(self.to_line(i, d).wait_send)
                pl.when(self.passes_on(d))(self.onward(i, d).wait_send)
            for d in range(line.levels):
                self.to_core(i, d).wait_send()
            self.keep(i).wait()


def spread_scratch(n, levels):
    dma = lambda *shape: pltpu.SemaphoreType.DMA(shape)
    return [dma(n, levels), dma(n, levels), dma(n, levels), dma(n, levels), dma(n), dma(n, levels)]


class Collect:
    def __init__(self, line, sources, slots, folds, relays, send, recv, relay_send, relay_recv):
        self.line, self.sources, self.slots = line, sources, slots
        self.folds, self.relays = folds, relays
        self.send, self.recv = send, recv
        self.relay_send, self.relay_recv = relay_send, relay_recv

    def clear(self):
        for slot in self.slots:
            for d in (1, self.line.levels - 1):

                @pl.when(self.line.from_far_end(d))
                def _(slot=slot, d=d):
                    slot[d] = jnp.zeros_like(slot[d])

    def direct(self, i, d):
        line = self.line
        return remote(
            self.sources[i].at[line.ahead[d]],
            self.slots[i].at[d],
            self.send.at[i, d],
            self.recv.at[i, d],
            line.device(line.ahead[d]),
        )

    def goes_direct(self, d):
        return jnp.logical_not(self.line.to_far_end(d) | self.line.by_way_to(d))

    def via(self, i):
        line = self.line
        far = jnp.where(line.bottom, line.levels - 1, 0)
        to = jnp.where(line.bottom, 1, line.levels - 2)
        return remote(
            self.sources[i].at[far],
            self.relays[i],
            self.relay_send.at[i],
            self.relay_recv.at[i],
            line.device(to),
        )

    def folded(self, i):
        line = self.line
        end = jnp.where(line.low, line.levels - 1, 0)
        slot = jnp.where(line.low, line.levels - 2, 2)
        return end, remote(
            self.folds[i],
            self.slots[i].at[slot],
            self.send.at[i, 0],
            self.recv.at[i, slot],
            line.device(end),
        )

    def start(self, i):
        line = self.line
        pl.when(line.bottom | line.top)(self.via(i).start)
        for d in range(1, line.levels):
            pl.when(self.goes_direct(d))(self.direct(i, d).start)

    def relay(self, i):
        line = self.line

        @pl.when(line.low | line.high)
        def _():
            end, copy = self.folded(i)
            self.via(i).wait_recv()
            self.folds[i][...] = (
                self.sources[i][end].astype(F32) + self.relays[i][...].astype(F32)
            ).astype(BF)
            copy.start()

    def total(self, i):
        line = self.line
        total = self.sources[i][line.z].astype(F32)
        for d in range(1, line.levels):
            block = self.slots[i].at[d]
            came = remote(block, block, self.send.at[i, d], self.recv.at[i, d], line.other_core)
            pl.when(jnp.logical_not(line.from_far_end(d)))(came.wait_recv)
            total = total + self.slots[i][d].astype(F32)
        return total.astype(BF)

    def end(self, i):
        line = self.line
        pl.when(line.bottom | line.top)(self.via(i).wait_send)
        pl.when(line.low | line.high)(self.folded(i)[1].wait_send)
        for d in range(1, line.levels):
            pl.when(self.goes_direct(d))(self.direct(i, d).wait_send)


def collect_scratch(shapes):
    dma = lambda *shape: pltpu.SemaphoreType.DMA(shape)
    n, levels = len(shapes), shapes[0][0]
    scratch = [pltpu.VMEM(a, BF) for a in shapes]
    scratch += [pltpu.VMEM(a[1:], BF) for a in shapes] * 2
    return scratch + [dma(n, levels), dma(n, levels), dma(n), dma(n)]


class CoreSum:
    def __init__(self, levels, pairs, away, came, send, recv):
        self.levels, self.away, self.came = levels, away, came
        self.send, self.recv = send, recv
        x, c, z, y = place()
        self.core, self.other_core = c, device(x, 1 - c, z, y)
        self.width = away.shape[2]
        self.entries, self.turned = [], {}
        first = 0
        for a, b in pairs:
            n = a.shape[1] // 2 // levels
            for k in range(b.shape[1] // self.width):
                self.entries.append((a, b, k, first, n))
                first += n

    def product(self, i, core, mine):
        a, b, k, _, _ = self.entries[i]
        key = (id(a), mine)
        if key not in self.turned:
            half = a.shape[1] // 2
            self.turned[key] = a[:, pl.ds(pl.multiple_of(core * half, 128), half)].T
        columns = pl.ds(k * self.width, self.width)
        return jnp.dot(self.turned[key], b[:, columns], preferred_element_type=F32)

    def move(self, i):
        rows = pl.ds(self.entries[i][3], self.entries[i][4])
        return remote(
            self.away.at[:, rows],
            self.came.at[:, rows],
            self.send.at[i],
            self.recv.at[i],
            self.other_core,
        )

    def give(self, which):
        for i in which:
            result = self.product(i, 1 - self.core, False)
            _, _, _, first, n = self.entries[i]
            for level in range(self.levels):
                self.away[level, pl.ds(first, n)] = result[level * n : (level + 1) * n].astype(BF)
            self.move(i).start()

    def keep(self, which, out):
        for i in which:
            result = self.product(i, self.core, True)
            _, _, _, first, n = self.entries[i]
            rows = pl.ds(first, n)
            self.move(i).wait_recv()
            for level in range(self.levels):
                block = result[level * n : (level + 1) * n]
                out[level, rows] = (block + self.came[level, rows].astype(F32)).astype(BF)

    def end(self):
        for i in range(len(self.entries)):
            self.move(i).wait_send()


class Gathered:
    def __init__(self, ref):
        self.ref = ref
        self.shape = (ref.shape[0] * ref.shape[1], ref.shape[2])

    def __getitem__(self, at):
        return jnp.concatenate([self.ref[t, :, at[1]] for t in range(GROUP)], axis=0)


def core_sum_shape(levels, pairs, width):
    rows = sum(a.shape[1] // 2 // levels * (b.shape[1] // width) for a, b in pairs)
    return (levels, rows, width)


def core_sum_scratch(levels, pairs, width):
    shape = core_sum_shape(levels, pairs, width)
    chunks = sum(b.shape[1] // width for _, b in pairs)
    return [
        pltpu.VMEM(shape, BF),
        pltpu.VMEM(shape, BF),
        pltpu.SemaphoreType.DMA((chunks,)),
        pltpu.SemaphoreType.DMA((chunks,)),
    ]


CW = 512


def ffn_gradient_kernel(levels, n, *refs):
    pairs = [refs[2 * i : 2 * i + 2] for i in range(n)]
    out = refs[2 * n]
    total = CoreSum(levels, pairs, *refs[2 * n + 1 :])
    greet([total.other_core])
    chunks = range(len(total.entries))
    total.give(chunks)
    total.keep(chunks, out)
    total.end()


def ffn_gradient(levels, pairs, collective_id):
    operands = [a for pair in pairs for a in pair]
    return pl.pallas_call(
        functools.partial(ffn_gradient_kernel, levels, len(pairs)),
        out_shape=jax.ShapeDtypeStruct(core_sum_shape(levels, pairs, CW), BF),
        in_specs=[VMEM] * len(operands),
        out_specs=VMEM,
        scratch_shapes=core_sum_scratch(levels, pairs, CW),
        compiler_params=params(collective_id),
        name="ffn_gradient",
    )(*operands)


def norm_scale(values):
    return lax.rsqrt(jnp.mean(values * values, axis=-1, keepdims=True) + EPSILON)


def line_order(flat, levels):
    n = 2 * levels
    w = flat.shape[1] // (2 * n)
    return jnp.concatenate(
        [flat[:, (i * n + j) * w : (i * n + j + 1) * w] for j in range(n) for i in range(2)], axis=1
    )


def place_order(flat, levels):
    n = 2 * levels
    w = flat.shape[1] // (2 * n)
    return jnp.concatenate(
        [flat[:, (j * 2 + i) * w : (j * 2 + i + 1) * w] for i in range(2) for j in range(n)], axis=1
    )


def square_kernel(mode, levels, collects, second, plan, follows, *refs):
    gathers = mode != "last"
    refs = list(refs)
    take = lambda n: [refs.pop(0) for _ in range(n)]
    part_ref = take(1)[0]
    rows_in = take(2 if mode in ("backward", "last") else 1)
    part2_ref, rows2_ref = take(2) if second else (None, None)
    pair_in, ready = take(2 * min(collects, 1)), take(max(collects - 1, 0))
    slab_ref = take(1)[0] if plan else None
    left_ref = take(1)[0] if follows else None
    kept_ref = take(1)[0] if gathers else None
    kept2_ref = take(1)[0] if second else None
    all_ref = take(1)[0] if gathers else None
    collect_out = take(collects) if gathers else None
    follow_out = take(1)[0] if follows else None
    plan_out = take(len(plan.arrays)) if plan else None
    if mode == "last":
        kept_ref, qkv_ref, sum_ref = take(3)
    scatter_refs = take(6)
    scatter2_refs = take(6) if second else None
    if gathers:
        ag_send, ag_recv = take(2)
    line = Line(levels)
    product = collect = None
    if collects:
        held = take(1)[0]
        slots, folds, relays = take(collects), take(collects), take(collects)
        collect = Collect(line, [held] + ready, slots, folds, relays, *take(4))
        product = CoreSum(levels, [pair_in], *take(4))
    follow = CoreSum(levels, [(left_ref, Gathered(all_ref))], *take(4)) if follows else None
    if plan:
        plan.bind([slab_ref, qkv_ref, sum_ref, kept_ref], plan_out, *take(3))
    x, c, z, y = place()
    me, at_x, at_y, at_xy = x * 2 + y, (1 - x) * 2 + y, x * 2 + 1 - y, (1 - x) * 2 + 1 - y
    to_x, to_y = device(1 - x, c, z, y), device(x, c, z, 1 - y)
    partners = [to_x, to_y]
    if collect:
        partners += line.partners + [line.other_core]
    greet(partners, plan)
    if collect:
        collect.clear()

    def finish_side():
        if collect and gathers:
            for i in range(collects):
                collect_out[i][...] = collect.total(i)
        elif collect:
            sum_ref[...] = collect.total(1)
            plan.start([2])
            total = collect.total(0)
            n = qkv_ref.shape[2]
            for t in range(GROUP):
                qkv_ref[0, t] = total[t * n : (t + 1) * n]
            plan.start([1])
        if collect:
            for i in range(collects):
                collect.end(i)
            product.end()
        if follow:
            follow.end()
        if plan:
            plan.wait()

    rows = rows_in[0].shape[0]
    half = rows // 2
    low, high = pl.ds(0, half), pl.ds(half, half)
    copies = []
    if gathers:
        x_low, y_high, x_high, y_low = [
            remote(all_ref.at[me, part], all_ref.at[me, part], ag_send.at[i], ag_recv.at[i], to)
            for i, (part, to) in enumerate([(low, to_x), (high, to_y), (high, to_x), (low, to_y)])
        ]
        there = all_ref.at[at_x, low]
        on_y = remote(there, there, ag_send.at[4], ag_recv.at[4], to_y)
        there = all_ref.at[at_y, high]
        on_x = remote(there, there, ag_send.at[5], ag_recv.at[5], to_x)
    class Scatter:
        def __init__(self, part_ref, diag, sums, from_x, from_y, send, recv):
            self.part_ref, self.diag, self.sums = part_ref, diag, sums
            self.from_x, self.from_y = from_x, from_y
            ends = [
                (part_ref.at[at_xy, low], diag.at[0], to_x),
                (part_ref.at[at_xy, high], diag.at[1], to_y),
                (part_ref.at[at_x, low], from_x.at[low], to_x),
                (part_ref.at[at_y, high], from_y.at[high], to_y),
                (sums.at[0], from_x.at[high], to_x),
                (sums.at[1], from_y.at[low], to_y),
            ]
            self.copies = [
                remote(src, dst, send.at[i], recv.at[i], to) for i, (src, dst, to) in enumerate(ends)
            ]

        def start(self):
            for copy in self.copies[:4]:
                copy.start()

        def relay(self):
            x_diag, y_diag, _, _, x_two, y_two = self.copies
            y_diag.wait_recv()
            self.sums[0] = (
                self.part_ref[at_x, high].astype(F32) + self.diag[1].astype(F32)
            ).astype(BF)
            x_two.start()
            x_diag.wait_recv()
            self.sums[1] = (
                self.part_ref[at_y, low].astype(F32) + self.diag[0].astype(F32)
            ).astype(BF)
            y_two.start()

        def wait_low(self):
            self.copies[2].wait_recv()
            self.copies[5].wait_recv()

        def wait_high(self):
            self.copies[4].wait_recv()
            self.copies[3].wait_recv()

        def total(self, part):
            return (
                self.part_ref[me, part].astype(F32)
                + self.from_x[part].astype(F32)
                + self.from_y[part].astype(F32)
            )

    scatter = Scatter(part_ref, *scatter_refs)
    scatter.start()
    if plan:
        plan.start([0])
    for i in range(1, collects):
        collect.start(i)
    if second:
        scatter2 = Scatter(part2_ref, *scatter2_refs)
        scatter2.start()
    if product:
        product.give([0])
    scatter.relay()
    copies += scatter.copies
    if product:
        product.keep([0], held)
        collect.start(0)
        for i in range(1, collects):
            collect.relay(i)

    def own_step(part):
        total = scatter.total(part)
        if mode == "forward":
            values = rows_in[0][part] + total
            kept_ref[part] = values
            all_ref[me, part] = line_order((values * norm_scale(values)).astype(BF), levels)
        else:
            total = place_order(total, levels)
            upstream, values = rows_in[0][part], rows_in[1][part]
            scale = norm_scale(values)
            norm = values * scale
            result = upstream + scale * (
                total - norm * jnp.mean(total * norm, axis=-1, keepdims=True)
            )
            kept_ref[part] = result.astype(kept_ref.dtype)
            if gathers:
                all_ref[me, part] = result.astype(BF)

    scatter.wait_low()
    own_step(low)
    if gathers:
        x_low.start()
        y_low.start()
    scatter.wait_high()
    own_step(high)
    if mode == "last":
        plan.start([3])

    def finish_second():
        scatter2.relay()
        scatter2.wait_low()
        scatter2.wait_high()
        kept2_ref[...] = (rows2_ref[...] + scatter2.total(slice(None))).astype(BF)
        copies.extend(scatter2.copies)

    if gathers:
        y_high.start()
        x_high.start()
        x_low.wait_recv()
        on_y.start()
        y_high.wait_recv()
        on_x.start()
        if collect:
            collect.relay(0)
        x_high.wait_recv()
        y_low.wait_recv()
        on_y.wait_recv()
        on_x.wait_recv()
        copies += [x_low, y_high, x_high, y_low, on_y, on_x]
    if follow:
        chunks = range(len(follow.entries))
        follow.give(chunks)
        follow.keep(chunks, follow_out)
    if collect and not gathers:
        collect.relay(0)
    if second:
        finish_second()
    for copy in copies:
        copy.wait_send()
    finish_side()


def square(
    mode, levels, parts, rows_in, collective_id, collect=(), ready=(), second=(), slab=None, left=None
):
    rows, width = rows_in[0].shape
    gathers = mode != "last"
    dma = lambda *shape: pltpu.SemaphoreType.DMA(shape)
    like = lambda kind: jax.ShapeDtypeStruct((rows, width), kind)
    for_scatter = [pltpu.VMEM((2, rows // 2, width), BF)] * 2
    for_scatter += [pltpu.VMEM((rows, width), BF)] * 2 + [dma(6), dma(6)]
    plan = None
    if mode == "last":
        n = collect[1].shape[1]
        qkv = jax.ShapeDtypeStruct((1, GROUP, collect[0].shape[1] // 2 // levels // GROUP, n), BF)
        out = jax.ShapeDtypeStruct(ready[0].shape[1:], BF)
        plan = Exchange(levels, [slab, qkv], [out], tokens=[like(BF)], back=True)
    operands = [parts] + list(rows_in) + list(second)
    operands += list(collect) + list(ready)
    in_specs = [VMEM] * len(operands)
    out_shape, scratch = [], []
    if mode == "last":
        scratch += [pltpu.VMEM(a.shape, BF) for a in (like(BF), qkv, out)]
    else:
        out_shape.append(like(F32))
    scratch += for_scatter
    if second:
        out_shape.append(like(BF))
        scratch += for_scatter
    if gathers:
        out_shape.append(jax.ShapeDtypeStruct((GROUP, rows, width), BF))
        scratch += [dma(6), dma(6)]
    out_specs = [VMEM] * len(out_shape)
    collects = 0
    if collect:
        shape = core_sum_shape(levels, [collect], collect[1].shape[1])
        shapes = [shape] + [a.shape for a in ready]
        collects = len(shapes)
        if gathers:
            out_specs += [VMEM] * collects
            out_shape += [jax.ShapeDtypeStruct(a[1:], BF) for a in shapes]
        scratch += [pltpu.VMEM(shape, BF)] + collect_scratch(shapes)
        scratch += core_sum_scratch(levels, [collect], shape[2])
    if left is not None:
        pairs = [(left, jax.ShapeDtypeStruct((GROUP * rows, width), BF))]
        operands.append(left)
        in_specs.append(VMEM)
        out_specs.append(VMEM)
        out_shape.append(jax.ShapeDtypeStruct(core_sum_shape(levels, pairs, CW), BF))
        scratch += core_sum_scratch(levels, pairs, CW)
    if plan:
        operands.append(slab)
        in_specs.append(ANY)
        out_specs += [ANY] * len(plan.arrays)
        out_shape += plan.out_shape
        scratch += plan.scratch
    return pl.pallas_call(
        functools.partial(
            square_kernel, mode, levels, collects, bool(second), plan, left is not None
        ),
        out_shape=out_shape,
        in_specs=in_specs,
        out_specs=out_specs,
        scratch_shapes=scratch,
        compiler_params=params(collective_id),
        name="square_" + mode,
    )(*operands)


PIECES = 4


def piece_rows(rows):
    return [pl.ds(i * (rows // PIECES), rows // PIECES) for i in range(PIECES)]


def dot_nt(a, b):
    return lax.dot_general(a, b, (((1,), (1,)), ((), ())), preferred_element_type=F32)


def dot_tn(a, b):
    return lax.dot_general(a, b, (((0,), (0,)), ((), ())), preferred_element_type=F32)


def two_heads(block, j):
    a = block[:, 2 * j * HD : (2 * j + 1) * HD]
    b = block[:, (2 * j + 1) * HD : (2 * j + 2) * HD]
    return jnp.concatenate([a, b], axis=0)


def visible_keys(z, level, span, row_segs, key_segs):
    rows = lax.broadcasted_iota(jnp.int32, (span, span), 0)
    cols = lax.broadcasted_iota(jnp.int32, (span, span), 1)
    mask = (row_segs == key_segs) & ((cols <= rows) | (level < z))
    return jnp.concatenate([mask, mask], axis=0)


def turn(block, cosine, sine):
    a, b = block[:, : HD // 2], block[:, HD // 2 :]
    return jnp.concatenate([a * cosine - b * sine, b * cosine + a * sine], axis=1)


def attend_kernel(planes, *refs):
    normed_ref, weight_ref, cos_ref, sin_ref, row_ref, key_ref = refs[:6]
    q_ref, kv_ref, out_ref, lse_ref = refs[6:10]
    send, recv = refs[10:]
    levels, span = kv_ref.shape[:2]
    x, c, z, y = place()
    up, down = chain(x, c, z, y, planes)
    here = level_of(c, z, planes)
    top = levels - 1
    scaling = 1.0 / math.sqrt(HD)
    barrier = pltpu.get_barrier_semaphore()

    @pl.when(here > 0)
    def _():
        pl.semaphore_signal(barrier, inc=1, device_id=down, device_id_type=MESH)

    cosine, sine = cos_ref[...], sin_ref[...]
    heads = lambda flat, n: [turn(flat[:, j * HD : (j + 1) * HD], cosine, sine) for j in range(n)]
    wide = q_ref.shape[1]
    own = jnp.dot(normed_ref[...], weight_ref[:, wide:], preferred_element_type=F32)
    half = own.shape[1] // 2
    kv_ref[here] = jnp.concatenate(heads(own[:, :half], 2) + [own[:, half:]], axis=1).astype(BF)

    def hop(distance):
        block = kv_ref.at[lax.rem(here - distance + levels, levels)]
        return remote(block, block, send.at[distance], recv.at[distance], up)

    @pl.when(here < top)
    def _():
        pl.semaphore_wait(barrier, 1)
        hop(0).start()

    own = jnp.dot(normed_ref[...], weight_ref[:, :wide], preferred_element_type=F32)
    q_ref[...] = jnp.concatenate(heads(own, 4), axis=1).astype(BF)
    queries = [two_heads(q_ref[...], j) for j in range(2)]

    def step(distance, carry):
        level = here - distance

        @pl.when(distance > 0)
        def _():
            block = kv_ref.at[level]
            remote(block, block, send.at[distance - 1], recv.at[distance - 1], up).wait_recv()

            @pl.when(here < top)
            def _():
                hop(distance).start()

        block = kv_ref[level]
        mask = visible_keys(here, level, span, row_ref[...], key_ref[level])
        after = []
        for j in range(2):
            top_old, total, accum = carry[3 * j : 3 * j + 3]
            keys = block[:, j * HD : (j + 1) * HD]
            values = block[:, (2 + j) * HD : (3 + j) * HD]
            scores = dot_nt(queries[j], keys) * scaling
            scores = jnp.where(mask, scores, NEGATIVE)
            new = jnp.maximum(top_old, jnp.max(scores, axis=-1, keepdims=True))
            scale = jnp.exp(top_old - new)
            weights = jnp.where(mask, jnp.exp(scores - new), 0.0)
            total = total * scale + jnp.sum(weights, axis=-1, keepdims=True)
            accum = accum * scale + jnp.dot(weights.astype(BF), values, preferred_element_type=F32)
            after += [new, total, accum]
        return tuple(after)

    start = (
        jnp.full((2 * span, 1), NEGATIVE, F32),
        jnp.zeros((2 * span, 1), F32),
        jnp.zeros((2 * span, HD), F32),
    )
    done = lax.fori_loop(0, here + 1, step, start + start)
    outs, lses = [], []
    for j in range(2):
        top_all, total, accum = done[3 * j : 3 * j + 3]
        result = (accum / total).astype(BF)
        lse = jnp.broadcast_to(top_all + jnp.log(total), (2 * span, 32))
        outs += [result[:span], result[span:]]
        lses += [lse[:span], lse[span:]]
    out_ref[...] = jnp.concatenate(outs, axis=1)
    lse_ref[...] = jnp.concatenate(lses, axis=1)

    @pl.when(here < top)
    def _():
        def sent(distance, nothing):
            hop(distance).wait_send()
            return nothing

        lax.fori_loop(0, here + 1, sent, 0)


def attend(operands, planes, collective_id):
    normed, weight = operands[:2]
    rows, levels = normed.shape[0], planes // 2
    wide = weight.shape[1] // 2
    shape = jax.ShapeDtypeStruct
    return pl.pallas_call(
        functools.partial(attend_kernel, planes),
        out_shape=[
            shape((rows, wide), BF),
            shape((levels, rows, wide), BF),
            shape((rows, wide), BF),
            shape((rows, 128), F32),
        ],
        in_specs=[VMEM] * len(operands),
        out_specs=[VMEM] * 4,
        scratch_shapes=[pltpu.SemaphoreType.DMA((levels,)), pltpu.SemaphoreType.DMA((levels,))],
        compiler_params=params(collective_id),
        name="attend",
    )(*operands)


def turn_back(block, cosine, sine):
    a, b = block[:, : HD // 2], block[:, HD // 2 :]
    return jnp.concatenate([a * cosine + b * sine, b * cosine - a * sine], axis=1)


def attend_back_kernel(planes, plan, *refs):
    refs = list(refs)
    take = lambda n: [refs.pop(0) for _ in range(n)]
    q_ref, kv_ref, row_ref, key_ref, out_ref, lse_ref, back_ref, cos_ref, sin_ref, mid_ref = take(10)
    side_in = take(len(plan.arrays) if plan else 0)
    dqkv_ref, dout_ref = take(2)
    side_out = take(len(plan.arrays) if plan else 0)
    part, came, sums, heads_q, heads_back, lse4, delta4, dq4, send, recv = take(10)
    own, away, came_out, out_send, out_recv = take(5)
    levels = kv_ref.shape[0]
    x, c, z, y = place()
    up, down = chain(x, c, z, y, planes)
    other_core = device(x, 1 - c, z, y)
    z = level_of(c, z, planes)
    top = levels - 1
    span = q_ref.shape[0]
    scaling = 1.0 / math.sqrt(HD)
    pieces = piece_rows(span)
    barrier = pltpu.get_barrier_semaphore()
    pl.semaphore_signal(barrier, inc=1, device_id=other_core, device_id_type=MESH)

    @pl.when(z < top)
    def _():
        pl.semaphore_signal(barrier, inc=1, device_id=up, device_id_type=MESH)

    expected = 1 + jnp.minimum(z, 1)
    if plan:
        plan.bind(side_in, side_out, *refs)
        expected = expected + plan.greet(barrier)
    pl.semaphore_wait(barrier, expected)
    if plan:
        plan.start()

    def hop(block, piece, source):
        rows = pieces[piece]
        return remote(
            source.at[block, rows],
            came.at[block, rows],
            send.at[block, piece],
            recv.at[block, piece],
            down,
        )

    lse_all = lse_ref[...]
    for j in range(2):
        back = two_heads(back_ref[...], j)
        heads_q[j] = two_heads(q_ref[...], j)
        heads_back[j] = back
        lse4[j] = jnp.concatenate(
            [lse_all[:, 64 * j : 64 * j + 1], lse_all[:, 64 * j + 32 : 64 * j + 33]], axis=0
        )
        out = two_heads(out_ref[...], j)
        delta4[j] = jnp.sum(back.astype(F32) * out.astype(F32), axis=-1, keepdims=True)
        dq4[j] = jnp.zeros((2 * span, HD), F32)

    def one_level(level, nothing):
        block = kv_ref[level]
        mask = visible_keys(z, level, span, row_ref[...], key_ref[level])
        dks, dvs = [], []
        for j in range(2):
            keys = block[:, j * HD : (j + 1) * HD]
            values = block[:, (2 + j) * HD : (3 + j) * HD]
            queries, back = heads_q[j], heads_back[j]
            scores = dot_nt(queries, keys) * scaling
            probs = jnp.where(mask, jnp.exp(scores - lse4[j]), 0.0)
            dprobs = dot_nt(back, values)
            dscores = (probs * (dprobs - delta4[j]) * scaling).astype(BF)
            dq4[j] += jnp.dot(dscores, keys, preferred_element_type=F32)
            dks.append(dot_tn(dscores, queries).astype(BF))
            dvs.append(dot_tn(probs.astype(BF), back).astype(BF))
        part[level] = jnp.concatenate(dks + dvs, axis=1)

        @pl.when((z == top) & (level < top))
        def _():
            for piece in range(PIECES):
                hop(level, piece, part).start()

        return nothing

    lax.fori_loop(0, z + 1, one_level, 0)

    rb = own.shape[1]
    wide = own.shape[2]
    for k in range(wide // CW):
        columns = pl.ds(k * CW, CW)
        product = dot_tn(out_ref[...], mid_ref[:, columns])
        for level in range(planes):
            first = product[2 * level * rb : (2 * level + 1) * rb]
            second = product[(2 * level + 1) * rb : (2 * level + 2) * rb]
            own[level, :, columns] = jnp.where(c == 0, first, second)
            away[level, :, columns] = jnp.where(c == 0, second, first).astype(BF)
    cross = remote(away, came_out, out_send.at[0], out_recv.at[0], other_core)
    cross.start()

    heads = []
    for j in range(2):
        both = dq4[j]
        heads += [
            turn_back(both[:span], cos_ref[...], sin_ref[...]),
            turn_back(both[span:], cos_ref[...], sin_ref[...]),
        ]
    dqkv_ref[:, : 4 * HD] = jnp.concatenate(heads, axis=1).astype(BF)

    def store(total, rows):
        cosine, sine = cos_ref[rows, :], sin_ref[rows, :]
        heads = [turn_back(total[:, j * HD : (j + 1) * HD], cosine, sine) for j in range(2)]
        dqkv_ref[rows, 4 * HD :] = jnp.concatenate(heads + [total[:, 2 * HD :]], axis=1).astype(BF)

    @pl.when(z == top)
    def _():
        for piece in range(PIECES):
            rows = pieces[piece]
            store(part[top, rows].astype(F32), rows)
        for block in range(top):
            for piece in range(PIECES):
                hop(block, piece, part).wait_send()

    @pl.when(z < top)
    def _():
        for block in range(top):

            @pl.when(block < z)
            def _(block=block):
                for piece in range(PIECES):
                    rows = pieces[piece]
                    hop(block, piece, sums).wait_recv()
                    sums[block, rows] = (
                        part[block, rows].astype(F32) + came[block, rows].astype(F32)
                    ).astype(BF)
                    hop(block, piece, sums).start()

            @pl.when(block == z)
            def _(block=block):
                for piece in range(PIECES):
                    rows = pieces[piece]
                    hop(block, piece, sums).wait_recv()
                    store(part[block, rows].astype(F32) + came[block, rows].astype(F32), rows)

        for block in range(top):

            @pl.when(block < z)
            def _(block=block):
                for piece in range(PIECES):
                    hop(block, piece, sums).wait_send()

    cross.wait_recv()
    for level in range(planes):
        dout_ref[level] = (own[level] + came_out[level].astype(F32)).astype(BF)
    cross.wait_send()
    if plan:
        plan.wait()


def attend_back(operands, rb, planes, collective_id, slabs=(), swaps=(), tokens=()):
    q, kv, mid_all = operands[0], operands[1], operands[-1]
    levels = kv.shape[0]
    rows, width = q.shape
    plan = Exchange(planes, slabs, swaps, (), tokens, True) if slabs or swaps else None
    side = plan.arrays if plan else []
    heads = (2, 2 * rows, HD)
    column = (2, 2 * rows, 1)
    dout = (planes, rb, mid_all.shape[1])
    return pl.pallas_call(
        functools.partial(attend_back_kernel, planes, plan),
        out_shape=[jax.ShapeDtypeStruct((rows, 2 * width), BF), jax.ShapeDtypeStruct(dout, BF)]
        + (plan.out_shape if plan else []),
        in_specs=[VMEM] * len(operands) + [ANY] * len(side),
        out_specs=[VMEM] * 2 + [ANY] * len(side),
        scratch_shapes=[
            pltpu.VMEM(kv.shape, BF),
            pltpu.VMEM(kv.shape, BF),
            pltpu.VMEM(kv.shape, BF),
            pltpu.VMEM(heads, BF),
            pltpu.VMEM(heads, BF),
            pltpu.VMEM(column, F32),
            pltpu.VMEM(column, F32),
            pltpu.VMEM(heads, F32),
            pltpu.SemaphoreType.DMA((levels, PIECES)),
            pltpu.SemaphoreType.DMA((levels, PIECES)),
            pltpu.VMEM(dout, F32),
            pltpu.VMEM(dout, BF),
            pltpu.VMEM(dout, BF),
            pltpu.SemaphoreType.DMA((1,)),
            pltpu.SemaphoreType.DMA((1,)),
        ]
        + (plan.scratch if plan else []),
        compiler_params=params(collective_id),
        name="attend_back",
    )(*operands, *side)


def cut_weights(levels, l, rbf, weights, gains, qkv_out, gu_out):
    query, key, value, gate, up = weights
    qw, kw, fw = query.shape[2] // GROUP, key.shape[2] // GROUP, gate.shape[2] // GROUP
    q, k, v = [(w[l].astype(F32) * gains[0][l]).astype(BF) for w in (query, key, value)]
    for t in range(GROUP):
        qkv_out[0, t] = jnp.concatenate(
            [
                q[:, t * qw : (t + 1) * qw],
                k[:, t * kw : (t + 1) * kw],
                v[:, t * kw : (t + 1) * kw],
            ],
            axis=1,
        )

    def feed_forward():
        g, u = [(w[l].astype(F32) * gains[1][l]).astype(BF) for w in (gate, up)]
        for t in range(GROUP):
            pieces = []
            for w in (g, u):
                for core in range(2):
                    for level in range(levels):
                        at = t * fw + (2 * level + core) * rbf
                        pieces.append(w[:, at : at + rbf])
            gu_out[0, t] = jnp.concatenate(pieces, axis=1)

    return feed_forward


def start_kernel(levels, layers, rbf, plan, *refs):
    refs = list(refs)
    take = lambda n: [refs.pop(0) for _ in range(n)]
    sources, gains = take(5), take(2)
    out_weight, down_weight, lanes, tokens, cotangent = take(5)
    all_ref = take(1)[0]
    spread_out = take(2)
    cuts = [take(2) for _ in range(layers - 1)]
    plan_out = take(7)
    weights = take(5)
    qkv_cut, gu_cut, normed = take(3)
    load = take(1)[0]
    plan_sems, gather_sems, spread_sems = take(3), take(3), take(6)
    loads = [pltpu.make_async_copy(a, b, load.at[i]) for i, (a, b) in enumerate(zip(sources, weights))]
    for copy in loads:
        copy.start()
    ins = [qkv_cut, gu_cut, out_weight.at[0], down_weight.at[0], lanes, tokens, cotangent]
    plan.bind(ins, plan_out, *plan_sems)
    line = Line(levels)
    greet(line.partners + [line.other_core], plan)
    spread = Spread(line, False, [plan_out[0].at[0], plan_out[2]], spread_out, *spread_sems)
    gather = Gather(normed, all_ref, *gather_sems)
    plan.start([5])
    plan.start([2, 4])
    for copy in loads:
        copy.wait()
    columns = [g[...].astype(F32).T for g in gains]
    gains = [[g[:, l : l + 1] for l in range(layers)] for g in columns]
    feed_forward = cut_weights(levels, 0, rbf, weights, gains, qkv_cut, gu_cut)
    plan.start([0])
    feed_forward()
    plan.wait([0, 2])
    spread.start()
    plan.wait([5])
    values = plan_out[5][...].astype(F32)
    normed[...] = line_order((values * norm_scale(values)).astype(BF), levels)
    gather.start()
    plan.start([1, 3])
    plan.start([6])
    for l in range(1, layers):
        cut_weights(levels, l, rbf, weights, gains, *cuts[l - 1])()
    gather.relay()
    spread.relay(others=False)
    gather.finish()
    spread.relay(ends=False)
    spread.finish()
    plan.wait([1, 3, 4, 6])


def start(levels, weights, gains, out_weight, down_weight, lanes, tokens, cotangent, collective_id):
    query, key, _, gate, _ = weights
    layers, rb, _ = query.shape
    rbf = down_weight.shape[1]
    rows, width = tokens.shape
    wide = (query.shape[2] + 2 * key.shape[2]) // GROUP
    shape = jax.ShapeDtypeStruct
    qkv_cut = shape((1, GROUP, rb, wide), BF)
    gu_cut = shape((1, GROUP, rb, 2 * gate.shape[2] // GROUP), BF)
    one = lambda a: shape(a.shape[1:], a.dtype)
    plan = Exchange(
        levels,
        [qkv_cut, gu_cut],
        [one(out_weight), one(down_weight)],
        [lanes],
        [tokens, cotangent],
    )
    spreads = [qkv_cut.shape[1:], out_weight.shape[1:]]
    out_shape = [shape((GROUP, rows, width), BF)]
    out_shape += [shape((2, levels) + a, BF) for a in spreads]
    out_shape += [qkv_cut, gu_cut] * (layers - 1) + plan.out_shape
    out_specs = [VMEM] + [ANY] * 2 + [VMEM] * (2 * layers - 2) + [ANY] * 5 + [VMEM, ANY]
    dma = lambda n: pltpu.SemaphoreType.DMA((n,))
    return pl.pallas_call(
        functools.partial(start_kernel, levels, layers, rbf, plan),
        out_shape=out_shape,
        in_specs=[ANY] * 5 + [VMEM] * 2 + [ANY] * 5,
        out_specs=out_specs,
        scratch_shapes=[pltpu.VMEM(a.shape, BF) for a in weights]
        + [pltpu.VMEM(a.shape, BF) for a in (qkv_cut, gu_cut, tokens)]
        + [dma(5)]
        + plan.scratch
        + [dma(6), dma(6), dma(1)]
        + spread_scratch(2, levels),
        compiler_params=params(collective_id, 63),
        name="start",
    )(*weights, *gains, out_weight, down_weight, lanes, tokens, cotangent)


def finish_kernel(levels, layers, *refs):
    grads = [refs[4 * l : 4 * l + 4] for l in range(layers)]
    weights, gain1, gain2, outs = (
        refs[4 * layers : 4 * layers + 5],
        refs[4 * layers + 5],
        refs[4 * layers + 6],
        refs[4 * layers + 7 :],
    )
    query, key, value, output, gate, up, down, gain1_out, gain2_out = outs
    qw, kw, fw = query.shape[2] // GROUP, key.shape[2] // GROUP, gate.shape[2] // GROUP
    rbf = down.shape[1]
    for l in range(layers):
        qkv, out, gu, dn = grads[l]

        def place_columns(target, weight, gain, pieces, total):
            raw = jnp.concatenate(pieces, axis=1).astype(F32)
            target[l] = raw * gain[l]
            dots = jnp.sum(raw * weight[l].astype(F32), axis=1, keepdims=True)
            return dots if total is None else total + dots

        total = None
        for target, weight, first, n in (
            (query, weights[0], 0, qw),
            (key, weights[1], qw, kw),
            (value, weights[2], qw + kw, kw),
        ):
            pieces = [qkv[0, t, :, first : first + n] for t in range(GROUP)]
            total = place_columns(target, weight, gain1, pieces, total)
        gain1_out[l] = total
        output[l] = out[...].astype(F32)
        total = None
        for target, weight, base in ((gate, weights[3], 0), (up, weights[4], fw)):
            pieces = []
            for t in range(GROUP):
                for level in range(levels):
                    for core in range(2):
                        at = base + (core * levels + level) * rbf
                        pieces.append(gu[at // CW, t, :, at % CW : at % CW + rbf])
            total = place_columns(target, weight, gain2, pieces, total)
        gain2_out[l] = total
        down[l] = jnp.concatenate([dn[k] for k in range(dn.shape[0])], axis=1).astype(F32)


def finish(levels, grads, weights, output_weight, down_weight, gain1, gain2):
    layers, rb, _ = output_weight.shape
    like = lambda a: jax.ShapeDtypeStruct(a.shape, F32)
    query, key, value, gate, up = weights
    column = jax.ShapeDtypeStruct((layers, rb, 1), F32)
    operands = [a for layer in grads for a in layer] + list(weights) + [gain1, gain2]
    out_shape = [like(a) for a in (query, key, value, output_weight, gate, up, down_weight)]
    return pl.pallas_call(
        functools.partial(finish_kernel, levels, layers),
        out_shape=out_shape + [column, column],
        in_specs=[VMEM] * len(operands),
        out_specs=[VMEM] * 9,
        compiler_params=params(),
        name="finish",
    )(*operands)


def feed_forward_kernel(normed, gu, down, gate, up, active, parts, gu_here, down_here, arrived):
    wide = gate.shape[1]
    halves = wide // CW
    copies = []
    for h in range(halves):
        for first in (h * CW, wide + h * CW):
            columns = pl.ds(first, CW)
            copies.append((gu.at[:, columns], gu_here.at[:, columns]))
        rows = pl.ds(h * CW, CW)
        copies.append((down.at[rows], down_here.at[rows]))
    copies = [pltpu.make_async_copy(a, b, arrived.at[i]) for i, (a, b) in enumerate(copies)]
    for copy in copies:
        copy.start()
    total = None
    for h in range(halves):
        columns = pl.ds(h * CW, CW)
        copies[3 * h].wait()
        g = jnp.dot(normed[...], gu_here[:, columns], preferred_element_type=F32)
        copies[3 * h + 1].wait()
        u = jnp.dot(
            normed[...], gu_here[:, pl.ds(wide + h * CW, CW)], preferred_element_type=F32
        )
        gate[:, columns] = g.astype(BF)
        up[:, columns] = u.astype(BF)
        a = (g / (1.0 + jnp.exp(-g)) * u).astype(BF)
        active[:, columns] = a
        copies[3 * h + 2].wait()
        part = jnp.dot(a, down_here[columns], preferred_element_type=F32)
        total = part if total is None else total + part
    parts[...] = total.astype(BF)


def feed_forward(normed, gu, down):
    rows, width = normed.shape
    wide = down.shape[0]
    shape = jax.ShapeDtypeStruct
    return pl.pallas_call(
        feed_forward_kernel,
        out_shape=[
            shape((rows, wide), BF),
            shape((rows, wide), BF),
            shape((rows, wide), BF),
            shape((rows, width), BF),
        ],
        in_specs=[VMEM, ANY, ANY],
        out_specs=[VMEM] * 4,
        scratch_shapes=[
            pltpu.VMEM(gu.shape, BF),
            pltpu.VMEM(down.shape, BF),
            pltpu.SemaphoreType.DMA((3 * (wide // CW),)),
        ],
        compiler_params=params(),
        name="feed_forward",
    )(normed, gu, down)


def rope_tables(positions, head_width):
    frequency = THETA ** (-(jnp.arange(head_width // 2, dtype=F32) * 2.0 / head_width))
    angles = positions.astype(F32)[..., None] * frequency
    return (jnp.cos(angles), jnp.sin(angles))


def doc_positions(segments):
    places = jnp.arange(segments.shape[1], dtype=jnp.int32)
    starts_new = jnp.concatenate(
        [jnp.ones((segments.shape[0], 1), dtype=jnp.bool_), segments[:, 1:] != segments[:, :-1]],
        axis=1,
    )
    starts = lax.cummax(jnp.where(starts_new, places[None, :], 0), axis=1)
    return places[None, :] - starts


def on_device(
    levels,
    tokens,
    segments,
    cotangent,
    query_weight,
    key_weight,
    value_weight,
    output_weight,
    attention_gain,
    gate_weight,
    up_weight,
    down_weight,
    feedforward_gain,
):
    _, rows, width = tokens.shape
    full_len = segments.shape[1]
    layers = query_weight.shape[0]
    rb = query_weight.shape[1]
    rbf = down_weight.shape[1]
    kv_width = KVH * HD
    ffn = gate_weight.shape[2]
    qw, kw, fw = width // GROUP, kv_width // GROUP, ffn // GROUP
    group_rows = GROUP * rows
    _, c, z, _ = place()
    here = level_of(c, z, levels)
    n_ctx = 2 * levels
    lines = [
        [(gx * 2 + gc) * n_ctx + gz * 2 + gy for gc in range(2) for gz in range(levels)]
        for gx in range(2)
        for gy in range(2)
    ]
    core_lines = [
        [gs * n_ctx + gz * 2 + gy for gz in range(levels)] for gs in range(4) for gy in range(2)
    ]
    def gather_line(part):
        return lax.all_gather(part, AXES, axis=0, tiled=True, axis_index_groups=lines)

    def scatter_line(total):
        return lax.psum_scatter(
            total, AXES, scatter_dimension=0, tiled=True, axis_index_groups=core_lines
        )

    def after(value, *others):
        return lax.optimization_barrier((value,) + others)[0]

    gain1 = attention_gain.astype(F32)[:, :, None]
    gain2 = feedforward_gain.astype(F32)[:, :, None]
    lanes = segments.reshape(full_len // 128, 128)
    normed, qkv0, out0, *cuts = start(
        levels,
        [query_weight, key_weight, value_weight, gate_weight, up_weight],
        [attention_gain, feedforward_gain],
        output_weight,
        down_weight,
        lanes,
        tokens.reshape(rows, width),
        cotangent.reshape(rows, width),
        1,
    )
    cuts, (_, gu_own, _, down_own, all_segments, residual, cotangent) = cuts[:-7], cuts[-7:]
    qkv_slabs, gu_slabs = [None] + cuts[0::2], [None] + cuts[1::2]
    normed = normed.reshape(group_rows, width)

    def all_ffn(gu, down):
        return gather_line(gu.reshape(GROUP * rb, 2 * fw)), gather_line(down)

    own_segments = lax.dynamic_index_in_dim(
        all_segments.reshape(4, full_len), sequence_of(z, levels), 0
    )
    first = here * group_rows
    positions = lax.dynamic_slice_in_dim(doc_positions(own_segments)[0], first, group_rows)
    cosine, sine = rope_tables(positions, HD)
    row_segs = lax.dynamic_slice_in_dim(own_segments[0], first, group_rows)[:, None]
    key_segs = own_segments.reshape(levels // 2, 1, group_rows)

    def split(parts):
        return parts.astype(BF).reshape(GROUP, rows, width)

    def in_square(mode, parts, rows_in, collective_id, **more):
        out = list(square(mode, levels, split(parts), rows_in, collective_id, **more))
        if mode != "last":
            at = 2 if "second" in more else 1
            out[at] = out[at].reshape(group_rows, width)
        return out

    dot = functools.partial(jnp.dot, preferred_element_type=F32)

    qkv_full, out_full, gu_full, down_full = [[None] * layers for _ in range(4)]
    qkv_full[0], out_full[0] = qkv0, out0
    gu_full[0], down_full[0] = all_ffn(gu_own, down_own)
    residual = residual.astype(F32)
    stored = []
    for l in range(layers):
        weight = after(qkv_full[l].reshape(width, qw + 2 * kw), normed)
        q, kv, attended, lse = attend(
            [normed, weight, cosine, sine, row_segs, key_segs], levels, 5
        )
        out_full[l] = (
            after(out_full[l], attended)
            .reshape(2, levels, rb, width)
            .transpose(1, 0, 2, 3)
            .reshape(qw, width)
        )
        middle, normed2 = in_square("forward", dot(attended, out_full[l]), [residual], 4)
        if l < layers - 1:
            _, gu_own, _, down_own, qkv_full[l + 1], out_full[l + 1], *gathered = exchange(
                levels,
                [after(qkv_slabs[l + 1], normed2), gu_slabs[l + 1]],
                [(output_weight, l + 1), (down_weight, l + 1)],
                8,
                spread=True,
                own=cotangent if l == 0 else None,
            )
            up_all = gathered[0].reshape(group_rows, width) if l == 0 else up_all
            gu_full[l + 1], down_full[l + 1] = all_ffn(gu_own, down_own)
        if l < layers - 1:
            gu = after(gu_full[l], normed2)
            gate, up, active, parts = feed_forward(normed2, gu, after(down_full[l], gu))
        else:
            gu = dot(normed2, after(gu_full[l], normed2))
            gate, up = gu[:, :fw], gu[:, fw:]
            active = (jax.nn.silu(gate) * up).astype(BF)
            gate, up = gate.astype(BF), up.astype(BF)
        stored.append((residual, normed, q, kv, attended, lse, middle, normed2, gate, up, active))
        if l < layers - 1:
            residual, normed = in_square("forward", parts, [middle], 4)

    def dot_t(a, b):
        return lax.dot_general(a, b, (((1,), (1,)), ((), ())), preferred_element_type=F32)

    upstream = cotangent.astype(F32)
    ffn_grads, attention_grads, down_grads, grads = [[None] * layers for _ in range(4)]

    def in_slabs(l):
        qkv_grad, out_grad = attention_grads[l]
        gu_grad = ffn_grads[l][0].reshape(2 * fw // CW, GROUP, rb, CW)
        qkv_grad = qkv_grad.reshape(1, GROUP, rb, qw + 2 * kw)
        return [qkv_grad, gu_grad], [out_grad]

    for l in reversed(range(layers)):
        residual, normed, q, kv, attended, lse, middle, normed2, gate, up, active = stored[l]
        if l == layers - 1:
            down_total = ffn_gradient(levels, [(active, up_all)], 13)
        down_full[l] = after(down_full[l], down_total)
        if l == layers - 1:
            block = split(dot(active, down_full[l])), middle
        dactive = dot_t(up_all, down_full[l])
        gate, up = gate.astype(F32), up.astype(F32)
        sig = jax.nn.sigmoid(gate)
        dgate = (dactive * up * sig * (1.0 + gate * (1.0 - sig))).astype(BF)
        dup = (dactive * gate * sig).astype(BF)
        dgu = jnp.concatenate([dgate, dup], axis=1)
        ffn_total = ffn_gradient(levels, [(normed2, dgu)], 16)
        ffn_grads[l] = [scatter_line(total.reshape(-1, CW)) for total in (ffn_total, down_total)]
        dnorm2 = dot_t(after(dgu, ffn_total), gu_full[l]).astype(BF)
        dmiddle, mid_all = in_square("backward", dnorm2, [upstream, middle], 10)
        back = dot_t(mid_all, out_full[l]).astype(BF)
        operands = [q, kv, row_segs, key_segs, attended, lse, back, cosine, sine, mid_all]
        if l < layers - 1:
            slabs, swaps = in_slabs(l + 1)
            moved = [block_output] if l == layers - 2 else []
            swaps = [ffn_grads[l][1]] + swaps
            dqkv, out_total, *landed = attend_back(
                operands, rb, levels, 15, slabs, swaps, moved
            )
            block_output = landed.pop() if moved else block_output
            down_grads[l] = landed.pop(len(slabs))
            grads[l + 1] = landed + [down_grads[l + 1]]
        else:
            dqkv, out_total, down_grads[l] = attend_back(
                operands, rb, levels, 6, [], [ffn_grads[l][1]]
            )
        dnorm1 = dot_t(dqkv, qkv_full[l].reshape(width, qw + 2 * kw)).astype(BF)
        collect = normed, dqkv
        if l == layers - 1:
            upstream, block_output, up_all, qkv_grad, out_grad, down_total = in_square(
                "backward",
                dnorm1,
                [dmiddle, residual],
                14,
                collect=collect,
                ready=[out_total],
                second=block,
                left=stored[l - 1][-1],
            )
        elif l > 0:
            upstream, up_all, qkv_grad, out_grad, down_total = in_square(
                "backward",
                dnorm1,
                [dmiddle, residual],
                18,
                collect=collect,
                ready=[out_total],
                left=stored[l - 1][-1],
            )
        else:
            gu_grad, qkv_grad, out_grad, tokens_grad = in_square(
                "last",
                dnorm1,
                [dmiddle, residual],
                11,
                collect=collect,
                ready=[out_total],
                slab=ffn_grads[l][0].reshape(2 * fw // CW, GROUP, rb, CW),
            )
        attention_grads[l] = [qkv_grad, out_grad]

    grads[0] = [qkv_grad, gu_grad, out_grad, down_grads[0]]
    ordered = [
        [qkv, out, gu, down.reshape(width // CW, rbf, CW)] for qkv, gu, out, down in grads
    ]
    results = finish(
        levels,
        ordered,
        [query_weight, key_weight, value_weight, gate_weight, up_weight],
        output_weight,
        down_weight,
        gain1,
        gain2,
    )
    query, key, value, output, gate, up, down, gain1_grad, gain2_grad = results
    return (
        block_output.reshape(1, rows, width),
        tokens_grad.astype(F32).reshape(1, rows, width),
        query,
        key,
        value,
        output,
        gain1_grad[:, :, 0],
        gate,
        up,
        down,
        gain2_grad[:, :, 0],
    )


def solution(mesh):
    levels = mesh.shape["ctx"] // 2
    rows3 = P(None, AXES, None)
    gains = P(None, AXES)
    return jax.shard_map(
        functools.partial(on_device, levels),
        mesh=mesh,
        in_specs=(
            P("seq", "ctx", None),
            P("seq", None),
            P("seq", "ctx", None),
            rows3,
            rows3,
            rows3,
            rows3,
            gains,
            rows3,
            rows3,
            rows3,
            gains,
        ),
        out_specs=(
            P("seq", "ctx", None),
            P("seq", "ctx", None),
            rows3,
            rows3,
            rows3,
            rows3,
            gains,
            rows3,
            rows3,
            rows3,
            gains,
        ),
        check_vma=False,
    )
```
